32 devices in a mesh: rows: 16 (over z, y, core), seq: 2 (over x).
Axes of the slice: x: 2, y: 2, z: 4, core: 2. Of those that a mesh axis runs over, the one named last changes fastest.
Arguments:
- hidden_in: bfloat16 [16, 1280, 512], P('rows', 'seq'), may hold values from -6 to 6
- memory: bfloat16 [16, 256, 512], P('rows', 'seq'), may hold values from -6 to 6
- grad_out: bfloat16 [16, 1280, 512], P('rows', 'seq'), may hold values from -6 to 6
- seg_ids: int32 [16, 1280], P('rows'), may hold values from 0 to 2, as said below
- mem_seg_ids: int32 [16, 256], P('rows'), may hold values from 0 to 2, as said below
- gains: bfloat16 [5, 512], P(None, 'seq'), may hold values from 0.25 to 1.75
- qkv_first: bfloat16 [512, 1536], P('seq'), may hold values from -0.25 to 0.25
- query_cross: bfloat16 [512, 512], P('seq'), may hold values from -0.25 to 0.25
- kv_cross: bfloat16 [512, 1024], P('seq'), may hold values from -0.25 to 0.25
- out_first: bfloat16 [1024, 512], P(None, 'seq'), may hold values from -2 to 2
- taps_left: bfloat16 [11, 512], P(None, 'seq'), may hold values from -1.75 to 1.75
- proj_left: bfloat16 [512, 1024], P('seq'), may hold values from -0.25 to 0.25
- taps_right: bfloat16 [7, 512], P(None, 'seq'), may hold values from -2 to 2
- proj_right: bfloat16 [512, 256], P('seq'), may hold values from -0.25 to 0.25
- mid_gain: bfloat16 [1024], P('seq'), may hold values from 0.25 to 1.75
- taps_mid: bfloat16 [7, 1024], P(None, 'seq'), may hold values from -2 to 2
- proj_mid: bfloat16 [1024, 512], P(None, 'seq'), may hold values from -0.375 to 0.375
- qkv_second: bfloat16 [512, 1536], P('seq'), may hold values from -0.25 to 0.25
- out_second: bfloat16 [512, 512], P('seq'), may hold values from -2 to 2
- query_last: bfloat16 [512, 512], P('seq'), may hold values from -0.25 to 0.25
- kv_last: bfloat16 [512, 1024], P('seq'), may hold values from -0.25 to 0.25
- out_last: bfloat16 [512, 512], P('seq'), may hold values from -2 to 2
- ffn_up: bfloat16 [512, 2048], P('seq'), may hold values from -0.25 to 0.25
- ffn_down: bfloat16 [2048, 512], P(None, 'seq'), may hold values from -0.125 to 0.125
Outputs:
- output: bfloat16 [16, 1280, 512], P('rows', 'seq')
- grad_in: float32 [16, 1280, 512], P('rows', 'seq')
- grad_mem: float32 [16, 256, 512], P('rows', 'seq')
- grad_gains: float32 [5, 512], P(None, 'seq')
- grad_qkv_first: float32 [512, 1536], P('seq')
- grad_query_cross: float32 [512, 512], P('seq')
- grad_kv_cross: float32 [512, 1024], P('seq')
- grad_out_first: float32 [1024, 512], P(None, 'seq')
- grad_taps_left: float32 [11, 512], P(None, 'seq')
- grad_proj_left: float32 [512, 1024], P('seq')
- grad_taps_right: float32 [7, 512], P(None, 'seq')
- grad_proj_right: float32 [512, 256], P('seq')
- grad_mid_gain: float32 [1024], P('seq')
- grad_taps_mid: float32 [7, 1024], P(None, 'seq')
- grad_proj_mid: float32 [1024, 512], P(None, 'seq')
- grad_qkv_second: float32 [512, 1536], P('seq')
- grad_out_second: float32 [512, 512], P('seq')
- grad_query_last: float32 [512, 512], P('seq')
- grad_kv_last: float32 [512, 1024], P('seq')
- grad_out_last: float32 [512, 512], P('seq')
- grad_ffn_up: float32 [512, 2048], P('seq')
- grad_ffn_down: float32 [2048, 512], P(None, 'seq')
The draws below stay inside these ranges and needn't reach their ends.
Inputs may be any that keep to these rules, and one draw needn't show every extreme that they name: `seg_ids`: in every row the ids never fall along the positions, and 0, 1 and 2 each occur. `mem_seg_ids`: in every row the ids never fall along the positions, and 0, 1 and 2 each occur.
All inputs are finite; a program needn't handle non-finite values.
Results may differ from the reference program's by a relative error of at most 0.02.
Values may be sent and summed in bfloat16 or wider, within the bound.
A program may use at most 320 MiB of HBM per device.

```python
import jax
import jax.numpy as jnp
from jax import lax

D = 512
FF = 2048
H_SELF = 16
H_CROSS = 8
WIDE = 1024
NARROW = 256
LEFT_TAPS = 11
RIGHT_TAPS = 7
MEM_DEV = 128
ROW_LEN = 1280
ROW_TOK = 640
MEM_LEN = 256
N_ROWS = 16


def three_segments(key, row_count, length, per_device):
    first_key, last_key = jax.random.split(key)
    first_end = jax.random.randint(first_key, (row_count, 1), 1, per_device // 8 + 1)
    last_start = jax.random.randint(last_key, (row_count, 1), length - per_device // 8, length)
    spots = jnp.arange(length, dtype=jnp.int32)[None, :]
    return (spots >= first_end).astype(jnp.int32) + (spots >= last_start).astype(jnp.int32)


def draw_seg_ids(key, part):
    key = jax.random.fold_in(key, 3)
    return three_segments(key, N_ROWS, ROW_LEN, ROW_TOK)


def draw_mem_seg_ids(key, part):
    key = jax.random.fold_in(key, 5)
    return three_segments(key, N_ROWS, MEM_LEN, MEM_DEV)


def block_levels(stream_key, extent, cuts, least, top_value):
    def one(axis_at, parts):
        steps = jax.random.uniform(jax.random.fold_in(jax.random.fold_in(stream_key, 6), axis_at), (parts,), jnp.float32, least / len(cuts), top_value / len(cuts))
        return jnp.repeat(jnp.exp(steps), extent[axis_at] // parts).reshape((-1,) + (1,) * (len(extent) - axis_at - 1))

    factor_of = one(*cuts[0])
    for cut in cuts[1:]:
        factor_of = factor_of * one(*cut)
    return factor_of


def gaussian(own_key, shape, spread, bound, cuts=(), held_as=jnp.bfloat16):
    gain = block_levels(own_key, shape, cuts, -0.22, 0.18) if cuts else 1.0
    drawn = jax.random.normal(own_key, shape, jnp.float32) * spread * gain
    return jnp.minimum(jnp.maximum(drawn, -bound), bound).astype(held_as)


def setup_inputs(seed: int = 0) -> dict:
    splits = jax.random.split(jax.random.key(seed), 25)
    return {
        "hidden_in": gaussian(splits[0], (N_ROWS, ROW_LEN, D), 1.0, 6.0, ((0, 16), (1, 2))),
        "memory": gaussian(splits[1], (N_ROWS, MEM_LEN, D), 1.0, 6.0, ((0, 16), (1, 2))),
        "grad_out": gaussian(splits[2], (N_ROWS, ROW_LEN, D), 1.0, 6.0, ((0, 16), (1, 2))),
        "seg_ids": draw_seg_ids(jax.random.fold_in(splits[24], 71), 0),
        "mem_seg_ids": draw_mem_seg_ids(jax.random.fold_in(splits[24], 71), 0),
        "gains": jnp.clip(1.0 + 0.15 * jax.random.normal(splits[5], (5, D), jnp.float32), 0.25, 1.75).astype(jnp.bfloat16),
        "qkv_first": gaussian(splits[6], (D, 3 * D), D ** -0.5, 0.25, ((0, 2),)),
        "query_cross": gaussian(splits[7], (D, D), D ** -0.5, 0.25, ((0, 2),)),
        "kv_cross": gaussian(splits[8], (D, 2 * D), D ** -0.5, 0.25, ((0, 2),)),
        "out_first": gaussian(splits[9], (2 * D, D), (D // 64) ** -0.5, 2.0, ((1, 2),)),
        "taps_left": gaussian(splits[10], (LEFT_TAPS, D), LEFT_TAPS ** -0.5, 1.75, ((1, 2),)),
        "proj_left": gaussian(splits[11], (D, WIDE), D ** -0.5, 0.25, ((0, 2),)),
        "taps_right": gaussian(splits[12], (RIGHT_TAPS, D), RIGHT_TAPS ** -0.5, 2.0, ((1, 2),)),
        "proj_right": gaussian(splits[13], (D, NARROW), D ** -0.5, 0.25, ((0, 2),)),
        "mid_gain": jnp.clip(1.0 + 0.15 * jax.random.normal(splits[14], (WIDE,), jnp.float32), 0.25, 1.75).astype(jnp.bfloat16),
        "taps_mid": gaussian(splits[15], (RIGHT_TAPS, WIDE), RIGHT_TAPS ** -0.5, 2.0, ((1, 2),)),
        "proj_mid": gaussian(splits[16], (WIDE, D), (WIDE // 4) ** -0.5, 0.375, ((1, 2),)),
        "qkv_second": gaussian(splits[17], (D, 3 * D), D ** -0.5, 0.25, ((0, 2),)),
        "out_second": gaussian(splits[18], (D, D), (D // 64) ** -0.5, 2.0, ((0, 2),)),
        "query_last": gaussian(splits[19], (D, D), D ** -0.5, 0.25, ((0, 2),)),
        "kv_last": gaussian(splits[20], (D, 2 * D), D ** -0.5, 0.25, ((0, 2),)),
        "out_last": gaussian(splits[21], (D, D), (D // 64) ** -0.5, 2.0, ((0, 2),)),
        "ffn_up": gaussian(splits[22], (D, FF), D ** -0.5, 0.25, ((0, 2),)),
        "ffn_down": gaussian(splits[23], (FF, D), FF ** -0.5, 0.125, ((1, 2),)),
    }


HIGH = lax.Precision.HIGHEST
NEG_BIG = -1e+30
EPSILON = 1e-06

@jax.custom_vjp
def low(v):
    return lax.optimization_barrier(v.astype(jnp.bfloat16)).astype(jnp.float32)

@jax.custom_vjp
def low_back(v):
    return v

def low_keep(v):
    return (low(v), None)

def low_pass(kept, grad):
    return (grad,)

def back_keep(v):
    return (v, None)

def back_low(kept, grad):
    return (low(grad),)
low.defvjp(low_keep, low_pass)
low_back.defvjp(back_keep, back_low)

def both_ways(values):
    return low_back(low(values))

def matmul(first, second):
    return jnp.dot(first, second, precision=HIGH, preferred_element_type=jnp.float32)

def layer_norm(values, gain_vec):
    centre = values - lax.optimization_barrier(jnp.mean(values, axis=-1, keepdims=True))
    inverse = lax.rsqrt(lax.optimization_barrier(jnp.mean(centre * centre, axis=-1, keepdims=True)) + EPSILON)
    return centre * inverse * gain_vec

def attend(queries, keys, values, head_count, allowed):
    tok_count, model_width = queries.shape
    head_size = model_width // head_count
    query_heads = queries.reshape(tok_count, head_count, head_size)
    key_heads = keys.reshape(keys.shape[0], head_count, head_size)
    value_heads = values.reshape(values.shape[0], head_count, head_size)
    scores = jnp.einsum('qhd,khd->hqk', query_heads, key_heads, precision=HIGH) * head_size ** (-0.5)
    scores = low_back(jnp.where(allowed[None], scores, NEG_BIG))
    row_max = lax.optimization_barrier(jnp.max(scores, axis=-1, keepdims=True))
    exp_terms = jnp.exp(scores - row_max)
    weights = exp_terms / lax.optimization_barrier(jnp.sum(exp_terms, axis=-1, keepdims=True))
    mixed_out = jnp.einsum('hqk,khd->qhd', low(weights), value_heads, precision=HIGH)
    return mixed_out.reshape(tok_count, model_width)

def causal_conv(values, tap_weights, seg_row):
    tok_count = values.shape[0]
    reach = tap_weights.shape[0]
    padded = jnp.concatenate([jnp.zeros((reach - 1, values.shape[1]), values.dtype), values], 0)
    seg_padded = jnp.concatenate([jnp.full((reach - 1,), -1, jnp.int32), seg_row.astype(jnp.int32)], 0)
    result_sum = jnp.zeros_like(values)
    for offset in range(reach):
        lower = reach - 1 - offset
        window_rows = padded[lower:lower + tok_count]
        same_seg = (seg_padded[lower:lower + tok_count] == seg_row)[:, None]
        result_sum = result_sum + jnp.where(same_seg, window_rows, 0.0) * tap_weights[offset]
    return result_sum

def row_cell(inputs, mem_rows, seg_row, mem_seg, gains, qkv_first, query_cross, kv_cross, out_first, taps_left, proj_left, taps_right, proj_right, mid_gain, taps_mid, proj_mid, qkv_second, out_second, query_last, kv_last, out_last, ffn_up, ffn_down):
    tok_count, model_width = inputs.shape
    places = jnp.arange(tok_count, dtype=jnp.int32)
    self_mask = jnp.logical_and(seg_row[:, None] == seg_row[None, :], places[None, :] <= places[:, None])
    cross_mask = seg_row[:, None] == mem_seg[None, :]
    normed = low(layer_norm(inputs, gains[0]))
    packed = both_ways(matmul(normed, qkv_first))
    first_att = both_ways(attend(packed[:, :model_width], packed[:, model_width:2 * model_width], packed[:, 2 * model_width:], H_SELF, self_mask))
    pairs_b = low(matmul(mem_rows, kv_cross))
    query_b = both_ways(matmul(normed, query_cross))
    second_att = both_ways(attend(query_b, pairs_b[:, :model_width], pairs_b[:, model_width:], H_CROSS, cross_mask))
    hidden_b = inputs + low_back(matmul(jnp.concatenate([first_att, second_att], 1), out_first))
    normed = low(layer_norm(hidden_b, gains[1]))
    conv_l = low(causal_conv(normed, taps_left, seg_row))
    pre_l = low_back(matmul(conv_l, proj_left))
    conv_r = low(causal_conv(normed, taps_right, seg_row))
    pre_r = low_back(matmul(conv_r, proj_right))
    merged = jax.nn.silu(pre_l) + jnp.pad(pre_r, ((0, 0), (0, WIDE - NARROW)))
    mixed = low(layer_norm(merged, mid_gain))
    conv_m = low(causal_conv(mixed, taps_mid, seg_row))
    hidden_c = hidden_b + low_back(matmul(conv_m, proj_mid))
    normed = low(layer_norm(hidden_c, gains[2]))
    packed = both_ways(matmul(normed, qkv_second))
    third_att = both_ways(attend(packed[:, :model_width], packed[:, model_width:2 * model_width], packed[:, 2 * model_width:], H_CROSS, self_mask))
    hidden_d = hidden_c + low_back(matmul(third_att, out_second))
    normed = low(layer_norm(hidden_d, gains[3]))
    pairs_d = low(matmul(mem_rows, kv_last))
    query_d = both_ways(matmul(normed, query_last))
    fourth_att = both_ways(attend(query_d, pairs_d[:, :model_width], pairs_d[:, model_width:], H_CROSS, cross_mask))
    hidden_e = hidden_d + low_back(matmul(fourth_att, out_last))
    normed = low(layer_norm(hidden_e, gains[4]))
    up_pre = low_back(matmul(normed, ffn_up))
    return hidden_e + low_back(matmul(low(jax.nn.silu(up_pre)), ffn_down))

def reference(hidden_in, memory, grad_out, seg_ids, mem_seg_ids, gains, qkv_first, query_cross, kv_cross, out_first, taps_left, proj_left, taps_right, proj_right, mid_gain, taps_mid, proj_mid, qkv_second, out_second, query_last, kv_last, out_last, ffn_up, ffn_down):
    params = tuple((w.astype(jnp.float32) for w in (gains, qkv_first, query_cross, kv_cross, out_first, taps_left, proj_left, taps_right, proj_right, mid_gain, taps_mid, proj_mid, qkv_second, out_second, query_last, kv_last, out_last, ffn_up, ffn_down)))

    def one_row(totals, row_data):
        inputs, mem_rows, upstream, seg_row, mem_seg = row_data

        def forward(inputs, mem_rows, *weights):
            return row_cell(inputs, mem_rows, seg_row, mem_seg, *weights)
        result, pull = jax.vjp(forward, inputs, mem_rows, *params)
        grads = pull(upstream)
        totals = tuple((acc_now + piece for acc_now, piece in zip(totals, grads[2:])))
        return (totals, (result.astype(jnp.bfloat16), grads[0], grads[1]))
    zeros_start = tuple((jnp.zeros_like(w) for w in params))
    totals, (outputs, grad_in, grad_mem) = lax.scan(one_row, zeros_start, (hidden_in.astype(jnp.float32), memory.astype(jnp.float32), grad_out.astype(jnp.float32), seg_ids.astype(jnp.int32), mem_seg_ids.astype(jnp.int32)))
    return (outputs, grad_in, grad_mem, totals[0], totals[1], totals[2], totals[3], totals[4], totals[5], totals[6], totals[7], totals[8], totals[9], totals[10], totals[11], totals[12], totals[13], totals[14], totals[15], totals[16], totals[17], totals[18])
```

```python
import functools

import jax
import jax.numpy as jnp
from jax import lax
from jax.experimental import pallas as pl
from jax.experimental.pallas import tpu as pltpu
from jax.sharding import PartitionSpec as P

H_SELF = 16
H_CROSS = 8
WIDE = 1024
NARROW = 256
LEFT_TAPS = 11
RIGHT_TAPS = 7


NEG_BIG = -1e30
EPSILON = 1e-06


def rotated(block, axis, distance):
    size = lax.axis_size(axis)
    return lax.ppermute(block, axis, [((i + distance) % size, i) for i in range(size)])


def core_swapped(block):
    return lax.ppermute(block, "rows", [(i, i ^ 1) for i in range(lax.axis_size("rows"))])


def in_place_order(relative, dim):
    count = len(relative)
    place = lax.axis_index("seq")
    orders = [
        jnp.concatenate([relative[(p - me) % count] for p in range(count)], dim)
        for me in range(count)
    ]
    result = orders[0]
    for me in range(1, count):
        result = jnp.where(place == me, orders[me], result)
    return result


def gathered(block, dim=0):
    count = lax.axis_size("seq")
    return in_place_order([block] + [rotated(block, "seq", d) for d in range(1, count)], dim)


def core_half(shard):
    half = shard.shape[0] // 2
    return lax.dynamic_slice_in_dim(shard, (lax.axis_index("rows") & 1) * half, half)


def flat_half(shard, dim):
    part = core_half(shard)
    if dim == 0:
        return part
    width = shard.shape[1]
    blocks = part.reshape(-1, width // 2, width)
    return jnp.swapaxes(blocks, 0, 1).reshape(width // 2, -1)


def unflat_half(part, shape, dim):
    if dim == 0:
        return part
    width = shape[1]
    blocks = part.reshape(width // 2, -1, width)
    return jnp.swapaxes(blocks, 0, 1).reshape(shape[0] // 2, width)


def group_gather(shards, dims, earlier):
    packed = jnp.concatenate([flat_half(shard, dim) for shard, dim in zip(shards, dims)], 1)
    packed, _ = after(packed, earlier)
    core = lax.axis_index("rows") & 1
    pieces = []
    for d in range(1, lax.axis_size("seq")):
        same = rotated(packed, "seq", d)
        pieces.append((same, core_swapped(same)))
    results = []
    offset = 0
    for shard, dim in zip(shards, dims):
        size = shard.size // 2 // packed.shape[0]
        relative = [shard]
        for same, other in pieces:
            same = unflat_half(same[:, offset : offset + size], shard.shape, dim)
            other = unflat_half(other[:, offset : offset + size], shard.shape, dim)
            relative.append(
                jnp.where(core == 0, jnp.concatenate([same, other], 0), jnp.concatenate([other, same], 0))
            )
        results.append(in_place_order(relative, dim))
        offset = offset + size
    return results, pieces[-1][0]


def small_gather(shards, dims, earlier):
    sizes = [shard.size for shard in shards]
    flat = jnp.concatenate([shard.reshape(-1) for shard in shards])
    flat, _ = after(padded_rows(flat, 2048, 0).reshape(-1, 128), earlier)
    parts = [flat] + [rotated(flat, "seq", d) for d in range(1, lax.axis_size("seq"))]
    parts = [part.reshape(-1) for part in parts]
    results = []
    offset = 0
    for shard, dim, size in zip(shards, dims, sizes):
        relative = [part[offset : offset + size].reshape(shard.shape) for part in parts]
        results.append(in_place_order(relative, dim))
        offset = offset + size
    return results, parts[-1]


def padded_rows(block, multiple, dim):
    extra = -block.shape[dim] % multiple
    if not extra:
        return block
    widths = [(0, 0)] * block.ndim
    widths[dim] = (0, extra)
    return jnp.pad(block, widths)


def small_columns(grads, width):
    seq_count = lax.axis_size("seq")
    rows = [
        jnp.moveaxis(grad.reshape(-1, seq_count, grad.shape[-1] // (seq_count * width), width), 1, 2).reshape(
            -1, seq_count * width
        )
        for grad in grads
    ]
    return padded_rows(jnp.concatenate(rows, 0), 128, 0).T.astype(jnp.bfloat16)


def small_shares(columns, grads, width):
    seq_count = lax.axis_size("seq")
    rows = columns.T
    results = []
    offset = 0
    for grad in grads:
        count = grad.size // (seq_count * width)
        shape = grad.shape[:-1] + (grad.shape[-1] // seq_count,)
        results.append(rows[offset : offset + count].reshape(shape))
        offset = offset + count
    return results


def halved_sum(block, axis, bit, dim):
    half = block.shape[dim] // 2
    upper = ((lax.axis_index(axis) & bit) != 0).astype(jnp.int32)
    kept = lax.dynamic_slice_in_dim(block, upper * half, half, dim)
    sent = lax.dynamic_slice_in_dim(block, (1 - upper) * half, half, dim)
    got = lax.ppermute(sent, axis, [(i, i ^ bit) for i in range(lax.axis_size(axis))])
    return (kept.astype(jnp.float32) + got.astype(jnp.float32)).astype(jnp.bfloat16)


def row_sum_owned(partial):
    bit = lax.axis_size("seq") // 2
    while bit:
        partial = halved_sum(partial, "seq", bit, 0)
        bit = bit // 2
    return partial.astype(jnp.float32)


def after(values, others):
    return lax.optimization_barrier((values, others))


def offload_rows(packed):
    seq_count = lax.axis_size("seq")
    row_count = lax.axis_size("rows")
    blocks = packed.reshape(seq_count, row_count, -1, packed.shape[1])
    blocks = jnp.swapaxes(blocks, 0, 1).reshape(packed.shape)
    return lax.psum_scatter(blocks, "rows", scatter_dimension=0, tiled=True)


def offload_seq(blocks):
    return lax.psum_scatter(blocks, "seq", scatter_dimension=0, tiled=True)


def offload_back(share):
    return lax.all_gather(share, "rows", axis=0, tiled=True)


def passed_along(block, axis, distance):
    devices = range(lax.axis_size(axis))
    route = [(i - distance, i) for i in devices if i - distance in devices]
    return lax.ppermute(block, axis, route)


def layer_norm(values, gain_vec):
    centre = values - jnp.mean(values, axis=-1, keepdims=True)
    inverse = lax.rsqrt(jnp.mean(centre * centre, axis=-1, keepdims=True) + EPSILON)
    return centre * inverse * gain_vec


def norm_back(values, gain_vec, upstream):
    centre = values - jnp.mean(values, axis=-1, keepdims=True)
    inverse = lax.rsqrt(jnp.mean(centre * centre, axis=-1, keepdims=True) + EPSILON)
    normed = centre * inverse
    scaled = upstream * gain_vec
    d_values = inverse * (
        scaled
        - jnp.mean(scaled, axis=-1, keepdims=True)
        - normed * jnp.mean(scaled * normed, axis=-1, keepdims=True)
    )
    return (d_values, jnp.sum(upstream * normed, axis=0))


def swish_slope(pre_act):
    sigma = jax.nn.sigmoid(pre_act)
    return sigma * (1.0 + pre_act * (1.0 - sigma))


def plain_dot(first, second):
    return jnp.dot(first, second, preferred_element_type=jnp.float32)


def left_dot(first, second):
    return jnp.einsum("nk,nm->km", first, second, preferred_element_type=jnp.float32)


def right_dot(grads_in, weight):
    return jnp.einsum("nm,km->nk", grads_in, weight, preferred_element_type=jnp.float32)


TILE = 256
SEG_ROWS = 16
LOG2E = 1.4426950408889634


def tiles_of(extent):
    return [(low, min(low + TILE, extent)) for low in range(0, extent, TILE)]


def tn_dot(first, second):
    return lax.dot_general(first, second, (((0,), (0,)), ((), ())), preferred_element_type=jnp.float32)


def nn_dot(first, second):
    return lax.dot_general(first, second, (((1,), (0,)), ((), ())), preferred_element_type=jnp.float32)


def nt_dot(first, second):
    return lax.dot_general(first, second, (((1,), (1,)), ((), ())), preferred_element_type=jnp.float32)


def row_numbers(width):
    return lax.broadcasted_iota(jnp.int32, (SEG_ROWS, width), 0)


def split_low(values, count):
    pieces = []
    for _ in range(count):
        piece = values.astype(jnp.bfloat16).astype(jnp.float32)
        pieces.append(piece)
        values = values - piece
    return pieces


def key_marks(key_seg, ones):
    rows = row_numbers(key_seg.shape[1])
    marked = jnp.logical_or(rows == key_seg, jnp.logical_and(rows >= 3, rows < 3 + ones))
    return jnp.where(marked, 1.0, 0.0).astype(jnp.bfloat16)


def query_marks(query_seg):
    rows = row_numbers(query_seg.shape[1])
    other = jnp.logical_and(rows < 3, rows != query_seg)
    return jnp.where(other, NEG_BIG, 0.0)


def with_rows(marks, first, pieces):
    rows = row_numbers(marks.shape[1])
    for k, piece in enumerate(pieces):
        marks = jnp.where(rows == first + k, piece, marks)
    return marks.astype(jnp.bfloat16)


def triangle(scores, low):
    key_at = lax.broadcasted_iota(jnp.int32, scores.shape, 0)
    query_at = lax.broadcasted_iota(jnp.int32, scores.shape, 1) + low
    return jnp.where(key_at <= query_at, scores, NEG_BIG)


def masked_scores(key_block, query_block, low, causal):
    scores = tn_dot(key_block, query_block)
    if not causal:
        return scores
    if low == 0:
        return triangle(scores, 0)
    return jnp.concatenate([scores[:low], triangle(scores[low:], 0)], 0)


def attend_kernel(heads, causal, place_ref, qt_ref, pair_ref, qseg_ref, kseg_ref, ot_ref, total_ref, kmark_ref):
    width, tokens = qt_ref.shape
    size = width // heads
    factor = size ** (-0.5) * LOG2E
    block = tokens if causal else pair_ref.shape[1]
    place = place_ref[0] if causal else 0
    kmark_ref[...] = key_marks(kseg_ref[...], 0)
    value_marks = jnp.where(row_numbers(block) == 0, 1.0, 0.0).astype(jnp.bfloat16)
    qmarks = query_marks(qseg_ref[...]).astype(jnp.bfloat16)

    def one_head(head, carry):
        own = pl.ds(pl.multiple_of(head * size, size), size)
        also = pl.ds(pl.multiple_of(width + head * size, size), size)
        query_rows = jnp.concatenate([qt_ref[own, :], qmarks], 0)

        def keys_at(start, count):
            lanes = pl.ds(pl.multiple_of(start, 128), count)
            return (
                jnp.concatenate([pair_ref[own, lanes], kmark_ref[:, lanes]], 0),
                jnp.concatenate([pair_ref[also, lanes], value_marks[:, :count]], 0),
            )

        for low, high in tiles_of(tokens):
            query_tile = query_rows[:, low:high]
            count = high if causal else block
            key_rows, value_rows = keys_at(place * block, count)
            scores = masked_scores(key_rows, query_tile, low, causal)
            peak = jnp.max(scores, axis=0, keepdims=True)
            weights = jnp.exp2((scores - peak) * factor).astype(jnp.bfloat16)
            summed = nn_dot(value_rows, weights)
            if causal:

                def earlier(step, state):
                    peak, summed = state
                    key_rows, value_rows = keys_at(step * block, block)
                    scores = tn_dot(key_rows, query_tile)
                    new_peak = jnp.maximum(peak, jnp.max(scores, axis=0, keepdims=True))
                    weights = jnp.exp2((scores - new_peak) * factor).astype(jnp.bfloat16)
                    summed = summed * jnp.exp2((peak - new_peak) * factor) + nn_dot(value_rows, weights)
                    return (new_peak, summed)

                peak, summed = lax.fori_loop(0, place, earlier, (peak, summed))
            total = summed[size : size + 1]
            ot_ref[own, low:high] = (summed[:size] / total).astype(jnp.bfloat16)
            total_ref[head, :, low:high] = peak + jnp.log2(total) / factor
        return carry

    lax.fori_loop(0, heads, one_head, 0)


def attend_back_kernel(
    heads, causal, place_ref, qt_ref, pair_ref, gt_ref, ot_ref, total_ref, qseg_ref, kseg_ref,
    dq_ref, dpair_ref, kmark_ref, dkh_ref, dvh_ref,
):
    width, tokens = qt_ref.shape
    size = width // heads
    scale = size ** (-0.5)
    factor = scale * LOG2E
    block = tokens if causal else pair_ref.shape[1]
    place = place_ref[0] if causal else 0
    kmark_ref[...] = key_marks(kseg_ref[...], 3)
    value_marks = jnp.where(row_numbers(block) < 2, 1.0, 0.0).astype(jnp.bfloat16)
    qmarks = query_marks(qseg_ref[...])

    def one_head(head, carry):
        own = pl.ds(pl.multiple_of(head * size, size), size)
        also = pl.ds(pl.multiple_of(width + head * size, size), size)
        query_plain = qt_ref[own, :]
        grad_plain = gt_ref[own, :]
        delta = jnp.sum(
            grad_plain.astype(jnp.float32) * ot_ref[own, :].astype(jnp.float32), axis=0, keepdims=True
        )
        total = total_ref[head]
        query_rows = jnp.concatenate([query_plain, with_rows(qmarks, 3, split_low(-total, 3))], 0)
        grad_rows = jnp.concatenate(
            [grad_plain, with_rows(jnp.zeros_like(qmarks), 0, split_low(-delta, 2))], 0
        )
        dkh_ref[...] = jnp.zeros_like(dkh_ref)
        dvh_ref[...] = jnp.zeros_like(dvh_ref)

        def on_block(start, count, low, high, diagonal):
            lanes = pl.ds(pl.multiple_of(start, 128), count)
            key_plain = pair_ref[own, lanes]
            key_rows = jnp.concatenate([key_plain, kmark_ref[:, lanes]], 0)
            value_rows = jnp.concatenate([pair_ref[also, lanes], value_marks[:, :count]], 0)
            scores = masked_scores(key_rows, query_rows[:, low:high], low, diagonal)
            weights = jnp.exp2(scores * factor)
            slopes = tn_dot(value_rows, grad_rows[:, low:high])
            d_scores = (weights * slopes).astype(jnp.bfloat16)
            dvh_ref[:, lanes] += nt_dot(grad_plain[:, low:high], weights.astype(jnp.bfloat16))
            dkh_ref[:, lanes] += nt_dot(query_plain[:, low:high], d_scores)
            return nn_dot(key_plain, d_scores)

        for low, high in tiles_of(tokens):
            d_query = on_block(place * block, high if causal else block, low, high, causal)
            if causal:
                d_query = lax.fori_loop(
                    0,
                    place,
                    lambda step, held: held + on_block(step * block, block, low, high, False),
                    d_query,
                )
            dq_ref[own, low:high] = (d_query * scale).astype(jnp.bfloat16)
        dpair_ref[own, :] = (dkh_ref[...] * scale).astype(jnp.bfloat16)
        dpair_ref[also, :] = dvh_ref[...].astype(jnp.bfloat16)
        return carry

    lax.fori_loop(0, heads, one_head, 0)


IN_SMEM = pl.BlockSpec(memory_space=pltpu.SMEM)
IN_VMEM = pl.BlockSpec(memory_space=pltpu.VMEM)
KERNEL_VMEM = 48 * 2**20


LANE_GROUP = 128
SPACING = 2


def share_sum_kernel(
    grad_ref, out_ref, core_ref, pair_ref, across_ref, near_ref, near_got_ref, part_ref, piece_ref, send_sem, recv_sem
):
    seq_count, _, half, total = grad_ref.shape
    far_count = lax.axis_size("rows") // 4
    row, place = lax.axis_index("rows"), lax.axis_index("seq")
    core, near, far = lax.rem(row, 2), lax.rem(row // 2, 2), row // 4
    mate = (row + 1 - 2 * core, place)
    close = (row + 2 - 4 * near, place)
    peers = [None] + [
        (lax.rem(far + d, far_count) * 4 + near * 2 + core, place) for d in range(1, far_count)
    ]
    sides = [None] + [(row, lax.rem(place + d, seq_count)) for d in range(1, seq_count)]
    step = 2 * far_count * LANE_GROUP
    wide = far_count * LANE_GROUP
    count = total // step

    barrier = pltpu.get_barrier_semaphore()
    friends = [mate, close] + peers[1:] + sides[1:]
    for friend in friends:
        pl.semaphore_signal(barrier, inc=1, device_id=friend, device_id_type=pl.DeviceIdType.MESH)
    pl.semaphore_wait(barrier, len(friends))

    def copy(chunk, slot, source, target, device):
        return pltpu.make_async_remote_copy(
            src_ref=source,
            dst_ref=target,
            send_sem=send_sem.at[chunk, slot],
            recv_sem=recv_sem.at[chunk, slot],
            device_id=device,
            device_id_type=pl.DeviceIdType.MESH,
        )

    first_side = 1
    near_slot = first_side + seq_count - 1
    first_peer = near_slot + 1
    first_back = first_peer + far_count - 1
    near_back_slot = first_back + far_count - 1
    last_slot = near_back_slot + 1

    def columns(chunk):
        return slice(chunk * step, (chunk + 1) * step)

    def core_copy(chunk):
        return copy(chunk, 0, grad_ref.at[:, 1 - core, :, columns(chunk)], core_ref.at[chunk], mate)

    def side_copy(chunk, d):
        away = lax.rem(place + d, seq_count)
        return copy(chunk, first_side + d - 1, pair_ref.at[chunk, away], across_ref.at[chunk, d - 1], sides[d])

    def near_copy(chunk):
        return copy(chunk, near_slot, near_ref.at[chunk, 1 - near], near_got_ref.at[chunk], close)

    def peer_copy(chunk, d):
        away = lax.rem(far + d, far_count)
        return copy(chunk, first_peer + d - 1, part_ref.at[chunk, away], piece_ref.at[chunk, d - 1], peers[d])

    def own_piece(chunk):
        start = chunk * step + near * wide + far * LANE_GROUP
        return out_ref.at[core, :, pl.ds(pl.multiple_of(start, LANE_GROUP), LANE_GROUP)]

    def back_copy(chunk, d):
        return copy(chunk, first_back + d - 1, own_piece(chunk), own_piece(chunk), peers[d])

    def near_back(chunk):
        start = chunk * step + near * wide
        block = out_ref.at[core, :, pl.ds(pl.multiple_of(start, LANE_GROUP), wide)]
        return copy(chunk, near_back_slot, block, block, close)

    def last_copy(chunk):
        block = out_ref.at[core, :, columns(chunk)]
        return copy(chunk, last_slot, block, block, mate)

    def stage_core(chunk):
        core_copy(chunk).start()

    def stage_side(chunk):
        core_copy(chunk).wait_recv()
        kept = grad_ref[:, core, :, columns(chunk)].astype(jnp.float32)
        pair_ref[chunk] = (kept + core_ref[chunk].astype(jnp.float32)).astype(jnp.bfloat16)
        for d in range(1, seq_count):
            side_copy(chunk, d).start()

    def stage_near(chunk):
        for d in range(1, seq_count):
            side_copy(chunk, d).wait_recv()
        summed = pair_ref[chunk, place].astype(jnp.float32)
        for d in range(1, seq_count):
            summed = summed + across_ref[chunk, d - 1].astype(jnp.float32)
        summed = summed.astype(jnp.bfloat16)
        for side in range(2):
            near_ref[chunk, side] = summed[:, side * wide : (side + 1) * wide]
        near_copy(chunk).start()

    def stage_peer(chunk):
        near_copy(chunk).wait_recv()
        summed = near_ref[chunk, near].astype(jnp.float32) + near_got_ref[chunk].astype(jnp.float32)
        summed = summed.astype(jnp.bfloat16)
        for piece in range(far_count):
            part_ref[chunk, piece] = summed[:, piece * LANE_GROUP : (piece + 1) * LANE_GROUP]
        for d in range(1, far_count):
            peer_copy(chunk, d).start()

    def stage_back(chunk):
        for d in range(1, far_count):
            peer_copy(chunk, d).wait_recv()
        summed = part_ref[chunk, far].astype(jnp.float32)
        for d in range(1, far_count):
            summed = summed + piece_ref[chunk, d - 1].astype(jnp.float32)
        own_piece(chunk)[...] = summed.astype(jnp.bfloat16)
        for d in range(1, far_count):
            back_copy(chunk, d).start()

    def stage_near_back(chunk):
        for d in range(1, far_count):
            back_copy(chunk, d).wait_recv()
        near_back(chunk).start()

    def stage_last(chunk):
        near_back(chunk).wait_recv()
        last_copy(chunk).start()

    def stage_done(chunk):
        last_copy(chunk).wait_recv()
        core_copy(chunk).wait_send()
        for d in range(1, seq_count):
            side_copy(chunk, d).wait_send()
        near_copy(chunk).wait_send()
        for d in range(1, far_count):
            peer_copy(chunk, d).wait_send()
            back_copy(chunk, d).wait_send()
        near_back(chunk).wait_send()
        last_copy(chunk).wait_send()

    for chunk in range(count):
        stage_core(chunk)
    for chunk in range(count):
        stage_side(chunk)
    stages = (stage_near, stage_peer, stage_back, stage_near_back, stage_last, stage_done)
    for tick in range(count + SPACING * (len(stages) - 1)):
        for late, stage in enumerate(stages):
            if 0 <= tick - SPACING * late < count:
                stage(tick - SPACING * late)


def share_summed(packed):
    seq_count = lax.axis_size("seq")
    far_count = lax.axis_size("rows") // 4
    half = packed.shape[0] // (2 * seq_count)
    step = 2 * far_count * LANE_GROUP
    packed = padded_rows(packed, step, 1)
    total = packed.shape[1]
    count = total // step
    slots = 4 + (seq_count - 1) + 2 * (far_count - 1)
    low = jnp.bfloat16
    out = pl.pallas_call(
        share_sum_kernel,
        out_shape=jax.ShapeDtypeStruct((2, half, total), low),
        in_specs=[IN_VMEM],
        out_specs=IN_VMEM,
        scratch_shapes=[
            pltpu.VMEM((count, seq_count, half, step), low),
            pltpu.VMEM((count, seq_count, half, step), low),
            pltpu.VMEM((count, seq_count - 1, half, step), low),
            pltpu.VMEM((count, 2, half, step // 2), low),
            pltpu.VMEM((count, half, step // 2), low),
            pltpu.VMEM((count, far_count, half, LANE_GROUP), low),
            pltpu.VMEM((count, far_count - 1, half, LANE_GROUP), low),
            pltpu.SemaphoreType.DMA((count, slots)),
            pltpu.SemaphoreType.DMA((count, slots)),
        ],
        compiler_params=pltpu.CompilerParams(
            collective_id=0, has_side_effects=True, vmem_limit_bytes=KERNEL_VMEM
        ),
        name="share_sum",
    )(packed.reshape(seq_count, 2, half, total))
    return out.reshape(2 * half, total)


def attend_forward(queries, pairs_t, heads, causal, query_seg, key_seg):
    width, tokens = queries.shape
    total_keys = pairs_t.shape[1]
    pairs = heads * tokens * total_keys
    return pl.pallas_call(
        functools.partial(attend_kernel, heads, causal),
        out_shape=(
            jax.ShapeDtypeStruct((width, tokens), jnp.bfloat16),
            jax.ShapeDtypeStruct((heads, 1, tokens), jnp.float32),
        ),
        in_specs=[IN_SMEM] + [IN_VMEM] * 4,
        out_specs=(IN_VMEM, IN_VMEM),
        scratch_shapes=[pltpu.VMEM((SEG_ROWS, total_keys), jnp.bfloat16)],
        compiler_params=pltpu.CompilerParams(vmem_limit_bytes=KERNEL_VMEM),
        cost_estimate=pl.CostEstimate(
            flops=pairs * 600, bytes_accessed=4 * width * total_keys, transcendentals=pairs
        ),
        name="attend_fwd",
    )(lax.axis_index("seq").reshape(1), queries, pairs_t, query_seg[None], key_seg[None])


def attend_back(queries, pairs_t, grads, outs, totals, heads, causal, query_seg, key_seg):
    width, tokens = queries.shape
    total_keys = pairs_t.shape[1]
    pairs = heads * tokens * total_keys
    size = width // heads
    return pl.pallas_call(
        functools.partial(attend_back_kernel, heads, causal),
        out_shape=(
            jax.ShapeDtypeStruct((width, tokens), jnp.bfloat16),
            jax.ShapeDtypeStruct((2 * width, total_keys), jnp.bfloat16),
        ),
        in_specs=[IN_SMEM] + [IN_VMEM] * 7,
        out_specs=(IN_VMEM, IN_VMEM),
        scratch_shapes=[
            pltpu.VMEM((SEG_ROWS, total_keys), jnp.bfloat16),
            pltpu.VMEM((size, total_keys), jnp.float32),
            pltpu.VMEM((size, total_keys), jnp.float32),
        ],
        compiler_params=pltpu.CompilerParams(vmem_limit_bytes=KERNEL_VMEM),
        cost_estimate=pl.CostEstimate(
            flops=pairs * 1500, bytes_accessed=8 * width * total_keys, transcendentals=pairs
        ),
        name="attend_bwd",
    )(
        lax.axis_index("seq").reshape(1), queries, pairs_t, grads, outs, totals,
        query_seg[None], key_seg[None],
    )


RIM = 16
ROW_TILE = 64


def row_tiles(extent, tile):
    return [(low, min(low + tile, extent)) for low in range(0, extent, tile)]


def halves_of(extent):
    middle = -(-extent // 32) * 16
    return [(0, middle), (middle, extent)]


def group_lanes(group):
    return pl.ds(pl.multiple_of(group * 128, 128), 128)


def wide_rows(column, width=128):
    return jnp.broadcast_to(column, (column.shape[0], width))


def loop_rows(extent, tile, body):
    def step(k, carry):
        body(pl.ds(pl.multiple_of(k * tile, tile), tile))
        return carry

    lax.fori_loop(0, extent // tile, step, 0)


def rows_normed(values):
    centre = values - jnp.mean(values, axis=-1, keepdims=True)
    inverse = lax.rsqrt(jnp.mean(centre * centre, axis=-1, keepdims=True) + EPSILON)
    return centre * inverse, inverse


def rows_norm_back(normed, inverse, gain_vec, upstream):
    scaled = upstream * gain_vec
    return inverse * (
        scaled
        - jnp.mean(scaled, axis=-1, keepdims=True)
        - normed * jnp.mean(scaled * normed, axis=-1, keepdims=True)
    )


def taps_forward(source_ref, first_row, since, lanes, low, high, weights):
    result = None
    for offset, weight in enumerate(weights):
        start = first_row + low - offset
        window = source_ref[start : start + high - low, lanes]
        if offset:
            window = jnp.where(since >= offset, window, 0.0)
        term = window * weight
        result = term if result is None else result + term
    return result


def conv_fwd_kernel(
    h1_ref, a2_ref, rim_ref, since_ref, tl_ref, tr_ref, tm_ref, mgain_ref, gain_ref, pl_ref, pr_ref, pm_ref,
    cl_ref, cr_ref, cm_ref, h2_ref, a3_ref,
    ext_ref, wide_ref, cle_ref, cre_ref, up_ref, mixed_ref,
):
    tokens, width = h1_ref.shape
    total = tokens + RIM
    narrow = pr_ref.shape[1]
    ext_ref[0:RIM, :] = jnp.zeros((RIM, width), jnp.float32)
    ext_ref[RIM : 2 * RIM, :] = rim_ref[...].astype(jnp.float32)
    ext_ref[2 * RIM :, :] = a2_ref[...].astype(jnp.float32)
    wide_ref[...] = wide_rows(since_ref[...])

    def first_convs(group, carry):
        lanes = group_lanes(group)
        left = [tl_ref[j : j + 1, lanes] for j in range(tl_ref.shape[0])]
        right = [tr_ref[j : j + 1, lanes] for j in range(tr_ref.shape[0])]
        for low, high in row_tiles(total, ROW_TILE):
            since = wide_ref[low:high, :]
            cle_ref[low:high, lanes] = taps_forward(ext_ref, RIM, since, lanes, low, high, left).astype(jnp.bfloat16)
            cre_ref[low:high, lanes] = taps_forward(ext_ref, RIM, since, lanes, low, high, right).astype(jnp.bfloat16)
        return carry

    lax.fori_loop(0, width // 128, first_convs, 0)
    cl_ref[...] = cle_ref[RIM:, :]
    cr_ref[...] = cre_ref[RIM:, :]
    for low, high in halves_of(total):
        up_ref[low:high, :] = nn_dot(cle_ref[low:high, :], pl_ref[...])
        mixed_ref[low:high, :narrow] = nn_dot(cre_ref[low:high, :], pr_ref[...])

    def merge_rows(rows):
        pre = up_ref[rows, :]
        merged = pre / (1.0 + jnp.exp(-pre))
        merged = jnp.concatenate([merged[:, :narrow] + mixed_ref[rows, :narrow], merged[:, narrow:]], 1)
        normed, _ = rows_normed(merged)
        mixed_ref[rows, :] = (normed * mgain_ref[...]).astype(jnp.bfloat16).astype(jnp.float32)

    loop_rows(total, 16, merge_rows)

    def mid_conv(group, carry):
        lanes = group_lanes(group)
        weights = [tm_ref[j : j + 1, lanes] for j in range(tm_ref.shape[0])]
        for low, high in row_tiles(tokens, ROW_TILE):
            since = wide_ref[RIM + low : RIM + high, :]
            cm_ref[low:high, lanes] = taps_forward(mixed_ref, RIM, since, lanes, low, high, weights).astype(jnp.bfloat16)
        return carry

    lax.fori_loop(0, mixed_ref.shape[1] // 128, mid_conv, 0)
    for low, high in halves_of(tokens):
        h2_ref[low:high, :] = h1_ref[low:high, :] + nn_dot(cm_ref[low:high, :], pm_ref[...])

    def norm_rows(rows):
        normed, _ = rows_normed(h2_ref[rows, :])
        a3_ref[rows, :] = (normed * gain_ref[...]).astype(jnp.bfloat16)

    loop_rows(tokens, 32, norm_rows)


def conv_forward(h1, a2, rim, since, taps_l, taps_r, taps_m, mid_gain, gain, proj_left, proj_right, proj_mid):
    tokens, width = h1.shape
    wide = proj_left.shape[1]
    total = tokens + RIM
    low, full = jnp.bfloat16, jnp.float32
    return pl.pallas_call(
        conv_fwd_kernel,
        out_shape=(
            jax.ShapeDtypeStruct((tokens, width), low),
            jax.ShapeDtypeStruct((tokens, width), low),
            jax.ShapeDtypeStruct((tokens, wide), low),
            jax.ShapeDtypeStruct((tokens, width), full),
            jax.ShapeDtypeStruct((tokens, width), low),
        ),
        in_specs=[IN_VMEM] * 12,
        out_specs=(IN_VMEM,) * 5,
        scratch_shapes=[
            pltpu.VMEM((total + RIM, width), full),
            pltpu.VMEM((total, 128), jnp.int32),
            pltpu.VMEM((total, width), low),
            pltpu.VMEM((total, width), low),
            pltpu.VMEM((total, wide), full),
            pltpu.VMEM((total, wide), full),
        ],
        compiler_params=pltpu.CompilerParams(vmem_limit_bytes=KERNEL_VMEM),
        cost_estimate=pl.CostEstimate(
            flops=tokens * width * wide * 20, bytes_accessed=tokens * width * 16, transcendentals=tokens * wide
        ),
        name="conv_fwd",
    )(h1, a2, rim, since, taps_l, taps_r, taps_m, mid_gain, gain, proj_left, proj_right, proj_mid)


def folded(values):
    return jnp.sum(values.reshape(-1, 8, values.shape[-1]), axis=0)


def taps_back(grad_ref, value, left, lanes, low, high, weights, result, sums):
    for offset, weight in enumerate(weights):
        window = grad_ref[low + offset : high + offset, lanes]
        if offset:
            window = jnp.where(left >= offset, window, 0.0)
        term = window * weight
        result = term if result is None else result + term
        if value is not None:
            product = folded(window * value)
            sums[offset] = product if sums[offset] is None else sums[offset] + product
    return result


def conv_bwd_kernel(
    g2_ref, brim_ref, cl_ref, clrim_ref, cr_ref, crrim_ref, cm_ref, a2_ref, h1_ref, left_ref,
    tl_ref, tr_ref, tm_ref, mgain_ref, gain_ref, pl_ref, pr_ref, pm_ref,
    g1_ref, dw_ref, dtl_ref, dtr_ref, dtm_ref, dmgain_ref, dgain_ref,
    bext_ref, cle_ref, cre_ref, wide_ref, grad_ref, up_ref, back_ref, normed_ref, inv_ref, dpl_ref, dpr_ref, a2f_ref,
):
    tokens, width = g2_ref.shape
    total = tokens + RIM
    wide, narrow = pl_ref.shape[1], pr_ref.shape[1]
    bext_ref[:tokens, :] = g2_ref[...].astype(jnp.bfloat16)
    bext_ref[tokens:, :] = brim_ref[...]
    cle_ref[:tokens, :] = cl_ref[...]
    cle_ref[tokens:, :] = clrim_ref[...]
    cre_ref[:tokens, :] = cr_ref[...]
    cre_ref[tokens:, :] = crrim_ref[...]
    a2f_ref[...] = a2_ref[...].astype(jnp.float32)
    wide_ref[...] = wide_rows(left_ref[...])
    grad_ref[total:, :] = jnp.zeros((RIM, wide), jnp.float32)
    dw_ref[:, :wide] = tn_dot(bext_ref[:tokens, :], cm_ref[...]).astype(jnp.bfloat16)
    for low, high in halves_of(total):
        grad_ref[low:high, :] = nt_dot(bext_ref[low:high, :], pm_ref[...])
        up_ref[low:high, :] = nn_dot(cle_ref[low:high, :], pl_ref[...])
        back_ref[low:high, :narrow] = nn_dot(cre_ref[low:high, :], pr_ref[...])

    def merge_rows(rows):
        pre = up_ref[rows, :]
        merged = pre / (1.0 + jnp.exp(-pre))
        merged = jnp.concatenate([merged[:, :narrow] + back_ref[rows, :narrow], merged[:, narrow:]], 1)
        normed, inverse = rows_normed(merged)
        normed_ref[rows, :] = normed
        inv_ref[rows, :] = wide_rows(inverse)

    loop_rows(total, 16, merge_rows)

    def mid_back(group, carry):
        lanes = group_lanes(group)
        weights = [tm_ref[j : j + 1, lanes] for j in range(tm_ref.shape[0])]
        sums = [None] * len(weights)
        gain_vec = mgain_ref[:, lanes]
        for low, high in row_tiles(total, ROW_TILE):
            value = None
            if high <= tokens:
                value = (normed_ref[low:high, lanes] * gain_vec).astype(jnp.bfloat16).astype(jnp.float32)
            back_ref[low:high, lanes] = taps_back(
                grad_ref, value, wide_ref[low:high, :], lanes, low, high, weights, None, sums
            )
        for j, piece in enumerate(sums):
            dtm_ref[j : j + 1, lanes] = jnp.sum(piece, axis=0, keepdims=True)
        return carry

    lax.fori_loop(0, wide // 128, mid_back, 0)

    def merge_back(rows):
        pre = up_ref[rows, :]
        normed = normed_ref[rows, :]
        d_merged = rows_norm_back(normed, inv_ref[rows, :][:, :1], mgain_ref[...], back_ref[rows, :])
        sigma = 1.0 / (1.0 + jnp.exp(-pre))
        dpl_ref[rows, :] = (d_merged * (sigma * (1.0 + pre * (1.0 - sigma)))).astype(jnp.bfloat16)
        dpr_ref[rows, :] = d_merged[:, :narrow].astype(jnp.bfloat16)

    loop_rows(total, 16, merge_back)
    gain_sum = jnp.zeros((8, wide), jnp.float32)

    def gain_rows(k, held):
        rows = pl.ds(pl.multiple_of(k * 16, 16), 16)
        return held + folded(back_ref[rows, :] * normed_ref[rows, :])

    gain_sum = lax.fori_loop(0, tokens // 16, gain_rows, gain_sum)
    dmgain_ref[...] = jnp.sum(gain_sum, axis=0, keepdims=True)
    dw_ref[:, wide : 2 * wide] = tn_dot(cle_ref[:tokens, :], dpl_ref[:tokens, :]).astype(jnp.bfloat16)
    dw_ref[:, 2 * wide :] = tn_dot(cre_ref[:tokens, :], dpr_ref[:tokens, :]).astype(jnp.bfloat16)
    for low, high in halves_of(total):
        grad_ref[low:high, :width] = nt_dot(dpl_ref[low:high, :], pl_ref[...])
        grad_ref[low:high, width : 2 * width] = nt_dot(dpr_ref[low:high, :], pr_ref[...])

    def first_back(group, carry):
        lanes = group_lanes(group)
        other = group_lanes(group + width // 128)
        weights_l = [tl_ref[j : j + 1, lanes] for j in range(tl_ref.shape[0])]
        weights_r = [tr_ref[j : j + 1, lanes] for j in range(tr_ref.shape[0])]
        sums_l = [None] * len(weights_l)
        sums_r = [None] * len(weights_r)
        for low, high in row_tiles(tokens, ROW_TILE):
            left = wide_ref[low:high, :]
            value = a2f_ref[low:high, lanes]
            held = taps_back(grad_ref, value, left, lanes, low, high, weights_l, None, sums_l)
            held = taps_back(grad_ref, value, left, other, low, high, weights_r, held, sums_r)
            back_ref[low:high, lanes] = held
        for j, piece in enumerate(sums_l):
            dtl_ref[j : j + 1, lanes] = jnp.sum(piece, axis=0, keepdims=True)
        for j, piece in enumerate(sums_r):
            dtr_ref[j : j + 1, lanes] = jnp.sum(piece, axis=0, keepdims=True)
        return carry

    lax.fori_loop(0, width // 128, first_back, 0)

    def finish(k, held):
        rows = pl.ds(pl.multiple_of(k * 32, 32), 32)
        normed, inverse = rows_normed(h1_ref[rows, :])
        upstream = back_ref[rows, :width]
        g1_ref[rows, :] = g2_ref[rows, :] + rows_norm_back(normed, inverse, gain_ref[...], upstream)
        return held + folded(upstream * normed)

    gain_sum = lax.fori_loop(0, tokens // 32, finish, jnp.zeros((8, width), jnp.float32))
    dgain_ref[...] = jnp.sum(gain_sum, axis=0, keepdims=True)


def conv_back(
    g2, brim, c_l, c_r, rims, c_m, a2, h1, left, taps_l, taps_r, taps_m, mid_gain, gain, proj_left, proj_right, proj_mid
):
    tokens, width = g2.shape
    wide, narrow = proj_left.shape[1], proj_right.shape[1]
    total = tokens + RIM
    low, full = jnp.bfloat16, jnp.float32
    return pl.pallas_call(
        conv_bwd_kernel,
        out_shape=(
            jax.ShapeDtypeStruct((tokens, width), full),
            jax.ShapeDtypeStruct((width, 2 * wide + narrow), low),
            jax.ShapeDtypeStruct(taps_l.shape, full),
            jax.ShapeDtypeStruct(taps_r.shape, full),
            jax.ShapeDtypeStruct(taps_m.shape, full),
            jax.ShapeDtypeStruct((1, wide), full),
            jax.ShapeDtypeStruct((1, width), full),
        ),
        in_specs=[IN_VMEM] * 18,
        out_specs=(IN_VMEM,) * 7,
        scratch_shapes=[
            pltpu.VMEM((total, width), low),
            pltpu.VMEM((total, width), low),
            pltpu.VMEM((total, width), low),
            pltpu.VMEM((total, 128), jnp.int32),
            pltpu.VMEM((total + RIM, wide), full),
            pltpu.VMEM((total, wide), full),
            pltpu.VMEM((total, wide), full),
            pltpu.VMEM((total, wide), full),
            pltpu.VMEM((total, 128), full),
            pltpu.VMEM((total, wide), low),
            pltpu.VMEM((total, narrow), low),
            pltpu.VMEM((tokens, width), full),
        ],
        compiler_params=pltpu.CompilerParams(vmem_limit_bytes=KERNEL_VMEM),
        cost_estimate=pl.CostEstimate(
            flops=tokens * width * wide * 40, bytes_accessed=tokens * width * 40, transcendentals=tokens * wide
        ),
        name="conv_bwd",
    )(
        g2, brim, c_l, rims[:, :width], c_r, rims[:, width:], c_m, a2, h1, left,
        taps_l, taps_r, taps_m, mid_gain, gain, proj_left, proj_right, proj_mid,
    )


def segment_reach(seg_row):
    length = seg_row.shape[0]
    first = jnp.sum(seg_row == 0)
    second = first + jnp.sum(seg_row == 1)
    spots = jnp.arange(length, dtype=jnp.int32)
    start = jnp.where(seg_row == 0, 0, jnp.where(seg_row == 1, first, second))
    stop = jnp.where(seg_row == 0, first, jnp.where(seg_row == 1, second, length))
    return spots - start, stop - 1 - spots


def turned_dot(weight, values):
    return jnp.einsum("kn,tk->nt", weight, values, preferred_element_type=jnp.float32)


def out_dot(turned, weight):
    return jnp.einsum("nt,nk->tk", turned, weight, preferred_element_type=jnp.float32)


def weight_dot(values, turned):
    return jnp.einsum("tk,nt->kn", values, turned, preferred_element_type=jnp.float32)


def out_weight_dot(turned, grads_in):
    return jnp.einsum("nt,tk->kn", turned, grads_in, preferred_element_type=jnp.float32)


def turned_back(grads_in, weight):
    return jnp.einsum("tk,nk->nt", grads_in, weight, preferred_element_type=jnp.float32)


def input_back(turned, weight):
    return jnp.einsum("nt,kn->tk", turned, weight, preferred_element_type=jnp.float32)


def self_attend(normed, normed_row, weight, head_count, own_seg, seg_row):
    model_width = normed.shape[1]
    queries = turned_dot(weight[:, :model_width], normed).astype(jnp.bfloat16)
    pairs = turned_dot(weight[:, model_width:], normed_row).astype(jnp.bfloat16)
    att_out, totals = attend_forward(queries, pairs, head_count, True, own_seg, seg_row)
    return (att_out, totals, queries, pairs, normed_row)


def self_back(normed, weight, grad_att, kept, head_count, own_seg, seg_row):
    att_out, totals, queries, pairs, normed_row = kept
    model_width = normed.shape[1]
    d_query, d_pairs = attend_back(
        queries, pairs, grad_att, att_out, totals, head_count, True, own_seg, seg_row
    )
    d_weight = jnp.concatenate([weight_dot(normed, d_query), weight_dot(normed_row, d_pairs)], 1)
    d_normed = input_back(d_query, weight[:, :model_width]) + row_sum_owned(
        input_back(d_pairs, weight[:, model_width:]).astype(jnp.bfloat16)
    )
    return (d_normed, d_weight)


def local(
    hidden_in,
    memory,
    grad_out,
    seg_ids,
    mem_seg_ids,
    gains,
    qkv_first,
    query_cross,
    kv_cross,
    out_first,
    taps_left,
    proj_left,
    taps_right,
    proj_right,
    mid_gain,
    taps_mid,
    proj_mid,
    qkv_second,
    out_second,
    query_last,
    kv_last,
    out_last,
    ffn_up,
    ffn_down,
):
    shards = (
        gains,
        qkv_first,
        query_cross,
        kv_cross,
        out_first,
        taps_left,
        proj_left,
        taps_right,
        proj_right,
        mid_gain,
        taps_mid,
        proj_mid,
        qkv_second,
        out_second,
        query_last,
        kv_last,
        out_last,
        ffn_up,
        ffn_down,
    )
    shard_dims = (1, 0, 0, 0, 1, 1, 0, 1, 0, 0, 1, 1, 0, 0, 0, 0, 0, 0, 1)
    small = (0, 5, 7, 9, 10)
    fulls = [None] * len(shards)
    row_inputs = gathered(hidden_in[0])
    found, earlier = small_gather([shards[k] for k in small], [shard_dims[k] for k in small], row_inputs)
    for k, whole in zip(small, found):
        fulls[k] = whole
    for group in ((1,), (2, 3), (4, 6, 8, 11)):
        if group == (2, 3):
            mem_rows = gathered(after(memory[0], earlier)[0])
        found, arrived = group_gather([shards[k] for k in group], [shard_dims[k] for k in group], earlier)
        if group == (1,):
            earlier = arrived
        for k, whole in zip(group, found):
            fulls[k] = whole
    (
        gains,
        qkv_first,
        query_cross,
        kv_cross,
        out_first,
        taps_left,
        proj_left,
        taps_right,
        proj_right,
        mid_gain,
        taps_mid,
        proj_mid,
        *_,
    ) = fulls
    inputs = hidden_in[0].astype(jnp.float32)
    seg_row = seg_ids[0]
    mem_seg = mem_seg_ids[0]
    tok_count, model_width = inputs.shape
    row_start = lax.axis_index("seq") * tok_count
    own_seg = lax.dynamic_slice_in_dim(seg_row, row_start, tok_count)
    since, left = segment_reach(seg_row)
    since = lax.dynamic_slice_in_dim(jnp.pad(since, (RIM, 0)), row_start, tok_count + RIM)[:, None]
    left = lax.dynamic_slice_in_dim(jnp.pad(left, (0, RIM)), row_start, tok_count + RIM)[:, None]
    gain_rows = gains.astype(jnp.float32)
    mid_gain_f = mid_gain.astype(jnp.float32)
    left_taps = taps_left.astype(jnp.float32)
    right_taps = taps_right.astype(jnp.float32)
    mid_taps = taps_mid.astype(jnp.float32)
    pairs_b = turned_dot(kv_cross, mem_rows).astype(jnp.bfloat16)
    normed_a = layer_norm(inputs, gain_rows[0]).astype(jnp.bfloat16)
    normed_row = layer_norm(row_inputs.astype(jnp.float32), gain_rows[0]).astype(jnp.bfloat16)
    kept_a = self_attend(normed_a, normed_row, qkv_first, H_SELF, own_seg, seg_row)
    query_b = turned_dot(query_cross, normed_a).astype(jnp.bfloat16)
    out_b, total_b = attend_forward(query_b, pairs_b, H_CROSS, False, own_seg, mem_seg)
    hidden_b = (
        inputs
        + out_dot(kept_a[0], out_first[:model_width])
        + out_dot(out_b, out_first[model_width:])
    )
    normed_c = layer_norm(hidden_b, gain_rows[1]).astype(jnp.bfloat16)
    (qkv_second, out_second, query_last, kv_last, out_last), _ = group_gather(
        shards[12:17], shard_dims[12:17], hidden_b
    )
    conv_l, conv_r, conv_m, hidden_c, normed_d = conv_forward(
        hidden_b,
        normed_c,
        passed_along(normed_c[tok_count - RIM :], "seq", 1),
        since,
        left_taps,
        right_taps,
        mid_taps,
        mid_gain_f[None],
        gain_rows[2:3],
        proj_left,
        proj_right,
        proj_mid,
    )
    (ffn_up, ffn_down), _ = group_gather(shards[17:], shard_dims[17:], hidden_c)
    pairs_d = turned_dot(kv_last, mem_rows).astype(jnp.bfloat16)
    conv_rims = passed_along(jnp.concatenate([conv_l[:RIM], conv_r[:RIM]], 1), "seq", -1)
    kept_c = self_attend(normed_d, gathered(normed_d), qkv_second, H_CROSS, own_seg, seg_row)
    att_c = kept_c[0]
    hidden_d = hidden_c + out_dot(att_c, out_second)
    normed_e = layer_norm(hidden_d, gain_rows[3]).astype(jnp.bfloat16)
    query_d = turned_dot(query_last, normed_e).astype(jnp.bfloat16)
    att_d, total_d = attend_forward(query_d, pairs_d, H_CROSS, False, own_seg, mem_seg)
    hidden_e = hidden_d + out_dot(att_d, out_last)
    normed_f = layer_norm(hidden_e, gain_rows[4]).astype(jnp.bfloat16)
    up_pre = plain_dot(normed_f, ffn_up)
    activ_low = jax.nn.silu(up_pre).astype(jnp.bfloat16)
    result = hidden_e + plain_dot(activ_low, ffn_down)
    grad_now = grad_out[0].astype(jnp.float32)
    branch = grad_now.astype(jnp.bfloat16)
    d_ffn_down = left_dot(branch, activ_low)
    d_up = (right_dot(branch, ffn_down) * swish_slope(up_pre)).astype(jnp.bfloat16)
    d_ffn_up = left_dot(normed_f, d_up)
    part_a = offload_rows(jnp.concatenate([d_ffn_up, d_ffn_down], 1).astype(jnp.bfloat16))
    d_hidden, g_five = norm_back(hidden_e, gain_rows[4], right_dot(d_up, ffn_up))
    grad_now = grad_now + d_hidden
    branch = grad_now.astype(jnp.bfloat16)
    d_out_last = out_weight_dot(att_d, branch)
    d_att = turned_back(branch, out_last).astype(jnp.bfloat16)
    dq_d, dkv_d = attend_back(
        query_d, pairs_d, d_att, att_d, total_d, H_CROSS, False, own_seg, mem_seg
    )
    d_query_last = weight_dot(normed_e, dq_d)
    d_hidden, g_four = norm_back(hidden_d, gain_rows[3], input_back(dq_d, query_last))
    grad_now = grad_now + d_hidden
    branch = grad_now.astype(jnp.bfloat16)
    d_out_second = out_weight_dot(att_c, branch)
    d_att = turned_back(branch, out_second).astype(jnp.bfloat16)
    d_normed, d_qkv_second = self_back(
        normed_d, qkv_second, d_att, kept_c, H_CROSS, own_seg, seg_row
    )
    d_kv_last = weight_dot(mem_rows, dkv_d)
    part_b = offload_rows(
        jnp.concatenate([d_out_last.T, d_query_last, d_kv_last, d_qkv_second, d_out_second.T], 1).astype(jnp.bfloat16)
    )
    d_hidden, g_three = norm_back(hidden_c, gain_rows[2], d_normed)
    grad_now = grad_now + d_hidden
    branch = grad_now.astype(jnp.bfloat16)
    grad_now, part_a = after(grad_now, part_a)
    part_a = offload_seq(part_a)
    grad_now, d_projections, d_taps_left, d_taps_right, d_taps_mid, d_mid_gain, g_two = conv_back(
        grad_now,
        passed_along(branch[:RIM], "seq", -1),
        conv_l,
        conv_r,
        conv_rims,
        conv_m,
        normed_c,
        hidden_b,
        left,
        left_taps,
        right_taps,
        mid_taps,
        mid_gain_f[None],
        gain_rows[1:2],
        proj_left,
        proj_right,
        proj_mid,
    )
    d_mid_gain, g_two = d_mid_gain[0], g_two[0]
    branch = grad_now.astype(jnp.bfloat16)
    d_out_first = jnp.concatenate(
        [out_weight_dot(kept_a[0], branch), out_weight_dot(out_b, branch)], 1
    )
    branch, (part_a, part_b) = after(branch, (part_a, part_b))
    part_a = offload_back(part_a)
    part_b = offload_seq(part_b)
    d_att_a = turned_back(branch, out_first[:model_width]).astype(jnp.bfloat16)
    d_att_b = turned_back(branch, out_first[model_width:]).astype(jnp.bfloat16)
    dq_b, dkv_b = attend_back(
        query_b, pairs_b, d_att_b, out_b, total_b, H_CROSS, False, own_seg, mem_seg
    )
    d_query_cross = weight_dot(normed_a, dq_b)
    d_normed, d_qkv_first = self_back(
        normed_a, qkv_first, d_att_a, kept_a, H_SELF, own_seg, seg_row
    )
    d_normed, part_b = after(d_normed, part_b)
    part_b = offload_back(part_b)
    d_normed = d_normed + input_back(dq_b, query_cross)
    d_hidden, g_one = norm_back(inputs, gain_rows[0], d_normed)
    grad_in = grad_now + d_hidden
    grad_mem = row_sum_owned(
        (input_back(dkv_b, kv_cross) + input_back(dkv_d, kv_last)).astype(jnp.bfloat16)
    )
    d_kv_cross = weight_dot(mem_rows, dkv_b)
    d_gains = jnp.stack([g_one, g_two, g_three, g_four, g_five], 0)
    wide, narrow = proj_left.shape[1], proj_right.shape[1]
    width = model_width // lax.axis_size("seq")
    small_grads = (d_gains, d_taps_left, d_taps_right, d_mid_gain, d_taps_mid)
    last = [d_projections] + [
        piece.astype(jnp.bfloat16) for piece in (d_out_first, d_kv_cross, d_query_cross, d_qkv_first)
    ]
    last.append(small_columns(small_grads, width))
    part_c = share_summed(jnp.concatenate(last, 1))
    shares = [None] * len(shards)
    up = ffn_up.shape[1]
    for part, group, sizes in (
        (part_a, (17, 18), (up, up)),
        (
            part_b,
            (16, 14, 15, 12, 13),
            (model_width, model_width, 2 * model_width, 3 * model_width, model_width),
        ),
        (
            part_c,
            (11, 6, 8, 4, 3, 2, 1),
            (wide, wide, narrow, 2 * model_width, 2 * model_width, model_width, 3 * model_width),
        ),
    ):
        offset = 0
        for k, size in zip(group, sizes):
            piece = part[:, offset : offset + size].astype(jnp.float32)
            shares[k] = piece if shard_dims[k] == 0 else piece.T
            offset = offset + size
    parts = small_shares(part_c[:, offset : offset + 128].astype(jnp.float32), small_grads, width)
    for k, piece in zip(small, parts):
        shares[k] = piece
    return (
        result.astype(jnp.bfloat16)[None],
        grad_in[None],
        grad_mem[None],
        shares[0],
        shares[1],
        shares[2],
        shares[3],
        shares[4],
        shares[5],
        shares[6],
        shares[7],
        shares[8],
        shares[9],
        shares[10],
        shares[11],
        shares[12],
        shares[13],
        shares[14],
        shares[15],
        shares[16],
        shares[17],
        shares[18],
    )


def solution(mesh):
    placed = (
        P("rows", "seq", None),
        P("rows", "seq", None),
        P("rows", "seq", None),
        P("rows", None),
        P("rows", None),
        P(None, "seq"),
        P("seq", None),
        P("seq", None),
        P("seq", None),
        P(None, "seq"),
        P(None, "seq"),
        P("seq", None),
        P(None, "seq"),
        P("seq", None),
        P("seq"),
        P(None, "seq"),
        P(None, "seq"),
        P("seq", None),
        P("seq", None),
        P("seq", None),
        P("seq", None),
        P("seq", None),
        P("seq", None),
        P(None, "seq"),
    )
    return jax.shard_map(
        local,
        mesh=mesh,
        in_specs=placed,
        out_specs=(
            P("rows", "seq", None),
            P("rows", "seq", None),
            P("rows", "seq", None),
            P(None, "seq"),
            P("seq", None),
            P("seq", None),
            P("seq", None),
            P(None, "seq"),
            P(None, "seq"),
            P("seq", None),
            P(None, "seq"),
            P("seq", None),
            P("seq"),
            P(None, "seq"),
            P(None, "seq"),
            P("seq", None),
            P("seq", None),
            P("seq", None),
            P("seq", None),
            P("seq", None),
            P("seq", None),
            P(None, "seq"),
        ),
        check_vma=False,
    )
```

```python
import functools

import jax
import jax.numpy as jnp
from jax import lax
from jax.experimental import pallas as pl
from jax.experimental.pallas import tpu as pltpu
from jax.sharding import PartitionSpec as P

H_SELF = 16
H_CROSS = 8
WIDE = 1024
NARROW = 256
LEFT_TAPS = 11
RIGHT_TAPS = 7


NEG_BIG = -1e30
EPSILON = 1e-06


def rotated(block, axis, distance):
    size = lax.axis_size(axis)
    return lax.ppermute(block, axis, [((i + distance) % size, i) for i in range(size)])


def core_swapped(block):
    return lax.ppermute(block, "rows", [(i, i ^ 1) for i in range(lax.axis_size("rows"))])


def in_place_order(relative, dim):
    count = len(relative)
    place = lax.axis_index("seq")
    orders = [
        jnp.concatenate([relative[(p - me) % count] for p in range(count)], dim)
        for me in range(count)
    ]
    result = orders[0]
    for me in range(1, count):
        result = jnp.where(place == me, orders[me], result)
    return result


def gathered(block, dim=0):
    count = lax.axis_size("seq")
    return in_place_order([block] + [rotated(block, "seq", d) for d in range(1, count)], dim)


def near_swapped(block):
    return lax.ppermute(block, "rows", [(i, i ^ 2) for i in range(lax.axis_size("rows"))])


def flat_share(shard, dim, index, count):
    size = shard.shape[0] // count
    part = lax.dynamic_slice_in_dim(shard, index * size, size)
    if dim == 0:
        return part
    width = shard.shape[1]
    blocks = part.reshape(-1, width // count, width)
    return jnp.swapaxes(blocks, 0, 1).reshape(width // count, -1)


def unflat_share(part, shape, dim, count):
    if dim == 0:
        return part
    width = shape[1]
    blocks = part.reshape(width // count, -1, width)
    return jnp.swapaxes(blocks, 0, 1).reshape(shape[0] // count, width)


def seq_rotated(packed):
    return [rotated(packed, "seq", d) for d in range(1, lax.axis_size("seq"))]


def packed_half(shards, dims):
    core = lax.axis_index("rows") & 1
    return jnp.concatenate([flat_share(shard, dim, core, 2) for shard, dim in zip(shards, dims)], 1)


def packed_quarter(shards, dims):
    index = lax.axis_index("rows") & 3
    return jnp.concatenate([flat_share(shard, dim, index, 4) for shard, dim in zip(shards, dims)], 1)


def ordered(bit, first, second):
    return jnp.where(bit == 0, jnp.concatenate([first, second], 0), jnp.concatenate([second, first], 0))


def joined_weight(shard, dim, pieces, offset, count):
    row = lax.axis_index("rows")
    size = shard.size // count // pieces[0].shape[0]

    def part(piece):
        return unflat_share(piece[:, offset : offset + size], shard.shape, dim, count)

    relative = [shard]
    if count == 2:
        for k in range(0, len(pieces), 2):
            relative.append(ordered(row & 1, part(pieces[k]), part(pieces[k + 1])))
    else:
        for k in range(0, len(pieces), 3):
            same, near, across = pieces[k : k + 3]
            rows = same.shape[0]
            own_pair = ordered(row & 1, part(same), part(across[:rows]))
            near_pair = ordered(row & 1, part(near), part(across[rows:]))
            relative.append(ordered(row & 2, own_pair, near_pair))
    return in_place_order(relative, dim), offset + size


def joined_group(shards, dims, pieces, count):
    results = []
    offset = 0
    for shard, dim in zip(shards, dims):
        full, offset = joined_weight(shard, dim, pieces, offset, count)
        results.append(full)
    return results


def interleaved(*lists):
    return [item for items in zip(*lists) for item in items]


def small_gather(shards, dims):
    sizes = [shard.size for shard in shards]
    flat = jnp.concatenate([shard.reshape(-1) for shard in shards])
    flat = padded_rows(flat, 2048, 0).reshape(-1, 128)
    parts = [flat] + [rotated(flat, "seq", d) for d in range(1, lax.axis_size("seq"))]
    parts = [part.reshape(-1) for part in parts]
    results = []
    offset = 0
    for shard, dim, size in zip(shards, dims, sizes):
        relative = [part[offset : offset + size].reshape(shard.shape) for part in parts]
        results.append(in_place_order(relative, dim))
        offset = offset + size
    return results


def padded_rows(block, multiple, dim):
    extra = -block.shape[dim] % multiple
    if not extra:
        return block
    widths = [(0, 0)] * block.ndim
    widths[dim] = (0, extra)
    return jnp.pad(block, widths)


def small_columns(grads, width):
    seq_count = lax.axis_size("seq")
    rows = [
        jnp.moveaxis(grad.reshape(-1, seq_count, grad.shape[-1] // (seq_count * width), width), 1, 2).reshape(
            -1, seq_count * width
        )
        for grad in grads
    ]
    return padded_rows(jnp.concatenate(rows, 0), 128, 0).T.astype(jnp.bfloat16)


def small_shares(columns, grads, width):
    seq_count = lax.axis_size("seq")
    rows = columns.T
    results = []
    offset = 0
    for grad in grads:
        count = grad.size // (seq_count * width)
        shape = grad.shape[:-1] + (grad.shape[-1] // seq_count,)
        results.append(rows[offset : offset + count].reshape(shape))
        offset = offset + count
    return results


def halved_sum(block, axis, bit, dim):
    half = block.shape[dim] // 2
    upper = ((lax.axis_index(axis) & bit) != 0).astype(jnp.int32)
    kept = lax.dynamic_slice_in_dim(block, upper * half, half, dim)
    sent = lax.dynamic_slice_in_dim(block, (1 - upper) * half, half, dim)
    got = lax.ppermute(sent, axis, [(i, i ^ bit) for i in range(lax.axis_size(axis))])
    return (kept.astype(jnp.float32) + got.astype(jnp.float32)).astype(jnp.bfloat16)


def row_sum_owned(partial):
    bit = lax.axis_size("seq") // 2
    while bit:
        partial = halved_sum(partial, "seq", bit, 0)
        bit = bit // 2
    return partial.astype(jnp.float32)


def after(values, others):
    return lax.optimization_barrier((values, others))


def offload_rows(packed, is_ordered):
    if not is_ordered:
        blocks = packed.reshape(lax.axis_size("seq"), lax.axis_size("rows"), -1, packed.shape[1])
        packed = jnp.swapaxes(blocks, 0, 1).reshape(packed.shape)
    return lax.psum_scatter(packed, "rows", scatter_dimension=0, tiled=True)


def offload_seq(blocks):
    return lax.psum_scatter(blocks, "seq", scatter_dimension=0, tiled=True)


def offload_back(share):
    return lax.all_gather(share, "rows", axis=0, tiled=True)


def passed_along(block, axis, distance):
    devices = range(lax.axis_size(axis))
    route = [(i - distance, i) for i in devices if i - distance in devices]
    return lax.ppermute(block, axis, route)


def layer_norm(values, gain_vec):
    centre = values - jnp.mean(values, axis=-1, keepdims=True)
    inverse = lax.rsqrt(jnp.mean(centre * centre, axis=-1, keepdims=True) + EPSILON)
    return centre * inverse * gain_vec


def norm_back(values, gain_vec, upstream):
    centre = values - jnp.mean(values, axis=-1, keepdims=True)
    inverse = lax.rsqrt(jnp.mean(centre * centre, axis=-1, keepdims=True) + EPSILON)
    normed = centre * inverse
    scaled = upstream * gain_vec
    d_values = inverse * (
        scaled
        - jnp.mean(scaled, axis=-1, keepdims=True)
        - normed * jnp.mean(scaled * normed, axis=-1, keepdims=True)
    )
    return (d_values, jnp.sum(upstream * normed, axis=0))


def swish_slope(pre_act):
    sigma = jax.nn.sigmoid(pre_act)
    return sigma * (1.0 + pre_act * (1.0 - sigma))


def plain_dot(first, second):
    return jnp.dot(first, second, preferred_element_type=jnp.float32)


def left_dot(first, second):
    return jnp.einsum("nk,nm->km", first, second, preferred_element_type=jnp.float32)


def right_dot(grads_in, weight):
    return jnp.einsum("nm,km->nk", grads_in, weight, preferred_element_type=jnp.float32)


TILE = 256
SEG_ROWS = 16
LOG2E = 1.4426950408889634


def tiles_of(extent):
    return [(low, min(low + TILE, extent)) for low in range(0, extent, TILE)]


def tn_dot(first, second):
    return lax.dot_general(first, second, (((0,), (0,)), ((), ())), preferred_element_type=jnp.float32)


def nn_dot(first, second):
    return lax.dot_general(first, second, (((1,), (0,)), ((), ())), preferred_element_type=jnp.float32)


def nt_dot(first, second):
    return lax.dot_general(first, second, (((1,), (1,)), ((), ())), preferred_element_type=jnp.float32)


def row_numbers(width):
    return lax.broadcasted_iota(jnp.int32, (SEG_ROWS, width), 0)


def split_low(values, count):
    pieces = []
    for _ in range(count):
        piece = values.astype(jnp.bfloat16).astype(jnp.float32)
        pieces.append(piece)
        values = values - piece
    return pieces


def key_marks(key_seg, ones):
    rows = row_numbers(key_seg.shape[1])
    marked = jnp.logical_or(rows == key_seg, jnp.logical_and(rows >= 3, rows < 3 + ones))
    return jnp.where(marked, 1.0, 0.0).astype(jnp.bfloat16)


def query_marks(query_seg):
    rows = row_numbers(query_seg.shape[1])
    other = jnp.logical_and(rows < 3, rows != query_seg)
    return jnp.where(other, NEG_BIG, 0.0)


def with_rows(marks, first, pieces):
    rows = row_numbers(marks.shape[1])
    for k, piece in enumerate(pieces):
        marks = jnp.where(rows == first + k, piece, marks)
    return marks.astype(jnp.bfloat16)


def triangle(scores, low):
    key_at = lax.broadcasted_iota(jnp.int32, scores.shape, 0)
    query_at = lax.broadcasted_iota(jnp.int32, scores.shape, 1) + low
    return jnp.where(key_at <= query_at, scores, NEG_BIG)


FWD_HEADS = 4
BWD_HEADS = 4


def attend_kernel(heads, causal, place_ref, *refs):
    attend_core(heads, causal, place_ref[0], *refs)


def attend_core(
    heads, causal, place, qt_ref, pair_ref, qseg_ref, kseg_ref, ot_ref, total_ref, kmark_ref, sum_ref, peak_ref, score_ref
):
    width, tokens = qt_ref.shape
    size = width // heads
    factor = size ** (-0.5) * LOG2E
    block = tokens if causal else pair_ref.shape[1]
    place = place if causal else 0
    kmark_ref[...] = key_marks(kseg_ref[...], 0)
    value_marks = jnp.where(row_numbers(TILE) == 0, 1.0, 0.0).astype(jnp.bfloat16)
    qmarks = query_marks(qseg_ref[...]).astype(jnp.bfloat16)
    tiles = tiles_of(tokens)

    def head_rows(head, base=0):
        return pl.ds(pl.multiple_of(base + head * size, size), size)

    def on_units(several, start, first):
        units = [(k, head, low, high) for k, head in enumerate(several) for low, high in tiles]

        def key_parts(unit):
            _, _, _, high = unit
            return tiles_of(high if first and causal else block)

        def lanes_of(part):
            return pl.ds(pl.multiple_of(start + part[0], 128), part[1] - part[0])

        def score_part(unit, slot, part):
            k, head, low, high = unit
            query_rows = jnp.concatenate([qt_ref[head_rows(head), low:high], qmarks[:, low:high]], 0)
            lanes = lanes_of(part)
            scores = tn_dot(jnp.concatenate([pair_ref[head_rows(head), lanes], kmark_ref[:, lanes]], 0), query_rows)
            if first and causal and part[0] >= low:
                scores = triangle(scores, low - part[0])
            score_ref[slot, part[0] : part[1], : high - low] = scores
            return jnp.max(scores, axis=0, keepdims=True)

        def value_part(unit, slot, part, peak):
            k, head, low, high = unit
            scores = score_ref[slot, part[0] : part[1], : high - low]
            weights = jnp.exp2((scores - peak) * factor).astype(jnp.bfloat16)
            value_rows = jnp.concatenate(
                [pair_ref[head_rows(head, width), lanes_of(part)], value_marks[:, : part[1] - part[0]]], 0
            )
            return nn_dot(value_rows, weights)

        held = None
        for at in range(len(units) + 1):
            unit = units[at] if at < len(units) else None
            parts = key_parts(unit) if unit else []
            old_parts = key_parts(held[0]) if held else []
            peak = None
            if unit and not first:
                peak = peak_ref[unit[0], :, unit[2] : unit[3]]
            before = peak
            summed = None
            for step in range(max(len(parts), len(old_parts))):
                if step < len(parts):
                    found = score_part(unit, at % 2, parts[step])
                    peak = found if peak is None else jnp.maximum(peak, found)
                if step < len(old_parts):
                    term = value_part(held[0], (at - 1) % 2, old_parts[step], held[1])
                    summed = term if summed is None else summed + term
            if held:
                k, _, low, high = held[0]
                if not first:
                    summed = summed + sum_ref[k, :, low:high] * jnp.exp2((held[2] - held[1]) * factor)
                sum_ref[k, :, low:high] = summed
                peak_ref[k, :, low:high] = held[1]
            held = (unit, peak, before)

    def some_heads(step, carry):
        several = [step * FWD_HEADS + k for k in range(FWD_HEADS)]
        on_units(several, place * block, True)
        if causal:

            def earlier(back, held):
                on_units(several, back * block, False)
                return held

            lax.fori_loop(0, place, earlier, 0)
        for k, head in enumerate(several):
            total = sum_ref[k, size : size + 1, :]
            ot_ref[head_rows(head), :] = (sum_ref[k, :size, :] / total).astype(jnp.bfloat16)
            total_ref[head] = peak_ref[k] + jnp.log2(total) / factor
        return carry

    lax.fori_loop(0, heads // FWD_HEADS, some_heads, 0)


def attend_back_kernel(heads, causal, place_ref, *refs):
    attend_back_core(heads, causal, place_ref[0], *refs)


def attend_back_core(
    heads, causal, place, qt_ref, pair_ref, gt_ref, ot_ref, total_ref, qseg_ref, kseg_ref,
    dq_ref, dpair_ref, kmark_ref, dkh_ref, dvh_ref, dqh_ref, qrow_ref, grow_ref, weight_ref, slope_ref,
):
    width, tokens = qt_ref.shape
    size = width // heads
    scale = size ** (-0.5)
    factor = scale * LOG2E
    block = tokens if causal else pair_ref.shape[1]
    place = place if causal else 0
    kmark_ref[...] = key_marks(kseg_ref[...], 3)
    value_marks = jnp.where(row_numbers(TILE) < 2, 1.0, 0.0).astype(jnp.bfloat16)
    qmarks = query_marks(qseg_ref[...])
    tiles = tiles_of(tokens)

    def head_rows(head, base=0):
        return pl.ds(pl.multiple_of(base + head * size, size), size)

    def prepare(k, head):
        own = head_rows(head)
        grads = gt_ref[own, :]
        delta = jnp.sum(grads.astype(jnp.float32) * ot_ref[own, :].astype(jnp.float32), axis=0, keepdims=True)
        qrow_ref[k, :size, :] = qt_ref[own, :]
        qrow_ref[k, size:, :] = with_rows(qmarks, 3, split_low(-total_ref[head], 3))
        grow_ref[k, :size, :] = grads
        grow_ref[k, size:, :] = with_rows(jnp.zeros_like(qmarks), 0, split_low(-delta, 2))

    def on_units(several, start, first):
        units = [(k, head, low, high) for k, head in enumerate(several) for low, high in tiles]

        def key_parts(unit):
            _, _, _, high = unit
            return tiles_of(high if first and causal else block)

        def lanes_of(part):
            return pl.ds(pl.multiple_of(start + part[0], 128), part[1] - part[0])

        def score_part(unit, slot, part):
            k, head, low, high = unit
            lanes = lanes_of(part)
            key_rows = jnp.concatenate([pair_ref[head_rows(head), lanes], kmark_ref[:, lanes]], 0)
            value_rows = jnp.concatenate(
                [pair_ref[head_rows(head, width), lanes], value_marks[:, : part[1] - part[0]]], 0
            )
            scores = tn_dot(key_rows, qrow_ref[k, :, low:high])
            if first and causal and part[0] >= low:
                scores = triangle(scores, low - part[0])
            weights = jnp.exp2(scores * factor)
            slopes = tn_dot(value_rows, grow_ref[k, :, low:high])
            weight_ref[slot, part[0] : part[1], : high - low] = weights.astype(jnp.bfloat16)
            slope_ref[slot, part[0] : part[1], : high - low] = (weights * slopes).astype(jnp.bfloat16)

        def grad_part(unit, slot, part):
            k, head, low, high = unit
            lanes = lanes_of(part)
            weights = weight_ref[slot, part[0] : part[1], : high - low]
            slopes = slope_ref[slot, part[0] : part[1], : high - low]
            dvh_ref[k, :, lanes] += nt_dot(grow_ref[k, :size, low:high], weights)
            dkh_ref[k, :, lanes] += nt_dot(qrow_ref[k, :size, low:high], slopes)
            return nn_dot(pair_ref[head_rows(head), lanes], slopes)

        held = None
        for at in range(len(units) + 1):
            unit = units[at] if at < len(units) else None
            parts = key_parts(unit) if unit else []
            old_parts = key_parts(held) if held else []
            summed = None
            for step in range(max(len(parts), len(old_parts))):
                if step < len(parts):
                    score_part(unit, at % 2, parts[step])
                if step < len(old_parts):
                    term = grad_part(held, (at - 1) % 2, old_parts[step])
                    summed = term if summed is None else summed + term
            if held:
                k, _, low, high = held
                if first:
                    dqh_ref[k, :, low:high] = summed
                else:
                    dqh_ref[k, :, low:high] += summed
            held = unit

    def some_heads(step, carry):
        several = [step * BWD_HEADS + k for k in range(BWD_HEADS)]
        dkh_ref[...] = jnp.zeros_like(dkh_ref)
        dvh_ref[...] = jnp.zeros_like(dvh_ref)
        for k, head in enumerate(several):
            prepare(k, head)
        on_units(several, place * block, True)
        if causal:

            def earlier(back, held):
                on_units(several, back * block, False)
                return held

            lax.fori_loop(0, place, earlier, 0)
        for k, head in enumerate(several):
            dq_ref[head_rows(head), :] = (dqh_ref[k] * scale).astype(jnp.bfloat16)
            dpair_ref[head_rows(head), :] = (dkh_ref[k] * scale).astype(jnp.bfloat16)
            dpair_ref[head_rows(head, width), :] = dvh_ref[k].astype(jnp.bfloat16)
        return carry

    lax.fori_loop(0, heads // BWD_HEADS, some_heads, 0)


IN_SMEM = pl.BlockSpec(memory_space=pltpu.SMEM)
IN_VMEM = pl.BlockSpec(memory_space=pltpu.VMEM)
KERNEL_VMEM = 48 * 2**20


LANE_GROUP = 128
SPACING = 1


def share_sum_kernel(
    part_count, *refs
):
    parts, refs = refs[:part_count], refs[part_count:]
    share_sum_core(parts, *refs)


def share_sum_core(
    parts, out_ref, grad_ref, core_ref, pair_ref, across_ref, near_ref, near_got_ref, part_ref, piece_ref, send_sem, recv_sem
):
    seq_count, _, half, total = grad_ref.shape
    far_count = lax.axis_size("rows") // 4
    row, place = lax.axis_index("rows"), lax.axis_index("seq")
    core, near, far = lax.rem(row, 2), lax.rem(row // 2, 2), row // 4
    mate = (row + 1 - 2 * core, place)
    close = (row + 2 - 4 * near, place)
    peers = [None] + [
        (lax.rem(far + d, far_count) * 4 + near * 2 + core, place) for d in range(1, far_count)
    ]
    sides = [None] + [(row, lax.rem(place + d, seq_count)) for d in range(1, seq_count)]
    step = 2 * far_count * LANE_GROUP
    wide = far_count * LANE_GROUP
    count = total // step

    barrier = pltpu.get_barrier_semaphore()
    friends = [mate, close] + peers[1:] + sides[1:]
    for friend in friends:
        pl.semaphore_signal(barrier, inc=1, device_id=friend, device_id_type=pl.DeviceIdType.MESH)
    pl.semaphore_wait(barrier, len(friends))

    def copy(chunk, slot, source, target, device):
        return pltpu.make_async_remote_copy(
            src_ref=source,
            dst_ref=target,
            send_sem=send_sem.at[chunk, slot],
            recv_sem=recv_sem.at[chunk, slot],
            device_id=device,
            device_id_type=pl.DeviceIdType.MESH,
        )

    first_side = 1
    near_slot = first_side + seq_count - 1
    first_peer = near_slot + 1
    first_back = first_peer + far_count - 1
    near_back_slot = first_back + far_count - 1
    last_slot = near_back_slot + 1

    def columns(chunk):
        return slice(chunk * step, (chunk + 1) * step)

    offset = 0
    for part in parts:
        size = part.shape[-1]
        grad_ref[:, :, :, offset : offset + size] = part[...]
        offset = offset + size
    if offset < total:
        grad_ref[:, :, :, offset:] = jnp.zeros((seq_count, 2, half, total - offset), jnp.bfloat16)

    def core_copy(chunk):
        return copy(chunk, 0, grad_ref.at[:, 1 - core, :, columns(chunk)], core_ref.at[chunk], mate)

    def side_copy(chunk, d):
        away = lax.rem(place + d, seq_count)
        return copy(chunk, first_side + d - 1, pair_ref.at[chunk, away], across_ref.at[chunk, d - 1], sides[d])

    def near_copy(chunk):
        return copy(chunk, near_slot, near_ref.at[chunk, 1 - near], near_got_ref.at[chunk], close)

    def peer_copy(chunk, d):
        away = lax.rem(far + d, far_count)
        return copy(chunk, first_peer + d - 1, part_ref.at[chunk, away], piece_ref.at[chunk, d - 1], peers[d])

    def own_piece(chunk):
        start = chunk * step + near * wide + far * LANE_GROUP
        return out_ref.at[core, :, pl.ds(pl.multiple_of(start, LANE_GROUP), LANE_GROUP)]

    def back_copy(chunk, d):
        return copy(chunk, first_back + d - 1, own_piece(chunk), own_piece(chunk), peers[d])

    def near_back(chunk):
        start = chunk * step + near * wide
        block = out_ref.at[core, :, pl.ds(pl.multiple_of(start, LANE_GROUP), wide)]
        return copy(chunk, near_back_slot, block, block, close)

    def last_copy(chunk):
        block = out_ref.at[core, :, columns(chunk)]
        return copy(chunk, last_slot, block, block, mate)

    def stage_core(chunk):
        core_copy(chunk).start()

    def stage_side(chunk):
        core_copy(chunk).wait_recv()
        kept = grad_ref[:, core, :, columns(chunk)].astype(jnp.float32)
        pair_ref[chunk] = (kept + core_ref[chunk].astype(jnp.float32)).astype(jnp.bfloat16)
        for d in range(1, seq_count):
            side_copy(chunk, d).start()

    def stage_near(chunk):
        for d in range(1, seq_count):
            side_copy(chunk, d).wait_recv()
        summed = pair_ref[chunk, place].astype(jnp.float32)
        for d in range(1, seq_count):
            summed = summed + across_ref[chunk, d - 1].astype(jnp.float32)
        summed = summed.astype(jnp.bfloat16)
        for side in range(2):
            near_ref[chunk, side] = summed[:, side * wide : (side + 1) * wide]
        near_copy(chunk).start()

    def stage_peer(chunk):
        near_copy(chunk).wait_recv()
        summed = near_ref[chunk, near].astype(jnp.float32) + near_got_ref[chunk].astype(jnp.float32)
        summed = summed.astype(jnp.bfloat16)
        for piece in range(far_count):
            part_ref[chunk, piece] = summed[:, piece * LANE_GROUP : (piece + 1) * LANE_GROUP]
        for d in range(1, far_count):
            peer_copy(chunk, d).start()

    def stage_back(chunk):
        for d in range(1, far_count):
            peer_copy(chunk, d).wait_recv()
        summed = part_ref[chunk, far].astype(jnp.float32)
        for d in range(1, far_count):
            summed = summed + piece_ref[chunk, d - 1].astype(jnp.float32)
        own_piece(chunk)[...] = summed.astype(jnp.bfloat16)
        for d in range(1, far_count):
            back_copy(chunk, d).start()

    def stage_near_back(chunk):
        for d in range(1, far_count):
            back_copy(chunk, d).wait_recv()
        near_back(chunk).start()

    def stage_last(chunk):
        near_back(chunk).wait_recv()
        last_copy(chunk).start()

    def stage_done(chunk):
        last_copy(chunk).wait_recv()
        core_copy(chunk).wait_send()
        for d in range(1, seq_count):
            side_copy(chunk, d).wait_send()
        near_copy(chunk).wait_send()
        for d in range(1, far_count):
            peer_copy(chunk, d).wait_send()
            back_copy(chunk, d).wait_send()
        near_back(chunk).wait_send()
        last_copy(chunk).wait_send()

    for chunk in range(count):
        stage_core(chunk)
    for chunk in range(count):
        stage_side(chunk)
    stages = (stage_near, stage_peer, stage_back, stage_near_back, stage_last, stage_done)
    for tick in range(count + SPACING * (len(stages) - 1)):
        for late, stage in enumerate(stages):
            if 0 <= tick - SPACING * late < count:
                stage(tick - SPACING * late)


def share_summed(parts):
    seq_count = lax.axis_size("seq")
    far_count = lax.axis_size("rows") // 4
    half = parts[0].shape[0] // (2 * seq_count)
    step = 2 * far_count * LANE_GROUP
    total = sum(part.shape[1] for part in parts)
    total = total + -total % step
    count = total // step
    slots = 4 + (seq_count - 1) + 2 * (far_count - 1)
    low = jnp.bfloat16
    out = pl.pallas_call(
        functools.partial(share_sum_kernel, len(parts)),
        out_shape=jax.ShapeDtypeStruct((2, half, total), low),
        in_specs=[IN_VMEM] * len(parts),
        out_specs=IN_VMEM,
        scratch_shapes=[
            pltpu.VMEM((seq_count, 2, half, total), low),
            pltpu.VMEM((count, seq_count, half, step), low),
            pltpu.VMEM((count, seq_count, half, step), low),
            pltpu.VMEM((count, seq_count - 1, half, step), low),
            pltpu.VMEM((count, 2, half, step // 2), low),
            pltpu.VMEM((count, half, step // 2), low),
            pltpu.VMEM((count, far_count, half, LANE_GROUP), low),
            pltpu.VMEM((count, far_count - 1, half, LANE_GROUP), low),
            pltpu.SemaphoreType.DMA((count, slots)),
            pltpu.SemaphoreType.DMA((count, slots)),
        ],
        compiler_params=pltpu.CompilerParams(
            collective_id=0, has_side_effects=True, vmem_limit_bytes=KERNEL_VMEM
        ),
        name="share_sum",
    )(*[part.reshape(seq_count, 2, half, part.shape[1]) for part in parts])
    return out.reshape(2 * half, total)


def attend_forward(queries, pairs_t, heads, causal, query_seg, key_seg):
    width, tokens = queries.shape
    total_keys = pairs_t.shape[1]
    pairs = heads * tokens * total_keys
    return pl.pallas_call(
        functools.partial(attend_kernel, heads, causal),
        out_shape=(
            jax.ShapeDtypeStruct((width, tokens), jnp.bfloat16),
            jax.ShapeDtypeStruct((heads, 1, tokens), jnp.float32),
        ),
        in_specs=[IN_SMEM] + [IN_VMEM] * 4,
        out_specs=(IN_VMEM, IN_VMEM),
        scratch_shapes=[
            pltpu.VMEM((SEG_ROWS, total_keys), jnp.bfloat16),
            pltpu.VMEM((FWD_HEADS, width // heads + SEG_ROWS, tokens), jnp.float32),
            pltpu.VMEM((FWD_HEADS, 1, tokens), jnp.float32),
            pltpu.VMEM((2, tokens if causal else total_keys, TILE), jnp.float32),
        ],
        compiler_params=pltpu.CompilerParams(vmem_limit_bytes=KERNEL_VMEM),
        cost_estimate=pl.CostEstimate(
            flops=pairs * 600, bytes_accessed=4 * width * total_keys, transcendentals=pairs
        ),
        name="attend_fwd",
    )(lax.axis_index("seq").reshape(1), queries, pairs_t, query_seg[None], key_seg[None])


def attend_back(queries, pairs_t, grads, outs, totals, heads, causal, query_seg, key_seg):
    width, tokens = queries.shape
    total_keys = pairs_t.shape[1]
    pairs = heads * tokens * total_keys
    size = width // heads
    return pl.pallas_call(
        functools.partial(attend_back_kernel, heads, causal),
        out_shape=(
            jax.ShapeDtypeStruct((width, tokens), jnp.bfloat16),
            jax.ShapeDtypeStruct((2 * width, total_keys), jnp.bfloat16),
        ),
        in_specs=[IN_SMEM] + [IN_VMEM] * 7,
        out_specs=(IN_VMEM, IN_VMEM),
        scratch_shapes=[
            pltpu.VMEM((SEG_ROWS, total_keys), jnp.bfloat16),
            pltpu.VMEM((BWD_HEADS, size, total_keys), jnp.float32),
            pltpu.VMEM((BWD_HEADS, size, total_keys), jnp.float32),
            pltpu.VMEM((BWD_HEADS, size, tokens), jnp.float32),
            pltpu.VMEM((BWD_HEADS, size + SEG_ROWS, tokens), jnp.bfloat16),
            pltpu.VMEM((BWD_HEADS, size + SEG_ROWS, tokens), jnp.bfloat16),
            pltpu.VMEM((2, tokens if causal else total_keys, TILE), jnp.bfloat16),
            pltpu.VMEM((2, tokens if causal else total_keys, TILE), jnp.bfloat16),
        ],
        compiler_params=pltpu.CompilerParams(vmem_limit_bytes=KERNEL_VMEM),
        cost_estimate=pl.CostEstimate(
            flops=pairs * 1500, bytes_accessed=8 * width * total_keys, transcendentals=pairs
        ),
        name="attend_bwd",
    )(
        lax.axis_index("seq").reshape(1), queries, pairs_t, grads, outs, totals,
        query_seg[None], key_seg[None],
    )


RIM = 16
ROW_TILE = 64
MERGE_ROWS = 64


def row_tiles(extent, tile):
    return [(low, min(low + tile, extent)) for low in range(0, extent, tile)]


def halves_of(extent):
    middle = -(-extent // 32) * 16
    return [(0, middle), (middle, extent)]


def group_lanes(group):
    return pl.ds(pl.multiple_of(group * 128, 128), 128)


def wide_rows(column, width=128):
    return jnp.broadcast_to(column, (column.shape[0], width))


def loop_rows(extent, tile, body):
    def step(k, carry):
        body(pl.ds(pl.multiple_of(k * tile, tile), tile))
        return carry

    whole = extent // tile
    lax.fori_loop(0, whole, step, 0)
    if whole * tile < extent:
        body(pl.ds(whole * tile, extent - whole * tile))


def rows_normed(values):
    centre = values - jnp.mean(values, axis=-1, keepdims=True)
    inverse = lax.rsqrt(jnp.mean(centre * centre, axis=-1, keepdims=True) + EPSILON)
    return centre * inverse, inverse


def rows_norm_back(normed, inverse, gain_vec, upstream):
    scaled = upstream * gain_vec
    return inverse * (
        scaled
        - jnp.mean(scaled, axis=-1, keepdims=True)
        - normed * jnp.mean(scaled * normed, axis=-1, keepdims=True)
    )


def taps_forward(source_ref, first_row, since, lanes, low, high, weights):
    result = None
    for offset, weight in enumerate(weights):
        start = first_row + low - offset
        window = source_ref[start : start + high - low, lanes]
        if offset:
            window = jnp.where(since >= offset, window, 0.0)
        term = window * weight
        result = term if result is None else result + term
    return result


def conv_fwd_kernel(
    h1_ref, a2_ref, rim_ref, since_ref, tl_ref, tr_ref, tm_ref, mgain_ref, gain_ref, pl_ref, pr_ref, pm_ref,
    cl_ref, cr_ref, cm_ref, h2_ref, a3_ref,
    ext_ref, wide_ref, cle_ref, cre_ref, up_ref, mixed_ref,
):
    tokens, width = h1_ref.shape
    total = tokens + RIM
    narrow = pr_ref.shape[1]
    ext_ref[0:RIM, :] = jnp.zeros((RIM, width), jnp.float32)
    ext_ref[RIM : 2 * RIM, :] = rim_ref[...].astype(jnp.float32)
    ext_ref[2 * RIM :, :] = a2_ref[...].astype(jnp.float32)
    wide_ref[...] = wide_rows(since_ref[...])

    def first_convs(group, carry):
        lanes = group_lanes(group)
        left = [tl_ref[j : j + 1, lanes] for j in range(tl_ref.shape[0])]
        right = [tr_ref[j : j + 1, lanes] for j in range(tr_ref.shape[0])]
        for low, high in row_tiles(total, ROW_TILE):
            since = wide_ref[low:high, :]
            cle_ref[low:high, lanes] = taps_forward(ext_ref, RIM, since, lanes, low, high, left).astype(jnp.bfloat16)
            cre_ref[low:high, lanes] = taps_forward(ext_ref, RIM, since, lanes, low, high, right).astype(jnp.bfloat16)
        return carry

    lax.fori_loop(0, width // 128, first_convs, 0)
    cl_ref[...] = cle_ref[RIM:, :]
    cr_ref[...] = cre_ref[RIM:, :]
    for low, high in halves_of(total):
        up_ref[low:high, :] = nn_dot(cle_ref[low:high, :], pl_ref[...])
        mixed_ref[low:high, :narrow] = nn_dot(cre_ref[low:high, :], pr_ref[...])

    def merge_rows(rows):
        pre = up_ref[rows, :]
        merged = pre / (1.0 + jnp.exp(-pre))
        merged = jnp.concatenate([merged[:, :narrow] + mixed_ref[rows, :narrow], merged[:, narrow:]], 1)
        normed, _ = rows_normed(merged)
        mixed_ref[rows, :] = (normed * mgain_ref[...]).astype(jnp.bfloat16).astype(jnp.float32)

    loop_rows(total, MERGE_ROWS, merge_rows)

    def mid_conv(group, carry):
        lanes = group_lanes(group)
        weights = [tm_ref[j : j + 1, lanes] for j in range(tm_ref.shape[0])]
        for low, high in row_tiles(tokens, ROW_TILE):
            since = wide_ref[RIM + low : RIM + high, :]
            cm_ref[low:high, lanes] = taps_forward(mixed_ref, RIM, since, lanes, low, high, weights).astype(jnp.bfloat16)
        return carry

    lax.fori_loop(0, mixed_ref.shape[1] // 128, mid_conv, 0)
    for low, high in halves_of(tokens):
        h2_ref[low:high, :] = h1_ref[low:high, :] + nn_dot(cm_ref[low:high, :], pm_ref[...])

    def norm_rows(rows):
        normed, _ = rows_normed(h2_ref[rows, :])
        a3_ref[rows, :] = (normed * gain_ref[...]).astype(jnp.bfloat16)

    loop_rows(tokens, 64, norm_rows)


def conv_forward(h1, a2, rim, since, taps_l, taps_r, taps_m, mid_gain, gain, proj_left, proj_right, proj_mid):
    tokens, width = h1.shape
    wide = proj_left.shape[1]
    total = tokens + RIM
    low, full = jnp.bfloat16, jnp.float32
    return pl.pallas_call(
        conv_fwd_kernel,
        out_shape=(
            jax.ShapeDtypeStruct((tokens, width), low),
            jax.ShapeDtypeStruct((tokens, width), low),
            jax.ShapeDtypeStruct((tokens, wide), low),
            jax.ShapeDtypeStruct((tokens, width), full),
            jax.ShapeDtypeStruct((tokens, width), low),
        ),
        in_specs=[IN_VMEM] * 12,
        out_specs=(IN_VMEM,) * 5,
        scratch_shapes=[
            pltpu.VMEM((total + RIM, width), full),
            pltpu.VMEM((total, 128), jnp.int32),
            pltpu.VMEM((total, width), low),
            pltpu.VMEM((total, width), low),
            pltpu.VMEM((total, wide), full),
            pltpu.VMEM((total, wide), full),
        ],
        compiler_params=pltpu.CompilerParams(vmem_limit_bytes=KERNEL_VMEM),
        cost_estimate=pl.CostEstimate(
            flops=tokens * width * wide * 20, bytes_accessed=tokens * width * 16, transcendentals=tokens * wide
        ),
        name="conv_fwd",
    )(h1, a2, rim, since, taps_l, taps_r, taps_m, mid_gain, gain, proj_left, proj_right, proj_mid)


def folded(values):
    return jnp.sum(values.reshape(-1, 8, values.shape[-1]), axis=0)


def taps_back(grad_ref, value, left, lanes, low, high, weights, result, sums):
    for offset, weight in enumerate(weights):
        window = grad_ref[low + offset : high + offset, lanes]
        if offset:
            window = jnp.where(left >= offset, window, 0.0)
        term = window * weight
        result = term if result is None else result + term
        if value is not None:
            product = folded(window * value)
            sums[offset] = product if sums[offset] is None else sums[offset] + product
    return result


def conv_bwd_kernel(
    g2_ref, brim_ref, cl_ref, clrim_ref, cr_ref, crrim_ref, cm_ref, a2_ref, h1_ref, left_ref,
    tl_ref, tr_ref, tm_ref, mgain_ref, gain_ref, pl_ref, pr_ref, pm_ref,
    g1_ref, dw_ref, dtl_ref, dtr_ref, dtm_ref, dmgain_ref, dgain_ref,
    bext_ref, cle_ref, cre_ref, wide_ref, grad_ref, up_ref, back_ref, normed_ref, inv_ref, dpl_ref, dpr_ref, a2f_ref,
):
    tokens, width = g2_ref.shape
    total = tokens + RIM
    wide, narrow = pl_ref.shape[1], pr_ref.shape[1]
    bext_ref[:tokens, :] = g2_ref[...].astype(jnp.bfloat16)
    bext_ref[tokens:, :] = brim_ref[...]
    cle_ref[:tokens, :] = cl_ref[...]
    cle_ref[tokens:, :] = clrim_ref[...]
    cre_ref[:tokens, :] = cr_ref[...]
    cre_ref[tokens:, :] = crrim_ref[...]
    a2f_ref[...] = a2_ref[...].astype(jnp.float32)
    wide_ref[...] = wide_rows(left_ref[...])
    grad_ref[total:, :] = jnp.zeros((RIM, wide), jnp.float32)
    dw_ref[:, :wide] = tn_dot(bext_ref[:tokens, :], cm_ref[...]).astype(jnp.bfloat16)
    for low, high in halves_of(total):
        grad_ref[low:high, :] = nt_dot(bext_ref[low:high, :], pm_ref[...])
        up_ref[low:high, :] = nn_dot(cle_ref[low:high, :], pl_ref[...])
        back_ref[low:high, :narrow] = nn_dot(cre_ref[low:high, :], pr_ref[...])

    def merge_rows(rows):
        pre = up_ref[rows, :]
        merged = pre / (1.0 + jnp.exp(-pre))
        merged = jnp.concatenate([merged[:, :narrow] + back_ref[rows, :narrow], merged[:, narrow:]], 1)
        normed, inverse = rows_normed(merged)
        normed_ref[rows, :] = normed
        inv_ref[rows, :] = wide_rows(inverse)

    loop_rows(total, MERGE_ROWS, merge_rows)

    def mid_back(group, carry):
        lanes = group_lanes(group)
        weights = [tm_ref[j : j + 1, lanes] for j in range(tm_ref.shape[0])]
        sums = [None] * len(weights)
        gain_vec = mgain_ref[:, lanes]
        for low, high in row_tiles(total, ROW_TILE):
            value = None
            if high <= tokens:
                value = (normed_ref[low:high, lanes] * gain_vec).astype(jnp.bfloat16).astype(jnp.float32)
            back_ref[low:high, lanes] = taps_back(
                grad_ref, value, wide_ref[low:high, :], lanes, low, high, weights, None, sums
            )
        for j, piece in enumerate(sums):
            dtm_ref[j : j + 1, lanes] = jnp.sum(piece, axis=0, keepdims=True)
        return carry

    lax.fori_loop(0, wide // 128, mid_back, 0)

    def merge_back(rows):
        pre = up_ref[rows, :]
        normed = normed_ref[rows, :]
        d_merged = rows_norm_back(normed, inv_ref[rows, :][:, :1], mgain_ref[...], back_ref[rows, :])
        sigma = 1.0 / (1.0 + jnp.exp(-pre))
        dpl_ref[rows, :] = (d_merged * (sigma * (1.0 + pre * (1.0 - sigma)))).astype(jnp.bfloat16)
        dpr_ref[rows, :] = d_merged[:, :narrow].astype(jnp.bfloat16)

    loop_rows(total, MERGE_ROWS, merge_back)
    gain_sum = jnp.zeros((8, wide), jnp.float32)

    def gain_rows(k, held):
        rows = pl.ds(pl.multiple_of(k * 16, 16), 16)
        return held + folded(back_ref[rows, :] * normed_ref[rows, :])

    gain_sum = lax.fori_loop(0, tokens // 16, gain_rows, gain_sum)
    dmgain_ref[...] = jnp.sum(gain_sum, axis=0, keepdims=True)
    dw_ref[:, wide : 2 * wide] = tn_dot(cle_ref[:tokens, :], dpl_ref[:tokens, :]).astype(jnp.bfloat16)
    dw_ref[:, 2 * wide :] = tn_dot(cre_ref[:tokens, :], dpr_ref[:tokens, :]).astype(jnp.bfloat16)
    for low, high in halves_of(total):
        grad_ref[low:high, :width] = nt_dot(dpl_ref[low:high, :], pl_ref[...])
        grad_ref[low:high, width : 2 * width] = nt_dot(dpr_ref[low:high, :], pr_ref[...])

    def first_back(group, carry):
        lanes = group_lanes(group)
        other = group_lanes(group + width // 128)
        weights_l = [tl_ref[j : j + 1, lanes] for j in range(tl_ref.shape[0])]
        weights_r = [tr_ref[j : j + 1, lanes] for j in range(tr_ref.shape[0])]
        sums_l = [None] * len(weights_l)
        sums_r = [None] * len(weights_r)
        for low, high in row_tiles(tokens, ROW_TILE):
            left = wide_ref[low:high, :]
            value = a2f_ref[low:high, lanes]
            held = taps_back(grad_ref, value, left, lanes, low, high, weights_l, None, sums_l)
            held = taps_back(grad_ref, value, left, other, low, high, weights_r, held, sums_r)
            back_ref[low:high, lanes] = held
        for j, piece in enumerate(sums_l):
            dtl_ref[j : j + 1, lanes] = jnp.sum(piece, axis=0, keepdims=True)
        for j, piece in enumerate(sums_r):
            dtr_ref[j : j + 1, lanes] = jnp.sum(piece, axis=0, keepdims=True)
        return carry

    lax.fori_loop(0, width // 128, first_back, 0)

    def finish(k, held):
        rows = pl.ds(pl.multiple_of(k * 64, 64), 64)
        normed, inverse = rows_normed(h1_ref[rows, :])
        upstream = back_ref[rows, :width]
        g1_ref[rows, :] = g2_ref[rows, :] + rows_norm_back(normed, inverse, gain_ref[...], upstream)
        return held + folded(upstream * normed)

    gain_sum = lax.fori_loop(0, tokens // 64, finish, jnp.zeros((8, width), jnp.float32))
    dgain_ref[...] = jnp.sum(gain_sum, axis=0, keepdims=True)


def conv_back(
    g2, brim, c_l, c_r, rims, c_m, a2, h1, left, taps_l, taps_r, taps_m, mid_gain, gain, proj_left, proj_right, proj_mid
):
    tokens, width = g2.shape
    wide, narrow = proj_left.shape[1], proj_right.shape[1]
    total = tokens + RIM
    low, full = jnp.bfloat16, jnp.float32
    return pl.pallas_call(
        conv_bwd_kernel,
        out_shape=(
            jax.ShapeDtypeStruct((tokens, width), full),
            jax.ShapeDtypeStruct((width, 2 * wide + narrow), low),
            jax.ShapeDtypeStruct(taps_l.shape, full),
            jax.ShapeDtypeStruct(taps_r.shape, full),
            jax.ShapeDtypeStruct(taps_m.shape, full),
            jax.ShapeDtypeStruct((1, wide), full),
            jax.ShapeDtypeStruct((1, width), full),
        ),
        in_specs=[IN_VMEM] * 18,
        out_specs=(IN_VMEM,) * 7,
        scratch_shapes=[
            pltpu.VMEM((total, width), low),
            pltpu.VMEM((total, width), low),
            pltpu.VMEM((total, width), low),
            pltpu.VMEM((total, 128), jnp.int32),
            pltpu.VMEM((total + RIM, wide), full),
            pltpu.VMEM((total, wide), full),
            pltpu.VMEM((total, wide), full),
            pltpu.VMEM((total, wide), full),
            pltpu.VMEM((total, 128), full),
            pltpu.VMEM((total, wide), low),
            pltpu.VMEM((total, narrow), low),
            pltpu.VMEM((tokens, width), full),
        ],
        compiler_params=pltpu.CompilerParams(vmem_limit_bytes=KERNEL_VMEM),
        cost_estimate=pl.CostEstimate(
            flops=tokens * width * wide * 40, bytes_accessed=tokens * width * 40, transcendentals=tokens * wide
        ),
        name="conv_bwd",
    )(
        g2, brim, c_l, rims[:, :width], c_r, rims[:, width:], c_m, a2, h1, left,
        taps_l, taps_r, taps_m, mid_gain, gain, proj_left, proj_right, proj_mid,
    )


MIDDLE_VMEM = 60 * 2**20
DOT_ROWS = 256


def load_weight(copies, sems, target_ref, own_ref, pieces, offset, place, near, core):
    width, size = own_ref.shape
    quarter = width // 4
    count = len(pieces) // 3 + 1
    columns = slice(offset, offset + size)
    parts = [(own_ref, place * width, width)]
    for d in range(1, count):
        source = lax.rem(place + d, count) * width
        same, close, across = pieces[3 * d - 3 : 3 * d]
        parts.append((same.at[:, columns], source + (2 * near + core) * quarter, quarter))
        parts.append((close.at[:, columns], source + (2 - 2 * near + core) * quarter, quarter))
        parts.append((across.at[:quarter, columns], source + (2 * near + 1 - core) * quarter, quarter))
        parts.append((across.at[quarter:, columns], source + (3 - 2 * near - core) * quarter, quarter))
    for source_ref, start, rows in parts:
        copy = pltpu.make_async_copy(
            source_ref, target_ref.at[pl.ds(pl.multiple_of(start, quarter), rows), :], sems.at[len(copies)]
        )
        copy.start()
        copies.append(copy)
    return offset + size


def wait_for(copies):
    for copy in copies:
        copy.wait()


def norm_into(target_ref, source_ref, gain_vec):
    def body(rows):
        normed, _ = rows_normed(source_ref[rows, :])
        target_ref[rows, :] = (normed * gain_vec).astype(jnp.bfloat16)

    loop_rows(source_ref.shape[0], 64, body)


def norm_back_into(target_ref, base_ref, source_ref, gain_vec, upstream_ref):
    def body(k, held):
        rows = pl.ds(pl.multiple_of(k * 64, 64), 64)
        normed, inverse = rows_normed(source_ref[rows, :])
        upstream = upstream_ref[rows, :]
        target_ref[rows, :] = base_ref[rows, :].astype(jnp.float32) + rows_norm_back(
            normed, inverse, gain_vec, upstream
        )
        return held + folded(upstream * normed)

    held = jnp.zeros((8, source_ref.shape[1]), jnp.float32)
    return jnp.sum(lax.fori_loop(0, source_ref.shape[0] // 64, body, held), axis=0, keepdims=True)


def chunks(extent):
    return row_tiles(extent, DOT_ROWS)


def project_into(target_ref, weight_ref, turned_ref, low, high):
    for start, stop in chunks(high - low):
        target_ref[start:stop, :] = tn_dot(weight_ref[:, low + start : low + stop], turned_ref[...]).astype(jnp.bfloat16)


def can_order(width):
    return width % (16 * lax.axis_size("seq") * lax.axis_size("rows")) == 0


def store_grad(target_ref, start, values):
    columns = slice(start, start + values.shape[1])
    values = values.astype(jnp.bfloat16)
    if not can_order(values.shape[0]):
        target_ref[:, columns] = values
        return
    seq_count, row_count = lax.axis_size("seq"), lax.axis_size("rows")
    size = values.shape[0] // (seq_count * row_count)
    for place in range(seq_count):
        for row in range(row_count):
            source, target = (place * row_count + row) * size, (row * seq_count + place) * size
            target_ref[target : target + size, columns] = values[source : source + size]


def middle_kernel(
    piece_count,
    place_ref, h2_ref, a3_ref, a3more_ref, mem_ref, gout_ref, gain_ref, qseg_ref, kseg_ref, mseg_ref, down_ref,
    qkv_own, out2_own, query_own, kv_own, out_own, up_own, *rest,
):
    pieces, rest = rest[:piece_count], rest[piece_count:]
    (
        result_ref, g3_ref, da3_ref, dw_ref, dgain_ref, dmem_ref,
        wqkv_ref, wout2_ref, wquery_ref, wkv_ref, wout_ref, wup_ref, sems,
        turned_ref, memt_ref, a4_ref, a4t_ref, qt_ref, pair_ref, attc_ref, totalc_ref,
        qdt_ref, paird_ref, attd_ref, totald_ref, h3_ref, h4_ref, act_ref, dup_ref, low_ref, gt_ref, dq_ref, dpair_ref, dpaird_ref,
        back_ref, wide_ref, kmark_ref, mmark_ref, sum_ref, peak_ref, score_ref,
        dkh_ref, dvh_ref, dkm_ref, dvm_ref, dqh_ref, qrow_ref, grow_ref, weight_ref, slope_ref,
    ) = rest
    tokens, width = h2_ref.shape
    place, near, core = place_ref[0], place_ref[1], place_ref[2]
    seq_count = piece_count // 3 + 1
    high_width = wup_ref.shape[1]
    first, copies = [], []
    offset = load_weight(first, sems.at[0], wqkv_ref, qkv_own, pieces, 0, place, near, core)
    for target, own in ((wout2_ref, out2_own), (wquery_ref, query_own), (wkv_ref, kv_own), (wout_ref, out_own)):
        offset = load_weight(copies, sems.at[1], target, own, pieces, offset, place, near, core)
    load_weight(copies, sems.at[1], wup_ref, up_own, pieces, offset, place, near, core)

    own = pl.ds(pl.multiple_of(place * tokens, 128), tokens)
    turned_ref[:, own] = a3_ref[...].T
    for d in range(1, seq_count):
        there = pl.ds(pl.multiple_of(lax.rem(place + d, seq_count) * tokens, 128), tokens)
        turned_ref[:, there] = a3more_ref[d - 1].T
    memt_ref[...] = mem_ref[...].T
    wait_for(first)
    project_into(qt_ref, wqkv_ref, turned_ref.at[:, own], 0, width)
    project_into(pair_ref, wqkv_ref, turned_ref, width, 3 * width)
    attend_core(
        H_CROSS, True, place, qt_ref, pair_ref, qseg_ref, kseg_ref, attc_ref, totalc_ref, kmark_ref, sum_ref, peak_ref, score_ref
    )
    wait_for(copies)
    for low, high in chunks(tokens):
        h3_ref[low:high, :] = h2_ref[low:high, :] + tn_dot(attc_ref[:, low:high], wout2_ref[...])
    norm_into(a4_ref, h3_ref, gain_ref[0:1, :])
    a4t_ref[...] = a4_ref[...].T
    project_into(qdt_ref, wquery_ref, a4t_ref, 0, width)
    project_into(paird_ref, wkv_ref, memt_ref, 0, 2 * width)
    attend_core(
        H_CROSS, False, 0, qdt_ref, paird_ref, qseg_ref, mseg_ref, attd_ref, totald_ref, mmark_ref, sum_ref, peak_ref, score_ref
    )
    for low, high in chunks(tokens):
        h4_ref[low:high, :] = h3_ref[low:high, :] + tn_dot(attd_ref[:, low:high], wout_ref[...])
    norm_into(a4_ref, h4_ref, gain_ref[1:2, :])

    for left, right in row_tiles(high_width, 512):
        for low, high in chunks(tokens):
            pre = nn_dot(a4_ref[low:high, :], wup_ref[:, left:right])
            sigma = 1.0 / (1.0 + jnp.exp(-pre))
            act_ref[low:high, left:right] = (pre * sigma).astype(jnp.bfloat16)
            slope = nt_dot(gout_ref[low:high, :], down_ref[left:right, :])
            dup_ref[low:high, left:right] = (slope * (sigma * (1.0 + pre * (1.0 - sigma)))).astype(jnp.bfloat16)
    for low, high in chunks(tokens):
        result_ref[low:high, :] = (h4_ref[low:high, :] + nn_dot(act_ref[low:high, :], down_ref[...])).astype(jnp.bfloat16)
        back_ref[low:high, :] = nt_dot(dup_ref[low:high, :], wup_ref[...])
    for left, right in row_tiles(high_width, 512):
        store_grad(dw_ref, left, tn_dot(a4_ref[...], dup_ref[:, left:right]))
        store_grad(dw_ref, high_width + left, tn_dot(gout_ref[...], act_ref[:, left:right]))

    at = 2 * high_width
    dgain_ref[1:2, :] = norm_back_into(h4_ref, gout_ref, h4_ref, gain_ref[1:2, :], back_ref)
    low_ref[...] = h4_ref[...].astype(jnp.bfloat16)
    store_grad(dw_ref, at, nn_dot(attd_ref[...], low_ref[...]))
    gt_ref[...] = nt_dot(wout_ref[...], low_ref[...]).astype(jnp.bfloat16)
    attend_back_core(
        H_CROSS, False, 0, qdt_ref, paird_ref, gt_ref, attd_ref, totald_ref, qseg_ref, mseg_ref,
        dq_ref, dpaird_ref, mmark_ref, dkm_ref, dvm_ref, dqh_ref, qrow_ref, grow_ref, weight_ref, slope_ref,
    )
    store_grad(dw_ref, at + width, nt_dot(a4t_ref[...], dq_ref[...]))
    store_grad(dw_ref, at + 2 * width, nt_dot(memt_ref[...], dpaird_ref[...]))
    dmem_ref[...] = nn_dot(wkv_ref[...], dpaird_ref[...])
    back_ref[...] = nn_dot(wquery_ref[...], dq_ref[...]).T
    dgain_ref[0:1, :] = norm_back_into(g3_ref, h4_ref, h3_ref, gain_ref[0:1, :], back_ref)
    low_ref[...] = g3_ref[...].astype(jnp.bfloat16)
    at = at + 4 * width
    store_grad(dw_ref, at + 3 * width, nn_dot(attc_ref[...], low_ref[...]))
    gt_ref[...] = nt_dot(wout2_ref[...], low_ref[...]).astype(jnp.bfloat16)
    attend_back_core(
        H_CROSS, True, place, qt_ref, pair_ref, gt_ref, attc_ref, totalc_ref, qseg_ref, kseg_ref,
        dq_ref, dpair_ref, kmark_ref, dkh_ref, dvh_ref, dqh_ref, qrow_ref, grow_ref, weight_ref, slope_ref,
    )
    store_grad(dw_ref, at, nt_dot(turned_ref[:, own], dq_ref[...]))
    for low, high in chunks(2 * width):
        store_grad(dw_ref, at + width + low, nt_dot(turned_ref[...], dpair_ref[low:high, :]))
    for low, high in chunks(width):
        wide_ref[low:high, :] = nn_dot(wqkv_ref[low:high, width:], dpair_ref[...])
        wide_ref[low:high, own] += nn_dot(wqkv_ref[low:high, :width], dq_ref[...])
    for low, high in row_tiles(wide_ref.shape[1], tokens):
        da3_ref[low:high, :] = wide_ref[:, low:high].T.astype(jnp.bfloat16)


def middle(h2, a3, a3_more, mem_rows, grad_out, gains, own_seg, seg_row, mem_seg, down, owns, pieces):
    tokens, width = h2.shape
    keys, mems = seg_row.shape[0], mem_seg.shape[0]
    high_width = down.shape[0]
    seq_count = keys // tokens
    size = width // H_CROSS
    low, full = jnp.bfloat16, jnp.float32
    longest = max(tokens, mems)
    v = pltpu.VMEM
    in_hbm = pl.BlockSpec(memory_space=pl.ANY)
    row = lax.axis_index("rows")
    places = jnp.stack([lax.axis_index("seq"), (row // 2) % 2, row % 2]).astype(jnp.int32)
    return pl.pallas_call(
        functools.partial(middle_kernel, len(pieces)),
        out_shape=(
            jax.ShapeDtypeStruct((tokens, width), low),
            jax.ShapeDtypeStruct((tokens, width), full),
            jax.ShapeDtypeStruct((keys, width), low),
            jax.ShapeDtypeStruct((width, 2 * high_width + 8 * width), low),
            jax.ShapeDtypeStruct((2, width), full),
            jax.ShapeDtypeStruct((width, mems), full),
        ),
        in_specs=[IN_SMEM] + [IN_VMEM] * 10 + [in_hbm] * (6 + len(pieces)),
        out_specs=(IN_VMEM,) * 6,
        scratch_shapes=[
            v((width, 3 * width), low),
            v((width, width), low),
            v((width, width), low),
            v((width, 2 * width), low),
            v((width, width), low),
            v((width, high_width), low),
            pltpu.SemaphoreType.DMA((2, 5 * (4 * seq_count - 3))),
            v((width, keys), low),
            v((width, mems), low),
            v((tokens, width), low),
            v((width, tokens), low),
            v((width, tokens), low),
            v((2 * width, keys), low),
            v((width, tokens), low),
            v((H_CROSS, 1, tokens), full),
            v((width, tokens), low),
            v((2 * width, mems), low),
            v((width, tokens), low),
            v((H_CROSS, 1, tokens), full),
            v((tokens, width), full),
            v((tokens, width), full),
            v((tokens, high_width), low),
            v((tokens, high_width), low),
            v((tokens, width), low),
            v((width, tokens), low),
            v((width, tokens), low),
            v((2 * width, keys), low),
            v((2 * width, mems), low),
            v((tokens, width), full),
            v((width, keys), full),
            v((SEG_ROWS, keys), low),
            v((SEG_ROWS, mems), low),
            v((FWD_HEADS, size + SEG_ROWS, tokens), full),
            v((FWD_HEADS, 1, tokens), full),
            v((2, longest, TILE), full),
            v((BWD_HEADS, size, keys), full),
            v((BWD_HEADS, size, keys), full),
            v((BWD_HEADS, size, mems), full),
            v((BWD_HEADS, size, mems), full),
            v((BWD_HEADS, size, tokens), full),
            v((BWD_HEADS, size + SEG_ROWS, tokens), low),
            v((BWD_HEADS, size + SEG_ROWS, tokens), low),
            v((2, longest, TILE), low),
            v((2, longest, TILE), low),
        ],
        compiler_params=pltpu.CompilerParams(vmem_limit_bytes=MIDDLE_VMEM),
        cost_estimate=pl.CostEstimate(
            flops=tokens * width * width * 200, bytes_accessed=tokens * width * 40, transcendentals=tokens * width * 20
        ),
        name="middle",
    )(
        places, h2, a3, a3_more, mem_rows, grad_out, gains, own_seg[None], seg_row[None], mem_seg[None], down,
        *owns, *pieces,
    )


def segment_reach(seg_row):
    length = seg_row.shape[0]
    first = jnp.sum(seg_row == 0)
    second = first + jnp.sum(seg_row == 1)
    spots = jnp.arange(length, dtype=jnp.int32)
    start = jnp.where(seg_row == 0, 0, jnp.where(seg_row == 1, first, second))
    stop = jnp.where(seg_row == 0, first, jnp.where(seg_row == 1, second, length))
    return spots - start, stop - 1 - spots


def turned_dot(weight, values):
    return jnp.einsum("kn,tk->nt", weight, values, preferred_element_type=jnp.float32)


def out_dot(turned, weight):
    return jnp.einsum("nt,nk->tk", turned, weight, preferred_element_type=jnp.float32)


def weight_dot(values, turned):
    return jnp.einsum("tk,nt->kn", values, turned, preferred_element_type=jnp.float32)


def out_weight_dot(turned, grads_in):
    return jnp.einsum("nt,tk->kn", turned, grads_in, preferred_element_type=jnp.float32)


def turned_back(grads_in, weight):
    return jnp.einsum("tk,nk->nt", grads_in, weight, preferred_element_type=jnp.float32)


def input_back(turned, weight):
    return jnp.einsum("nt,kn->tk", turned, weight, preferred_element_type=jnp.float32)


def self_attend(normed, normed_row, weight, head_count, own_seg, seg_row):
    model_width = normed.shape[1]
    queries = turned_dot(weight[:, :model_width], normed).astype(jnp.bfloat16)
    pairs = turned_dot(weight[:, model_width:], normed_row).astype(jnp.bfloat16)
    att_out, totals = attend_forward(queries, pairs, head_count, True, own_seg, seg_row)
    return (att_out, totals, queries, pairs, normed_row)


def self_back(normed, weight, grad_att, kept, head_count, own_seg, seg_row):
    att_out, totals, queries, pairs, normed_row = kept
    model_width = normed.shape[1]
    d_query, d_pairs = attend_back(
        queries, pairs, grad_att, att_out, totals, head_count, True, own_seg, seg_row
    )
    d_weight = jnp.concatenate([weight_dot(normed, d_query), weight_dot(normed_row, d_pairs)], 1)
    d_normed = input_back(d_query, weight[:, :model_width]) + row_sum_owned(
        input_back(d_pairs, weight[:, model_width:]).astype(jnp.bfloat16)
    )
    return (d_normed, d_weight)


def local(
    hidden_in,
    memory,
    grad_out,
    seg_ids,
    mem_seg_ids,
    gains,
    qkv_first,
    query_cross,
    kv_cross,
    out_first,
    taps_left,
    proj_left,
    taps_right,
    proj_right,
    mid_gain,
    taps_mid,
    proj_mid,
    qkv_second,
    out_second,
    query_last,
    kv_last,
    out_last,
    ffn_up,
    ffn_down,
):
    shards = (
        gains,
        qkv_first,
        query_cross,
        kv_cross,
        out_first,
        taps_left,
        proj_left,
        taps_right,
        proj_right,
        mid_gain,
        taps_mid,
        proj_mid,
        qkv_second,
        out_second,
        query_last,
        kv_last,
        out_last,
        ffn_up,
        ffn_down,
    )
    shard_dims = (1, 0, 0, 0, 1, 1, 0, 1, 0, 0, 1, 1, 0, 0, 0, 0, 0, 0, 1)
    small = (0, 5, 7, 9, 10)
    seq_count = lax.axis_size("seq")

    def select(group):
        return [shards[k] for k in group], [shard_dims[k] for k in group]

    first_group, second_group, conv_group, middle_group = (1,), (2, 3, 4), (6, 8, 11), (12, 13, 14, 15, 16, 17, 18)
    hidden_more = seq_rotated(hidden_in[0])
    first_same = seq_rotated(packed_half(*select(first_group)))
    gains, taps_left, taps_right, mid_gain, taps_mid = small_gather(*select(small))
    first_other = [core_swapped(piece) for piece in first_same]
    (qkv_first,) = joined_group(*select(first_group), interleaved(first_same, first_other), 2)
    packed, _ = after((packed_half(*select(second_group)), memory[0]), first_same)
    second_same, mem_more = seq_rotated(packed[0]), seq_rotated(packed[1])
    row_inputs = in_place_order([hidden_in[0]] + hidden_more, 0)
    mem_rows = in_place_order([memory[0]] + mem_more, 0)
    inputs = hidden_in[0].astype(jnp.float32)
    seg_row = seg_ids[0]
    mem_seg = mem_seg_ids[0]
    tok_count, model_width = inputs.shape
    row_start = lax.axis_index("seq") * tok_count
    own_seg = lax.dynamic_slice_in_dim(seg_row, row_start, tok_count)
    since, left = segment_reach(seg_row)
    since = lax.dynamic_slice_in_dim(jnp.pad(since, (RIM, 0)), row_start, tok_count + RIM)[:, None]
    left = lax.dynamic_slice_in_dim(jnp.pad(left, (0, RIM)), row_start, tok_count + RIM)[:, None]
    gain_rows = gains.astype(jnp.float32)
    mid_gain_f = mid_gain.astype(jnp.float32)
    left_taps = taps_left.astype(jnp.float32)
    right_taps = taps_right.astype(jnp.float32)
    mid_taps = taps_mid.astype(jnp.float32)
    normed_a = layer_norm(inputs, gain_rows[0]).astype(jnp.bfloat16)
    normed_row = layer_norm(row_inputs.astype(jnp.float32), gain_rows[0]).astype(jnp.bfloat16)
    normed_a, second_same = after(normed_a, second_same)
    second_other = [core_swapped(piece) for piece in second_same]
    packed, _ = after((packed_quarter(*select(conv_group)), packed_quarter(*select(middle_group))), second_same)
    conv_same, middle_same = seq_rotated(packed[0]), seq_rotated(packed[1])
    kept_a = self_attend(normed_a, normed_row, qkv_first, H_SELF, own_seg, seg_row)
    att_a, (second_other, conv_same) = after(kept_a[0], (second_other, conv_same))
    kept_a = (att_a,) + kept_a[1:]
    conv_near = [near_swapped(piece) for piece in conv_same]
    query_cross, kv_cross, out_first = joined_group(*select(second_group), interleaved(second_same, second_other), 2)
    pairs_b = turned_dot(kv_cross, mem_rows).astype(jnp.bfloat16)
    query_b = turned_dot(query_cross, normed_a).astype(jnp.bfloat16)
    out_b, total_b = attend_forward(query_b, pairs_b, H_CROSS, False, own_seg, mem_seg)
    out_b, conv_near = after(out_b, conv_near)
    conv_across = [core_swapped(jnp.concatenate(pair, 0)) for pair in zip(conv_same, conv_near)]
    hidden_b = (
        inputs
        + out_dot(kept_a[0], out_first[:model_width])
        + out_dot(out_b, out_first[model_width:])
    )
    hidden_b, middle_same = after(hidden_b, middle_same)
    middle_near = [near_swapped(piece) for piece in middle_same]
    proj_left, proj_right, proj_mid = joined_group(
        *select(conv_group), interleaved(conv_same, conv_near, conv_across), 4
    )
    normed_c = layer_norm(hidden_b, gain_rows[1]).astype(jnp.bfloat16)
    conv_l, conv_r, conv_m, hidden_c, normed_d = conv_forward(
        hidden_b,
        normed_c,
        passed_along(normed_c[tok_count - RIM :], "seq", 1),
        since,
        left_taps,
        right_taps,
        mid_taps,
        mid_gain_f[None],
        gain_rows[2:3],
        proj_left,
        proj_right,
        proj_mid,
    )
    normed_d, middle_near = after(normed_d, middle_near)
    middle_across = [core_swapped(jnp.concatenate(pair, 0)) for pair in zip(middle_same, middle_near)]
    middle_pieces = interleaved(middle_same, middle_near, middle_across)
    down_at = sum(shard.shape[1] for shard in shards[12:18])
    down, _ = joined_weight(shards[18], 1, middle_pieces, down_at, 4)
    conv_rims = passed_along(jnp.concatenate([conv_l[:RIM], conv_r[:RIM]], 1), "seq", -1)
    more = jnp.stack(seq_rotated(normed_d))
    result, grad_now, d_normed, d_middle, d_gains_late, d_mem = middle(
        hidden_c,
        normed_d,
        more,
        mem_rows,
        grad_out[0],
        gain_rows[3:5],
        own_seg,
        seg_row,
        mem_seg,
        down,
        shards[12:18],
        middle_pieces,
    )
    part_a = offload_rows(d_middle, can_order(model_width))
    d_hidden, g_three = norm_back(hidden_c, gain_rows[2], row_sum_owned(d_normed))
    grad_now = grad_now + d_hidden
    branch = grad_now.astype(jnp.bfloat16)
    grad_now, d_projections, d_taps_left, d_taps_right, d_taps_mid, d_mid_gain, g_two = conv_back(
        grad_now,
        passed_along(branch[:RIM], "seq", -1),
        conv_l,
        conv_r,
        conv_rims,
        conv_m,
        normed_c,
        hidden_b,
        left,
        left_taps,
        right_taps,
        mid_taps,
        mid_gain_f[None],
        gain_rows[1:2],
        proj_left,
        proj_right,
        proj_mid,
    )
    d_mid_gain, g_two = d_mid_gain[0], g_two[0]
    branch = grad_now.astype(jnp.bfloat16)
    d_out_first = jnp.concatenate(
        [out_weight_dot(kept_a[0], branch), out_weight_dot(out_b, branch)], 1
    )
    d_att_a = turned_back(branch, out_first[:model_width]).astype(jnp.bfloat16)
    d_att_b = turned_back(branch, out_first[model_width:]).astype(jnp.bfloat16)
    dq_b, dkv_b = attend_back(
        query_b, pairs_b, d_att_b, out_b, total_b, H_CROSS, False, own_seg, mem_seg
    )
    d_query_cross = weight_dot(normed_a, dq_b)
    d_normed, d_qkv_first = self_back(
        normed_a, qkv_first, d_att_a, kept_a, H_SELF, own_seg, seg_row
    )
    d_normed, part_a = after(d_normed, part_a)
    part_a = offload_seq(part_a)
    d_normed = d_normed + input_back(dq_b, query_cross)
    d_hidden, g_one = norm_back(inputs, gain_rows[0], d_normed)
    grad_in = grad_now + d_hidden
    grad_mem = row_sum_owned(
        (input_back(dkv_b, kv_cross) + d_mem.T).astype(jnp.bfloat16)
    )
    d_kv_cross = weight_dot(mem_rows, dkv_b)
    d_gains = jnp.concatenate([jnp.stack([g_one, g_two, g_three], 0), d_gains_late], 0)
    wide, narrow = proj_left.shape[1], proj_right.shape[1]
    width = model_width // lax.axis_size("seq")
    small_grads = (d_gains, d_taps_left, d_taps_right, d_mid_gain, d_taps_mid)
    last = [d_projections] + [
        piece.astype(jnp.bfloat16) for piece in (d_out_first, d_kv_cross, d_query_cross, d_qkv_first)
    ]
    last.append(small_columns(small_grads, width))
    part_c = share_summed(last)
    shares = [None] * len(shards)
    up = down.shape[0]
    part_a = offload_back(part_a)
    for part, group, sizes in (
        (
            part_a,
            (17, 18, 16, 14, 15, 12, 13),
            (up, up, model_width, model_width, 2 * model_width, 3 * model_width, model_width),
        ),
        (
            part_c,
            (11, 6, 8, 4, 3, 2, 1),
            (wide, wide, narrow, 2 * model_width, 2 * model_width, model_width, 3 * model_width),
        ),
    ):
        offset = 0
        for k, size in zip(group, sizes):
            piece = part[:, offset : offset + size].astype(jnp.float32)
            shares[k] = piece if shard_dims[k] == 0 else piece.T
            offset = offset + size
    parts = small_shares(part_c[:, offset : offset + 128].astype(jnp.float32), small_grads, width)
    for k, piece in zip(small, parts):
        shares[k] = piece
    return (
        result[None],
        grad_in[None],
        grad_mem[None],
        shares[0],
        shares[1],
        shares[2],
        shares[3],
        shares[4],
        shares[5],
        shares[6],
        shares[7],
        shares[8],
        shares[9],
        shares[10],
        shares[11],
        shares[12],
        shares[13],
        shares[14],
        shares[15],
        shares[16],
        shares[17],
        shares[18],
    )


def solution(mesh):
    placed = (
        P("rows", "seq", None),
        P("rows", "seq", None),
        P("rows", "seq", None),
        P("rows", None),
        P("rows", None),
        P(None, "seq"),
        P("seq", None),
        P("seq", None),
        P("seq", None),
        P(None, "seq"),
        P(None, "seq"),
        P("seq", None),
        P(None, "seq"),
        P("seq", None),
        P("seq"),
        P(None, "seq"),
        P(None, "seq"),
        P("seq", None),
        P("seq", None),
        P("seq", None),
        P("seq", None),
        P("seq", None),
        P("seq", None),
        P(None, "seq"),
    )
    return jax.shard_map(
        local,
        mesh=mesh,
        in_specs=placed,
        out_specs=(
            P("rows", "seq", None),
            P("rows", "seq", None),
            P("rows", "seq", None),
            P(None, "seq"),
            P("seq", None),
            P("seq", None),
            P("seq", None),
            P(None, "seq"),
            P(None, "seq"),
            P("seq", None),
            P(None, "seq"),
            P("seq", None),
            P("seq"),
            P(None, "seq"),
            P(None, "seq"),
            P("seq", None),
            P("seq", None),
            P("seq", None),
            P("seq", None),
            P("seq", None),
            P("seq", None),
            P(None, "seq"),
        ),
        check_vma=False,
    )
```

```python
import functools

import jax
import jax.numpy as jnp
from jax import lax
from jax.experimental import pallas as pl
from jax.experimental.pallas import tpu as pltpu
from jax.sharding import PartitionSpec as P

H_SELF = 16
H_CROSS = 8
WIDE = 1024
NARROW = 256
LEFT_TAPS = 11
RIGHT_TAPS = 7


NEG_BIG = -1e30
EPSILON = 1e-06


def rotated(block, axis, distance):
    size = lax.axis_size(axis)
    return lax.ppermute(block, axis, [((i + distance) % size, i) for i in range(size)])


def core_swapped(block):
    return lax.ppermute(block, "rows", [(i, i ^ 1) for i in range(lax.axis_size("rows"))])


def in_place_order(relative, dim):
    count = len(relative)
    place = lax.axis_index("seq")
    orders = [
        jnp.concatenate([relative[(p - me) % count] for p in range(count)], dim)
        for me in range(count)
    ]
    result = orders[0]
    for me in range(1, count):
        result = jnp.where(place == me, orders[me], result)
    return result


def gathered(block, dim=0):
    count = lax.axis_size("seq")
    return in_place_order([block] + [rotated(block, "seq", d) for d in range(1, count)], dim)


def near_swapped(block):
    return lax.ppermute(block, "rows", [(i, i ^ 2) for i in range(lax.axis_size("rows"))])


def flat_share(shard, dim, index, count):
    size = shard.shape[0] // count
    part = lax.dynamic_slice_in_dim(shard, index * size, size)
    if dim == 0:
        return part
    width = shard.shape[1]
    blocks = part.reshape(-1, width // count, width)
    return jnp.swapaxes(blocks, 0, 1).reshape(width // count, -1)


def unflat_share(part, shape, dim, count):
    if dim == 0:
        return part
    width = shape[1]
    blocks = part.reshape(width // count, -1, width)
    return jnp.swapaxes(blocks, 0, 1).reshape(shape[0] // count, width)


def seq_rotated(packed):
    return [rotated(packed, "seq", d) for d in range(1, lax.axis_size("seq"))]


def packed_half(shards, dims):
    core = lax.axis_index("rows") & 1
    return jnp.concatenate([flat_share(shard, dim, core, 2) for shard, dim in zip(shards, dims)], 1)


def packed_quarter(shards, dims):
    index = lax.axis_index("rows") & 3
    return jnp.concatenate([flat_share(shard, dim, index, 4) for shard, dim in zip(shards, dims)], 1)


def ordered(bit, first, second):
    return jnp.where(bit == 0, jnp.concatenate([first, second], 0), jnp.concatenate([second, first], 0))


def joined_weight(shard, dim, pieces, offset, count):
    row = lax.axis_index("rows")
    size = shard.size // count // pieces[0].shape[0]

    def part(piece):
        return unflat_share(piece[:, offset : offset + size], shard.shape, dim, count)

    relative = [shard]
    if count == 2:
        for k in range(0, len(pieces), 2):
            relative.append(ordered(row & 1, part(pieces[k]), part(pieces[k + 1])))
    else:
        for k in range(0, len(pieces), 3):
            same, near, across = pieces[k : k + 3]
            rows = same.shape[0]
            own_pair = ordered(row & 1, part(same), part(across[:rows]))
            near_pair = ordered(row & 1, part(near), part(across[rows:]))
            relative.append(ordered(row & 2, own_pair, near_pair))
    return in_place_order(relative, dim), offset + size


def joined_group(shards, dims, pieces, count):
    results = []
    offset = 0
    for shard, dim in zip(shards, dims):
        full, offset = joined_weight(shard, dim, pieces, offset, count)
        results.append(full)
    return results


def interleaved(*lists):
    return [item for items in zip(*lists) for item in items]


def small_gather(shards, dims):
    sizes = [shard.size for shard in shards]
    flat = jnp.concatenate([shard.reshape(-1) for shard in shards])
    flat = padded_rows(flat, 2048, 0).reshape(-1, 128)
    parts = [flat] + [rotated(flat, "seq", d) for d in range(1, lax.axis_size("seq"))]
    parts = [part.reshape(-1) for part in parts]
    results = []
    offset = 0
    for shard, dim, size in zip(shards, dims, sizes):
        relative = [part[offset : offset + size].reshape(shard.shape) for part in parts]
        results.append(in_place_order(relative, dim))
        offset = offset + size
    return results


def padded_rows(block, multiple, dim):
    extra = -block.shape[dim] % multiple
    if not extra:
        return block
    widths = [(0, 0)] * block.ndim
    widths[dim] = (0, extra)
    return jnp.pad(block, widths)


def small_rows(grads, width):
    seq_count = lax.axis_size("seq")
    rows = [
        jnp.moveaxis(grad.reshape(-1, seq_count, grad.shape[-1] // (seq_count * width), width), 1, 2).reshape(
            -1, seq_count * width
        )
        for grad in grads
    ]
    return padded_rows(jnp.concatenate(rows, 0), 128, 0)


def small_shares(columns, grads, width):
    seq_count = lax.axis_size("seq")
    rows = columns.T
    results = []
    offset = 0
    for grad in grads:
        count = grad.size // (seq_count * width)
        shape = grad.shape[:-1] + (grad.shape[-1] // seq_count,)
        results.append(rows[offset : offset + count].reshape(shape))
        offset = offset + count
    return results


def halved_sum(block, axis, bit, dim):
    half = block.shape[dim] // 2
    upper = ((lax.axis_index(axis) & bit) != 0).astype(jnp.int32)
    kept = lax.dynamic_slice_in_dim(block, upper * half, half, dim)
    sent = lax.dynamic_slice_in_dim(block, (1 - upper) * half, half, dim)
    got = lax.ppermute(sent, axis, [(i, i ^ bit) for i in range(lax.axis_size(axis))])
    return (kept.astype(jnp.float32) + got.astype(jnp.float32)).astype(jnp.bfloat16)


def row_sum_owned(partial):
    bit = lax.axis_size("seq") // 2
    while bit:
        partial = halved_sum(partial, "seq", bit, 0)
        bit = bit // 2
    return partial.astype(jnp.float32)


def after(values, others):
    return lax.optimization_barrier((values, others))


def passed_along(block, axis, distance):
    devices = range(lax.axis_size(axis))
    route = [(i - distance, i) for i in devices if i - distance in devices]
    return lax.ppermute(block, axis, route)


def layer_norm(values, gain_vec):
    centre = values - jnp.mean(values, axis=-1, keepdims=True)
    inverse = lax.rsqrt(jnp.mean(centre * centre, axis=-1, keepdims=True) + EPSILON)
    return centre * inverse * gain_vec


def norm_back(values, gain_vec, upstream):
    centre = values - jnp.mean(values, axis=-1, keepdims=True)
    inverse = lax.rsqrt(jnp.mean(centre * centre, axis=-1, keepdims=True) + EPSILON)
    normed = centre * inverse
    scaled = upstream * gain_vec
    d_values = inverse * (
        scaled
        - jnp.mean(scaled, axis=-1, keepdims=True)
        - normed * jnp.mean(scaled * normed, axis=-1, keepdims=True)
    )
    return (d_values, jnp.sum(upstream * normed, axis=0))


def swish_slope(pre_act):
    sigma = jax.nn.sigmoid(pre_act)
    return sigma * (1.0 + pre_act * (1.0 - sigma))


def plain_dot(first, second):
    return jnp.dot(first, second, preferred_element_type=jnp.float32)


def left_dot(first, second):
    return jnp.einsum("nk,nm->km", first, second, preferred_element_type=jnp.float32)


def right_dot(grads_in, weight):
    return jnp.einsum("nm,km->nk", grads_in, weight, preferred_element_type=jnp.float32)


TILE = 256
SEG_ROWS = 16
LOG2E = 1.4426950408889634


def tiles_of(extent):
    return [(low, min(low + TILE, extent)) for low in range(0, extent, TILE)]


def tn_dot(first, second):
    return lax.dot_general(first, second, (((0,), (0,)), ((), ())), preferred_element_type=jnp.float32)


def nn_dot(first, second):
    return lax.dot_general(first, second, (((1,), (0,)), ((), ())), preferred_element_type=jnp.float32)


def nt_dot(first, second):
    return lax.dot_general(first, second, (((1,), (1,)), ((), ())), preferred_element_type=jnp.float32)


def row_numbers(width):
    return lax.broadcasted_iota(jnp.int32, (SEG_ROWS, width), 0)


def split_low(values, count):
    pieces = []
    for _ in range(count):
        piece = values.astype(jnp.bfloat16).astype(jnp.float32)
        pieces.append(piece)
        values = values - piece
    return pieces


def key_marks(key_seg, ones):
    rows = row_numbers(key_seg.shape[1])
    marked = jnp.logical_or(rows == key_seg, jnp.logical_and(rows >= 3, rows < 3 + ones))
    return jnp.where(marked, 1.0, 0.0).astype(jnp.bfloat16)


def query_marks(query_seg):
    rows = row_numbers(query_seg.shape[1])
    other = jnp.logical_and(rows < 3, rows != query_seg)
    return jnp.where(other, NEG_BIG, 0.0)


def with_rows(marks, first, pieces):
    rows = row_numbers(marks.shape[1])
    for k, piece in enumerate(pieces):
        marks = jnp.where(rows == first + k, piece, marks)
    return marks.astype(jnp.bfloat16)


def triangle(scores, low):
    key_at = lax.broadcasted_iota(jnp.int32, scores.shape, 0)
    query_at = lax.broadcasted_iota(jnp.int32, scores.shape, 1) + low
    return jnp.where(key_at <= query_at, scores, NEG_BIG)


FWD_HEADS = 4
BWD_HEADS = 4


def attend_kernel(heads, causal, place_ref, *refs):
    attend_core(heads, causal, place_ref[0], *refs)


def attend_core(
    heads, causal, place, qt_ref, pair_ref, qseg_ref, kseg_ref, ot_ref, total_ref, kmark_ref, sum_ref, peak_ref, score_ref
):
    width, tokens = qt_ref.shape
    size = width // heads
    factor = size ** (-0.5) * LOG2E
    block = tokens if causal else pair_ref.shape[1]
    place = place if causal else 0
    kmark_ref[...] = key_marks(kseg_ref[...], 0)
    value_marks = jnp.where(row_numbers(TILE) == 0, 1.0, 0.0).astype(jnp.bfloat16)
    qmarks = query_marks(qseg_ref[...]).astype(jnp.bfloat16)
    tiles = tiles_of(tokens)

    def head_rows(head, base=0):
        return pl.ds(pl.multiple_of(base + head * size, size), size)

    def on_units(several, start, first):
        units = [(k, head, low, high) for k, head in enumerate(several) for low, high in tiles]

        def key_parts(unit):
            _, _, _, high = unit
            return tiles_of(high if first and causal else block)

        def lanes_of(part):
            return pl.ds(pl.multiple_of(start + part[0], 128), part[1] - part[0])

        def score_part(unit, slot, part):
            k, head, low, high = unit
            query_rows = jnp.concatenate([qt_ref[head_rows(head), low:high], qmarks[:, low:high]], 0)
            lanes = lanes_of(part)
            scores = tn_dot(jnp.concatenate([pair_ref[head_rows(head), lanes], kmark_ref[:, lanes]], 0), query_rows)
            if first and causal and part[0] >= low:
                scores = triangle(scores, low - part[0])
            score_ref[slot, part[0] : part[1], : high - low] = scores
            return jnp.max(scores, axis=0, keepdims=True)

        def value_part(unit, slot, part, peak):
            k, head, low, high = unit
            scores = score_ref[slot, part[0] : part[1], : high - low]
            weights = jnp.exp2((scores - peak) * factor).astype(jnp.bfloat16)
            value_rows = jnp.concatenate(
                [pair_ref[head_rows(head, width), lanes_of(part)], value_marks[:, : part[1] - part[0]]], 0
            )
            return nn_dot(value_rows, weights)

        held = None
        for at in range(len(units) + 1):
            unit = units[at] if at < len(units) else None
            parts = key_parts(unit) if unit else []
            old_parts = key_parts(held[0]) if held else []
            peak = None
            if unit and not first:
                peak = peak_ref[unit[0], :, unit[2] : unit[3]]
            before = peak
            summed = None
            for step in range(max(len(parts), len(old_parts))):
                if step < len(parts):
                    found = score_part(unit, at % 2, parts[step])
                    peak = found if peak is None else jnp.maximum(peak, found)
                if step < len(old_parts):
                    term = value_part(held[0], (at - 1) % 2, old_parts[step], held[1])
                    summed = term if summed is None else summed + term
            if held:
                k, _, low, high = held[0]
                if not first:
                    summed = summed + sum_ref[k, :, low:high] * jnp.exp2((held[2] - held[1]) * factor)
                sum_ref[k, :, low:high] = summed
                peak_ref[k, :, low:high] = held[1]
            held = (unit, peak, before)

    def some_heads(step, carry):
        several = [step * FWD_HEADS + k for k in range(FWD_HEADS)]
        on_units(several, place * block, True)
        if causal:

            def earlier(back, held):
                on_units(several, back * block, False)
                return held

            lax.fori_loop(0, place, earlier, 0)
        for k, head in enumerate(several):
            total = sum_ref[k, size : size + 1, :]
            ot_ref[head_rows(head), :] = (sum_ref[k, :size, :] / total).astype(jnp.bfloat16)
            total_ref[head] = peak_ref[k] + jnp.log2(total) / factor
        return carry

    lax.fori_loop(0, heads // FWD_HEADS, some_heads, 0)


def attend_back_kernel(heads, causal, place_ref, *refs):
    attend_back_core(heads, causal, place_ref[0], *refs)


def attend_back_core(
    heads, causal, place, qt_ref, pair_ref, gt_ref, ot_ref, total_ref, qseg_ref, kseg_ref,
    dq_ref, dpair_ref, kmark_ref, dkh_ref, dvh_ref, dqh_ref, qrow_ref, grow_ref, weight_ref, slope_ref,
    pump=None,
):
    width, tokens = qt_ref.shape
    size = width // heads
    scale = size ** (-0.5)
    factor = scale * LOG2E
    block = tokens if causal else pair_ref.shape[1]
    place = place if causal else 0
    kmark_ref[...] = key_marks(kseg_ref[...], 3)
    value_marks = jnp.where(row_numbers(TILE) < 2, 1.0, 0.0).astype(jnp.bfloat16)
    qmarks = query_marks(qseg_ref[...])
    tiles = tiles_of(tokens)

    def head_rows(head, base=0):
        return pl.ds(pl.multiple_of(base + head * size, size), size)

    def prepare(k, head):
        own = head_rows(head)
        grads = gt_ref[own, :]
        delta = jnp.sum(grads.astype(jnp.float32) * ot_ref[own, :].astype(jnp.float32), axis=0, keepdims=True)
        qrow_ref[k, :size, :] = qt_ref[own, :]
        qrow_ref[k, size : size + SEG_ROWS, :] = with_rows(qmarks, 3, split_low(-total_ref[head], 3))
        grow_ref[k, :size, :] = grads
        grow_ref[k, size : size + SEG_ROWS, :] = with_rows(jnp.zeros_like(qmarks), 0, split_low(-delta, 2))

    def on_units(several, start, first):
        units = [(k, head, low, high) for k, head in enumerate(several) for low, high in tiles]

        def key_parts(unit):
            _, _, _, high = unit
            return tiles_of(high if first and causal else block)

        def lanes_of(part):
            return pl.ds(pl.multiple_of(start + part[0], 128), part[1] - part[0])

        def score_part(unit, slot, part):
            k, head, low, high = unit
            lanes = lanes_of(part)
            key_rows = jnp.concatenate([pair_ref[head_rows(head), lanes], kmark_ref[:, lanes]], 0)
            value_rows = jnp.concatenate(
                [pair_ref[head_rows(head, width), lanes], value_marks[:, : part[1] - part[0]]], 0
            )
            scores = tn_dot(key_rows, qrow_ref[k, : size + SEG_ROWS, low:high])
            if first and causal and part[0] >= low:
                scores = triangle(scores, low - part[0])
            weights = jnp.exp2(scores * factor)
            slopes = tn_dot(value_rows, grow_ref[k, : size + SEG_ROWS, low:high])
            weight_ref[slot, part[0] : part[1], : high - low] = weights.astype(jnp.bfloat16)
            slope_ref[slot, part[0] : part[1], : high - low] = (weights * slopes).astype(jnp.bfloat16)

        def grad_part(unit, slot, part):
            k, head, low, high = unit
            lanes = lanes_of(part)
            weights = weight_ref[slot, part[0] : part[1], : high - low]
            slopes = slope_ref[slot, part[0] : part[1], : high - low]
            dvh_ref[k, :, lanes] += nt_dot(grow_ref[k, :size, low:high], weights)
            dkh_ref[k, :, lanes] += nt_dot(qrow_ref[k, :size, low:high], slopes)
            return nn_dot(pair_ref[head_rows(head), lanes], slopes)

        held = None
        for at in range(len(units) + 1):
            unit = units[at] if at < len(units) else None
            parts = key_parts(unit) if unit else []
            old_parts = key_parts(held) if held else []
            summed = None
            for step in range(max(len(parts), len(old_parts))):
                if step < len(parts):
                    score_part(unit, at % 2, parts[step])
                if step < len(old_parts):
                    term = grad_part(held, (at - 1) % 2, old_parts[step])
                    summed = term if summed is None else summed + term
            if held:
                k, _, low, high = held
                if first:
                    dqh_ref[k, :size, low:high] = summed
                else:
                    dqh_ref[k, :size, low:high] += summed
            held = unit

    def some_heads(step, carry):
        several = [step * BWD_HEADS + k for k in range(BWD_HEADS)]
        if pump is not None:
            pump(step)
        dkh_ref[...] = jnp.zeros_like(dkh_ref)
        dvh_ref[...] = jnp.zeros_like(dvh_ref)
        for k, head in enumerate(several):
            prepare(k, head)
        on_units(several, place * block, True)
        if causal:

            def earlier(back, held):
                on_units(several, back * block, False)
                return held

            lax.fori_loop(0, place, earlier, 0)
        for k, head in enumerate(several):
            dq_ref[head_rows(head), :] = (dqh_ref[k, :size, :] * scale).astype(jnp.bfloat16)
            dpair_ref[head_rows(head), :] = (dkh_ref[k] * scale).astype(jnp.bfloat16)
            dpair_ref[head_rows(head, width), :] = dvh_ref[k].astype(jnp.bfloat16)
        return carry

    lax.fori_loop(0, heads // BWD_HEADS, some_heads, 0)


IN_SMEM = pl.BlockSpec(memory_space=pltpu.SMEM)
IN_VMEM = pl.BlockSpec(memory_space=pltpu.VMEM)
KERNEL_VMEM = 48 * 2**20


LANE_GROUP = 128


def attend_forward(queries, pairs_t, heads, causal, query_seg, key_seg):
    width, tokens = queries.shape
    total_keys = pairs_t.shape[1]
    pairs = heads * tokens * total_keys
    return pl.pallas_call(
        functools.partial(attend_kernel, heads, causal),
        out_shape=(
            jax.ShapeDtypeStruct((width, tokens), jnp.bfloat16),
            jax.ShapeDtypeStruct((heads, 1, tokens), jnp.float32),
        ),
        in_specs=[IN_SMEM] + [IN_VMEM] * 4,
        out_specs=(IN_VMEM, IN_VMEM),
        scratch_shapes=[
            pltpu.VMEM((SEG_ROWS, total_keys), jnp.bfloat16),
            pltpu.VMEM((FWD_HEADS, width // heads + SEG_ROWS, tokens), jnp.float32),
            pltpu.VMEM((FWD_HEADS, 1, tokens), jnp.float32),
            pltpu.VMEM((2, tokens if causal else total_keys, TILE), jnp.float32),
        ],
        compiler_params=pltpu.CompilerParams(vmem_limit_bytes=KERNEL_VMEM),
        cost_estimate=pl.CostEstimate(
            flops=pairs * 600, bytes_accessed=4 * width * total_keys, transcendentals=pairs
        ),
        name="attend_fwd",
    )(lax.axis_index("seq").reshape(1), queries, pairs_t, query_seg[None], key_seg[None])


def attend_back(queries, pairs_t, grads, outs, totals, heads, causal, query_seg, key_seg):
    width, tokens = queries.shape
    total_keys = pairs_t.shape[1]
    pairs = heads * tokens * total_keys
    size = width // heads
    return pl.pallas_call(
        functools.partial(attend_back_kernel, heads, causal),
        out_shape=(
            jax.ShapeDtypeStruct((width, tokens), jnp.bfloat16),
            jax.ShapeDtypeStruct((2 * width, total_keys), jnp.bfloat16),
        ),
        in_specs=[IN_SMEM] + [IN_VMEM] * 7,
        out_specs=(IN_VMEM, IN_VMEM),
        scratch_shapes=[
            pltpu.VMEM((SEG_ROWS, total_keys), jnp.bfloat16),
            pltpu.VMEM((BWD_HEADS, size, total_keys), jnp.float32),
            pltpu.VMEM((BWD_HEADS, size, total_keys), jnp.float32),
            pltpu.VMEM((BWD_HEADS, size, tokens), jnp.float32),
            pltpu.VMEM((BWD_HEADS, size + SEG_ROWS, tokens), jnp.bfloat16),
            pltpu.VMEM((BWD_HEADS, size + SEG_ROWS, tokens), jnp.bfloat16),
            pltpu.VMEM((2, tokens if causal else total_keys, TILE), jnp.bfloat16),
            pltpu.VMEM((2, tokens if causal else total_keys, TILE), jnp.bfloat16),
        ],
        compiler_params=pltpu.CompilerParams(vmem_limit_bytes=KERNEL_VMEM),
        cost_estimate=pl.CostEstimate(
            flops=pairs * 1500, bytes_accessed=8 * width * total_keys, transcendentals=pairs
        ),
        name="attend_bwd",
    )(
        lax.axis_index("seq").reshape(1), queries, pairs_t, grads, outs, totals,
        query_seg[None], key_seg[None],
    )


RIM = 16
ROW_TILE = 64
MERGE_ROWS = 64


def row_tiles(extent, tile):
    return [(low, min(low + tile, extent)) for low in range(0, extent, tile)]


def halves_of(extent):
    middle = -(-extent // 32) * 16
    return [(0, middle), (middle, extent)]


def group_lanes(group):
    return pl.ds(pl.multiple_of(group * 128, 128), 128)


def wide_rows(column, width=128):
    return jnp.broadcast_to(column, (column.shape[0], width))


def loop_rows(extent, tile, body):
    def step(k, carry):
        body(pl.ds(pl.multiple_of(k * tile, tile), tile))
        return carry

    whole = extent // tile
    lax.fori_loop(0, whole, step, 0)
    if whole * tile < extent:
        body(pl.ds(whole * tile, extent - whole * tile))


def rows_normed(values):
    centre = values - jnp.mean(values, axis=-1, keepdims=True)
    inverse = lax.rsqrt(jnp.mean(centre * centre, axis=-1, keepdims=True) + EPSILON)
    return centre * inverse, inverse


def rows_norm_back(normed, inverse, gain_vec, upstream):
    scaled = upstream * gain_vec
    return inverse * (
        scaled
        - jnp.mean(scaled, axis=-1, keepdims=True)
        - normed * jnp.mean(scaled * normed, axis=-1, keepdims=True)
    )


def taps_forward(source_ref, first_row, since, lanes, low, high, weights):
    result = None
    for offset, weight in enumerate(weights):
        start = first_row + low - offset
        window = source_ref[start : start + high - low, lanes]
        if offset:
            window = jnp.where(since >= offset, window, 0.0)
        term = window * weight
        result = term if result is None else result + term
    return result


def conv_fwd_kernel(
    h1_ref, a2_ref, rim_ref, since_ref, tl_ref, tr_ref, tm_ref, mgain_ref, gain_ref, pl_ref, pr_ref, pm_ref,
    cl_ref, cr_ref, cm_ref, h2_ref, a3_ref,
    ext_ref, wide_ref, cle_ref, cre_ref, up_ref, mixed_ref,
):
    tokens, width = h1_ref.shape
    total = tokens + RIM
    narrow = pr_ref.shape[1]
    ext_ref[0:RIM, :] = jnp.zeros((RIM, width), jnp.float32)
    ext_ref[RIM : 2 * RIM, :] = rim_ref[...].astype(jnp.float32)
    ext_ref[2 * RIM :, :] = a2_ref[...].astype(jnp.float32)
    wide_ref[...] = wide_rows(since_ref[...])

    def first_convs(group, carry):
        lanes = group_lanes(group)
        left = [tl_ref[j : j + 1, lanes] for j in range(tl_ref.shape[0])]
        right = [tr_ref[j : j + 1, lanes] for j in range(tr_ref.shape[0])]
        for low, high in row_tiles(total, ROW_TILE):
            since = wide_ref[low:high, :]
            cle_ref[low:high, lanes] = taps_forward(ext_ref, RIM, since, lanes, low, high, left).astype(jnp.bfloat16)
            cre_ref[low:high, lanes] = taps_forward(ext_ref, RIM, since, lanes, low, high, right).astype(jnp.bfloat16)
        return carry

    lax.fori_loop(0, width // 128, first_convs, 0)
    cl_ref[...] = cle_ref[RIM:, :]
    cr_ref[...] = cre_ref[RIM:, :]
    for low, high in halves_of(total):
        up_ref[low:high, :] = nn_dot(cle_ref[low:high, :], pl_ref[...])
        mixed_ref[low:high, :narrow] = nn_dot(cre_ref[low:high, :], pr_ref[...])

    def merge_rows(rows):
        pre = up_ref[rows, :]
        merged = pre / (1.0 + jnp.exp(-pre))
        merged = jnp.concatenate([merged[:, :narrow] + mixed_ref[rows, :narrow], merged[:, narrow:]], 1)
        normed, _ = rows_normed(merged)
        mixed_ref[rows, :] = (normed * mgain_ref[...]).astype(jnp.bfloat16).astype(jnp.float32)

    loop_rows(total, MERGE_ROWS, merge_rows)

    def mid_conv(group, carry):
        lanes = group_lanes(group)
        weights = [tm_ref[j : j + 1, lanes] for j in range(tm_ref.shape[0])]
        for low, high in row_tiles(tokens, ROW_TILE):
            since = wide_ref[RIM + low : RIM + high, :]
            cm_ref[low:high, lanes] = taps_forward(mixed_ref, RIM, since, lanes, low, high, weights).astype(jnp.bfloat16)
        return carry

    lax.fori_loop(0, mixed_ref.shape[1] // 128, mid_conv, 0)
    for low, high in halves_of(tokens):
        h2_ref[low:high, :] = h1_ref[low:high, :] + nn_dot(cm_ref[low:high, :], pm_ref[...])

    def norm_rows(rows):
        normed, _ = rows_normed(h2_ref[rows, :])
        a3_ref[rows, :] = (normed * gain_ref[...]).astype(jnp.bfloat16)

    loop_rows(tokens, 64, norm_rows)


def conv_forward(h1, a2, rim, since, taps_l, taps_r, taps_m, mid_gain, gain, proj_left, proj_right, proj_mid):
    tokens, width = h1.shape
    wide = proj_left.shape[1]
    total = tokens + RIM
    low, full = jnp.bfloat16, jnp.float32
    return pl.pallas_call(
        conv_fwd_kernel,
        out_shape=(
            jax.ShapeDtypeStruct((tokens, width), low),
            jax.ShapeDtypeStruct((tokens, width), low),
            jax.ShapeDtypeStruct((tokens, wide), low),
            jax.ShapeDtypeStruct((tokens, width), full),
            jax.ShapeDtypeStruct((tokens, width), low),
        ),
        in_specs=[IN_VMEM] * 12,
        out_specs=(IN_VMEM,) * 5,
        scratch_shapes=[
            pltpu.VMEM((total + RIM, width), full),
            pltpu.VMEM((total, 128), jnp.int32),
            pltpu.VMEM((total, width), low),
            pltpu.VMEM((total, width), low),
            pltpu.VMEM((total, wide), full),
            pltpu.VMEM((total, wide), full),
        ],
        compiler_params=pltpu.CompilerParams(vmem_limit_bytes=KERNEL_VMEM),
        cost_estimate=pl.CostEstimate(
            flops=tokens * width * wide * 20, bytes_accessed=tokens * width * 16, transcendentals=tokens * wide
        ),
        name="conv_fwd",
    )(h1, a2, rim, since, taps_l, taps_r, taps_m, mid_gain, gain, proj_left, proj_right, proj_mid)


def folded(values):
    return jnp.sum(values.reshape(-1, 8, values.shape[-1]), axis=0)


def taps_back(grad_ref, value, left, lanes, low, high, weights, result, sums):
    for offset, weight in enumerate(weights):
        window = grad_ref[low + offset : high + offset, lanes]
        if offset:
            window = jnp.where(left >= offset, window, 0.0)
        term = window * weight
        result = term if result is None else result + term
        if value is not None:
            product = folded(window * value)
            sums[offset] = product if sums[offset] is None else sums[offset] + product
    return result


def conv_bwd_kernel(
    g2_ref, brim_ref, cl_ref, clrim_ref, cr_ref, crrim_ref, cm_ref, a2_ref, h1_ref, left_ref,
    tl_ref, tr_ref, tm_ref, mgain_ref, gain_ref, pl_ref, pr_ref, pm_ref,
    g1_ref, dw_ref, dtl_ref, dtr_ref, dtm_ref, dmgain_ref, dgain_ref,
    bext_ref, cle_ref, cre_ref, wide_ref, grad_ref, up_ref, back_ref, normed_ref, inv_ref, dpl_ref, dpr_ref, a2f_ref,
):
    tokens, width = g2_ref.shape
    total = tokens + RIM
    wide, narrow = pl_ref.shape[1], pr_ref.shape[1]
    bext_ref[:tokens, :] = g2_ref[...].astype(jnp.bfloat16)
    bext_ref[tokens:, :] = brim_ref[...]
    cle_ref[:tokens, :] = cl_ref[...]
    cle_ref[tokens:, :] = clrim_ref[...]
    cre_ref[:tokens, :] = cr_ref[...]
    cre_ref[tokens:, :] = crrim_ref[...]
    a2f_ref[...] = a2_ref[...].astype(jnp.float32)
    wide_ref[...] = wide_rows(left_ref[...])
    grad_ref[total:, :] = jnp.zeros((RIM, wide), jnp.float32)
    dw_ref[:, :wide] = tn_dot(bext_ref[:tokens, :], cm_ref[...]).astype(jnp.bfloat16)
    for low, high in halves_of(total):
        grad_ref[low:high, :] = nt_dot(bext_ref[low:high, :], pm_ref[...])
        up_ref[low:high, :] = nn_dot(cle_ref[low:high, :], pl_ref[...])
        back_ref[low:high, :narrow] = nn_dot(cre_ref[low:high, :], pr_ref[...])

    def merge_rows(rows):
        pre = up_ref[rows, :]
        merged = pre / (1.0 + jnp.exp(-pre))
        merged = jnp.concatenate([merged[:, :narrow] + back_ref[rows, :narrow], merged[:, narrow:]], 1)
        normed, inverse = rows_normed(merged)
        normed_ref[rows, :] = normed
        inv_ref[rows, :] = wide_rows(inverse)

    loop_rows(total, MERGE_ROWS, merge_rows)

    def mid_back(group, carry):
        lanes = group_lanes(group)
        weights = [tm_ref[j : j + 1, lanes] for j in range(tm_ref.shape[0])]
        sums = [None] * len(weights)
        gain_vec = mgain_ref[:, lanes]
        for low, high in row_tiles(total, ROW_TILE):
            value = None
            if high <= tokens:
                value = (normed_ref[low:high, lanes] * gain_vec).astype(jnp.bfloat16).astype(jnp.float32)
            back_ref[low:high, lanes] = taps_back(
                grad_ref, value, wide_ref[low:high, :], lanes, low, high, weights, None, sums
            )
        for j, piece in enumerate(sums):
            dtm_ref[j : j + 1, lanes] = jnp.sum(piece, axis=0, keepdims=True)
        return carry

    lax.fori_loop(0, wide // 128, mid_back, 0)

    def merge_back(rows):
        pre = up_ref[rows, :]
        normed = normed_ref[rows, :]
        d_merged = rows_norm_back(normed, inv_ref[rows, :][:, :1], mgain_ref[...], back_ref[rows, :])
        sigma = 1.0 / (1.0 + jnp.exp(-pre))
        dpl_ref[rows, :] = (d_merged * (sigma * (1.0 + pre * (1.0 - sigma)))).astype(jnp.bfloat16)
        dpr_ref[rows, :] = d_merged[:, :narrow].astype(jnp.bfloat16)

    loop_rows(total, MERGE_ROWS, merge_back)
    gain_sum = jnp.zeros((8, wide), jnp.float32)

    def gain_rows(k, held):
        rows = pl.ds(pl.multiple_of(k * 16, 16), 16)
        return held + folded(back_ref[rows, :] * normed_ref[rows, :])

    gain_sum = lax.fori_loop(0, tokens // 16, gain_rows, gain_sum)
    dmgain_ref[...] = jnp.sum(gain_sum, axis=0, keepdims=True)
    dw_ref[:, wide : 2 * wide] = tn_dot(cle_ref[:tokens, :], dpl_ref[:tokens, :]).astype(jnp.bfloat16)
    dw_ref[:, 2 * wide :] = tn_dot(cre_ref[:tokens, :], dpr_ref[:tokens, :]).astype(jnp.bfloat16)
    for low, high in halves_of(total):
        grad_ref[low:high, :width] = nt_dot(dpl_ref[low:high, :], pl_ref[...])
        grad_ref[low:high, width : 2 * width] = nt_dot(dpr_ref[low:high, :], pr_ref[...])

    def first_back(group, carry):
        lanes = group_lanes(group)
        other = group_lanes(group + width // 128)
        weights_l = [tl_ref[j : j + 1, lanes] for j in range(tl_ref.shape[0])]
        weights_r = [tr_ref[j : j + 1, lanes] for j in range(tr_ref.shape[0])]
        sums_l = [None] * len(weights_l)
        sums_r = [None] * len(weights_r)
        for low, high in row_tiles(tokens, ROW_TILE):
            left = wide_ref[low:high, :]
            value = a2f_ref[low:high, lanes]
            held = taps_back(grad_ref, value, left, lanes, low, high, weights_l, None, sums_l)
            held = taps_back(grad_ref, value, left, other, low, high, weights_r, held, sums_r)
            back_ref[low:high, lanes] = held
        for j, piece in enumerate(sums_l):
            dtl_ref[j : j + 1, lanes] = jnp.sum(piece, axis=0, keepdims=True)
        for j, piece in enumerate(sums_r):
            dtr_ref[j : j + 1, lanes] = jnp.sum(piece, axis=0, keepdims=True)
        return carry

    lax.fori_loop(0, width // 128, first_back, 0)

    def finish(k, held):
        rows = pl.ds(pl.multiple_of(k * 64, 64), 64)
        normed, inverse = rows_normed(h1_ref[rows, :])
        upstream = back_ref[rows, :width]
        g1_ref[rows, :] = g2_ref[rows, :] + rows_norm_back(normed, inverse, gain_ref[...], upstream)
        return held + folded(upstream * normed)

    gain_sum = lax.fori_loop(0, tokens // 64, finish, jnp.zeros((8, width), jnp.float32))
    dgain_ref[...] = jnp.sum(gain_sum, axis=0, keepdims=True)


def conv_back(
    g2, brim, c_l, c_r, rims, c_m, a2, h1, left, taps_l, taps_r, taps_m, mid_gain, gain, proj_left, proj_right, proj_mid
):
    tokens, width = g2.shape
    wide, narrow = proj_left.shape[1], proj_right.shape[1]
    total = tokens + RIM
    low, full = jnp.bfloat16, jnp.float32
    return pl.pallas_call(
        conv_bwd_kernel,
        out_shape=(
            jax.ShapeDtypeStruct((tokens, width), full),
            jax.ShapeDtypeStruct((width, 2 * wide + narrow), low),
            jax.ShapeDtypeStruct(taps_l.shape, full),
            jax.ShapeDtypeStruct(taps_r.shape, full),
            jax.ShapeDtypeStruct(taps_m.shape, full),
            jax.ShapeDtypeStruct((1, wide), full),
            jax.ShapeDtypeStruct((1, width), full),
        ),
        in_specs=[IN_VMEM] * 18,
        out_specs=(IN_VMEM,) * 7,
        scratch_shapes=[
            pltpu.VMEM((total, width), low),
            pltpu.VMEM((total, width), low),
            pltpu.VMEM((total, width), low),
            pltpu.VMEM((total, 128), jnp.int32),
            pltpu.VMEM((total + RIM, wide), full),
            pltpu.VMEM((total, wide), full),
            pltpu.VMEM((total, wide), full),
            pltpu.VMEM((total, wide), full),
            pltpu.VMEM((total, 128), full),
            pltpu.VMEM((total, wide), low),
            pltpu.VMEM((total, narrow), low),
            pltpu.VMEM((tokens, width), full),
        ],
        compiler_params=pltpu.CompilerParams(vmem_limit_bytes=KERNEL_VMEM),
        cost_estimate=pl.CostEstimate(
            flops=tokens * width * wide * 40, bytes_accessed=tokens * width * 40, transcendentals=tokens * wide
        ),
        name="conv_bwd",
    )(
        g2, brim, c_l, rims[:, :width], c_r, rims[:, width:], c_m, a2, h1, left,
        taps_l, taps_r, taps_m, mid_gain, gain, proj_left, proj_right, proj_mid,
    )


MIDDLE_VMEM = 60 * 2**20
DOT_ROWS = 256


def load_weight(copies, sems, target_ref, own_ref, pieces, offset, place, near, core):
    width, size = own_ref.shape
    quarter = width // 4
    count = len(pieces) // 3 + 1
    columns = slice(offset, offset + size)
    parts = [(own_ref, place * width, width)]
    for d in range(1, count):
        source = lax.rem(place + d, count) * width
        same, close, across = pieces[3 * d - 3 : 3 * d]
        parts.append((same.at[:, columns], source + (2 * near + core) * quarter, quarter))
        parts.append((close.at[:, columns], source + (2 - 2 * near + core) * quarter, quarter))
        parts.append((across.at[:quarter, columns], source + (2 * near + 1 - core) * quarter, quarter))
        parts.append((across.at[quarter:, columns], source + (3 - 2 * near - core) * quarter, quarter))
    for source_ref, start, rows in parts:
        copy = pltpu.make_async_copy(
            source_ref, target_ref.at[pl.ds(pl.multiple_of(start, quarter), rows), :], sems.at[len(copies)]
        )
        copy.start()
        copies.append(copy)
    return offset + size


def wait_for(copies):
    for copy in copies:
        copy.wait()


def norm_into(target_ref, source_ref, gain_vec):
    def body(rows):
        normed, _ = rows_normed(source_ref[rows, :])
        target_ref[rows, :] = (normed * gain_vec).astype(jnp.bfloat16)

    loop_rows(source_ref.shape[0], 64, body)


def norm_back_into(target_ref, base_ref, source_ref, gain_vec, upstream_ref):
    def body(k, held):
        rows = pl.ds(pl.multiple_of(k * 64, 64), 64)
        normed, inverse = rows_normed(source_ref[rows, :])
        upstream = upstream_ref[rows, :]
        target_ref[rows, :] = base_ref[rows, :].astype(jnp.float32) + rows_norm_back(
            normed, inverse, gain_vec, upstream
        )
        return held + folded(upstream * normed)

    held = jnp.zeros((8, source_ref.shape[1]), jnp.float32)
    return jnp.sum(lax.fori_loop(0, source_ref.shape[0] // 64, body, held), axis=0, keepdims=True)


def chunks(extent):
    return row_tiles(extent, DOT_ROWS)


def project_into(target_ref, weight_ref, turned_ref, low, high):
    for start, stop in chunks(high - low):
        target_ref[start:stop, :] = tn_dot(weight_ref[:, low + start : low + stop], turned_ref[...]).astype(jnp.bfloat16)


def store_grad(target_ref, start, values):
    target_ref[:, start : start + values.shape[1]] = values.astype(jnp.bfloat16)


def middle_kernel(
    piece_count,
    place_ref, h2_ref, a3_ref, a3more_ref, mem_ref, gout_ref, gain_ref, qseg_ref, kseg_ref, mseg_ref, down_ref,
    qkv_own, out2_own, query_own, kv_own, out_own, up_own, *rest,
):
    pieces, rest = rest[:piece_count], rest[piece_count:]
    (
        result_ref, g3_ref, da3_ref, dw_ref, dgain_ref, dmem_ref,
        wqkv_ref, wout2_ref, wquery_ref, wkv_ref, wout_ref, wup_ref, sems,
        turned_ref, memt_ref, a4_ref, a4t_ref, qt_ref, pair_ref, attc_ref, totalc_ref,
        qdt_ref, paird_ref, attd_ref, totald_ref, h3_ref, h4_ref, act_ref, dup_ref, low_ref, gt_ref, dq_ref, dpair_ref, dpaird_ref,
        back_ref, wide_ref, kmark_ref, mmark_ref, sum_ref, peak_ref, score_ref,
        dkh_ref, dvh_ref, dkm_ref, dvm_ref, dqh_ref, qrow_ref, grow_ref, weight_ref, slope_ref,
    ) = rest
    tokens, width = h2_ref.shape
    place, near, core = place_ref[0], place_ref[1], place_ref[2]
    seq_count = piece_count // 3 + 1
    high_width = wup_ref.shape[1]
    first, copies = [], []
    offset = load_weight(first, sems.at[0], wqkv_ref, qkv_own, pieces, 0, place, near, core)
    for target, own in ((wout2_ref, out2_own), (wquery_ref, query_own), (wkv_ref, kv_own), (wout_ref, out_own)):
        offset = load_weight(copies, sems.at[1], target, own, pieces, offset, place, near, core)
    load_weight(copies, sems.at[1], wup_ref, up_own, pieces, offset, place, near, core)

    own = pl.ds(pl.multiple_of(place * tokens, 128), tokens)
    turned_ref[:, own] = a3_ref[...].T
    for d in range(1, seq_count):
        there = pl.ds(pl.multiple_of(lax.rem(place + d, seq_count) * tokens, 128), tokens)
        turned_ref[:, there] = a3more_ref[d - 1].T
    memt_ref[...] = mem_ref[...].T
    wait_for(first)
    project_into(qt_ref, wqkv_ref, turned_ref.at[:, own], 0, width)
    project_into(pair_ref, wqkv_ref, turned_ref, width, 3 * width)
    attend_core(
        H_CROSS, True, place, qt_ref, pair_ref, qseg_ref, kseg_ref, attc_ref, totalc_ref, kmark_ref, sum_ref, peak_ref, score_ref
    )
    wait_for(copies)
    for low, high in chunks(tokens):
        h3_ref[low:high, :] = h2_ref[low:high, :] + tn_dot(attc_ref[:, low:high], wout2_ref[...])
    norm_into(a4_ref, h3_ref, gain_ref[0:1, :])
    a4t_ref[...] = a4_ref[...].T
    project_into(qdt_ref, wquery_ref, a4t_ref, 0, width)
    project_into(paird_ref, wkv_ref, memt_ref, 0, 2 * width)
    attend_core(
        H_CROSS, False, 0, qdt_ref, paird_ref, qseg_ref, mseg_ref, attd_ref, totald_ref, mmark_ref, sum_ref, peak_ref, score_ref
    )
    for low, high in chunks(tokens):
        h4_ref[low:high, :] = h3_ref[low:high, :] + tn_dot(attd_ref[:, low:high], wout_ref[...])
    norm_into(a4_ref, h4_ref, gain_ref[1:2, :])

    for left, right in row_tiles(high_width, 512):
        for low, high in chunks(tokens):
            pre = nn_dot(a4_ref[low:high, :], wup_ref[:, left:right])
            sigma = 1.0 / (1.0 + jnp.exp(-pre))
            act_ref[low:high, left:right] = (pre * sigma).astype(jnp.bfloat16)
            slope = nt_dot(gout_ref[low:high, :], down_ref[left:right, :])
            dup_ref[low:high, left:right] = (slope * (sigma * (1.0 + pre * (1.0 - sigma)))).astype(jnp.bfloat16)
    for low, high in chunks(tokens):
        result_ref[low:high, :] = (h4_ref[low:high, :] + nn_dot(act_ref[low:high, :], down_ref[...])).astype(jnp.bfloat16)
        back_ref[low:high, :] = nt_dot(dup_ref[low:high, :], wup_ref[...])
    for left, right in row_tiles(high_width, 512):
        store_grad(dw_ref, left, tn_dot(a4_ref[...], dup_ref[:, left:right]))
        store_grad(dw_ref, high_width + left, tn_dot(gout_ref[...], act_ref[:, left:right]))

    at = 2 * high_width
    dgain_ref[1:2, :] = norm_back_into(h4_ref, gout_ref, h4_ref, gain_ref[1:2, :], back_ref)
    low_ref[...] = h4_ref[...].astype(jnp.bfloat16)
    store_grad(dw_ref, at, nn_dot(attd_ref[...], low_ref[...]))
    gt_ref[...] = nt_dot(wout_ref[...], low_ref[...]).astype(jnp.bfloat16)
    attend_back_core(
        H_CROSS, False, 0, qdt_ref, paird_ref, gt_ref, attd_ref, totald_ref, qseg_ref, mseg_ref,
        dq_ref, dpaird_ref, mmark_ref, dkm_ref, dvm_ref, dqh_ref, qrow_ref, grow_ref, weight_ref, slope_ref,
    )
    store_grad(dw_ref, at + width, nt_dot(a4t_ref[...], dq_ref[...]))
    store_grad(dw_ref, at + 2 * width, nt_dot(memt_ref[...], dpaird_ref[...]))
    dmem_ref[...] = nn_dot(wkv_ref[...], dpaird_ref[...]).astype(jnp.bfloat16)
    back_ref[...] = nn_dot(wquery_ref[...], dq_ref[...]).T
    dgain_ref[0:1, :] = norm_back_into(g3_ref, h4_ref, h3_ref, gain_ref[0:1, :], back_ref)
    low_ref[...] = g3_ref[...].astype(jnp.bfloat16)
    at = at + 4 * width
    store_grad(dw_ref, at + 3 * width, nn_dot(attc_ref[...], low_ref[...]))
    gt_ref[...] = nt_dot(wout2_ref[...], low_ref[...]).astype(jnp.bfloat16)
    attend_back_core(
        H_CROSS, True, place, qt_ref, pair_ref, gt_ref, attc_ref, totalc_ref, qseg_ref, kseg_ref,
        dq_ref, dpair_ref, kmark_ref, dkh_ref, dvh_ref, dqh_ref, qrow_ref, grow_ref, weight_ref, slope_ref,
    )
    store_grad(dw_ref, at, nt_dot(turned_ref[:, own], dq_ref[...]))
    for low, high in chunks(2 * width):
        store_grad(dw_ref, at + width + low, nt_dot(turned_ref[...], dpair_ref[low:high, :]))
    for low, high in chunks(width):
        wide_ref[low:high, :] = nn_dot(wqkv_ref[low:high, width:], dpair_ref[...])
        wide_ref[low:high, own] += nn_dot(wqkv_ref[low:high, :width], dq_ref[...])
    for low, high in row_tiles(wide_ref.shape[1], tokens):
        da3_ref[low:high, :] = wide_ref[:, low:high].T.astype(jnp.bfloat16)


def middle(h2, a3, a3_more, mem_rows, grad_out, gains, own_seg, seg_row, mem_seg, down, owns, pieces):
    tokens, width = h2.shape
    keys, mems = seg_row.shape[0], mem_seg.shape[0]
    high_width = down.shape[0]
    seq_count = keys // tokens
    size = width // H_CROSS
    low, full = jnp.bfloat16, jnp.float32
    longest = max(tokens, mems)
    v = pltpu.VMEM
    in_hbm = pl.BlockSpec(memory_space=pl.ANY)
    row = lax.axis_index("rows")
    places = jnp.stack([lax.axis_index("seq"), (row // 2) % 2, row % 2]).astype(jnp.int32)
    return pl.pallas_call(
        functools.partial(middle_kernel, len(pieces)),
        out_shape=(
            jax.ShapeDtypeStruct((tokens, width), low),
            jax.ShapeDtypeStruct((tokens, width), full),
            jax.ShapeDtypeStruct((keys, width), low),
            jax.ShapeDtypeStruct((width, 2 * high_width + 8 * width), low),
            jax.ShapeDtypeStruct((2, width), full),
            jax.ShapeDtypeStruct((width, mems), low),
        ),
        in_specs=[IN_SMEM] + [IN_VMEM] * 10 + [in_hbm] * (6 + len(pieces)),
        out_specs=(IN_VMEM,) * 6,
        scratch_shapes=[
            v((width, 3 * width), low),
            v((width, width), low),
            v((width, width), low),
            v((width, 2 * width), low),
            v((width, width), low),
            v((width, high_width), low),
            pltpu.SemaphoreType.DMA((2, 5 * (4 * seq_count - 3))),
            v((width, keys), low),
            v((width, mems), low),
            v((tokens, width), low),
            v((width, tokens), low),
            v((width, tokens), low),
            v((2 * width, keys), low),
            v((width, tokens), low),
            v((H_CROSS, 1, tokens), full),
            v((width, tokens), low),
            v((2 * width, mems), low),
            v((width, tokens), low),
            v((H_CROSS, 1, tokens), full),
            v((tokens, width), full),
            v((tokens, width), full),
            v((tokens, high_width), low),
            v((tokens, high_width), low),
            v((tokens, width), low),
            v((width, tokens), low),
            v((width, tokens), low),
            v((2 * width, keys), low),
            v((2 * width, mems), low),
            v((tokens, width), full),
            v((width, keys), full),
            v((SEG_ROWS, keys), low),
            v((SEG_ROWS, mems), low),
            v((FWD_HEADS, size + SEG_ROWS, tokens), full),
            v((FWD_HEADS, 1, tokens), full),
            v((2, longest, TILE), full),
            v((BWD_HEADS, size, keys), full),
            v((BWD_HEADS, size, keys), full),
            v((BWD_HEADS, size, mems), full),
            v((BWD_HEADS, size, mems), full),
            v((BWD_HEADS, size, tokens), full),
            v((BWD_HEADS, size + SEG_ROWS, tokens), low),
            v((BWD_HEADS, size + SEG_ROWS, tokens), low),
            v((2, longest, TILE), low),
            v((2, longest, TILE), low),
        ],
        compiler_params=pltpu.CompilerParams(vmem_limit_bytes=MIDDLE_VMEM),
        cost_estimate=pl.CostEstimate(
            flops=tokens * width * width * 200, bytes_accessed=tokens * width * 40, transcendentals=tokens * width * 20
        ),
        name="middle",
    )(
        places, h2, a3, a3_more, mem_rows, grad_out, gains, own_seg[None], seg_row[None], mem_seg[None], down,
        *owns, *pieces,
    )


HOST_VMEM = 63 * 2**20 + 2**19


class ShareSum:
    def __init__(self, seq_count, half, total, out_ref, core_ref, across_ref, close_ref, piece_ref, mine_ref, sems):
        self.seq_count, self.half, self.total = seq_count, half, total
        self.out_ref, self.core_ref, self.across_ref = out_ref, core_ref, across_ref
        self.close_ref, self.piece_ref, self.mine_ref = close_ref, piece_ref, mine_ref
        self.send_sem, self.recv_sem, self.local_sem = sems
        self.far_count = lax.axis_size("rows") // 4
        row, place = lax.axis_index("rows"), lax.axis_index("seq")
        self.core, self.near, self.far, self.place = lax.rem(row, 2), lax.rem(row // 2, 2), row // 4, place
        self.mate = (row + 1 - 2 * self.core, place)
        self.close = (row + 2 - 4 * self.near, place)
        self.peers = [None] + [
            (lax.rem(self.far + d, self.far_count) * 4 + self.near * 2 + self.core, place)
            for d in range(1, self.far_count)
        ]
        self.sides = [None] + [(row, lax.rem(place + d, seq_count)) for d in range(1, seq_count)]
        self.step = 2 * self.far_count * LANE_GROUP
        self.wide = self.far_count * LANE_GROUP
        self.count = total // self.step

    def enter(self):
        barrier = pltpu.get_barrier_semaphore()
        friends = [self.mate, self.close] + self.peers[1:] + self.sides[1:]
        for friend in friends:
            pl.semaphore_signal(barrier, inc=1, device_id=friend, device_id_type=pl.DeviceIdType.MESH)
        pl.semaphore_wait(barrier, len(friends))

    def columns(self, chunk):
        return pl.ds(pl.multiple_of(chunk * self.step, LANE_GROUP), self.step)

    def copy(self, chunk, slot, source, target, device):
        return pltpu.make_async_remote_copy(
            src_ref=source,
            dst_ref=target,
            send_sem=self.send_sem.at[chunk, slot],
            recv_sem=self.recv_sem.at[chunk, slot],
            device_id=device,
            device_id_type=pl.DeviceIdType.MESH,
        )

    def core_copy(self, chunk, source_ref, at):
        return self.copy(chunk, 0, source_ref.at[:, 1 - self.core, :, self.columns(at)], self.core_ref.at[chunk], self.mate)

    def side_copy(self, chunk, d):
        away = lax.rem(self.place + d, self.seq_count)
        return self.copy(chunk, d, self.core_ref.at[chunk, away], self.across_ref.at[chunk, d - 1], self.sides[d])

    def near_copy(self, chunk):
        lanes = pl.ds(pl.multiple_of((1 - self.near) * self.wide, LANE_GROUP), self.wide)
        return self.copy(
            chunk, self.seq_count, self.across_ref.at[chunk, 0, :, lanes], self.close_ref.at[chunk], self.close
        )

    def peer_copy(self, chunk, d):
        away = lax.rem(self.far + d, self.far_count)
        lanes = pl.ds(pl.multiple_of(away * LANE_GROUP, LANE_GROUP), LANE_GROUP)
        return self.copy(
            chunk, self.seq_count + d, self.close_ref.at[chunk, :, lanes], self.piece_ref.at[chunk, d - 1], self.peers[d]
        )

    def own_lanes(self, chunk):
        start = chunk * self.step + self.near * self.wide + self.far * LANE_GROUP
        return pl.ds(pl.multiple_of(start, LANE_GROUP), LANE_GROUP)

    def keep_copy(self, chunk):
        return pltpu.make_async_copy(
            self.mine_ref.at[chunk], self.out_ref.at[self.core, :, self.own_lanes(chunk)], self.local_sem.at[chunk]
        )

    def back_copy(self, chunk, d):
        return self.copy(
            chunk,
            self.seq_count + self.far_count - 1 + d,
            self.mine_ref.at[chunk],
            self.out_ref.at[self.core, :, self.own_lanes(chunk)],
            self.peers[d],
        )

    def near_back(self, chunk):
        start = pl.multiple_of(chunk * self.step + self.near * self.wide, LANE_GROUP)
        block = self.out_ref.at[self.core, :, pl.ds(start, self.wide)]
        return self.copy(chunk, self.seq_count + 2 * self.far_count - 1, block, block, self.close)

    def last_copy(self, chunk):
        block = self.out_ref.at[self.core, :, self.columns(chunk)]
        return self.copy(chunk, self.seq_count + 2 * self.far_count, block, block, self.mate)

    def run_side(self, chunk, kept):
        self.core_ref[chunk] = (kept.astype(jnp.float32) + self.core_ref[chunk].astype(jnp.float32)).astype(jnp.bfloat16)
        for d in range(1, self.seq_count):
            self.side_copy(chunk, d).start()

    def run_near(self, chunk):
        for d in range(1, self.seq_count):
            self.side_copy(chunk, d).wait_recv()
        summed = self.core_ref[chunk, self.place].astype(jnp.float32)
        for d in range(1, self.seq_count):
            summed = summed + self.across_ref[chunk, d - 1].astype(jnp.float32)
        self.across_ref[chunk, 0] = summed.astype(jnp.bfloat16)
        self.near_copy(chunk).start()

    def run_peer(self, chunk):
        self.near_copy(chunk).wait_recv()
        lanes = pl.ds(pl.multiple_of(self.near * self.wide, LANE_GROUP), self.wide)
        summed = self.across_ref[chunk, 0, :, lanes].astype(jnp.float32) + self.close_ref[chunk].astype(jnp.float32)
        self.close_ref[chunk] = summed.astype(jnp.bfloat16)
        for d in range(1, self.far_count):
            self.peer_copy(chunk, d).start()

    def run_back(self, chunk):
        for d in range(1, self.far_count):
            self.peer_copy(chunk, d).wait_recv()
        lanes = pl.ds(pl.multiple_of(self.far * LANE_GROUP, LANE_GROUP), LANE_GROUP)
        summed = self.close_ref[chunk, :, lanes].astype(jnp.float32)
        for d in range(1, self.far_count):
            summed = summed + self.piece_ref[chunk, d - 1].astype(jnp.float32)
        self.mine_ref[chunk] = summed.astype(jnp.bfloat16)
        self.keep_copy(chunk).start()
        for d in range(1, self.far_count):
            self.back_copy(chunk, d).start()

    def run_near_back(self, chunk):
        self.keep_copy(chunk).wait()
        for d in range(1, self.far_count):
            self.back_copy(chunk, d).wait_recv()
        self.near_back(chunk).start()

    def run_last(self, chunk):
        self.near_back(chunk).wait_recv()
        self.last_copy(chunk).start()

    def finish(self, chunk):
        self.last_copy(chunk).wait_recv()
        for d in range(1, self.seq_count):
            self.side_copy(chunk, d).wait_send()
        self.near_copy(chunk).wait_send()
        for d in range(1, self.far_count):
            self.peer_copy(chunk, d).wait_send()
            self.back_copy(chunk, d).wait_send()
        self.near_back(chunk).wait_send()
        self.last_copy(chunk).wait_send()

    def tick(self, number):
        stages = (self.run_near, self.run_peer, self.run_back, self.run_near_back, self.run_last, self.finish)
        for late, stage in enumerate(stages):
            if 0 <= number - late < self.count:
                stage(number - late)


def closing_kernel(
    g1_ref, rows_ref, memt_ref, gain_ref, atta_ref, totala_ref, qa_ref, paira_ref,
    attb_ref, totalb_ref, qb_ref, pairb_ref, dmem_ref, small_ref, qseg_ref, kseg_ref, mseg_ref,
    wqkv_ref, wquery_ref, wkv_ref, wout_ref, early_ref, conv_ref,
    da1_ref, dmemory_ref, out_ref,
    turned_ref, branch_ref, gt_ref, dqa_ref, dqb_ref, dpaira_ref, dpairb_ref, kmark_ref, mmark_ref,
    dkh_ref, dvh_ref, dkm_ref, dvm_ref, dqh_ref, qrow_ref, grow_ref, weight_ref, slope_ref,
    late_ref, kept_ref, core_ref, across_ref, close_ref, piece_ref, mine_ref,
    send_sem, recv_sem, local_sem, kept_sem, conv_sem,
):
    tokens, width = g1_ref.shape
    keys = rows_ref.shape[0]
    place = lax.axis_index("seq")
    seq_count, _, half, early = early_ref.shape
    conv_size = conv_ref.shape[-1]
    share = ShareSum(
        seq_count, half, out_ref.shape[-1], out_ref, core_ref, across_ref, close_ref, piece_ref, mine_ref,
        (send_sem, recv_sem, local_sem),
    )
    step = share.step
    early_count = early // step
    middle_count = (conv_size + 5 * width + step - 1) // step
    share.enter()
    slots = kept_ref.shape[0]

    def kept_copy(chunk):
        return pltpu.make_async_copy(
            early_ref.at[:, share.core, :, share.columns(chunk)], kept_ref.at[chunk % slots], kept_sem.at[chunk]
        )

    conv_copy = pltpu.make_async_copy(conv_ref, late_ref.at[:, :, :, :conv_size], conv_sem)
    for chunk in range(early_count):
        share.core_copy(chunk, early_ref, chunk).start()
    for chunk in range(slots):
        kept_copy(chunk).start()
    conv_copy.start()

    def store_late(start, values):
        size = values.shape[1]
        late_ref[:, :, :, start : start + size] = values.astype(jnp.bfloat16).reshape(seq_count, 2, half, size)

    def start_late(first, count):
        for chunk in range(first, first + count):
            share.core_copy(early_count + chunk, late_ref, chunk).start()

    def side_early(first):
        for chunk in range(first, min(first + slots, early_count)):
            share.core_copy(chunk, early_ref, chunk).wait_recv()
            kept_copy(chunk).wait()
            share.run_side(chunk, kept_ref[chunk % slots])
            if chunk + slots < early_count:
                kept_copy(chunk + slots).start()

    def side_late(first, count):
        for chunk in range(first, first + count):
            share.core_copy(early_count + chunk, late_ref, chunk).wait_recv()
            share.run_side(
                early_count + chunk, late_ref[:, share.core, :, chunk * step : (chunk + 1) * step]
            )

    own = pl.ds(pl.multiple_of(place * tokens, 128), tokens)
    for low, high in row_tiles(keys, 128):
        normed, _ = rows_normed(rows_ref[low:high, :].astype(jnp.float32))
        turned_ref[:, low:high] = (normed * gain_ref[...]).astype(jnp.bfloat16).T
    branch_ref[...] = g1_ref[...].astype(jnp.bfloat16).T
    conv_copy.wait()
    store_late(conv_size, nt_dot(branch_ref[...], atta_ref[...]))
    store_late(conv_size + width, nt_dot(branch_ref[...], attb_ref[...]))
    gt_ref[...] = nn_dot(wout_ref[width:, :], branch_ref[...]).astype(jnp.bfloat16)
    side_early(0)
    attend_back_core(
        H_CROSS, False, 0, qb_ref, pairb_ref, gt_ref, attb_ref, totalb_ref, qseg_ref, mseg_ref,
        dqb_ref, dpairb_ref, mmark_ref, dkm_ref, dvm_ref, dqh_ref, qrow_ref, grow_ref, weight_ref, slope_ref,
    )
    for first in range(slots, early_count, slots):
        side_early(first)
    at = conv_size + 2 * width
    store_late(at, nt_dot(memt_ref[...], dpairb_ref[...]))
    store_late(at + 2 * width, nt_dot(turned_ref[:, own], dqb_ref[...]))
    at = at + 3 * width
    after = middle_count * step
    if at < after:
        late_ref[:, :, :, at:after] = jnp.zeros((seq_count, 2, half, after - at), jnp.bfloat16)
    start_late(0, middle_count)
    dmemory_ref[...] = (dmem_ref[...].astype(jnp.float32) + nn_dot(wkv_ref[...], dpairb_ref[...])).T.astype(jnp.bfloat16)
    gt_ref[...] = nn_dot(wout_ref[:width, :], branch_ref[...]).astype(jnp.bfloat16)

    def pump(k):
        @pl.when(k == 1)
        def _():
            side_late(0, middle_count)

        @pl.when(k >= 1)
        def _():
            share.run_near(k - 1)

        @pl.when(k >= 2)
        def _():
            share.run_peer(k - 2)

        @pl.when(k >= 3)
        def _():
            share.run_back(k - 3)

    attend_back_core(
        H_SELF, True, place, qa_ref, paira_ref, gt_ref, atta_ref, totala_ref, qseg_ref, kseg_ref,
        dqa_ref, dpaira_ref, kmark_ref, dkh_ref, dvh_ref, dqh_ref, qrow_ref, grow_ref, weight_ref, slope_ref, pump,
    )
    ticks = H_SELF // BWD_HEADS - 1
    share.tick(ticks)
    store_late(after, nt_dot(turned_ref[:, own], dqa_ref[...]))
    for low, high in chunks(2 * width):
        store_late(after + width + low, nt_dot(turned_ref[...], dpaira_ref[low:high, :]))
    share.tick(ticks + 1)
    gain_sum = jnp.zeros((8, width), jnp.float32)
    for away in range(seq_count):
        start = lax.rem(place + away, seq_count) * tokens
        for low, high in row_tiles(tokens, 128):
            lanes = pl.ds(pl.multiple_of(start + low, 128), high - low)
            upstream = nn_dot(wqkv_ref[:, width:], dpaira_ref[:, lanes])
            if away == 0:
                upstream = upstream + nn_dot(wqkv_ref[:, :width], dqa_ref[:, low:high])
                upstream = upstream + nn_dot(wquery_ref[...], dqb_ref[:, low:high])
            upstream = upstream.T
            normed, _ = rows_normed(rows_ref[lanes, :].astype(jnp.float32))
            gain_sum = gain_sum + folded(upstream * normed)
            da1_ref[lanes, :] = upstream.astype(jnp.bfloat16)
    small = small_ref[...]
    is_first = lax.broadcasted_iota(jnp.int32, small.shape, 0) == 0
    small = jnp.where(is_first, jnp.sum(gain_sum, axis=0, keepdims=True), small)
    at = after + 3 * width
    store_late(at, small.T)
    at = at + small.shape[0]
    if at < late_ref.shape[-1]:
        late_ref[:, :, :, at:] = jnp.zeros((seq_count, 2, half, late_ref.shape[-1] - at), jnp.bfloat16)
    last_count = share.count - early_count - middle_count
    start_late(middle_count, last_count)
    share.tick(ticks + 2)
    side_late(middle_count, last_count)
    for number in range(ticks + 3, share.count + 5):
        share.tick(number)
    for chunk in range(early_count):
        share.core_copy(chunk, early_ref, chunk).wait_send()
    for chunk in range(share.count - early_count):
        share.core_copy(early_count + chunk, late_ref, chunk).wait_send()


def closing(
    g1, row_inputs, mem_turned, gain, self_kept, cross_kept, d_mem, small, own_seg, seg_row, mem_seg,
    qkv, query, pairs_weight, out, early, conv,
):
    tokens, width = g1.shape
    keys, mems = row_inputs.shape[0], mem_turned.shape[1]
    seq_count = keys // tokens
    half = width // (2 * seq_count)
    far_count = lax.axis_size("rows") // 4
    step = 2 * far_count * LANE_GROUP
    size = width // H_CROSS
    middle_total = conv.shape[1] + 5 * width
    middle_total = middle_total + -middle_total % step
    last_total = 3 * width + small.shape[0]
    last_total = last_total + -last_total % step
    early_total = early.shape[1]
    late = middle_total + last_total
    count = (early_total + late) // step
    slots = 3 + (seq_count - 1) + 2 * far_count
    kept_slots = max(1, 2**19 // (seq_count * half * step))
    low, full = jnp.bfloat16, jnp.float32
    longest = max(tokens, mems)
    v = pltpu.VMEM
    in_hbm = pl.BlockSpec(memory_space=pl.ANY)
    dma = pltpu.SemaphoreType.DMA
    d_normed, d_memory, share = pl.pallas_call(
        closing_kernel,
        out_shape=(
            jax.ShapeDtypeStruct((keys, width), low),
            jax.ShapeDtypeStruct((mems, width), low),
            jax.ShapeDtypeStruct((2, half, early_total + late), low),
        ),
        in_specs=[IN_VMEM] * 21 + [in_hbm] * 2,
        out_specs=(IN_VMEM, IN_VMEM, in_hbm),
        scratch_shapes=[
            v((width, keys), low),
            v((width, tokens), low),
            v((width, tokens), low),
            v((width, tokens), low),
            v((width, tokens), low),
            v((2 * width, keys), low),
            v((2 * width, mems), low),
            v((SEG_ROWS, keys), low),
            v((SEG_ROWS, mems), low),
            v((BWD_HEADS, width // H_SELF, keys), full),
            v((BWD_HEADS, width // H_SELF, keys), full),
            v((BWD_HEADS, size, mems), full),
            v((BWD_HEADS, size, mems), full),
            v((BWD_HEADS, size, tokens), full),
            v((BWD_HEADS, size + SEG_ROWS, tokens), low),
            v((BWD_HEADS, size + SEG_ROWS, tokens), low),
            v((2, longest, TILE), low),
            v((2, longest, TILE), low),
            v((seq_count, 2, half, late), low),
            v((kept_slots, seq_count, half, step), low),
            v((count, seq_count, half, step), low),
            v((count, seq_count - 1, half, step), low),
            v((count, half, step // 2), low),
            v((count, far_count - 1, half, LANE_GROUP), low),
            v((count, half, LANE_GROUP), low),
            dma((count, slots)),
            dma((count, slots)),
            dma((count,)),
            dma((early_total // step,)),
            dma(()),
        ],
        compiler_params=pltpu.CompilerParams(
            collective_id=0, has_side_effects=True, vmem_limit_bytes=HOST_VMEM
        ),
        cost_estimate=pl.CostEstimate(
            flops=tokens * width * width * 200, bytes_accessed=tokens * width * 40, transcendentals=tokens * width * 20
        ),
        name="closing",
    )(
        g1, row_inputs, mem_turned, gain, *self_kept, *cross_kept, d_mem, small,
        own_seg[None], seg_row[None], mem_seg[None], qkv, query, pairs_weight, out,
        early.reshape(seq_count, 2, half, early_total), conv.reshape(seq_count, 2, half, conv.shape[1]),
    )
    return d_normed, d_memory, share.reshape(2 * half, early_total + late), early_total, early_total + middle_total


def segment_reach(seg_row):
    length = seg_row.shape[0]
    first = jnp.sum(seg_row == 0)
    second = first + jnp.sum(seg_row == 1)
    spots = jnp.arange(length, dtype=jnp.int32)
    start = jnp.where(seg_row == 0, 0, jnp.where(seg_row == 1, first, second))
    stop = jnp.where(seg_row == 0, first, jnp.where(seg_row == 1, second, length))
    return spots - start, stop - 1 - spots


def turned_dot(weight, values):
    return jnp.einsum("kn,tk->nt", weight, values, preferred_element_type=jnp.float32)


def out_dot(turned, weight):
    return jnp.einsum("nt,nk->tk", turned, weight, preferred_element_type=jnp.float32)


def weight_dot(values, turned):
    return jnp.einsum("tk,nt->kn", values, turned, preferred_element_type=jnp.float32)


def out_weight_dot(turned, grads_in):
    return jnp.einsum("nt,tk->kn", turned, grads_in, preferred_element_type=jnp.float32)


def turned_back(grads_in, weight):
    return jnp.einsum("tk,nk->nt", grads_in, weight, preferred_element_type=jnp.float32)


def input_back(turned, weight):
    return jnp.einsum("nt,kn->tk", turned, weight, preferred_element_type=jnp.float32)


def self_attend(normed, normed_row, weight, head_count, own_seg, seg_row):
    model_width = normed.shape[1]
    queries = turned_dot(weight[:, :model_width], normed).astype(jnp.bfloat16)
    pairs = turned_dot(weight[:, model_width:], normed_row).astype(jnp.bfloat16)
    att_out, totals = attend_forward(queries, pairs, head_count, True, own_seg, seg_row)
    return (att_out, totals, queries, pairs, normed_row)


def self_back(normed, weight, grad_att, kept, head_count, own_seg, seg_row):
    att_out, totals, queries, pairs, normed_row = kept
    model_width = normed.shape[1]
    d_query, d_pairs = attend_back(
        queries, pairs, grad_att, att_out, totals, head_count, True, own_seg, seg_row
    )
    d_weight = jnp.concatenate([weight_dot(normed, d_query), weight_dot(normed_row, d_pairs)], 1)
    d_normed = input_back(d_query, weight[:, :model_width]) + row_sum_owned(
        input_back(d_pairs, weight[:, model_width:]).astype(jnp.bfloat16)
    )
    return (d_normed, d_weight)


def local(
    hidden_in,
    memory,
    grad_out,
    seg_ids,
    mem_seg_ids,
    gains,
    qkv_first,
    query_cross,
    kv_cross,
    out_first,
    taps_left,
    proj_left,
    taps_right,
    proj_right,
    mid_gain,
    taps_mid,
    proj_mid,
    qkv_second,
    out_second,
    query_last,
    kv_last,
    out_last,
    ffn_up,
    ffn_down,
):
    shards = (
        gains,
        qkv_first,
        query_cross,
        kv_cross,
        out_first,
        taps_left,
        proj_left,
        taps_right,
        proj_right,
        mid_gain,
        taps_mid,
        proj_mid,
        qkv_second,
        out_second,
        query_last,
        kv_last,
        out_last,
        ffn_up,
        ffn_down,
    )
    shard_dims = (1, 0, 0, 0, 1, 1, 0, 1, 0, 0, 1, 1, 0, 0, 0, 0, 0, 0, 1)
    small = (0, 5, 7, 9, 10)
    seq_count = lax.axis_size("seq")

    def select(group):
        return [shards[k] for k in group], [shard_dims[k] for k in group]

    first_group, second_group, conv_group, middle_group = (1,), (2, 3, 4), (6, 8, 11), (12, 13, 14, 15, 16, 17, 18)
    hidden_more = seq_rotated(hidden_in[0])
    first_same = seq_rotated(packed_half(*select(first_group)))
    gains, taps_left, taps_right, mid_gain, taps_mid = small_gather(*select(small))
    first_other = [core_swapped(piece) for piece in first_same]
    (qkv_first,) = joined_group(*select(first_group), interleaved(first_same, first_other), 2)
    packed, _ = after((packed_half(*select(second_group)), memory[0]), first_same)
    second_same, mem_more = seq_rotated(packed[0]), seq_rotated(packed[1])
    row_inputs = in_place_order([hidden_in[0]] + hidden_more, 0)
    mem_rows = in_place_order([memory[0]] + mem_more, 0)
    inputs = hidden_in[0].astype(jnp.float32)
    seg_row = seg_ids[0]
    mem_seg = mem_seg_ids[0]
    tok_count, model_width = inputs.shape
    row_start = lax.axis_index("seq") * tok_count
    own_seg = lax.dynamic_slice_in_dim(seg_row, row_start, tok_count)
    since, left = segment_reach(seg_row)
    since = lax.dynamic_slice_in_dim(jnp.pad(since, (RIM, 0)), row_start, tok_count + RIM)[:, None]
    left = lax.dynamic_slice_in_dim(jnp.pad(left, (0, RIM)), row_start, tok_count + RIM)[:, None]
    gain_rows = gains.astype(jnp.float32)
    mid_gain_f = mid_gain.astype(jnp.float32)
    left_taps = taps_left.astype(jnp.float32)
    right_taps = taps_right.astype(jnp.float32)
    mid_taps = taps_mid.astype(jnp.float32)
    normed_a = layer_norm(inputs, gain_rows[0]).astype(jnp.bfloat16)
    normed_row = layer_norm(row_inputs.astype(jnp.float32), gain_rows[0]).astype(jnp.bfloat16)
    normed_a, second_same = after(normed_a, second_same)
    second_other = [core_swapped(piece) for piece in second_same]
    packed, _ = after((packed_quarter(*select(conv_group)), packed_quarter(*select(middle_group))), second_same)
    conv_same, middle_same = seq_rotated(packed[0]), seq_rotated(packed[1])
    kept_a = self_attend(normed_a, normed_row, qkv_first, H_SELF, own_seg, seg_row)
    att_a, (second_other, conv_same) = after(kept_a[0], (second_other, conv_same))
    kept_a = (att_a,) + kept_a[1:]
    conv_near = [near_swapped(piece) for piece in conv_same]
    query_cross, kv_cross, out_first = joined_group(*select(second_group), interleaved(second_same, second_other), 2)
    pairs_b = turned_dot(kv_cross, mem_rows).astype(jnp.bfloat16)
    query_b = turned_dot(query_cross, normed_a).astype(jnp.bfloat16)
    out_b, total_b = attend_forward(query_b, pairs_b, H_CROSS, False, own_seg, mem_seg)
    out_b, conv_near = after(out_b, conv_near)
    conv_across = [core_swapped(jnp.concatenate(pair, 0)) for pair in zip(conv_same, conv_near)]
    hidden_b = (
        inputs
        + out_dot(kept_a[0], out_first[:model_width])
        + out_dot(out_b, out_first[model_width:])
    )
    hidden_b, middle_same = after(hidden_b, middle_same)
    middle_near = [near_swapped(piece) for piece in middle_same]
    proj_left, proj_right, proj_mid = joined_group(
        *select(conv_group), interleaved(conv_same, conv_near, conv_across), 4
    )
    normed_c = layer_norm(hidden_b, gain_rows[1]).astype(jnp.bfloat16)
    conv_l, conv_r, conv_m, hidden_c, normed_d = conv_forward(
        hidden_b,
        normed_c,
        passed_along(normed_c[tok_count - RIM :], "seq", 1),
        since,
        left_taps,
        right_taps,
        mid_taps,
        mid_gain_f[None],
        gain_rows[2:3],
        proj_left,
        proj_right,
        proj_mid,
    )
    normed_d, middle_near = after(normed_d, middle_near)
    middle_across = [core_swapped(jnp.concatenate(pair, 0)) for pair in zip(middle_same, middle_near)]
    middle_pieces = interleaved(middle_same, middle_near, middle_across)
    down_at = sum(shard.shape[1] for shard in shards[12:18])
    down, _ = joined_weight(shards[18], 1, middle_pieces, down_at, 4)
    conv_rims = passed_along(jnp.concatenate([conv_l[:RIM], conv_r[:RIM]], 1), "seq", -1)
    more = jnp.stack(seq_rotated(normed_d))
    result, grad_now, d_normed, d_middle, d_gains_late, d_mem = middle(
        hidden_c,
        normed_d,
        more,
        mem_rows,
        grad_out[0],
        gain_rows[3:5],
        own_seg,
        seg_row,
        mem_seg,
        down,
        shards[12:18],
        middle_pieces,
    )
    d_hidden, g_three = norm_back(hidden_c, gain_rows[2], row_sum_owned(d_normed))
    grad_now = grad_now + d_hidden
    branch = grad_now.astype(jnp.bfloat16)
    grad_now, d_projections, d_taps_left, d_taps_right, d_taps_mid, d_mid_gain, g_two = conv_back(
        grad_now,
        passed_along(branch[:RIM], "seq", -1),
        conv_l,
        conv_r,
        conv_rims,
        conv_m,
        normed_c,
        hidden_b,
        left,
        left_taps,
        right_taps,
        mid_taps,
        mid_gain_f[None],
        gain_rows[1:2],
        proj_left,
        proj_right,
        proj_mid,
    )
    d_mid_gain, g_two = d_mid_gain[0], g_two[0]
    d_gains = jnp.concatenate([jnp.stack([jnp.zeros_like(g_two), g_two, g_three], 0), d_gains_late], 0)
    wide, narrow = proj_left.shape[1], proj_right.shape[1]
    width = model_width // lax.axis_size("seq")
    small_grads = (d_gains, d_taps_left, d_taps_right, d_mid_gain, d_taps_mid)
    d_normed, d_memory, share, second_at, third_at = closing(
        grad_now,
        row_inputs,
        mem_rows.T,
        gain_rows[:1],
        kept_a[:4],
        (out_b, total_b, query_b, pairs_b),
        d_mem,
        small_rows(small_grads, width),
        own_seg,
        seg_row,
        mem_seg,
        qkv_first,
        query_cross,
        kv_cross,
        out_first,
        d_middle,
        d_projections,
    )
    d_hidden, _ = norm_back(inputs, gain_rows[0], row_sum_owned(d_normed))
    grad_in = grad_now + d_hidden
    grad_mem = row_sum_owned(d_memory)
    shares = [None] * len(shards)
    up = down.shape[0]
    for offset, group, sizes in (
        (
            0,
            (17, 18, 16, 14, 15, 12, 13),
            (up, up, model_width, model_width, 2 * model_width, 3 * model_width, model_width),
        ),
        (
            second_at,
            (11, 6, 8, 4, 3, 2),
            (wide, wide, narrow, 2 * model_width, 2 * model_width, model_width),
        ),
        (third_at, (1,), (3 * model_width,)),
    ):
        for k, size in zip(group, sizes):
            piece = share[:, offset : offset + size].astype(jnp.float32)
            shares[k] = piece if shard_dims[k] == 0 else piece.T
            offset = offset + size
    parts = small_shares(share[:, offset : offset + 128].astype(jnp.float32), small_grads, width)
    for k, piece in zip(small, parts):
        shares[k] = piece
    return (
        result[None],
        grad_in[None],
        grad_mem[None],
        shares[0],
        shares[1],
        shares[2],
        shares[3],
        shares[4],
        shares[5],
        shares[6],
        shares[7],
        shares[8],
        shares[9],
        shares[10],
        shares[11],
        shares[12],
        shares[13],
        shares[14],
        shares[15],
        shares[16],
        shares[17],
        shares[18],
    )


def solution(mesh):
    placed = (
        P("rows", "seq", None),
        P("rows", "seq", None),
        P("rows", "seq", None),
        P("rows", None),
        P("rows", None),
        P(None, "seq"),
        P("seq", None),
        P("seq", None),
        P("seq", None),
        P(None, "seq"),
        P(None, "seq"),
        P("seq", None),
        P(None, "seq"),
        P("seq", None),
        P("seq"),
        P(None, "seq"),
        P(None, "seq"),
        P("seq", None),
        P("seq", None),
        P("seq", None),
        P("seq", None),
        P("seq", None),
        P("seq", None),
        P(None, "seq"),
    )
    return jax.shard_map(
        local,
        mesh=mesh,
        in_specs=placed,
        out_specs=(
            P("rows", "seq", None),
            P("rows", "seq", None),
            P("rows", "seq", None),
            P(None, "seq"),
            P("seq", None),
            P("seq", None),
            P("seq", None),
            P(None, "seq"),
            P(None, "seq"),
            P("seq", None),
            P(None, "seq"),
            P("seq", None),
            P("seq"),
            P(None, "seq"),
            P(None, "seq"),
            P("seq", None),
            P("seq", None),
            P("seq", None),
            P("seq", None),
            P("seq", None),
            P("seq", None),
            P(None, "seq"),
        ),
        check_vma=False,
    )
```

```python
import functools

import jax
import jax.numpy as jnp
from jax import lax
from jax.experimental import pallas as pl
from jax.experimental.pallas import tpu as pltpu
from jax.sharding import PartitionSpec as P

H_SELF = 16
H_CROSS = 8
WIDE = 1024
NARROW = 256
LEFT_TAPS = 11
RIGHT_TAPS = 7


NEG_BIG = -1e30
EPSILON = 1e-06


def rotated(block, axis, distance):
    size = lax.axis_size(axis)
    return lax.ppermute(block, axis, [((i + distance) % size, i) for i in range(size)])


def core_swapped(block):
    return lax.ppermute(block, "rows", [(i, i ^ 1) for i in range(lax.axis_size("rows"))])


def in_place_order(relative, dim):
    count = len(relative)
    place = lax.axis_index("seq")
    orders = [
        jnp.concatenate([relative[(p - me) % count] for p in range(count)], dim)
        for me in range(count)
    ]
    result = orders[0]
    for me in range(1, count):
        result = jnp.where(place == me, orders[me], result)
    return result


def gathered(block, dim=0):
    count = lax.axis_size("seq")
    return in_place_order([block] + [rotated(block, "seq", d) for d in range(1, count)], dim)


def near_swapped(block):
    return lax.ppermute(block, "rows", [(i, i ^ 2) for i in range(lax.axis_size("rows"))])


def flat_share(shard, dim, index, count):
    size = shard.shape[0] // count
    part = lax.dynamic_slice_in_dim(shard, index * size, size)
    if dim == 0:
        return part
    width = shard.shape[1]
    blocks = part.reshape(-1, width // count, width)
    return jnp.swapaxes(blocks, 0, 1).reshape(width // count, -1)


def unflat_share(part, shape, dim, count):
    if dim == 0:
        return part
    width = shape[1]
    blocks = part.reshape(width // count, -1, width)
    return jnp.swapaxes(blocks, 0, 1).reshape(shape[0] // count, width)


def seq_rotated(packed):
    return [rotated(packed, "seq", d) for d in range(1, lax.axis_size("seq"))]


def packed_half(shards, dims):
    core = lax.axis_index("rows") & 1
    return jnp.concatenate([flat_share(shard, dim, core, 2) for shard, dim in zip(shards, dims)], 1)


def packed_quarter(shards, dims):
    index = lax.axis_index("rows") & 3
    return jnp.concatenate([flat_share(shard, dim, index, 4) for shard, dim in zip(shards, dims)], 1)


def ordered(bit, first, second):
    return jnp.where(bit == 0, jnp.concatenate([first, second], 0), jnp.concatenate([second, first], 0))


def joined_weight(shard, dim, pieces, offset, count):
    row = lax.axis_index("rows")
    size = shard.size // count // pieces[0].shape[0]

    def part(piece):
        return unflat_share(piece[:, offset : offset + size], shard.shape, dim, count)

    relative = [shard]
    if count == 2:
        for k in range(0, len(pieces), 2):
            relative.append(ordered(row & 1, part(pieces[k]), part(pieces[k + 1])))
    else:
        for k in range(0, len(pieces), 3):
            same, near, across = pieces[k : k + 3]
            rows = same.shape[0]
            own_pair = ordered(row & 1, part(same), part(across[:rows]))
            near_pair = ordered(row & 1, part(near), part(across[rows:]))
            relative.append(ordered(row & 2, own_pair, near_pair))
    return in_place_order(relative, dim), offset + size


def joined_group(shards, dims, pieces, count):
    results = []
    offset = 0
    for shard, dim in zip(shards, dims):
        full, offset = joined_weight(shard, dim, pieces, offset, count)
        results.append(full)
    return results


def interleaved(*lists):
    return [item for items in zip(*lists) for item in items]


def small_gather(shards, dims):
    sizes = [shard.size for shard in shards]
    flat = jnp.concatenate([shard.reshape(-1) for shard in shards])
    flat = padded_rows(flat, 2048, 0).reshape(-1, 128)
    parts = [flat] + [rotated(flat, "seq", d) for d in range(1, lax.axis_size("seq"))]
    parts = [part.reshape(-1) for part in parts]
    results = []
    offset = 0
    for shard, dim, size in zip(shards, dims, sizes):
        relative = [part[offset : offset + size].reshape(shard.shape) for part in parts]
        results.append(in_place_order(relative, dim))
        offset = offset + size
    return results


def padded_rows(block, multiple, dim):
    extra = -block.shape[dim] % multiple
    if not extra:
        return block
    widths = [(0, 0)] * block.ndim
    widths[dim] = (0, extra)
    return jnp.pad(block, widths)


def small_rows(grads, width):
    seq_count = lax.axis_size("seq")
    rows = [
        jnp.moveaxis(grad.reshape(-1, seq_count, grad.shape[-1] // (seq_count * width), width), 1, 2).reshape(
            -1, seq_count * width
        )
        for grad in grads
    ]
    return padded_rows(jnp.concatenate(rows, 0), 128, 0)


def halved_sum(block, axis, bit, dim):
    half = block.shape[dim] // 2
    upper = ((lax.axis_index(axis) & bit) != 0).astype(jnp.int32)
    kept = lax.dynamic_slice_in_dim(block, upper * half, half, dim)
    sent = lax.dynamic_slice_in_dim(block, (1 - upper) * half, half, dim)
    got = lax.ppermute(sent, axis, [(i, i ^ bit) for i in range(lax.axis_size(axis))])
    return (kept.astype(jnp.float32) + got.astype(jnp.float32)).astype(jnp.bfloat16)


def row_sum_owned(partial):
    bit = lax.axis_size("seq") // 2
    while bit:
        partial = halved_sum(partial, "seq", bit, 0)
        bit = bit // 2
    return partial.astype(jnp.float32)


def after(values, others):
    return lax.optimization_barrier((values, others))


def passed_along(block, axis, distance):
    devices = range(lax.axis_size(axis))
    route = [(i - distance, i) for i in devices if i - distance in devices]
    return lax.ppermute(block, axis, route)


def layer_norm(values, gain_vec):
    centre = values - jnp.mean(values, axis=-1, keepdims=True)
    inverse = lax.rsqrt(jnp.mean(centre * centre, axis=-1, keepdims=True) + EPSILON)
    return centre * inverse * gain_vec


def norm_back(values, gain_vec, upstream):
    centre = values - jnp.mean(values, axis=-1, keepdims=True)
    inverse = lax.rsqrt(jnp.mean(centre * centre, axis=-1, keepdims=True) + EPSILON)
    normed = centre * inverse
    scaled = upstream * gain_vec
    d_values = inverse * (
        scaled
        - jnp.mean(scaled, axis=-1, keepdims=True)
        - normed * jnp.mean(scaled * normed, axis=-1, keepdims=True)
    )
    return (d_values, jnp.sum(upstream * normed, axis=0))


def swish_slope(pre_act):
    sigma = jax.nn.sigmoid(pre_act)
    return sigma * (1.0 + pre_act * (1.0 - sigma))


def plain_dot(first, second):
    return jnp.dot(first, second, preferred_element_type=jnp.float32)


def left_dot(first, second):
    return jnp.einsum("nk,nm->km", first, second, preferred_element_type=jnp.float32)


def right_dot(grads_in, weight):
    return jnp.einsum("nm,km->nk", grads_in, weight, preferred_element_type=jnp.float32)


TILE = 256
SEG_ROWS = 16
LOG2E = 1.4426950408889634


def tiles_of(extent):
    return [(low, min(low + TILE, extent)) for low in range(0, extent, TILE)]


def tn_dot(first, second):
    return lax.dot_general(first, second, (((0,), (0,)), ((), ())), preferred_element_type=jnp.float32)


def nn_dot(first, second):
    return lax.dot_general(first, second, (((1,), (0,)), ((), ())), preferred_element_type=jnp.float32)


def nt_dot(first, second):
    return lax.dot_general(first, second, (((1,), (1,)), ((), ())), preferred_element_type=jnp.float32)


def row_numbers(width):
    return lax.broadcasted_iota(jnp.int32, (SEG_ROWS, width), 0)


def split_low(values, count):
    pieces = []
    for _ in range(count):
        piece = values.astype(jnp.bfloat16).astype(jnp.float32)
        pieces.append(piece)
        values = values - piece
    return pieces


def key_marks(key_seg, ones):
    rows = row_numbers(key_seg.shape[1])
    marked = jnp.logical_or(rows == key_seg, jnp.logical_and(rows >= 3, rows < 3 + ones))
    return jnp.where(marked, 1.0, 0.0).astype(jnp.bfloat16)


def query_marks(query_seg):
    rows = row_numbers(query_seg.shape[1])
    other = jnp.logical_and(rows < 3, rows != query_seg)
    return jnp.where(other, NEG_BIG, 0.0)


def with_rows(marks, first, pieces):
    rows = row_numbers(marks.shape[1])
    for k, piece in enumerate(pieces):
        marks = jnp.where(rows == first + k, piece, marks)
    return marks.astype(jnp.bfloat16)


def triangle(scores, low):
    key_at = lax.broadcasted_iota(jnp.int32, scores.shape, 0)
    query_at = lax.broadcasted_iota(jnp.int32, scores.shape, 1) + low
    return jnp.where(key_at <= query_at, scores, NEG_BIG)


FWD_HEADS = 4
BWD_HEADS = 4


def attend_kernel(heads, causal, place_ref, *refs):
    attend_core(heads, causal, place_ref[0], *refs)


def attend_core(
    heads, causal, place, qt_ref, pair_ref, qseg_ref, kseg_ref, ot_ref, total_ref, kmark_ref, sum_ref, peak_ref, score_ref
):
    width, tokens = qt_ref.shape
    size = width // heads
    factor = size ** (-0.5) * LOG2E
    block = tokens if causal else pair_ref.shape[1]
    place = place if causal else 0
    kmark_ref[...] = key_marks(kseg_ref[...], 0)
    value_marks = jnp.where(row_numbers(TILE) == 0, 1.0, 0.0).astype(jnp.bfloat16)
    qmarks = query_marks(qseg_ref[...]).astype(jnp.bfloat16)
    tiles = tiles_of(tokens)

    def head_rows(head, base=0):
        return pl.ds(pl.multiple_of(base + head * size, size), size)

    def on_units(several, start, first):
        units = [(k, head, low, high) for k, head in enumerate(several) for low, high in tiles]

        def key_parts(unit):
            _, _, _, high = unit
            return tiles_of(high if first and causal else block)

        def lanes_of(part):
            return pl.ds(pl.multiple_of(start + part[0], 128), part[1] - part[0])

        def score_part(unit, slot, part):
            k, head, low, high = unit
            query_rows = jnp.concatenate([qt_ref[head_rows(head), low:high], qmarks[:, low:high]], 0)
            lanes = lanes_of(part)
            scores = tn_dot(jnp.concatenate([pair_ref[head_rows(head), lanes], kmark_ref[:, lanes]], 0), query_rows)
            if first and causal and part[0] >= low:
                scores = triangle(scores, low - part[0])
            score_ref[slot, part[0] : part[1], : high - low] = scores
            return jnp.max(scores, axis=0, keepdims=True)

        def value_part(unit, slot, part, peak):
            k, head, low, high = unit
            scores = score_ref[slot, part[0] : part[1], : high - low]
            weights = jnp.exp2((scores - peak) * factor).astype(jnp.bfloat16)
            value_rows = jnp.concatenate(
                [pair_ref[head_rows(head, width), lanes_of(part)], value_marks[:, : part[1] - part[0]]], 0
            )
            return nn_dot(value_rows, weights)

        held = None
        for at in range(len(units) + 1):
            unit = units[at] if at < len(units) else None
            parts = key_parts(unit) if unit else []
            old_parts = key_parts(held[0]) if held else []
            peak = None
            if unit and not first:
                peak = peak_ref[unit[0], :, unit[2] : unit[3]]
            before = peak
            summed = None
            for step in range(max(len(parts), len(old_parts))):
                if step < len(parts):
                    found = score_part(unit, at % 2, parts[step])
                    peak = found if peak is None else jnp.maximum(peak, found)
                if step < len(old_parts):
                    term = value_part(held[0], (at - 1) % 2, old_parts[step], held[1])
                    summed = term if summed is None else summed + term
            if held:
                k, _, low, high = held[0]
                if not first:
                    summed = summed + sum_ref[k, :, low:high] * jnp.exp2((held[2] - held[1]) * factor)
                sum_ref[k, :, low:high] = summed
                peak_ref[k, :, low:high] = held[1]
            held = (unit, peak, before)

    def some_heads(step, carry):
        several = [step * FWD_HEADS + k for k in range(FWD_HEADS)]
        on_units(several, place * block, True)
        if causal:

            def earlier(back, held):
                on_units(several, back * block, False)
                return held

            lax.fori_loop(0, place, earlier, 0)
        for k, head in enumerate(several):
            total = sum_ref[k, size : size + 1, :]
            ot_ref[head_rows(head), :] = (sum_ref[k, :size, :] / total).astype(jnp.bfloat16)
            total_ref[head] = peak_ref[k] + jnp.log2(total) / factor
        return carry

    lax.fori_loop(0, heads // FWD_HEADS, some_heads, 0)


def attend_back_kernel(heads, causal, place_ref, *refs):
    attend_back_core(heads, causal, place_ref[0], *refs)


def attend_back_core(
    heads, causal, place, qt_ref, pair_ref, gt_ref, ot_ref, total_ref, qseg_ref, kseg_ref,
    dq_ref, dpair_ref, kmark_ref, dkh_ref, dvh_ref, dqh_ref, qrow_ref, grow_ref, weight_ref, slope_ref,
    pump=None,
):
    width, tokens = qt_ref.shape
    size = width // heads
    scale = size ** (-0.5)
    factor = scale * LOG2E
    block = tokens if causal else pair_ref.shape[1]
    place = place if causal else 0
    kmark_ref[...] = key_marks(kseg_ref[...], 3)
    value_marks = jnp.where(row_numbers(TILE) < 2, 1.0, 0.0).astype(jnp.bfloat16)
    qmarks = query_marks(qseg_ref[...])
    tiles = tiles_of(tokens)

    def head_rows(head, base=0):
        return pl.ds(pl.multiple_of(base + head * size, size), size)

    def prepare(k, head):
        own = head_rows(head)
        grads = gt_ref[own, :]
        delta = jnp.sum(grads.astype(jnp.float32) * ot_ref[own, :].astype(jnp.float32), axis=0, keepdims=True)
        qrow_ref[k, :size, :] = qt_ref[own, :]
        qrow_ref[k, size : size + SEG_ROWS, :] = with_rows(qmarks, 3, split_low(-total_ref[head], 3))
        grow_ref[k, :size, :] = grads
        grow_ref[k, size : size + SEG_ROWS, :] = with_rows(jnp.zeros_like(qmarks), 0, split_low(-delta, 2))

    def on_units(several, start, first):
        units = [(k, head, low, high) for k, head in enumerate(several) for low, high in tiles]

        def key_parts(unit):
            _, _, _, high = unit
            return tiles_of(high if first and causal else block)

        def lanes_of(part):
            return pl.ds(pl.multiple_of(start + part[0], 128), part[1] - part[0])

        def score_part(unit, slot, part):
            k, head, low, high = unit
            lanes = lanes_of(part)
            key_rows = jnp.concatenate([pair_ref[head_rows(head), lanes], kmark_ref[:, lanes]], 0)
            value_rows = jnp.concatenate(
                [pair_ref[head_rows(head, width), lanes], value_marks[:, : part[1] - part[0]]], 0
            )
            scores = tn_dot(key_rows, qrow_ref[k, : size + SEG_ROWS, low:high])
            if first and causal and part[0] >= low:
                scores = triangle(scores, low - part[0])
            weights = jnp.exp2(scores * factor)
            slopes = tn_dot(value_rows, grow_ref[k, : size + SEG_ROWS, low:high])
            weight_ref[slot, part[0] : part[1], : high - low] = weights.astype(jnp.bfloat16)
            slope_ref[slot, part[0] : part[1], : high - low] = (weights * slopes).astype(jnp.bfloat16)

        def grad_part(unit, slot, part):
            k, head, low, high = unit
            lanes = lanes_of(part)
            weights = weight_ref[slot, part[0] : part[1], : high - low]
            slopes = slope_ref[slot, part[0] : part[1], : high - low]
            dvh_ref[k, :, lanes] += nt_dot(grow_ref[k, :size, low:high], weights)
            dkh_ref[k, :, lanes] += nt_dot(qrow_ref[k, :size, low:high], slopes)
            return nn_dot(pair_ref[head_rows(head), lanes], slopes)

        held = None
        for at in range(len(units) + 1):
            unit = units[at] if at < len(units) else None
            parts = key_parts(unit) if unit else []
            old_parts = key_parts(held) if held else []
            summed = None
            for step in range(max(len(parts), len(old_parts))):
                if step < len(parts):
                    score_part(unit, at % 2, parts[step])
                if step < len(old_parts):
                    term = grad_part(held, (at - 1) % 2, old_parts[step])
                    summed = term if summed is None else summed + term
            if held:
                k, _, low, high = held
                if first:
                    dqh_ref[k, :size, low:high] = summed
                else:
                    dqh_ref[k, :size, low:high] += summed
            held = unit

    def some_heads(step, carry):
        several = [step * BWD_HEADS + k for k in range(BWD_HEADS)]
        if pump is not None:
            pump(step)
        dkh_ref[...] = jnp.zeros_like(dkh_ref)
        dvh_ref[...] = jnp.zeros_like(dvh_ref)
        for k, head in enumerate(several):
            prepare(k, head)
        on_units(several, place * block, True)
        if causal:

            def earlier(back, held):
                on_units(several, back * block, False)
                return held

            lax.fori_loop(0, place, earlier, 0)
        for k, head in enumerate(several):
            dq_ref[head_rows(head), :] = (dqh_ref[k, :size, :] * scale).astype(jnp.bfloat16)
            dpair_ref[head_rows(head), :] = (dkh_ref[k] * scale).astype(jnp.bfloat16)
            dpair_ref[head_rows(head, width), :] = dvh_ref[k].astype(jnp.bfloat16)
        return carry

    lax.fori_loop(0, heads // BWD_HEADS, some_heads, 0)


IN_SMEM = pl.BlockSpec(memory_space=pltpu.SMEM)
IN_VMEM = pl.BlockSpec(memory_space=pltpu.VMEM)
KERNEL_VMEM = 48 * 2**20
HOST_VMEM = 63 * 2**20 + 2**19


LANE_GROUP = 128
SWAP_TICK = 4


def attend_forward(queries, pairs_t, heads, causal, query_seg, key_seg):
    width, tokens = queries.shape
    total_keys = pairs_t.shape[1]
    pairs = heads * tokens * total_keys
    return pl.pallas_call(
        functools.partial(attend_kernel, heads, causal),
        out_shape=(
            jax.ShapeDtypeStruct((width, tokens), jnp.bfloat16),
            jax.ShapeDtypeStruct((heads, 1, tokens), jnp.float32),
        ),
        in_specs=[IN_SMEM] + [IN_VMEM] * 4,
        out_specs=(IN_VMEM, IN_VMEM),
        scratch_shapes=[
            pltpu.VMEM((SEG_ROWS, total_keys), jnp.bfloat16),
            pltpu.VMEM((FWD_HEADS, width // heads + SEG_ROWS, tokens), jnp.float32),
            pltpu.VMEM((FWD_HEADS, 1, tokens), jnp.float32),
            pltpu.VMEM((2, tokens if causal else total_keys, TILE), jnp.float32),
        ],
        compiler_params=pltpu.CompilerParams(vmem_limit_bytes=KERNEL_VMEM),
        cost_estimate=pl.CostEstimate(
            flops=pairs * 600, bytes_accessed=4 * width * total_keys, transcendentals=pairs
        ),
        name="attend_fwd",
    )(lax.axis_index("seq").reshape(1), queries, pairs_t, query_seg[None], key_seg[None])


def attend_back(queries, pairs_t, grads, outs, totals, heads, causal, query_seg, key_seg):
    width, tokens = queries.shape
    total_keys = pairs_t.shape[1]
    pairs = heads * tokens * total_keys
    size = width // heads
    return pl.pallas_call(
        functools.partial(attend_back_kernel, heads, causal),
        out_shape=(
            jax.ShapeDtypeStruct((width, tokens), jnp.bfloat16),
            jax.ShapeDtypeStruct((2 * width, total_keys), jnp.bfloat16),
        ),
        in_specs=[IN_SMEM] + [IN_VMEM] * 7,
        out_specs=(IN_VMEM, IN_VMEM),
        scratch_shapes=[
            pltpu.VMEM((SEG_ROWS, total_keys), jnp.bfloat16),
            pltpu.VMEM((BWD_HEADS, size, total_keys), jnp.float32),
            pltpu.VMEM((BWD_HEADS, size, total_keys), jnp.float32),
            pltpu.VMEM((BWD_HEADS, size, tokens), jnp.float32),
            pltpu.VMEM((BWD_HEADS, size + SEG_ROWS, tokens), jnp.bfloat16),
            pltpu.VMEM((BWD_HEADS, size + SEG_ROWS, tokens), jnp.bfloat16),
            pltpu.VMEM((2, tokens if causal else total_keys, TILE), jnp.bfloat16),
            pltpu.VMEM((2, tokens if causal else total_keys, TILE), jnp.bfloat16),
        ],
        compiler_params=pltpu.CompilerParams(vmem_limit_bytes=KERNEL_VMEM),
        cost_estimate=pl.CostEstimate(
            flops=pairs * 1500, bytes_accessed=8 * width * total_keys, transcendentals=pairs
        ),
        name="attend_bwd",
    )(
        lax.axis_index("seq").reshape(1), queries, pairs_t, grads, outs, totals,
        query_seg[None], key_seg[None],
    )


RIM = 16
ROW_TILE = 64
MERGE_ROWS = 64


def row_tiles(extent, tile):
    return [(low, min(low + tile, extent)) for low in range(0, extent, tile)]


def halves_of(extent):
    middle = -(-extent // 32) * 16
    return [(0, middle), (middle, extent)]


def group_lanes(group):
    return pl.ds(pl.multiple_of(group * 128, 128), 128)


def wide_rows(column, width=128):
    return jnp.broadcast_to(column, (column.shape[0], width))


def loop_rows(extent, tile, body):
    def step(k, carry):
        body(pl.ds(pl.multiple_of(k * tile, tile), tile))
        return carry

    whole = extent // tile
    lax.fori_loop(0, whole, step, 0)
    if whole * tile < extent:
        body(pl.ds(whole * tile, extent - whole * tile))


def rows_normed(values):
    centre = values - jnp.mean(values, axis=-1, keepdims=True)
    inverse = lax.rsqrt(jnp.mean(centre * centre, axis=-1, keepdims=True) + EPSILON)
    return centre * inverse, inverse


def rows_norm_back(normed, inverse, gain_vec, upstream):
    scaled = upstream * gain_vec
    return inverse * (
        scaled
        - jnp.mean(scaled, axis=-1, keepdims=True)
        - normed * jnp.mean(scaled * normed, axis=-1, keepdims=True)
    )


def taps_forward(source_ref, first_row, since, lanes, low, high, weights):
    result = None
    for offset, weight in enumerate(weights):
        start = first_row + low - offset
        window = source_ref[start : start + high - low, lanes]
        if offset:
            window = jnp.where(since >= offset, window, 0.0)
        term = window * weight
        result = term if result is None else result + term
    return result


def conv_fwd_kernel(
    h1_ref, a2_ref, rim_ref, since_ref, tl_ref, tr_ref, tm_ref, mgain_ref, gain_ref, pl_ref, pr_ref, pm_ref,
    cl_ref, cr_ref, cm_ref, h2_ref, a3_ref,
    ext_ref, wide_ref, cle_ref, cre_ref, up_ref, mixed_ref,
):
    tokens, width = h1_ref.shape
    total = tokens + RIM
    narrow = pr_ref.shape[1]
    ext_ref[0:RIM, :] = jnp.zeros((RIM, width), jnp.float32)
    ext_ref[RIM : 2 * RIM, :] = rim_ref[...].astype(jnp.float32)
    ext_ref[2 * RIM :, :] = a2_ref[...].astype(jnp.float32)
    wide_ref[...] = wide_rows(since_ref[...])

    def first_convs(group, carry):
        lanes = group_lanes(group)
        left = [tl_ref[j : j + 1, lanes] for j in range(tl_ref.shape[0])]
        right = [tr_ref[j : j + 1, lanes] for j in range(tr_ref.shape[0])]
        for low, high in row_tiles(total, ROW_TILE):
            since = wide_ref[low:high, :]
            cle_ref[low:high, lanes] = taps_forward(ext_ref, RIM, since, lanes, low, high, left).astype(jnp.bfloat16)
            cre_ref[low:high, lanes] = taps_forward(ext_ref, RIM, since, lanes, low, high, right).astype(jnp.bfloat16)
        return carry

    lax.fori_loop(0, width // 128, first_convs, 0)
    cl_ref[...] = cle_ref[RIM:, :]
    cr_ref[...] = cre_ref[RIM:, :]
    for low, high in halves_of(total):
        up_ref[low:high, :] = nn_dot(cle_ref[low:high, :], pl_ref[...])
        mixed_ref[low:high, :narrow] = nn_dot(cre_ref[low:high, :], pr_ref[...])

    def merge_rows(rows):
        pre = up_ref[rows, :]
        merged = pre / (1.0 + jnp.exp(-pre))
        merged = jnp.concatenate([merged[:, :narrow] + mixed_ref[rows, :narrow], merged[:, narrow:]], 1)
        normed, _ = rows_normed(merged)
        mixed_ref[rows, :] = (normed * mgain_ref[...]).astype(jnp.bfloat16).astype(jnp.float32)

    loop_rows(total, MERGE_ROWS, merge_rows)

    def mid_conv(group, carry):
        lanes = group_lanes(group)
        weights = [tm_ref[j : j + 1, lanes] for j in range(tm_ref.shape[0])]
        for low, high in row_tiles(tokens, ROW_TILE):
            since = wide_ref[RIM + low : RIM + high, :]
            cm_ref[low:high, lanes] = taps_forward(mixed_ref, RIM, since, lanes, low, high, weights).astype(jnp.bfloat16)
        return carry

    lax.fori_loop(0, mixed_ref.shape[1] // 128, mid_conv, 0)
    for low, high in halves_of(tokens):
        h2_ref[low:high, :] = h1_ref[low:high, :] + nn_dot(cm_ref[low:high, :], pm_ref[...])

    def norm_rows(rows):
        normed, _ = rows_normed(h2_ref[rows, :])
        a3_ref[rows, :] = (normed * gain_ref[...]).astype(jnp.bfloat16)

    loop_rows(tokens, 64, norm_rows)


def conv_forward(h1, a2, rim, since, taps_l, taps_r, taps_m, mid_gain, gain, proj_left, proj_right, proj_mid):
    tokens, width = h1.shape
    wide = proj_left.shape[1]
    total = tokens + RIM
    low, full = jnp.bfloat16, jnp.float32
    return pl.pallas_call(
        conv_fwd_kernel,
        out_shape=(
            jax.ShapeDtypeStruct((tokens, width), low),
            jax.ShapeDtypeStruct((tokens, width), low),
            jax.ShapeDtypeStruct((tokens, wide), low),
            jax.ShapeDtypeStruct((tokens, width), full),
            jax.ShapeDtypeStruct((tokens, width), low),
        ),
        in_specs=[IN_VMEM] * 12,
        out_specs=(IN_VMEM,) * 5,
        scratch_shapes=[
            pltpu.VMEM((total + RIM, width), full),
            pltpu.VMEM((total, 128), jnp.int32),
            pltpu.VMEM((total, width), low),
            pltpu.VMEM((total, width), low),
            pltpu.VMEM((total, wide), full),
            pltpu.VMEM((total, wide), full),
        ],
        compiler_params=pltpu.CompilerParams(vmem_limit_bytes=KERNEL_VMEM),
        cost_estimate=pl.CostEstimate(
            flops=tokens * width * wide * 20, bytes_accessed=tokens * width * 16, transcendentals=tokens * wide
        ),
        name="conv_fwd",
    )(h1, a2, rim, since, taps_l, taps_r, taps_m, mid_gain, gain, proj_left, proj_right, proj_mid)


def folded(values):
    return jnp.sum(values.reshape(-1, 8, values.shape[-1]), axis=0)


def taps_back(grad_ref, value, left, lanes, low, high, weights, result, sums):
    for offset, weight in enumerate(weights):
        window = grad_ref[low + offset : high + offset, lanes]
        if offset:
            window = jnp.where(left >= offset, window, 0.0)
        term = window * weight
        result = term if result is None else result + term
        if value is not None:
            product = folded(window * value)
            sums[offset] = product if sums[offset] is None else sums[offset] + product
    return result


def conv_bwd_kernel(
    g2_ref, brim_ref, cl_ref, clrim_ref, cr_ref, crrim_ref, cm_ref, a2_ref, h1_ref, left_ref,
    tl_ref, tr_ref, tm_ref, mgain_ref, gain_ref, pl_ref, pr_ref, pm_ref, across_in_ref, second_ref,
    g1_ref, dw_ref, dtl_ref, dtr_ref, dtm_ref, dmgain_ref, dgain_ref, mine_ref, across_out_ref,
    bext_ref, cle_ref, cre_ref, wide_ref, grad_ref, up_ref, back_ref, normed_ref, inv_ref, dpl_ref, dpr_ref, a2f_ref,
    kept_ref, core_ref, across_ref, close_ref, piece_ref, send_sem, recv_sem, kept_sem,
):
    tokens, width = g2_ref.shape
    total = tokens + RIM
    wide, narrow = pl_ref.shape[1], pr_ref.shape[1]
    share = ShareSum(
        send_sem, recv_sem, core=core_ref, across=across_ref, close=close_ref, piece=piece_ref, mine=mine_ref
    )
    first_count = mine_ref.shape[0]
    step = share.step
    firsts, seconds = range(first_count), range(first_count, first_count + core_ref.shape[0])
    share.core_first = first_count
    share.enter([share.mate, share.close] + share.peers[1:] + share.sides[1:])
    kept_copy = pltpu.make_async_copy(
        second_ref.at[:, share.core, :, : kept_ref.shape[-1]], kept_ref, kept_sem
    )
    kept_copy.start()
    for chunk in seconds:
        share.core_copy(chunk, second_ref, chunk - first_count).start()
    for chunk in firsts:
        share.early_sums[chunk] = across_in_ref.at[:, chunk * step : (chunk + 1) * step]
        share.near_copy(chunk).start()
    bext_ref[:tokens, :] = g2_ref[...].astype(jnp.bfloat16)
    bext_ref[tokens:, :] = brim_ref[...]
    cle_ref[:tokens, :] = cl_ref[...]
    cle_ref[tokens:, :] = clrim_ref[...]
    cre_ref[:tokens, :] = cr_ref[...]
    cre_ref[tokens:, :] = crrim_ref[...]
    a2f_ref[...] = a2_ref[...].astype(jnp.float32)
    wide_ref[...] = wide_rows(left_ref[...])
    grad_ref[total:, :] = jnp.zeros((RIM, wide), jnp.float32)
    dw_ref[:, :wide] = tn_dot(bext_ref[:tokens, :], cm_ref[...]).astype(jnp.bfloat16)
    for low, high in halves_of(total):
        grad_ref[low:high, :] = nt_dot(bext_ref[low:high, :], pm_ref[...])
        up_ref[low:high, :] = nn_dot(cle_ref[low:high, :], pl_ref[...])
        back_ref[low:high, :narrow] = nn_dot(cre_ref[low:high, :], pr_ref[...])

    kept_copy.wait()
    for chunk in seconds:
        at = (chunk - first_count) * step
        share.core_copy(chunk, second_ref, chunk - first_count).wait_recv()
        share.run_side(chunk, kept_ref[:, :, at : at + step])

    def merge_rows(rows):
        pre = up_ref[rows, :]
        merged = pre / (1.0 + jnp.exp(-pre))
        merged = jnp.concatenate([merged[:, :narrow] + back_ref[rows, :narrow], merged[:, narrow:]], 1)
        normed, inverse = rows_normed(merged)
        normed_ref[rows, :] = normed
        inv_ref[rows, :] = wide_rows(inverse)

    loop_rows(total, MERGE_ROWS, merge_rows)

    def mid_back(group, carry):
        lanes = group_lanes(group)
        weights = [tm_ref[j : j + 1, lanes] for j in range(tm_ref.shape[0])]
        sums = [None] * len(weights)
        gain_vec = mgain_ref[:, lanes]
        for low, high in row_tiles(total, ROW_TILE):
            value = None
            if high <= tokens:
                value = (normed_ref[low:high, lanes] * gain_vec).astype(jnp.bfloat16).astype(jnp.float32)
            back_ref[low:high, lanes] = taps_back(
                grad_ref, value, wide_ref[low:high, :], lanes, low, high, weights, None, sums
            )
        for j, piece in enumerate(sums):
            dtm_ref[j : j + 1, lanes] = jnp.sum(piece, axis=0, keepdims=True)
        return carry

    lax.fori_loop(0, wide // 128, mid_back, 0)

    def merge_back(rows):
        pre = up_ref[rows, :]
        normed = normed_ref[rows, :]
        d_merged = rows_norm_back(normed, inv_ref[rows, :][:, :1], mgain_ref[...], back_ref[rows, :])
        sigma = 1.0 / (1.0 + jnp.exp(-pre))
        dpl_ref[rows, :] = (d_merged * (sigma * (1.0 + pre * (1.0 - sigma)))).astype(jnp.bfloat16)
        dpr_ref[rows, :] = d_merged[:, :narrow].astype(jnp.bfloat16)

    loop_rows(total, MERGE_ROWS, merge_back)
    for chunk in firsts:
        share.run_peer(chunk)
    gain_sum = jnp.zeros((8, wide), jnp.float32)

    def gain_rows(k, held):
        rows = pl.ds(pl.multiple_of(k * 16, 16), 16)
        return held + folded(back_ref[rows, :] * normed_ref[rows, :])

    gain_sum = lax.fori_loop(0, tokens // 16, gain_rows, gain_sum)
    dmgain_ref[...] = jnp.sum(gain_sum, axis=0, keepdims=True)
    dw_ref[:, wide : 2 * wide] = tn_dot(cle_ref[:tokens, :], dpl_ref[:tokens, :]).astype(jnp.bfloat16)
    dw_ref[:, 2 * wide :] = tn_dot(cre_ref[:tokens, :], dpr_ref[:tokens, :]).astype(jnp.bfloat16)
    for low, high in halves_of(total):
        grad_ref[low:high, :width] = nt_dot(dpl_ref[low:high, :], pl_ref[...])
        grad_ref[low:high, width : 2 * width] = nt_dot(dpr_ref[low:high, :], pr_ref[...])

    def first_back(group, carry):
        lanes = group_lanes(group)
        other = group_lanes(group + width // 128)
        weights_l = [tl_ref[j : j + 1, lanes] for j in range(tl_ref.shape[0])]
        weights_r = [tr_ref[j : j + 1, lanes] for j in range(tr_ref.shape[0])]
        sums_l = [None] * len(weights_l)
        sums_r = [None] * len(weights_r)
        for low, high in row_tiles(tokens, ROW_TILE):
            left = wide_ref[low:high, :]
            value = a2f_ref[low:high, lanes]
            held = taps_back(grad_ref, value, left, lanes, low, high, weights_l, None, sums_l)
            held = taps_back(grad_ref, value, left, other, low, high, weights_r, held, sums_r)
            back_ref[low:high, lanes] = held
        for j, piece in enumerate(sums_l):
            dtl_ref[j : j + 1, lanes] = jnp.sum(piece, axis=0, keepdims=True)
        for j, piece in enumerate(sums_r):
            dtr_ref[j : j + 1, lanes] = jnp.sum(piece, axis=0, keepdims=True)
        return carry

    lax.fori_loop(0, width // 128, first_back, 0)

    def finish(k, held):
        rows = pl.ds(pl.multiple_of(k * 64, 64), 64)
        normed, inverse = rows_normed(h1_ref[rows, :])
        upstream = back_ref[rows, :width]
        g1_ref[rows, :] = g2_ref[rows, :] + rows_norm_back(normed, inverse, gain_ref[...], upstream)
        return held + folded(upstream * normed)

    gain_sum = lax.fori_loop(0, tokens // 64, finish, jnp.zeros((8, width), jnp.float32))
    dgain_ref[...] = jnp.sum(gain_sum, axis=0, keepdims=True)
    for chunk in firsts:
        share.peer_sum(chunk)
        share.near_copy(chunk).wait_send()
        share.sent_peers(chunk)
    for chunk in seconds:
        at = (chunk - first_count) * step
        across_out_ref[:, at : at + step] = share.side_sum(chunk, first_count)
        share.core_copy(chunk, second_ref, chunk - first_count).wait_send()
        share.sent_sides(chunk)


def conv_back(
    g2, brim, c_l, c_r, rims, c_m, a2, h1, left, taps_l, taps_r, taps_m, mid_gain, gain, proj_left, proj_right, proj_mid,
    across, second,
):
    tokens, width = g2.shape
    wide, narrow = proj_left.shape[1], proj_right.shape[1]
    total = tokens + RIM
    low, full = jnp.bfloat16, jnp.float32
    seq_count, far_count = lax.axis_size("seq"), lax.axis_size("rows") // 4
    half = width // (2 * seq_count)
    step = 2 * far_count * LANE_GROUP
    first_count, second_count = across.shape[1] // step, second.shape[1] // step - 1
    count = first_count + second_count
    slots = 1 + seq_count + far_count
    in_hbm = pl.BlockSpec(memory_space=pl.ANY)
    dma = pltpu.SemaphoreType.DMA
    return pl.pallas_call(
        conv_bwd_kernel,
        out_shape=(
            jax.ShapeDtypeStruct((tokens, width), full),
            jax.ShapeDtypeStruct((width, 2 * wide + narrow), low),
            jax.ShapeDtypeStruct(taps_l.shape, full),
            jax.ShapeDtypeStruct(taps_r.shape, full),
            jax.ShapeDtypeStruct(taps_m.shape, full),
            jax.ShapeDtypeStruct((1, wide), full),
            jax.ShapeDtypeStruct((1, width), full),
            jax.ShapeDtypeStruct((first_count, half, LANE_GROUP), low),
            jax.ShapeDtypeStruct((half, second_count * step), low),
        ),
        in_specs=[IN_VMEM] * 19 + [in_hbm],
        out_specs=(IN_VMEM,) * 9,
        scratch_shapes=[
            pltpu.VMEM((total, width), low),
            pltpu.VMEM((total, width), low),
            pltpu.VMEM((total, width), low),
            pltpu.VMEM((total, 128), jnp.int32),
            pltpu.VMEM((total + RIM, wide), full),
            pltpu.VMEM((total, wide), full),
            pltpu.VMEM((total, wide), full),
            pltpu.VMEM((total, wide), full),
            pltpu.VMEM((total, 128), full),
            pltpu.VMEM((total, wide), low),
            pltpu.VMEM((total, narrow), low),
            pltpu.VMEM((tokens, width), full),
            pltpu.VMEM((seq_count, half, second_count * step), low),
            pltpu.VMEM((second_count, seq_count, half, step), low),
            pltpu.VMEM((second_count, seq_count - 1, half, step), low),
            pltpu.VMEM((first_count, half, step // 2), low),
            pltpu.VMEM((first_count, far_count - 1, half, LANE_GROUP), low),
            dma((count, slots)),
            dma((count, slots)),
            dma(()),
        ],
        compiler_params=pltpu.CompilerParams(
            collective_id=1, has_side_effects=True, vmem_limit_bytes=HOST_VMEM
        ),
        cost_estimate=pl.CostEstimate(
            flops=tokens * width * wide * 40, bytes_accessed=tokens * width * 40, transcendentals=tokens * wide
        ),
        name="conv_bwd",
    )(
        g2, brim, c_l, rims[:, :width], c_r, rims[:, width:], c_m, a2, h1, left,
        taps_l, taps_r, taps_m, mid_gain, gain, proj_left, proj_right, proj_mid,
        across, second.reshape(seq_count, 2, half, second.shape[1]),
    )


MIDDLE_VMEM = 60 * 2**20
DOT_ROWS = 256


def load_weight(copies, sems, target_ref, own_ref, pieces, offset, place, near, core):
    width, size = own_ref.shape
    quarter = width // 4
    count = len(pieces) // 3 + 1
    columns = slice(offset, offset + size)
    parts = [(own_ref, place * width, width)]
    for d in range(1, count):
        source = lax.rem(place + d, count) * width
        same, close, across = pieces[3 * d - 3 : 3 * d]
        parts.append((same.at[:, columns], source + (2 * near + core) * quarter, quarter))
        parts.append((close.at[:, columns], source + (2 - 2 * near + core) * quarter, quarter))
        parts.append((across.at[:quarter, columns], source + (2 * near + 1 - core) * quarter, quarter))
        parts.append((across.at[quarter:, columns], source + (3 - 2 * near - core) * quarter, quarter))
    for source_ref, start, rows in parts:
        copy = pltpu.make_async_copy(
            source_ref, target_ref.at[pl.ds(pl.multiple_of(start, quarter), rows), :], sems.at[len(copies)]
        )
        copy.start()
        copies.append(copy)
    return offset + size


def wait_for(copies):
    for copy in copies:
        copy.wait()


def norm_into(target_ref, source_ref, gain_vec):
    def body(rows):
        normed, _ = rows_normed(source_ref[rows, :])
        target_ref[rows, :] = (normed * gain_vec).astype(jnp.bfloat16)

    loop_rows(source_ref.shape[0], 64, body)


def norm_back_into(target_ref, base_ref, source_ref, gain_vec, upstream_ref):
    def body(k, held):
        rows = pl.ds(pl.multiple_of(k * 64, 64), 64)
        normed, inverse = rows_normed(source_ref[rows, :])
        upstream = upstream_ref[rows, :]
        target_ref[rows, :] = base_ref[rows, :].astype(jnp.float32) + rows_norm_back(
            normed, inverse, gain_vec, upstream
        )
        return held + folded(upstream * normed)

    held = jnp.zeros((8, source_ref.shape[1]), jnp.float32)
    return jnp.sum(lax.fori_loop(0, source_ref.shape[0] // 64, body, held), axis=0, keepdims=True)


def chunks(extent):
    return row_tiles(extent, DOT_ROWS)


def project_into(target_ref, weight_ref, turned_ref, low, high):
    for start, stop in chunks(high - low):
        target_ref[start:stop, :] = tn_dot(weight_ref[:, low + start : low + stop], turned_ref[...]).astype(jnp.bfloat16)


def store_grad(target_ref, start, values):
    target_ref[:, start : start + values.shape[1]] = values.astype(jnp.bfloat16)


def middle_kernel(
    piece_count,
    h2_ref, a3_ref, a3more_ref, mem_ref, gout_ref, gain_ref, qseg_ref, kseg_ref, mseg_ref, down_ref,
    qkv_own, out2_own, query_own, kv_own, out_own, up_own, *rest,
):
    pieces, rest = rest[:piece_count], rest[piece_count:]
    (
        result_ref, g3_ref, da3_ref, dw_ref, dgain_ref, dmem_ref, across_out_ref,
        wqkv_ref, wout2_ref, wquery_ref, wkv_ref, wout_ref, wup_ref, sems,
        turned_ref, memt_ref, a4_ref, a4t_ref, qt_ref, pair_ref, attc_ref, totalc_ref,
        qdt_ref, paird_ref, attd_ref, totald_ref, h3_ref, h4_ref, act_ref, dup_ref, low_ref, gt_ref, dq_ref, dpair_ref, dpaird_ref,
        back_ref, wide_ref, kmark_ref, mmark_ref, sum_ref, peak_ref, score_ref,
        dkh_ref, dvh_ref, dkm_ref, dvm_ref, dqh_ref, qrow_ref, grow_ref, weight_ref, slope_ref,
        first_ref, core_ref, across_ref, send_sem, recv_sem,
    ) = rest
    tokens, width = h2_ref.shape
    share = ShareSum(send_sem, recv_sem, core=core_ref, across=across_ref)
    place, near, core = share.place, share.near, share.core
    share.enter([share.mate] + share.sides[1:])
    seq_count = piece_count // 3 + 1
    high_width = wup_ref.shape[1]
    first, copies = [], []
    offset = load_weight(first, sems.at[0], wqkv_ref, qkv_own, pieces, 0, place, near, core)
    for target, own in ((wout2_ref, out2_own), (wquery_ref, query_own), (wkv_ref, kv_own), (wout_ref, out_own)):
        offset = load_weight(copies, sems.at[1], target, own, pieces, offset, place, near, core)
    load_weight(copies, sems.at[1], wup_ref, up_own, pieces, offset, place, near, core)

    own = pl.ds(pl.multiple_of(place * tokens, 128), tokens)
    turned_ref[:, own] = a3_ref[...].T
    for d in range(1, seq_count):
        there = pl.ds(pl.multiple_of(lax.rem(place + d, seq_count) * tokens, 128), tokens)
        turned_ref[:, there] = a3more_ref[d - 1].T
    memt_ref[...] = mem_ref[...].T
    wait_for(first)
    project_into(qt_ref, wqkv_ref, turned_ref.at[:, own], 0, width)
    project_into(pair_ref, wqkv_ref, turned_ref, width, 3 * width)
    attend_core(
        H_CROSS, True, place, qt_ref, pair_ref, qseg_ref, kseg_ref, attc_ref, totalc_ref, kmark_ref, sum_ref, peak_ref, score_ref
    )
    wait_for(copies)
    for low, high in chunks(tokens):
        h3_ref[low:high, :] = h2_ref[low:high, :] + tn_dot(attc_ref[:, low:high], wout2_ref[...])
    norm_into(a4_ref, h3_ref, gain_ref[0:1, :])
    a4t_ref[...] = a4_ref[...].T
    project_into(qdt_ref, wquery_ref, a4t_ref, 0, width)
    project_into(paird_ref, wkv_ref, memt_ref, 0, 2 * width)
    attend_core(
        H_CROSS, False, 0, qdt_ref, paird_ref, qseg_ref, mseg_ref, attd_ref, totald_ref, mmark_ref, sum_ref, peak_ref, score_ref
    )
    for low, high in chunks(tokens):
        h4_ref[low:high, :] = h3_ref[low:high, :] + tn_dot(attd_ref[:, low:high], wout_ref[...])
    norm_into(a4_ref, h4_ref, gain_ref[1:2, :])

    for left, right in row_tiles(high_width, 512):
        for low, high in chunks(tokens):
            pre = nn_dot(a4_ref[low:high, :], wup_ref[:, left:right])
            sigma = 1.0 / (1.0 + jnp.exp(-pre))
            act_ref[low:high, left:right] = (pre * sigma).astype(jnp.bfloat16)
            slope = nt_dot(gout_ref[low:high, :], down_ref[left:right, :])
            dup_ref[low:high, left:right] = (slope * (sigma * (1.0 + pre * (1.0 - sigma)))).astype(jnp.bfloat16)
    for low, high in chunks(tokens):
        result_ref[low:high, :] = (h4_ref[low:high, :] + nn_dot(act_ref[low:high, :], down_ref[...])).astype(jnp.bfloat16)
        back_ref[low:high, :] = nt_dot(dup_ref[low:high, :], wup_ref[...])
    seq_count, _, half, first_total = first_ref.shape
    firsts = range(first_total // share.step)

    def store_first(start, values):
        size = values.shape[1]
        first_ref[:, :, :, start : start + size] = values.astype(jnp.bfloat16).reshape(seq_count, 2, half, size)

    for left, right in row_tiles(high_width, 512):
        store_first(left, tn_dot(a4_ref[...], dup_ref[:, left:right]))
        store_first(high_width + left, tn_dot(gout_ref[...], act_ref[:, left:right]))

    for chunk in firsts:
        share.core_copy(chunk, first_ref, chunk).start()
    at = 0
    dgain_ref[1:2, :] = norm_back_into(h4_ref, gout_ref, h4_ref, gain_ref[1:2, :], back_ref)
    low_ref[...] = h4_ref[...].astype(jnp.bfloat16)
    store_grad(dw_ref, at, nn_dot(attd_ref[...], low_ref[...]))
    gt_ref[...] = nt_dot(wout_ref[...], low_ref[...]).astype(jnp.bfloat16)
    attend_back_core(
        H_CROSS, False, 0, qdt_ref, paird_ref, gt_ref, attd_ref, totald_ref, qseg_ref, mseg_ref,
        dq_ref, dpaird_ref, mmark_ref, dkm_ref, dvm_ref, dqh_ref, qrow_ref, grow_ref, weight_ref, slope_ref,
    )
    store_grad(dw_ref, at + width, nt_dot(a4t_ref[...], dq_ref[...]))
    store_grad(dw_ref, at + 2 * width, nt_dot(memt_ref[...], dpaird_ref[...]))
    for chunk in firsts:
        share.core_copy(chunk, first_ref, chunk).wait_recv()
        share.run_side(chunk, first_ref[:, core, :, chunk * share.step : (chunk + 1) * share.step])
    dmem_ref[...] = nn_dot(wkv_ref[...], dpaird_ref[...]).astype(jnp.bfloat16)
    back_ref[...] = nn_dot(wquery_ref[...], dq_ref[...]).T
    dgain_ref[0:1, :] = norm_back_into(g3_ref, h4_ref, h3_ref, gain_ref[0:1, :], back_ref)
    low_ref[...] = g3_ref[...].astype(jnp.bfloat16)
    at = at + 4 * width
    store_grad(dw_ref, at + 3 * width, nn_dot(attc_ref[...], low_ref[...]))
    gt_ref[...] = nt_dot(wout2_ref[...], low_ref[...]).astype(jnp.bfloat16)
    attend_back_core(
        H_CROSS, True, place, qt_ref, pair_ref, gt_ref, attc_ref, totalc_ref, qseg_ref, kseg_ref,
        dq_ref, dpair_ref, kmark_ref, dkh_ref, dvh_ref, dqh_ref, qrow_ref, grow_ref, weight_ref, slope_ref,
    )
    store_grad(dw_ref, at, nt_dot(turned_ref[:, own], dq_ref[...]))
    for low, high in chunks(2 * width):
        store_grad(dw_ref, at + width + low, nt_dot(turned_ref[...], dpair_ref[low:high, :]))
    for low, high in chunks(width):
        wide_ref[low:high, :] = nn_dot(wqkv_ref[low:high, width:], dpair_ref[...])
        wide_ref[low:high, own] += nn_dot(wqkv_ref[low:high, :width], dq_ref[...])
    for low, high in row_tiles(wide_ref.shape[1], tokens):
        da3_ref[low:high, :] = wide_ref[:, low:high].T.astype(jnp.bfloat16)
    for chunk in firsts:
        across_out_ref[:, chunk * share.step : (chunk + 1) * share.step] = share.side_sum(chunk)
        share.core_copy(chunk, first_ref, chunk).wait_send()
        share.sent_sides(chunk)


def middle(h2, a3, a3_more, mem_rows, grad_out, gains, own_seg, seg_row, mem_seg, down, owns, pieces):
    tokens, width = h2.shape
    keys, mems = seg_row.shape[0], mem_seg.shape[0]
    high_width = down.shape[0]
    seq_count = keys // tokens
    size = width // H_CROSS
    low, full = jnp.bfloat16, jnp.float32
    longest = max(tokens, mems)
    v = pltpu.VMEM
    in_hbm = pl.BlockSpec(memory_space=pl.ANY)
    half = width // (2 * seq_count)
    step = lax.axis_size("rows") // 2 * LANE_GROUP
    count = 2 * high_width // step
    dma = pltpu.SemaphoreType.DMA
    return pl.pallas_call(
        functools.partial(middle_kernel, len(pieces)),
        out_shape=(
            jax.ShapeDtypeStruct((tokens, width), low),
            jax.ShapeDtypeStruct((tokens, width), full),
            jax.ShapeDtypeStruct((keys, width), low),
            jax.ShapeDtypeStruct((width, 8 * width), low),
            jax.ShapeDtypeStruct((2, width), full),
            jax.ShapeDtypeStruct((width, mems), low),
            jax.ShapeDtypeStruct((half, 2 * high_width), low),
        ),
        in_specs=[IN_VMEM] * 10 + [in_hbm] * (6 + len(pieces)),
        out_specs=(IN_VMEM,) * 7,
        scratch_shapes=[
            v((width, 3 * width), low),
            v((width, width), low),
            v((width, width), low),
            v((width, 2 * width), low),
            v((width, width), low),
            v((width, high_width), low),
            pltpu.SemaphoreType.DMA((2, 5 * (4 * seq_count - 3))),
            v((width, keys), low),
            v((width, mems), low),
            v((tokens, width), low),
            v((width, tokens), low),
            v((width, tokens), low),
            v((2 * width, keys), low),
            v((width, tokens), low),
            v((H_CROSS, 1, tokens), full),
            v((width, tokens), low),
            v((2 * width, mems), low),
            v((width, tokens), low),
            v((H_CROSS, 1, tokens), full),
            v((tokens, width), full),
            v((tokens, width), full),
            v((tokens, high_width), low),
            v((tokens, high_width), low),
            v((tokens, width), low),
            v((width, tokens), low),
            v((width, tokens), low),
            v((2 * width, keys), low),
            v((2 * width, mems), low),
            v((tokens, width), full),
            v((width, keys), full),
            v((SEG_ROWS, keys), low),
            v((SEG_ROWS, mems), low),
            v((FWD_HEADS, size + SEG_ROWS, tokens), full),
            v((FWD_HEADS, 1, tokens), full),
            v((2, longest, TILE), full),
            v((BWD_HEADS, size, keys), full),
            v((BWD_HEADS, size, keys), full),
            v((BWD_HEADS, size, mems), full),
            v((BWD_HEADS, size, mems), full),
            v((BWD_HEADS, size, tokens), full),
            v((BWD_HEADS, size + SEG_ROWS, tokens), low),
            v((BWD_HEADS, size + SEG_ROWS, tokens), low),
            v((2, longest, TILE), low),
            v((2, longest, TILE), low),
            v((seq_count, 2, half, 2 * high_width), low),
            v((count, seq_count, half, step), low),
            v((count, seq_count - 1, half, step), low),
            dma((count, seq_count)),
            dma((count, seq_count)),
        ],
        compiler_params=pltpu.CompilerParams(
            collective_id=0, has_side_effects=True, vmem_limit_bytes=HOST_VMEM
        ),
        cost_estimate=pl.CostEstimate(
            flops=tokens * width * width * 200, bytes_accessed=tokens * width * 40, transcendentals=tokens * width * 20
        ),
        name="middle",
    )(
        h2, a3, a3_more, mem_rows, grad_out, gains, own_seg[None], seg_row[None], mem_seg[None], down,
        *owns, *pieces,
    )


class ShareSum:
    def __init__(self, send_sem, recv_sem, core=None, across=None, close=None, piece=None, mine=None, out=None, local_sem=None):
        self.send_sem, self.recv_sem, self.local_sem = send_sem, recv_sem, local_sem
        self.core_ref, self.across_ref, self.close_ref = core, across, close
        self.piece_ref, self.mine_ref, self.out_ref = piece, mine, out
        self.seq_count = lax.axis_size("seq")
        self.far_count = lax.axis_size("rows") // 4
        row, place = lax.axis_index("rows"), lax.axis_index("seq")
        self.core, self.near, self.far, self.place = lax.rem(row, 2), lax.rem(row // 2, 2), row // 4, place
        self.mate = (row + 1 - 2 * self.core, place)
        self.close = (row + 2 - 4 * self.near, place)
        self.peers = [None] + [
            (lax.rem(self.far + d, self.far_count) * 4 + self.near * 2 + self.core, place)
            for d in range(1, self.far_count)
        ]
        self.sides = [None] + [(row, lax.rem(place + d, self.seq_count)) for d in range(1, self.seq_count)]
        self.step = 2 * self.far_count * LANE_GROUP
        self.wide = self.far_count * LANE_GROUP
        self.core_first = 0
        self.early_sums = {}

    def enter(self, friends):
        barrier = pltpu.get_barrier_semaphore()
        for friend in friends:
            pl.semaphore_signal(barrier, inc=1, device_id=friend, device_id_type=pl.DeviceIdType.MESH)
        pl.semaphore_wait(barrier, len(friends))

    def columns(self, chunk):
        return pl.ds(pl.multiple_of(chunk * self.step, LANE_GROUP), self.step)

    def copy(self, chunk, slot, source, target, device):
        return pltpu.make_async_remote_copy(
            src_ref=source,
            dst_ref=target,
            send_sem=self.send_sem.at[chunk, slot],
            recv_sem=self.recv_sem.at[chunk, slot],
            device_id=device,
            device_id_type=pl.DeviceIdType.MESH,
        )

    def core_copy(self, chunk, source_ref, at):
        return self.copy(chunk, 0, source_ref.at[:, 1 - self.core, :, self.columns(at)], self.core_ref.at[chunk - self.core_first], self.mate)

    def side_copy(self, chunk, d):
        away = lax.rem(self.place + d, self.seq_count)
        return self.copy(chunk, d, self.core_ref.at[chunk - self.core_first, away], self.across_ref.at[chunk - self.core_first, d - 1], self.sides[d])

    def sum_at(self, chunk):
        if chunk in self.early_sums:
            return self.early_sums[chunk]
        return self.across_ref.at[chunk - self.core_first, 0]

    def near_copy(self, chunk):
        lanes = pl.ds(pl.multiple_of((1 - self.near) * self.wide, LANE_GROUP), self.wide)
        return self.copy(
            chunk, self.seq_count, self.sum_at(chunk).at[:, lanes], self.close_ref.at[chunk], self.close
        )

    def peer_copy(self, chunk, d):
        away = lax.rem(self.far + d, self.far_count)
        lanes = pl.ds(pl.multiple_of(away * LANE_GROUP, LANE_GROUP), LANE_GROUP)
        return self.copy(
            chunk, self.seq_count + d, self.close_ref.at[chunk, :, lanes], self.piece_ref.at[chunk, d - 1], self.peers[d]
        )

    def own_lanes(self, chunk):
        start = chunk * self.step + self.near * self.wide + self.far * LANE_GROUP
        return pl.ds(pl.multiple_of(start, LANE_GROUP), LANE_GROUP)

    def keep_copy(self, chunk):
        return pltpu.make_async_copy(
            self.mine_ref.at[chunk], self.out_ref.at[self.core, :, self.own_lanes(chunk)], self.local_sem.at[chunk]
        )

    def back_copy(self, chunk, d):
        return self.copy(
            chunk,
            self.seq_count + self.far_count - 1 + d,
            self.mine_ref.at[chunk],
            self.out_ref.at[self.core, :, self.own_lanes(chunk)],
            self.peers[d],
        )

    def near_back(self, chunk):
        start = pl.multiple_of(chunk * self.step + self.near * self.wide, LANE_GROUP)
        block = self.out_ref.at[self.core, :, pl.ds(start, self.wide)]
        return self.copy(chunk, self.seq_count + 2 * self.far_count - 1, block, block, self.close)

    def last_copy(self, chunk):
        block = self.out_ref.at[self.core, :, self.columns(chunk)]
        return self.copy(chunk, self.seq_count + 2 * self.far_count, block, block, self.mate)

    def run_side(self, chunk, kept):
        at = chunk - self.core_first
        self.core_ref[at] = (kept.astype(jnp.float32) + self.core_ref[at].astype(jnp.float32)).astype(jnp.bfloat16)
        for d in range(1, self.seq_count):
            self.side_copy(chunk, d).start()

    def side_sum(self, chunk, first=0):
        for d in range(1, self.seq_count):
            self.side_copy(chunk, d).wait_recv()
        summed = self.core_ref[chunk - first, self.place].astype(jnp.float32)
        for d in range(1, self.seq_count):
            summed = summed + self.across_ref[chunk - first, d - 1].astype(jnp.float32)
        return summed.astype(jnp.bfloat16)

    def run_near(self, chunk):
        self.sum_at(chunk)[...] = self.side_sum(chunk, self.core_first)
        self.near_copy(chunk).start()

    def run_peer(self, chunk):
        self.near_copy(chunk).wait_recv()
        lanes = pl.ds(pl.multiple_of(self.near * self.wide, LANE_GROUP), self.wide)
        summed = self.sum_at(chunk)[:, lanes].astype(jnp.float32) + self.close_ref[chunk].astype(jnp.float32)
        self.close_ref[chunk] = summed.astype(jnp.bfloat16)
        for d in range(1, self.far_count):
            self.peer_copy(chunk, d).start()

    def peer_sum(self, chunk):
        for d in range(1, self.far_count):
            self.peer_copy(chunk, d).wait_recv()
        lanes = pl.ds(pl.multiple_of(self.far * LANE_GROUP, LANE_GROUP), LANE_GROUP)
        summed = self.close_ref[chunk, :, lanes].astype(jnp.float32)
        for d in range(1, self.far_count):
            summed = summed + self.piece_ref[chunk, d - 1].astype(jnp.float32)
        self.mine_ref[chunk] = summed.astype(jnp.bfloat16)

    def run_back(self, chunk):
        self.peer_sum(chunk)
        self.start_back(chunk)

    def start_back(self, chunk):
        self.keep_copy(chunk).start()
        for d in range(1, self.far_count):
            self.back_copy(chunk, d).start()

    def run_near_back(self, chunk):
        self.keep_copy(chunk).wait()
        for d in range(1, self.far_count):
            self.back_copy(chunk, d).wait_recv()
        self.near_back(chunk).start()

    def run_last(self, chunk):
        self.near_back(chunk).wait_recv()
        self.last_copy(chunk).start()

    def sent_sides(self, chunk):
        for d in range(1, self.seq_count):
            self.side_copy(chunk, d).wait_send()

    def sent_peers(self, chunk):
        for d in range(1, self.far_count):
            self.peer_copy(chunk, d).wait_send()

    def sent_backs(self, chunk):
        for d in range(1, self.far_count):
            self.back_copy(chunk, d).wait_send()
        self.near_back(chunk).wait_send()
        self.last_copy(chunk).wait_send()


def closing_kernel(
    g1_ref, rows_ref, memt_ref, gain_ref, atta_ref, totala_ref, qa_ref, paira_ref,
    attb_ref, totalb_ref, qb_ref, pairb_ref, dmem_ref, small_ref, qseg_ref, kseg_ref, mseg_ref,
    wqkv_ref, wquery_ref, wkv_ref, wout_ref, mine_in_ref, across_in_ref, second_ref, conv_ref,
    grad_in_ref, grad_mem_ref, out_ref,
    turned_ref, branch_ref, gt_ref, dqa_ref, dqb_ref, dpaira_ref, dpairb_ref, kmark_ref, mmark_ref,
    dkh_ref, dvh_ref, dkm_ref, dvm_ref, dqh_ref, qrow_ref, grow_ref, weight_ref, slope_ref,
    late_ref, core_ref, across_ref, close_ref, piece_ref, mine_ref,
    send_sem, recv_sem, local_sem, conv_sem,
    da1_ref, da1_in_ref, upstream_ref, dmemory_ref, dmemory_in_ref, swap_send, swap_recv,
):
    tokens, width = g1_ref.shape
    keys = rows_ref.shape[0]
    place = lax.axis_index("seq")
    seq_count, _, half, conv_size = conv_ref.shape
    share = ShareSum(
        send_sem, recv_sem, core=core_ref, across=across_ref, close=close_ref, piece=piece_ref, mine=mine_ref,
        out=out_ref, local_sem=local_sem,
    )
    step = share.step
    first_count, second_count = mine_in_ref.shape[0], across_in_ref.shape[1] // step
    early_count = first_count + second_count
    count = out_ref.shape[-1] // step
    extra = second_ref.shape[-1] - second_count * step
    conv_end = extra + conv_size
    middle_count = (conv_end + 5 * width + step - 1) // step
    last_count = count - early_count - middle_count
    share.core_first = early_count
    share.enter([share.mate, share.close] + share.peers[1:] + share.sides[1:])
    late_copies = (
        pltpu.make_async_copy(second_ref.at[:, :, :, second_count * step :], late_ref.at[:, :, :, :extra], conv_sem.at[0]),
        pltpu.make_async_copy(conv_ref, late_ref.at[:, :, :, extra:conv_end], conv_sem.at[1]),
    )
    for copy in late_copies:
        copy.start()
    firsts = range(first_count)
    seconds = range(first_count, early_count)
    middles = range(early_count, early_count + middle_count)
    lasts = range(early_count + middle_count, count)
    for chunk in firsts:
        mine_ref[chunk] = mine_in_ref[chunk]
        share.start_back(chunk)
    for chunk in seconds:
        at = (chunk - first_count) * step
        share.early_sums[chunk] = across_in_ref.at[:, at : at + step]
        share.near_copy(chunk).start()

    def store_late(start, values):
        size = values.shape[1]
        late_ref[:, :, :, start : start + size] = values.astype(jnp.bfloat16).reshape(seq_count, 2, half, size)

    def start_late(chunk):
        share.core_copy(chunk, late_ref, chunk - early_count).start()

    def side_late(chunk):
        at = (chunk - early_count) * step
        share.core_copy(chunk, late_ref, chunk - early_count).wait_recv()
        share.run_side(chunk, late_ref[:, share.core, :, at : at + step])

    own = pl.ds(pl.multiple_of(place * tokens, 128), tokens)
    ready = conv_end // step
    with_out = (conv_end + 2 * width) // step
    branch_ref[...] = g1_ref[...].astype(jnp.bfloat16).T
    for copy in late_copies:
        copy.wait()
    for chunk in middles[:ready]:
        start_late(chunk)
    store_late(conv_end, nt_dot(branch_ref[...], atta_ref[...]))
    store_late(conv_end + width, nt_dot(branch_ref[...], attb_ref[...]))
    for chunk in middles[ready:with_out]:
        start_late(chunk)
    for chunk in middles[:ready]:
        side_late(chunk)
    gt_ref[...] = nn_dot(wout_ref[width:, :], branch_ref[...]).astype(jnp.bfloat16)
    for low, high in row_tiles(keys, 128):
        normed, _ = rows_normed(rows_ref[low:high, :].astype(jnp.float32))
        turned_ref[:, low:high] = (normed * gain_ref[...]).astype(jnp.bfloat16).T
    for chunk in middles[ready:with_out]:
        side_late(chunk)
    attend_back_core(
        H_CROSS, False, 0, qb_ref, pairb_ref, gt_ref, attb_ref, totalb_ref, qseg_ref, mseg_ref,
        dqb_ref, dpairb_ref, mmark_ref, dkm_ref, dvm_ref, dqh_ref, qrow_ref, grow_ref, weight_ref, slope_ref,
    )
    at = conv_end + 2 * width
    store_late(at, nt_dot(memt_ref[...], dpairb_ref[...]))
    store_late(at + 2 * width, nt_dot(turned_ref[:, own], dqb_ref[...]))
    at = at + 3 * width
    after = middle_count * step
    if at < after:
        late_ref[:, :, :, at:after] = jnp.zeros((seq_count, 2, half, after - at), jnp.bfloat16)
    for chunk in middles[with_out:]:
        start_late(chunk)
    dmemory_ref[...] = (dmem_ref[...].astype(jnp.float32) + nn_dot(wkv_ref[...], dpairb_ref[...])).T.astype(jnp.bfloat16)
    gt_ref[...] = nn_dot(wout_ref[:width, :], branch_ref[...]).astype(jnp.bfloat16)

    done = {}

    def advance(chunk):
        stages = (share.run_near, share.run_peer, share.run_back, share.run_near_back, share.run_last)
        stages[done.setdefault(chunk, 3 if chunk in firsts else 1 if chunk in seconds else 0)](chunk)
        done[chunk] += 1

    def advance_all(*groups):
        for group in groups:
            for chunk in group:
                advance(chunk)

    def first_pump():
        advance_all(seconds, middles[:1])

    def second_pump():
        for chunk in middles[with_out:]:
            side_late(chunk)
        advance_all(firsts, middles[:2])

    def third_pump():
        advance_all(seconds, middles[:3])

    def fourth_pump():
        advance_all(firsts, middles[:4])

    def pump(k):
        for at, action in enumerate((first_pump, second_pump, third_pump, fourth_pump)):
            pl.when(k == at)(action)

    attend_back_core(
        H_SELF, True, place, qa_ref, paira_ref, gt_ref, atta_ref, totala_ref, qseg_ref, kseg_ref,
        dqa_ref, dpaira_ref, kmark_ref, dkh_ref, dvh_ref, dqh_ref, qrow_ref, grow_ref, weight_ref, slope_ref, pump,
    )
    entered = [len(middles[:4])]
    flow = list(middles) + list(lasts)

    def tick():
        older = [chunk for chunk in flow[: entered[0]] if done[chunk] < 5]
        advance_all(older, flow[entered[0] : entered[0] + 1])
        entered[0] += 1

    advance_all(seconds)
    tick()
    store_late(after, nt_dot(turned_ref[:, own], dqa_ref[...]))
    for low, high in chunks(2 * width):
        store_late(after + width + low, nt_dot(turned_ref[...], dpaira_ref[low:high, :]))
    start_late(lasts[0])
    tick()
    gain_sum = jnp.zeros((8, width), jnp.float32)
    for away in [*range(1, seq_count), 0]:
        start = lax.rem(place + away, seq_count) * tokens
        for low, high in row_tiles(tokens, 128):
            lanes = pl.ds(pl.multiple_of(start + low, 128), high - low)
            upstream = nn_dot(wqkv_ref[:, width:], dpaira_ref[:, lanes])
            if away == 0:
                upstream = upstream + nn_dot(wqkv_ref[:, :width], dqa_ref[:, low:high])
                upstream = upstream + nn_dot(wquery_ref[...], dqb_ref[:, low:high])
            upstream = upstream.T
            normed, _ = rows_normed(rows_ref[lanes, :].astype(jnp.float32))
            gain_sum = gain_sum + folded(upstream * normed)
            if away == 0:
                upstream_ref[low:high, :] = upstream
            else:
                da1_ref[away - 1, low:high, :] = upstream.astype(jnp.bfloat16)

    def swap(kind, away, source, target):
        return pltpu.make_async_remote_copy(
            src_ref=source,
            dst_ref=target,
            send_sem=swap_send.at[kind, away - 1],
            recv_sem=swap_recv.at[kind, away - 1],
            device_id=share.sides[away],
            device_id_type=pl.DeviceIdType.MESH,
        )

    mem_own = dmemory_in_ref.shape[1]

    def row_swap(away):
        return swap(0, away, da1_ref.at[away - 1], da1_in_ref.at[away - 1])

    def mem_swap(away):
        start = pl.multiple_of(lax.rem(place + away, seq_count) * mem_own, mem_own)
        return swap(1, away, dmemory_ref.at[pl.ds(start, mem_own), :], dmemory_in_ref.at[away - 1])

    def start_swaps():
        for away in range(1, seq_count):
            pl.when(place + away >= seq_count)(row_swap(away).start)
            mem_swap(away).start()

    def finish_swaps():
        for away in range(1, seq_count):

            @pl.when(place < away)
            def _():
                row_swap(away).wait_recv()
                upstream_ref[...] += da1_in_ref[away - 1].astype(jnp.float32)

        own_start = pl.multiple_of(place * tokens, 128)
        for low, high in row_tiles(tokens, 128):
            values = rows_ref[pl.ds(pl.multiple_of(own_start + low, 128), high - low), :].astype(jnp.float32)
            normed, inverse = rows_normed(values)
            grad_in_ref[low:high, :] = g1_ref[low:high, :] + rows_norm_back(
                normed, inverse, gain_ref[...], upstream_ref[low:high, :]
            )
        total = dmemory_ref[pl.ds(pl.multiple_of(place * mem_own, mem_own), mem_own), :].astype(jnp.float32)
        for away in range(1, seq_count):
            mem_swap(away).wait_recv()
            total = total + dmemory_in_ref[away - 1].astype(jnp.float32)
        grad_mem_ref[...] = total
        for away in range(1, seq_count):
            pl.when(place + away >= seq_count)(row_swap(away).wait_send)
            mem_swap(away).wait_send()

    small = small_ref[...]
    is_first = lax.broadcasted_iota(jnp.int32, small.shape, 0) == 0
    small = jnp.where(is_first, jnp.sum(gain_sum, axis=0, keepdims=True), small)
    at = after + 3 * width
    store_late(at, small.T)
    at = at + small.shape[0]
    if at < late_ref.shape[-1]:
        late_ref[:, :, :, at:] = jnp.zeros((seq_count, 2, half, late_ref.shape[-1] - at), jnp.bfloat16)
    for chunk in lasts[1:]:
        start_late(chunk)
    side_late(lasts[0])
    advance_all(seconds)
    for chunk in lasts[1:]:
        side_late(chunk)
    start_swaps()
    ticks = 0
    while any(done.get(chunk, 0) < 5 for chunk in flow):
        tick()
        ticks += 1
        if ticks == SWAP_TICK:
            finish_swaps()
    for chunk in range(count):
        share.last_copy(chunk).wait_recv()
        share.sent_backs(chunk)
    for chunk in range(first_count, count):
        share.near_copy(chunk).wait_send()
        share.sent_peers(chunk)
    for chunk in range(early_count, count):
        share.core_copy(chunk, late_ref, chunk - early_count).wait_send()
        share.sent_sides(chunk)


def closing(
    g1, row_inputs, mem_turned, gain, self_kept, cross_kept, d_mem, small, own_seg, seg_row, mem_seg,
    qkv, query, pairs_weight, out, mine, across, second, conv,
):
    tokens, width = g1.shape
    keys, mems = row_inputs.shape[0], mem_turned.shape[1]
    seq_count = keys // tokens
    half = width // (2 * seq_count)
    far_count = lax.axis_size("rows") // 4
    step = 2 * far_count * LANE_GROUP
    size = width // H_CROSS
    middle_total = second.shape[1] - across.shape[1] + conv.shape[1] + 5 * width
    middle_total = middle_total + -middle_total % step
    last_total = 3 * width + small.shape[0]
    last_total = last_total + -last_total % step
    early_total = mine.shape[0] * step + across.shape[1]
    late = middle_total + last_total
    count = (early_total + late) // step
    slots = 3 + (seq_count - 1) + 2 * far_count
    low, full = jnp.bfloat16, jnp.float32
    longest = max(tokens, mems)
    v = pltpu.VMEM
    in_hbm = pl.BlockSpec(memory_space=pl.ANY)
    dma = pltpu.SemaphoreType.DMA
    grad_in, grad_mem, share = pl.pallas_call(
        closing_kernel,
        out_shape=(
            jax.ShapeDtypeStruct((tokens, width), full),
            jax.ShapeDtypeStruct((mems // seq_count, width), full),
            jax.ShapeDtypeStruct((2, half, early_total + late), low),
        ),
        in_specs=[IN_VMEM] * 23 + [in_hbm] * 2,
        out_specs=(IN_VMEM, IN_VMEM, in_hbm),
        scratch_shapes=[
            v((width, keys), low),
            v((width, tokens), low),
            v((width, tokens), low),
            v((width, tokens), low),
            v((width, tokens), low),
            v((2 * width, keys), low),
            v((2 * width, mems), low),
            v((SEG_ROWS, keys), low),
            v((SEG_ROWS, mems), low),
            v((BWD_HEADS, width // H_SELF, keys), full),
            v((BWD_HEADS, width // H_SELF, keys), full),
            v((BWD_HEADS, size, mems), full),
            v((BWD_HEADS, size, mems), full),
            v((BWD_HEADS, size, tokens), full),
            v((BWD_HEADS, size + SEG_ROWS, tokens), low),
            v((BWD_HEADS, size + SEG_ROWS, tokens), low),
            v((2, longest, TILE), low),
            v((2, longest, TILE), low),
            v((seq_count, 2, half, late), low),
            v((late // step, seq_count, half, step), low),
            v((late // step, seq_count - 1, half, step), low),
            v((count, half, step // 2), low),
            v((count, far_count - 1, half, LANE_GROUP), low),
            v((count, half, LANE_GROUP), low),
            dma((count, slots)),
            dma((count, slots)),
            dma((count,)),
            dma((2,)),
            v((seq_count - 1, tokens, width), low),
            v((seq_count - 1, tokens, width), low),
            v((tokens, width), full),
            v((mems, width), low),
            v((seq_count - 1, mems // seq_count, width), low),
            dma((2, seq_count - 1)),
            dma((2, seq_count - 1)),
        ],
        compiler_params=pltpu.CompilerParams(
            collective_id=2, has_side_effects=True, vmem_limit_bytes=HOST_VMEM
        ),
        cost_estimate=pl.CostEstimate(
            flops=tokens * width * width * 200, bytes_accessed=tokens * width * 40, transcendentals=tokens * width * 20
        ),
        name="closing",
    )(
        g1, row_inputs, mem_turned, gain, *self_kept, *cross_kept, d_mem, small,
        own_seg[None], seg_row[None], mem_seg[None], qkv, query, pairs_weight, out,
        mine, across, second.reshape(seq_count, 2, half, second.shape[1]), conv.reshape(seq_count, 2, half, conv.shape[1]),
    )
    return grad_in, grad_mem, share.reshape(2 * half, early_total + late), early_total + middle_total


def finishing_kernel(plan, small_at, share_ref, *outs):
    for (offset, size, dim), out_ref in zip(plan, outs):
        if dim == 0:
            out_ref[...] = share_ref[:, offset : offset + size].astype(jnp.float32)
        else:
            for low, high in row_tiles(size, 256):
                out_ref[low:high, :] = share_ref[:, offset + low : offset + high].astype(jnp.float32).T
    rows = share_ref[:, small_at : small_at + 128].astype(jnp.float32).T
    width = rows.shape[1]
    at = 0
    for out_ref in outs[len(plan) :]:
        for row in range(out_ref.shape[0]):
            for low in range(0, out_ref.shape[1], width):
                out_ref[row : row + 1, low : low + width] = rows[at : at + 1, :]
                at = at + 1


def finishing(share, plan, small_at, small_shapes):
    width = share.shape[0]
    shapes = [(width, size) if dim == 0 else (size, width) for _, size, dim in plan] + small_shapes
    return pl.pallas_call(
        functools.partial(finishing_kernel, plan, small_at),
        out_shape=tuple(jax.ShapeDtypeStruct(shape, jnp.float32) for shape in shapes),
        in_specs=[IN_VMEM],
        out_specs=(IN_VMEM,) * len(shapes),
        compiler_params=pltpu.CompilerParams(vmem_limit_bytes=KERNEL_VMEM),
        name="finishing",
    )(share)


def segment_reach(seg_row):
    length = seg_row.shape[0]
    first = jnp.sum(seg_row == 0)
    second = first + jnp.sum(seg_row == 1)
    spots = jnp.arange(length, dtype=jnp.int32)
    start = jnp.where(seg_row == 0, 0, jnp.where(seg_row == 1, first, second))
    stop = jnp.where(seg_row == 0, first, jnp.where(seg_row == 1, second, length))
    return spots - start, stop - 1 - spots


def turned_dot(weight, values):
    return jnp.einsum("kn,tk->nt", weight, values, preferred_element_type=jnp.float32)


def out_dot(turned, weight):
    return jnp.einsum("nt,nk->tk", turned, weight, preferred_element_type=jnp.float32)


def weight_dot(values, turned):
    return jnp.einsum("tk,nt->kn", values, turned, preferred_element_type=jnp.float32)


def out_weight_dot(turned, grads_in):
    return jnp.einsum("nt,tk->kn", turned, grads_in, preferred_element_type=jnp.float32)


def turned_back(grads_in, weight):
    return jnp.einsum("tk,nk->nt", grads_in, weight, preferred_element_type=jnp.float32)


def input_back(turned, weight):
    return jnp.einsum("nt,kn->tk", turned, weight, preferred_element_type=jnp.float32)


def self_attend(normed, normed_row, weight, head_count, own_seg, seg_row):
    model_width = normed.shape[1]
    queries = turned_dot(weight[:, :model_width], normed).astype(jnp.bfloat16)
    pairs = turned_dot(weight[:, model_width:], normed_row).astype(jnp.bfloat16)
    att_out, totals = attend_forward(queries, pairs, head_count, True, own_seg, seg_row)
    return (att_out, totals, queries, pairs, normed_row)


def self_back(normed, weight, grad_att, kept, head_count, own_seg, seg_row):
    att_out, totals, queries, pairs, normed_row = kept
    model_width = normed.shape[1]
    d_query, d_pairs = attend_back(
        queries, pairs, grad_att, att_out, totals, head_count, True, own_seg, seg_row
    )
    d_weight = jnp.concatenate([weight_dot(normed, d_query), weight_dot(normed_row, d_pairs)], 1)
    d_normed = input_back(d_query, weight[:, :model_width]) + row_sum_owned(
        input_back(d_pairs, weight[:, model_width:]).astype(jnp.bfloat16)
    )
    return (d_normed, d_weight)


def local(
    hidden_in,
    memory,
    grad_out,
    seg_ids,
    mem_seg_ids,
    gains,
    qkv_first,
    query_cross,
    kv_cross,
    out_first,
    taps_left,
    proj_left,
    taps_right,
    proj_right,
    mid_gain,
    taps_mid,
    proj_mid,
    qkv_second,
    out_second,
    query_last,
    kv_last,
    out_last,
    ffn_up,
    ffn_down,
):
    shards = (
        gains,
        qkv_first,
        query_cross,
        kv_cross,
        out_first,
        taps_left,
        proj_left,
        taps_right,
        proj_right,
        mid_gain,
        taps_mid,
        proj_mid,
        qkv_second,
        out_second,
        query_last,
        kv_last,
        out_last,
        ffn_up,
        ffn_down,
    )
    shard_dims = (1, 0, 0, 0, 1, 1, 0, 1, 0, 0, 1, 1, 0, 0, 0, 0, 0, 0, 1)
    small = (0, 5, 7, 9, 10)
    seq_count = lax.axis_size("seq")

    def select(group):
        return [shards[k] for k in group], [shard_dims[k] for k in group]

    first_group, second_group, conv_group, middle_group = (1,), (2, 3, 4), (6, 8, 11), (12, 13, 14, 15, 16, 17, 18)
    hidden_more = seq_rotated(hidden_in[0])
    first_same = seq_rotated(packed_half(*select(first_group)))
    gains, taps_left, taps_right, mid_gain, taps_mid = small_gather(*select(small))
    first_other = [core_swapped(piece) for piece in first_same]
    (qkv_first,) = joined_group(*select(first_group), interleaved(first_same, first_other), 2)
    packed, _ = after((packed_half(*select(second_group)), memory[0]), first_same)
    second_same, mem_more = seq_rotated(packed[0]), seq_rotated(packed[1])
    row_inputs = in_place_order([hidden_in[0]] + hidden_more, 0)
    mem_rows = in_place_order([memory[0]] + mem_more, 0)
    inputs = hidden_in[0].astype(jnp.float32)
    seg_row = seg_ids[0]
    mem_seg = mem_seg_ids[0]
    tok_count, model_width = inputs.shape
    row_start = lax.axis_index("seq") * tok_count
    own_seg = lax.dynamic_slice_in_dim(seg_row, row_start, tok_count)
    since, left = segment_reach(seg_row)
    since = lax.dynamic_slice_in_dim(jnp.pad(since, (RIM, 0)), row_start, tok_count + RIM)[:, None]
    left = lax.dynamic_slice_in_dim(jnp.pad(left, (0, RIM)), row_start, tok_count + RIM)[:, None]
    gain_rows = gains.astype(jnp.float32)
    mid_gain_f = mid_gain.astype(jnp.float32)
    left_taps = taps_left.astype(jnp.float32)
    right_taps = taps_right.astype(jnp.float32)
    mid_taps = taps_mid.astype(jnp.float32)
    normed_a = layer_norm(inputs, gain_rows[0]).astype(jnp.bfloat16)
    normed_row = layer_norm(row_inputs.astype(jnp.float32), gain_rows[0]).astype(jnp.bfloat16)
    normed_a, second_same = after(normed_a, second_same)
    second_other = [core_swapped(piece) for piece in second_same]
    packed, _ = after((packed_quarter(*select(conv_group)), packed_quarter(*select(middle_group))), second_same)
    conv_same, middle_same = seq_rotated(packed[0]), seq_rotated(packed[1])
    kept_a = self_attend(normed_a, normed_row, qkv_first, H_SELF, own_seg, seg_row)
    att_a, (second_other, conv_same) = after(kept_a[0], (second_other, conv_same))
    kept_a = (att_a,) + kept_a[1:]
    conv_near = [near_swapped(piece) for piece in conv_same]
    query_cross, kv_cross, out_first = joined_group(*select(second_group), interleaved(second_same, second_other), 2)
    pairs_b = turned_dot(kv_cross, mem_rows).astype(jnp.bfloat16)
    query_b = turned_dot(query_cross, normed_a).astype(jnp.bfloat16)
    out_b, total_b = attend_forward(query_b, pairs_b, H_CROSS, False, own_seg, mem_seg)
    out_b, conv_near = after(out_b, conv_near)
    conv_across = [core_swapped(jnp.concatenate(pair, 0)) for pair in zip(conv_same, conv_near)]
    hidden_b = (
        inputs
        + out_dot(kept_a[0], out_first[:model_width])
        + out_dot(out_b, out_first[model_width:])
    )
    hidden_b, middle_same = after(hidden_b, middle_same)
    middle_near = [near_swapped(piece) for piece in middle_same]
    proj_left, proj_right, proj_mid = joined_group(
        *select(conv_group), interleaved(conv_same, conv_near, conv_across), 4
    )
    normed_c = layer_norm(hidden_b, gain_rows[1]).astype(jnp.bfloat16)
    conv_l, conv_r, conv_m, hidden_c, normed_d = conv_forward(
        hidden_b,
        normed_c,
        passed_along(normed_c[tok_count - RIM :], "seq", 1),
        since,
        left_taps,
        right_taps,
        mid_taps,
        mid_gain_f[None],
        gain_rows[2:3],
        proj_left,
        proj_right,
        proj_mid,
    )
    normed_d, middle_near = after(normed_d, middle_near)
    middle_across = [core_swapped(jnp.concatenate(pair, 0)) for pair in zip(middle_same, middle_near)]
    middle_pieces = interleaved(middle_same, middle_near, middle_across)
    down_at = sum(shard.shape[1] for shard in shards[12:18])
    down, _ = joined_weight(shards[18], 1, middle_pieces, down_at, 4)
    conv_rims = passed_along(jnp.concatenate([conv_l[:RIM], conv_r[:RIM]], 1), "seq", -1)
    more = jnp.stack(seq_rotated(normed_d))
    result, grad_now, d_normed, d_middle, d_gains_late, d_mem, across_first = middle(
        hidden_c,
        normed_d,
        more,
        mem_rows,
        grad_out[0],
        gain_rows[3:5],
        own_seg,
        seg_row,
        mem_seg,
        down,
        shards[12:18],
        middle_pieces,
    )
    d_hidden, g_three = norm_back(hidden_c, gain_rows[2], row_sum_owned(d_normed))
    grad_now = grad_now + d_hidden
    branch = grad_now.astype(jnp.bfloat16)
    grad_now, d_projections, d_taps_left, d_taps_right, d_taps_mid, d_mid_gain, g_two, mine, across = conv_back(
        grad_now,
        passed_along(branch[:RIM], "seq", -1),
        conv_l,
        conv_r,
        conv_rims,
        conv_m,
        normed_c,
        hidden_b,
        left,
        left_taps,
        right_taps,
        mid_taps,
        mid_gain_f[None],
        gain_rows[1:2],
        proj_left,
        proj_right,
        proj_mid,
        across_first,
        d_middle,
    )
    d_mid_gain, g_two = d_mid_gain[0], g_two[0]
    d_gains = jnp.concatenate([jnp.stack([jnp.zeros_like(g_two), g_two, g_three], 0), d_gains_late], 0)
    wide, narrow = proj_left.shape[1], proj_right.shape[1]
    width = model_width // lax.axis_size("seq")
    small_grads = (d_gains, d_taps_left, d_taps_right, d_mid_gain, d_taps_mid)
    grad_in, grad_mem, share, last_at = closing(
        grad_now,
        row_inputs,
        mem_rows.T,
        gain_rows[:1],
        kept_a[:4],
        (out_b, total_b, query_b, pairs_b),
        d_mem,
        small_rows(small_grads, width),
        own_seg,
        seg_row,
        mem_seg,
        qkv_first,
        query_cross,
        kv_cross,
        out_first,
        mine,
        across,
        d_middle,
        d_projections,
    )
    shares = [None] * len(shards)
    up = down.shape[0]
    plan, order, offset = [], (17, 18, 16, 14, 15, 12, 13, 11, 6, 8, 4, 3, 2, 1), 0
    for k, size in zip(
        order,
        (up, up, model_width, model_width, 2 * model_width, 3 * model_width, model_width)
        + (wide, wide, narrow, 2 * model_width, 2 * model_width, model_width, 3 * model_width),
    ):
        offset = last_at if k == 1 else offset
        plan.append((offset, size, shard_dims[k]))
        offset = offset + size
    small_shapes = [shards[k].shape if k != 9 else (1, shards[k].shape[0]) for k in small]
    found = finishing(share, plan, offset, small_shapes)
    for k, piece in zip(order + small, found):
        shares[k] = piece.reshape(shards[k].shape)
    return (
        result[None],
        grad_in[None],
        grad_mem[None],
        shares[0],
        shares[1],
        shares[2],
        shares[3],
        shares[4],
        shares[5],
        shares[6],
        shares[7],
        shares[8],
        shares[9],
        shares[10],
        shares[11],
        shares[12],
        shares[13],
        shares[14],
        shares[15],
        shares[16],
        shares[17],
        shares[18],
    )


def solution(mesh):
    placed = (
        P("rows", "seq", None),
        P("rows", "seq", None),
        P("rows", "seq", None),
        P("rows", None),
        P("rows", None),
        P(None, "seq"),
        P("seq", None),
        P("seq", None),
        P("seq", None),
        P(None, "seq"),
        P(None, "seq"),
        P("seq", None),
        P(None, "seq"),
        P("seq", None),
        P("seq"),
        P(None, "seq"),
        P(None, "seq"),
        P("seq", None),
        P("seq", None),
        P("seq", None),
        P("seq", None),
        P("seq", None),
        P("seq", None),
        P(None, "seq"),
    )
    return jax.shard_map(
        local,
        mesh=mesh,
        in_specs=placed,
        out_specs=(
            P("rows", "seq", None),
            P("rows", "seq", None),
            P("rows", "seq", None),
            P(None, "seq"),
            P("seq", None),
            P("seq", None),
            P("seq", None),
            P(None, "seq"),
            P(None, "seq"),
            P("seq", None),
            P(None, "seq"),
            P("seq", None),
            P("seq"),
            P(None, "seq"),
            P(None, "seq"),
            P("seq", None),
            P("seq", None),
            P("seq", None),
            P("seq", None),
            P("seq", None),
            P("seq", None),
            P(None, "seq"),
        ),
        check_vma=False,
    )
```

```python
import functools

import jax
import jax.numpy as jnp
from jax import lax
from jax.experimental import pallas as pl
from jax.experimental.pallas import tpu as pltpu
from jax.sharding import PartitionSpec as P

H_SELF = 16
H_CROSS = 8
WIDE = 1024
NARROW = 256
LEFT_TAPS = 11
RIGHT_TAPS = 7


NEG_BIG = -1e30
EPSILON = 1e-06


def rotated(block, axis, distance):
    size = lax.axis_size(axis)
    return lax.ppermute(block, axis, [((i + distance) % size, i) for i in range(size)])


def core_swapped(block):
    return lax.ppermute(block, "rows", [(i, i ^ 1) for i in range(lax.axis_size("rows"))])


def in_place_order(relative, dim):
    count = len(relative)
    place = lax.axis_index("seq")
    orders = [
        jnp.concatenate([relative[(p - me) % count] for p in range(count)], dim)
        for me in range(count)
    ]
    result = orders[0]
    for me in range(1, count):
        result = jnp.where(place == me, orders[me], result)
    return result


def gathered(block, dim=0):
    count = lax.axis_size("seq")
    return in_place_order([block] + [rotated(block, "seq", d) for d in range(1, count)], dim)


def near_swapped(block):
    return lax.ppermute(block, "rows", [(i, i ^ 2) for i in range(lax.axis_size("rows"))])


def flat_share(shard, dim, index, count):
    size = shard.shape[0] // count
    part = lax.dynamic_slice_in_dim(shard, index * size, size)
    if dim == 0:
        return part
    width = shard.shape[1]
    blocks = part.reshape(-1, width // count, width)
    return jnp.swapaxes(blocks, 0, 1).reshape(width // count, -1)


def unflat_share(part, shape, dim, count):
    if dim == 0:
        return part
    width = shape[1]
    blocks = part.reshape(width // count, -1, width)
    return jnp.swapaxes(blocks, 0, 1).reshape(shape[0] // count, width)


def seq_rotated(packed):
    return [rotated(packed, "seq", d) for d in range(1, lax.axis_size("seq"))]


def packed_half(shards, dims):
    core = lax.axis_index("rows") & 1
    return jnp.concatenate([flat_share(shard, dim, core, 2) for shard, dim in zip(shards, dims)], 1)


def packed_quarter(shards, dims):
    index = lax.axis_index("rows") & 3
    return jnp.concatenate([flat_share(shard, dim, index, 4) for shard, dim in zip(shards, dims)], 1)


def ordered(bit, first, second):
    return jnp.where(bit == 0, jnp.concatenate([first, second], 0), jnp.concatenate([second, first], 0))


def joined_weight(shard, dim, pieces, offset, count):
    row = lax.axis_index("rows")
    size = shard.size // count // pieces[0].shape[0]

    def part(piece):
        return unflat_share(piece[:, offset : offset + size], shard.shape, dim, count)

    relative = [shard]
    if count == 2:
        for k in range(0, len(pieces), 2):
            relative.append(ordered(row & 1, part(pieces[k]), part(pieces[k + 1])))
    else:
        for k in range(0, len(pieces), 3):
            same, near, across = pieces[k : k + 3]
            rows = same.shape[0]
            own_pair = ordered(row & 1, part(same), part(across[:rows]))
            near_pair = ordered(row & 1, part(near), part(across[rows:]))
            relative.append(ordered(row & 2, own_pair, near_pair))
    return in_place_order(relative, dim), offset + size


def joined_group(shards, dims, pieces, count):
    results = []
    offset = 0
    for shard, dim in zip(shards, dims):
        full, offset = joined_weight(shard, dim, pieces, offset, count)
        results.append(full)
    return results


def interleaved(*lists):
    return [item for items in zip(*lists) for item in items]


def small_gather(shards, dims):
    sizes = [shard.size for shard in shards]
    flat = jnp.concatenate([shard.reshape(-1) for shard in shards])
    flat = padded_rows(flat, 2048, 0).reshape(-1, 128)
    parts = [flat] + [rotated(flat, "seq", d) for d in range(1, lax.axis_size("seq"))]
    parts = [part.reshape(-1) for part in parts]
    results = []
    offset = 0
    for shard, dim, size in zip(shards, dims, sizes):
        relative = [part[offset : offset + size].reshape(shard.shape) for part in parts]
        results.append(in_place_order(relative, dim))
        offset = offset + size
    return results


def padded_rows(block, multiple, dim):
    extra = -block.shape[dim] % multiple
    if not extra:
        return block
    widths = [(0, 0)] * block.ndim
    widths[dim] = (0, extra)
    return jnp.pad(block, widths)


def halved_sum(block, axis, bit, dim):
    half = block.shape[dim] // 2
    upper = ((lax.axis_index(axis) & bit) != 0).astype(jnp.int32)
    kept = lax.dynamic_slice_in_dim(block, upper * half, half, dim)
    sent = lax.dynamic_slice_in_dim(block, (1 - upper) * half, half, dim)
    got = lax.ppermute(sent, axis, [(i, i ^ bit) for i in range(lax.axis_size(axis))])
    return (kept.astype(jnp.float32) + got.astype(jnp.float32)).astype(jnp.bfloat16)


def row_sum_owned(partial):
    bit = lax.axis_size("seq") // 2
    while bit:
        partial = halved_sum(partial, "seq", bit, 0)
        bit = bit // 2
    return partial.astype(jnp.float32)


def after(values, others):
    return lax.optimization_barrier((values, others))


def passed_along(block, axis, distance):
    devices = range(lax.axis_size(axis))
    route = [(i - distance, i) for i in devices if i - distance in devices]
    return lax.ppermute(block, axis, route)


def layer_norm(values, gain_vec):
    centre = values - jnp.mean(values, axis=-1, keepdims=True)
    inverse = lax.rsqrt(jnp.mean(centre * centre, axis=-1, keepdims=True) + EPSILON)
    return centre * inverse * gain_vec


def norm_back(values, gain_vec, upstream):
    centre = values - jnp.mean(values, axis=-1, keepdims=True)
    inverse = lax.rsqrt(jnp.mean(centre * centre, axis=-1, keepdims=True) + EPSILON)
    normed = centre * inverse
    scaled = upstream * gain_vec
    d_values = inverse * (
        scaled
        - jnp.mean(scaled, axis=-1, keepdims=True)
        - normed * jnp.mean(scaled * normed, axis=-1, keepdims=True)
    )
    return (d_values, jnp.sum(upstream * normed, axis=0))


def swish_slope(pre_act):
    sigma = jax.nn.sigmoid(pre_act)
    return sigma * (1.0 + pre_act * (1.0 - sigma))


def plain_dot(first, second):
    return jnp.dot(first, second, preferred_element_type=jnp.float32)


def left_dot(first, second):
    return jnp.einsum("nk,nm->km", first, second, preferred_element_type=jnp.float32)


def right_dot(grads_in, weight):
    return jnp.einsum("nm,km->nk", grads_in, weight, preferred_element_type=jnp.float32)


TILE = 256
SEG_ROWS = 16
LOG2E = 1.4426950408889634


def tiles_of(extent):
    return [(low, min(low + TILE, extent)) for low in range(0, extent, TILE)]


def tn_dot(first, second):
    return lax.dot_general(first, second, (((0,), (0,)), ((), ())), preferred_element_type=jnp.float32)


def nn_dot(first, second):
    return lax.dot_general(first, second, (((1,), (0,)), ((), ())), preferred_element_type=jnp.float32)


def nt_dot(first, second):
    return lax.dot_general(first, second, (((1,), (1,)), ((), ())), preferred_element_type=jnp.float32)


def row_numbers(width):
    return lax.broadcasted_iota(jnp.int32, (SEG_ROWS, width), 0)


def split_low(values, count):
    pieces = []
    for _ in range(count):
        piece = values.astype(jnp.bfloat16).astype(jnp.float32)
        pieces.append(piece)
        values = values - piece
    return pieces


def key_marks(key_seg, ones):
    rows = row_numbers(key_seg.shape[1])
    marked = jnp.logical_or(rows == key_seg, jnp.logical_and(rows >= 3, rows < 3 + ones))
    return jnp.where(marked, 1.0, 0.0).astype(jnp.bfloat16)


def query_marks(query_seg):
    rows = row_numbers(query_seg.shape[1])
    other = jnp.logical_and(rows < 3, rows != query_seg)
    return jnp.where(other, NEG_BIG, 0.0)


def with_rows(marks, first, pieces):
    rows = row_numbers(marks.shape[1])
    for k, piece in enumerate(pieces):
        marks = jnp.where(rows == first + k, piece, marks)
    return marks.astype(jnp.bfloat16)


def triangle(scores, low):
    key_at = lax.broadcasted_iota(jnp.int32, scores.shape, 0)
    query_at = lax.broadcasted_iota(jnp.int32, scores.shape, 1) + low
    return jnp.where(key_at <= query_at, scores, NEG_BIG)


FWD_HEADS = 4
BWD_HEADS = 4


def attend_kernel(heads, causal, place_ref, *refs):
    attend_core(heads, causal, place_ref[0], *refs)


def attend_core(
    heads, causal, place, qt_ref, pair_ref, qseg_ref, kseg_ref, ot_ref, total_ref, kmark_ref, sum_ref, peak_ref, score_ref,
    between=None,
):
    width, tokens = qt_ref.shape
    size = width // heads
    factor = size ** (-0.5) * LOG2E
    block = tokens if causal else pair_ref.shape[1]
    place = place if causal else 0
    kmark_ref[...] = key_marks(kseg_ref[...], 0)
    value_marks = jnp.where(row_numbers(TILE) == 0, 1.0, 0.0).astype(jnp.bfloat16)
    qmarks = query_marks(qseg_ref[...]).astype(jnp.bfloat16)
    tiles = tiles_of(tokens)

    def head_rows(head, base=0):
        return pl.ds(pl.multiple_of(base + head * size, size), size)

    def on_units(several, start, first):
        units = [
            (k if between is None else head, head, low, high)
            for k, head in enumerate(several)
            for low, high in tiles
        ]

        def key_parts(unit):
            _, _, _, high = unit
            return tiles_of(high if first and causal else block)

        def lanes_of(part):
            return pl.ds(pl.multiple_of(start + part[0], 128), part[1] - part[0])

        def score_part(unit, slot, part):
            k, head, low, high = unit
            query_rows = jnp.concatenate([qt_ref[head_rows(head), low:high], qmarks[:, low:high]], 0)
            lanes = lanes_of(part)
            scores = tn_dot(jnp.concatenate([pair_ref[head_rows(head), lanes], kmark_ref[:, lanes]], 0), query_rows)
            if first and causal and part[0] >= low:
                scores = triangle(scores, low - part[0])
            score_ref[slot, part[0] : part[1], : high - low] = scores
            return jnp.max(scores, axis=0, keepdims=True)

        def value_part(unit, slot, part, peak):
            k, head, low, high = unit
            scores = score_ref[slot, part[0] : part[1], : high - low]
            weights = jnp.exp2((scores - peak) * factor).astype(jnp.bfloat16)
            value_rows = jnp.concatenate(
                [pair_ref[head_rows(head, width), lanes_of(part)], value_marks[:, : part[1] - part[0]]], 0
            )
            return nn_dot(value_rows, weights)

        held = None
        for at in range(len(units) + 1):
            unit = units[at] if at < len(units) else None
            parts = key_parts(unit) if unit else []
            old_parts = key_parts(held[0]) if held else []
            peak = None
            if unit and not first:
                peak = peak_ref[unit[0], :, unit[2] : unit[3]]
            before = peak
            summed = None
            for step in range(max(len(parts), len(old_parts))):
                if step < len(parts):
                    found = score_part(unit, at % 2, parts[step])
                    peak = found if peak is None else jnp.maximum(peak, found)
                if step < len(old_parts):
                    term = value_part(held[0], (at - 1) % 2, old_parts[step], held[1])
                    summed = term if summed is None else summed + term
            if held:
                k, _, low, high = held[0]
                if not first:
                    summed = summed + sum_ref[k, :, low:high] * jnp.exp2((held[2] - held[1]) * factor)
                sum_ref[k, :, low:high] = summed
                peak_ref[k, :, low:high] = held[1]
            held = (unit, peak, before)

    def group_of(step):
        return [step * FWD_HEADS + k for k in range(FWD_HEADS)]

    def start_heads(step, carry):
        on_units(group_of(step), place * block, True)
        return carry

    def finish_heads(step, carry):
        several = group_of(step)
        if causal:

            def earlier(back, held):
                on_units(several, back * block, False)
                return held

            lax.fori_loop(0, place, earlier, 0)
        for k, head in enumerate(several):
            slot = k if between is None else head
            total = sum_ref[slot, size : size + 1, :]
            ot_ref[head_rows(head), :] = (sum_ref[slot, :size, :] / total).astype(jnp.bfloat16)
            total_ref[head] = peak_ref[slot] + jnp.log2(total) / factor
        return carry

    if between is None:
        lax.fori_loop(0, heads // FWD_HEADS, lambda k, held: finish_heads(k, start_heads(k, held)), 0)
    else:
        lax.fori_loop(0, heads // FWD_HEADS, start_heads, 0)
        between()
        lax.fori_loop(0, heads // FWD_HEADS, finish_heads, 0)


def attend_back_kernel(heads, causal, place_ref, *refs):
    attend_back_core(heads, causal, place_ref[0], *refs)


def attend_back_core(
    heads, causal, place, qt_ref, pair_ref, gt_ref, ot_ref, total_ref, qseg_ref, kseg_ref,
    dq_ref, dpair_ref, kmark_ref, dkh_ref, dvh_ref, dqh_ref, qrow_ref, grow_ref, weight_ref, slope_ref,
    pump=None,
):
    width, tokens = qt_ref.shape
    size = width // heads
    scale = size ** (-0.5)
    factor = scale * LOG2E
    block = tokens if causal else pair_ref.shape[1]
    place = place if causal else 0
    kmark_ref[...] = key_marks(kseg_ref[...], 3)
    value_marks = jnp.where(row_numbers(TILE) < 2, 1.0, 0.0).astype(jnp.bfloat16)
    qmarks = query_marks(qseg_ref[...])
    tiles = tiles_of(tokens)

    def head_rows(head, base=0):
        return pl.ds(pl.multiple_of(base + head * size, size), size)

    def prepare(k, head):
        own = head_rows(head)
        grads = gt_ref[own, :]
        delta = jnp.sum(grads.astype(jnp.float32) * ot_ref[own, :].astype(jnp.float32), axis=0, keepdims=True)
        qrow_ref[k, :size, :] = qt_ref[own, :]
        qrow_ref[k, size : size + SEG_ROWS, :] = with_rows(qmarks, 3, split_low(-total_ref[head], 3))
        grow_ref[k, :size, :] = grads
        grow_ref[k, size : size + SEG_ROWS, :] = with_rows(jnp.zeros_like(qmarks), 0, split_low(-delta, 2))

    def on_units(several, start, first):
        units = [(k, head, low, high) for k, head in enumerate(several) for low, high in tiles]

        def key_parts(unit):
            _, _, _, high = unit
            return tiles_of(high if first and causal else block)

        def lanes_of(part):
            return pl.ds(pl.multiple_of(start + part[0], 128), part[1] - part[0])

        def score_part(unit, slot, part):
            k, head, low, high = unit
            lanes = lanes_of(part)
            key_rows = jnp.concatenate([pair_ref[head_rows(head), lanes], kmark_ref[:, lanes]], 0)
            value_rows = jnp.concatenate(
                [pair_ref[head_rows(head, width), lanes], value_marks[:, : part[1] - part[0]]], 0
            )
            scores = tn_dot(key_rows, qrow_ref[k, : size + SEG_ROWS, low:high])
            if first and causal and part[0] >= low:
                scores = triangle(scores, low - part[0])
            weights = jnp.exp2(scores * factor)
            slopes = tn_dot(value_rows, grow_ref[k, : size + SEG_ROWS, low:high])
            weight_ref[slot, part[0] : part[1], : high - low] = weights.astype(jnp.bfloat16)
            slope_ref[slot, part[0] : part[1], : high - low] = (weights * slopes).astype(jnp.bfloat16)

        def grad_part(unit, slot, part):
            k, head, low, high = unit
            lanes = lanes_of(part)
            weights = weight_ref[slot, part[0] : part[1], : high - low]
            slopes = slope_ref[slot, part[0] : part[1], : high - low]
            dvh_ref[k, :, lanes] += nt_dot(grow_ref[k, :size, low:high], weights)
            dkh_ref[k, :, lanes] += nt_dot(qrow_ref[k, :size, low:high], slopes)
            return nn_dot(pair_ref[head_rows(head), lanes], slopes)

        held = None
        for at in range(len(units) + 1):
            unit = units[at] if at < len(units) else None
            parts = key_parts(unit) if unit else []
            old_parts = key_parts(held) if held else []
            summed = None
            for step in range(max(len(parts), len(old_parts))):
                if step < len(parts):
                    score_part(unit, at % 2, parts[step])
                if step < len(old_parts):
                    term = grad_part(held, (at - 1) % 2, old_parts[step])
                    summed = term if summed is None else summed + term
            if held:
                k, _, low, high = held
                if first:
                    dqh_ref[k, :size, low:high] = summed
                else:
                    dqh_ref[k, :size, low:high] += summed
            held = unit

    def some_heads(step, carry):
        several = [step * BWD_HEADS + k for k in range(BWD_HEADS)]
        if pump is not None:
            pump(step)
        dkh_ref[...] = jnp.zeros_like(dkh_ref)
        dvh_ref[...] = jnp.zeros_like(dvh_ref)
        for k, head in enumerate(several):
            prepare(k, head)
        on_units(several, place * block, True)
        if causal:

            def earlier(back, held):
                on_units(several, back * block, False)
                return held

            lax.fori_loop(0, place, earlier, 0)
        for k, head in enumerate(several):
            dq_ref[head_rows(head), :] = (dqh_ref[k, :size, :] * scale).astype(jnp.bfloat16)
            dpair_ref[head_rows(head), :] = (dkh_ref[k] * scale).astype(jnp.bfloat16)
            dpair_ref[head_rows(head, width), :] = dvh_ref[k].astype(jnp.bfloat16)
        return carry

    lax.fori_loop(0, heads // BWD_HEADS, some_heads, 0)


IN_SMEM = pl.BlockSpec(memory_space=pltpu.SMEM)
IN_VMEM = pl.BlockSpec(memory_space=pltpu.VMEM)
KERNEL_VMEM = 48 * 2**20
HOST_VMEM = 63 * 2**20 + 2**19


LANE_GROUP = 128
SWAP_TICK = 4


def attend_forward(queries, pairs_t, heads, causal, query_seg, key_seg):
    width, tokens = queries.shape
    total_keys = pairs_t.shape[1]
    pairs = heads * tokens * total_keys
    return pl.pallas_call(
        functools.partial(attend_kernel, heads, causal),
        out_shape=(
            jax.ShapeDtypeStruct((width, tokens), jnp.bfloat16),
            jax.ShapeDtypeStruct((heads, 1, tokens), jnp.float32),
        ),
        in_specs=[IN_SMEM] + [IN_VMEM] * 4,
        out_specs=(IN_VMEM, IN_VMEM),
        scratch_shapes=[
            pltpu.VMEM((SEG_ROWS, total_keys), jnp.bfloat16),
            pltpu.VMEM((FWD_HEADS, width // heads + SEG_ROWS, tokens), jnp.float32),
            pltpu.VMEM((FWD_HEADS, 1, tokens), jnp.float32),
            pltpu.VMEM((2, tokens if causal else total_keys, TILE), jnp.float32),
        ],
        compiler_params=pltpu.CompilerParams(vmem_limit_bytes=KERNEL_VMEM),
        cost_estimate=pl.CostEstimate(
            flops=pairs * 600, bytes_accessed=4 * width * total_keys, transcendentals=pairs
        ),
        name="attend_fwd",
    )(lax.axis_index("seq").reshape(1), queries, pairs_t, query_seg[None], key_seg[None])


def attend_back(queries, pairs_t, grads, outs, totals, heads, causal, query_seg, key_seg):
    width, tokens = queries.shape
    total_keys = pairs_t.shape[1]
    pairs = heads * tokens * total_keys
    size = width // heads
    return pl.pallas_call(
        functools.partial(attend_back_kernel, heads, causal),
        out_shape=(
            jax.ShapeDtypeStruct((width, tokens), jnp.bfloat16),
            jax.ShapeDtypeStruct((2 * width, total_keys), jnp.bfloat16),
        ),
        in_specs=[IN_SMEM] + [IN_VMEM] * 7,
        out_specs=(IN_VMEM, IN_VMEM),
        scratch_shapes=[
            pltpu.VMEM((SEG_ROWS, total_keys), jnp.bfloat16),
            pltpu.VMEM((BWD_HEADS, size, total_keys), jnp.float32),
            pltpu.VMEM((BWD_HEADS, size, total_keys), jnp.float32),
            pltpu.VMEM((BWD_HEADS, size, tokens), jnp.float32),
            pltpu.VMEM((BWD_HEADS, size + SEG_ROWS, tokens), jnp.bfloat16),
            pltpu.VMEM((BWD_HEADS, size + SEG_ROWS, tokens), jnp.bfloat16),
            pltpu.VMEM((2, tokens if causal else total_keys, TILE), jnp.bfloat16),
            pltpu.VMEM((2, tokens if causal else total_keys, TILE), jnp.bfloat16),
        ],
        compiler_params=pltpu.CompilerParams(vmem_limit_bytes=KERNEL_VMEM),
        cost_estimate=pl.CostEstimate(
            flops=pairs * 1500, bytes_accessed=8 * width * total_keys, transcendentals=pairs
        ),
        name="attend_bwd",
    )(
        lax.axis_index("seq").reshape(1), queries, pairs_t, grads, outs, totals,
        query_seg[None], key_seg[None],
    )


RIM = 16
ROW_TILE = 64
MERGE_ROWS = 64


def row_tiles(extent, tile):
    return [(low, min(low + tile, extent)) for low in range(0, extent, tile)]


def halves_of(extent):
    middle = -(-extent // 32) * 16
    return [(0, middle), (middle, extent)]


def group_lanes(group):
    return pl.ds(pl.multiple_of(group * 128, 128), 128)


def wide_rows(column, width=128):
    return jnp.broadcast_to(column, (column.shape[0], width))


def loop_rows(extent, tile, body):
    def step(k, carry):
        body(pl.ds(pl.multiple_of(k * tile, tile), tile))
        return carry

    whole = extent // tile
    lax.fori_loop(0, whole, step, 0)
    if whole * tile < extent:
        body(pl.ds(whole * tile, extent - whole * tile))


def rows_normed(values):
    centre = values - jnp.mean(values, axis=-1, keepdims=True)
    inverse = lax.rsqrt(jnp.mean(centre * centre, axis=-1, keepdims=True) + EPSILON)
    return centre * inverse, inverse


def rows_norm_back(normed, inverse, gain_vec, upstream):
    scaled = upstream * gain_vec
    return inverse * (
        scaled
        - jnp.mean(scaled, axis=-1, keepdims=True)
        - normed * jnp.mean(scaled * normed, axis=-1, keepdims=True)
    )


def taps_forward(source_ref, first_row, since, lanes, low, high, weights):
    result = None
    for offset, weight in enumerate(weights):
        start = first_row + low - offset
        window = source_ref[start : start + high - low, lanes]
        if offset:
            window = jnp.where(since >= offset, window, 0.0)
        term = window * weight
        result = term if result is None else result + term
    return result


def conv_fwd_kernel(
    h1_ref, a2_ref, rim_ref, since_ref, tl_ref, tr_ref, tm_ref, mgain_ref, gain_ref, pl_ref, pr_ref, pm_ref,
    cl_ref, cr_ref, cm_ref, h2_ref, a3_ref,
    ext_ref, wide_ref, cle_ref, cre_ref, up_ref, mixed_ref,
):
    tokens, width = h1_ref.shape
    total = tokens + RIM
    narrow = pr_ref.shape[1]
    ext_ref[0:RIM, :] = jnp.zeros((RIM, width), jnp.float32)
    ext_ref[RIM : 2 * RIM, :] = rim_ref[...].astype(jnp.float32)
    ext_ref[2 * RIM :, :] = a2_ref[...].astype(jnp.float32)
    wide_ref[...] = wide_rows(since_ref[...])

    def first_convs(group, carry):
        lanes = group_lanes(group)
        left = [tl_ref[j : j + 1, lanes] for j in range(tl_ref.shape[0])]
        right = [tr_ref[j : j + 1, lanes] for j in range(tr_ref.shape[0])]
        for low, high in row_tiles(total, ROW_TILE):
            since = wide_ref[low:high, :]
            cle_ref[low:high, lanes] = taps_forward(ext_ref, RIM, since, lanes, low, high, left).astype(jnp.bfloat16)
            cre_ref[low:high, lanes] = taps_forward(ext_ref, RIM, since, lanes, low, high, right).astype(jnp.bfloat16)
        return carry

    lax.fori_loop(0, width // 128, first_convs, 0)
    cl_ref[...] = cle_ref[RIM:, :]
    cr_ref[...] = cre_ref[RIM:, :]
    for low, high in halves_of(total):
        up_ref[low:high, :] = nn_dot(cle_ref[low:high, :], pl_ref[...])
        mixed_ref[low:high, :narrow] = nn_dot(cre_ref[low:high, :], pr_ref[...])

    def merge_rows(rows):
        pre = up_ref[rows, :]
        merged = pre / (1.0 + jnp.exp(-pre))
        merged = jnp.concatenate([merged[:, :narrow] + mixed_ref[rows, :narrow], merged[:, narrow:]], 1)
        normed, _ = rows_normed(merged)
        mixed_ref[rows, :] = (normed * mgain_ref[...]).astype(jnp.bfloat16).astype(jnp.float32)

    loop_rows(total, MERGE_ROWS, merge_rows)

    def mid_conv(group, carry):
        lanes = group_lanes(group)
        weights = [tm_ref[j : j + 1, lanes] for j in range(tm_ref.shape[0])]
        for low, high in row_tiles(tokens, ROW_TILE):
            since = wide_ref[RIM + low : RIM + high, :]
            cm_ref[low:high, lanes] = taps_forward(mixed_ref, RIM, since, lanes, low, high, weights).astype(jnp.bfloat16)
        return carry

    lax.fori_loop(0, mixed_ref.shape[1] // 128, mid_conv, 0)
    for low, high in halves_of(tokens):
        h2_ref[low:high, :] = h1_ref[low:high, :] + nn_dot(cm_ref[low:high, :], pm_ref[...])

    def norm_rows(rows):
        normed, _ = rows_normed(h2_ref[rows, :])
        a3_ref[rows, :] = (normed * gain_ref[...]).astype(jnp.bfloat16)

    loop_rows(tokens, 64, norm_rows)


def conv_forward(h1, a2, rim, since, taps_l, taps_r, taps_m, mid_gain, gain, proj_left, proj_right, proj_mid):
    tokens, width = h1.shape
    wide = proj_left.shape[1]
    total = tokens + RIM
    low, full = jnp.bfloat16, jnp.float32
    return pl.pallas_call(
        conv_fwd_kernel,
        out_shape=(
            jax.ShapeDtypeStruct((tokens, width), low),
            jax.ShapeDtypeStruct((tokens, width), low),
            jax.ShapeDtypeStruct((tokens, wide), low),
            jax.ShapeDtypeStruct((tokens, width), full),
            jax.ShapeDtypeStruct((tokens, width), low),
        ),
        in_specs=[IN_VMEM] * 12,
        out_specs=(IN_VMEM,) * 5,
        scratch_shapes=[
            pltpu.VMEM((total + RIM, width), full),
            pltpu.VMEM((total, 128), jnp.int32),
            pltpu.VMEM((total, width), low),
            pltpu.VMEM((total, width), low),
            pltpu.VMEM((total, wide), full),
            pltpu.VMEM((total, wide), full),
        ],
        compiler_params=pltpu.CompilerParams(vmem_limit_bytes=KERNEL_VMEM),
        cost_estimate=pl.CostEstimate(
            flops=tokens * width * wide * 20, bytes_accessed=tokens * width * 16, transcendentals=tokens * wide
        ),
        name="conv_fwd",
    )(h1, a2, rim, since, taps_l, taps_r, taps_m, mid_gain, gain, proj_left, proj_right, proj_mid)


def folded(values):
    return jnp.sum(values.reshape(-1, 8, values.shape[-1]), axis=0)


def taps_back(grad_ref, value, left, lanes, low, high, weights, result, sums):
    for offset, weight in enumerate(weights):
        window = grad_ref[low + offset : high + offset, lanes]
        if offset:
            window = jnp.where(left >= offset, window, 0.0)
        term = window * weight
        result = term if result is None else result + term
        if value is not None:
            product = folded(window * value)
            sums[offset] = product if sums[offset] is None else sums[offset] + product
    return result


def conv_bwd_kernel(
    g2_ref, brim_ref, cl_ref, clrim_ref, cr_ref, crrim_ref, cm_ref, a2_ref, h1_ref, left_ref,
    tl_ref, tr_ref, tm_ref, mgain_ref, gain_ref, pl_ref, pr_ref, pm_ref, mine_ref, second_ref,
    g1_ref, dw_ref, dtl_ref, dtr_ref, dtm_ref, dmgain_ref, dgain_ref, out_ref, across_out_ref,
    bext_ref, cle_ref, cre_ref, wide_ref, grad_ref, up_ref, back_ref, normed_ref, inv_ref, dpl_ref, dpr_ref, a2f_ref,
    kept_ref, core_ref, across_ref, send_sem, recv_sem, local_sem, kept_sem,
):
    tokens, width = g2_ref.shape
    total = tokens + RIM
    wide, narrow = pl_ref.shape[1], pr_ref.shape[1]
    share = ShareSum(
        send_sem, recv_sem, core=core_ref, across=across_ref, mine=mine_ref, out=out_ref, local_sem=local_sem
    )
    first_count = mine_ref.shape[0]
    step = share.step
    firsts, seconds = range(first_count), range(first_count, first_count + core_ref.shape[0])
    share.core_first = first_count
    share.enter([share.mate, share.close] + share.peers[1:] + share.sides[1:])
    kept_copy = pltpu.make_async_copy(
        second_ref.at[:, share.core, :, : kept_ref.shape[-1]], kept_ref, kept_sem
    )
    kept_copy.start()
    for chunk in seconds:
        share.core_copy(chunk, second_ref, chunk - first_count).start()
    for chunk in firsts:
        share.start_back(chunk)
    bext_ref[:tokens, :] = g2_ref[...].astype(jnp.bfloat16)
    bext_ref[tokens:, :] = brim_ref[...]
    cle_ref[:tokens, :] = cl_ref[...]
    cle_ref[tokens:, :] = clrim_ref[...]
    cre_ref[:tokens, :] = cr_ref[...]
    cre_ref[tokens:, :] = crrim_ref[...]
    a2f_ref[...] = a2_ref[...].astype(jnp.float32)
    wide_ref[...] = wide_rows(left_ref[...])
    grad_ref[total:, :] = jnp.zeros((RIM, wide), jnp.float32)
    dw_ref[:, :wide] = tn_dot(bext_ref[:tokens, :], cm_ref[...]).astype(jnp.bfloat16)
    for low, high in halves_of(total):
        grad_ref[low:high, :] = nt_dot(bext_ref[low:high, :], pm_ref[...])
        up_ref[low:high, :] = nn_dot(cle_ref[low:high, :], pl_ref[...])
        back_ref[low:high, :narrow] = nn_dot(cre_ref[low:high, :], pr_ref[...])

    kept_copy.wait()
    for chunk in seconds:
        at = (chunk - first_count) * step
        share.core_copy(chunk, second_ref, chunk - first_count).wait_recv()
        share.run_side(chunk, kept_ref[:, :, at : at + step])

    def merge_rows(rows):
        pre = up_ref[rows, :]
        merged = pre / (1.0 + jnp.exp(-pre))
        merged = jnp.concatenate([merged[:, :narrow] + back_ref[rows, :narrow], merged[:, narrow:]], 1)
        normed, inverse = rows_normed(merged)
        normed_ref[rows, :] = normed
        inv_ref[rows, :] = wide_rows(inverse)

    loop_rows(total, MERGE_ROWS, merge_rows)

    def mid_back(group, carry):
        lanes = group_lanes(group)
        weights = [tm_ref[j : j + 1, lanes] for j in range(tm_ref.shape[0])]
        sums = [None] * len(weights)
        gain_vec = mgain_ref[:, lanes]
        for low, high in row_tiles(total, ROW_TILE):
            value = None
            if high <= tokens:
                value = (normed_ref[low:high, lanes] * gain_vec).astype(jnp.bfloat16).astype(jnp.float32)
            back_ref[low:high, lanes] = taps_back(
                grad_ref, value, wide_ref[low:high, :], lanes, low, high, weights, None, sums
            )
        for j, piece in enumerate(sums):
            dtm_ref[j : j + 1, lanes] = jnp.sum(piece, axis=0, keepdims=True)
        return carry

    lax.fori_loop(0, wide // 128, mid_back, 0)

    def merge_back(rows):
        pre = up_ref[rows, :]
        normed = normed_ref[rows, :]
        d_merged = rows_norm_back(normed, inv_ref[rows, :][:, :1], mgain_ref[...], back_ref[rows, :])
        sigma = 1.0 / (1.0 + jnp.exp(-pre))
        dpl_ref[rows, :] = (d_merged * (sigma * (1.0 + pre * (1.0 - sigma)))).astype(jnp.bfloat16)
        dpr_ref[rows, :] = d_merged[:, :narrow].astype(jnp.bfloat16)

    loop_rows(total, MERGE_ROWS, merge_back)
    for chunk in firsts:
        share.run_near_back(chunk)
    gain_sum = jnp.zeros((8, wide), jnp.float32)

    def gain_rows(k, held):
        rows = pl.ds(pl.multiple_of(k * 16, 16), 16)
        return held + folded(back_ref[rows, :] * normed_ref[rows, :])

    gain_sum = lax.fori_loop(0, tokens // 16, gain_rows, gain_sum)
    dmgain_ref[...] = jnp.sum(gain_sum, axis=0, keepdims=True)
    dw_ref[:, wide : 2 * wide] = tn_dot(cle_ref[:tokens, :], dpl_ref[:tokens, :]).astype(jnp.bfloat16)
    dw_ref[:, 2 * wide :] = tn_dot(cre_ref[:tokens, :], dpr_ref[:tokens, :]).astype(jnp.bfloat16)
    for low, high in halves_of(total):
        grad_ref[low:high, :width] = nt_dot(dpl_ref[low:high, :], pl_ref[...])
        grad_ref[low:high, width : 2 * width] = nt_dot(dpr_ref[low:high, :], pr_ref[...])

    def first_back(group, carry):
        lanes = group_lanes(group)
        other = group_lanes(group + width // 128)
        weights_l = [tl_ref[j : j + 1, lanes] for j in range(tl_ref.shape[0])]
        weights_r = [tr_ref[j : j + 1, lanes] for j in range(tr_ref.shape[0])]
        sums_l = [None] * len(weights_l)
        sums_r = [None] * len(weights_r)
        for low, high in row_tiles(tokens, ROW_TILE):
            left = wide_ref[low:high, :]
            value = a2f_ref[low:high, lanes]
            held = taps_back(grad_ref, value, left, lanes, low, high, weights_l, None, sums_l)
            held = taps_back(grad_ref, value, left, other, low, high, weights_r, held, sums_r)
            back_ref[low:high, lanes] = held
        for j, piece in enumerate(sums_l):
            dtl_ref[j : j + 1, lanes] = jnp.sum(piece, axis=0, keepdims=True)
        for j, piece in enumerate(sums_r):
            dtr_ref[j : j + 1, lanes] = jnp.sum(piece, axis=0, keepdims=True)
        return carry

    lax.fori_loop(0, width // 128, first_back, 0)

    def finish(k, held):
        rows = pl.ds(pl.multiple_of(k * 64, 64), 64)
        normed, inverse = rows_normed(h1_ref[rows, :])
        upstream = back_ref[rows, :width]
        g1_ref[rows, :] = g2_ref[rows, :] + rows_norm_back(normed, inverse, gain_ref[...], upstream)
        return held + folded(upstream * normed)

    gain_sum = lax.fori_loop(0, tokens // 64, finish, jnp.zeros((8, width), jnp.float32))
    dgain_ref[...] = jnp.sum(gain_sum, axis=0, keepdims=True)
    for chunk in firsts:
        share.run_last(chunk)
    for chunk in seconds:
        at = (chunk - first_count) * step
        across_out_ref[:, at : at + step] = share.side_sum(chunk, first_count)
        share.core_copy(chunk, second_ref, chunk - first_count).wait_send()
        share.sent_sides(chunk)
    for chunk in firsts:
        share.last_copy(chunk).wait_recv()
        share.sent_backs(chunk)


def conv_back(
    g2, brim, c_l, c_r, rims, c_m, a2, h1, left, taps_l, taps_r, taps_m, mid_gain, gain, proj_left, proj_right, proj_mid,
    mine, second,
):
    tokens, width = g2.shape
    wide, narrow = proj_left.shape[1], proj_right.shape[1]
    total = tokens + RIM
    low, full = jnp.bfloat16, jnp.float32
    seq_count, far_count = lax.axis_size("seq"), lax.axis_size("rows") // 4
    half = width // (2 * seq_count)
    step = 2 * far_count * LANE_GROUP
    first_count, second_count = mine.shape[0], second.shape[1] // step - 1
    count = first_count + second_count
    slots = seq_count + 1 + 2 * far_count
    in_hbm = pl.BlockSpec(memory_space=pl.ANY)
    dma = pltpu.SemaphoreType.DMA
    return pl.pallas_call(
        conv_bwd_kernel,
        out_shape=(
            jax.ShapeDtypeStruct((tokens, width), full),
            jax.ShapeDtypeStruct((width, 2 * wide + narrow), low),
            jax.ShapeDtypeStruct(taps_l.shape, full),
            jax.ShapeDtypeStruct(taps_r.shape, full),
            jax.ShapeDtypeStruct(taps_m.shape, full),
            jax.ShapeDtypeStruct((1, wide), full),
            jax.ShapeDtypeStruct((1, width), full),
            jax.ShapeDtypeStruct((2, half, first_count * step), low),
            jax.ShapeDtypeStruct((half, second_count * step), low),
        ),
        in_specs=[IN_VMEM] * 19 + [in_hbm],
        out_specs=(IN_VMEM,) * 7 + (in_hbm, IN_VMEM),
        scratch_shapes=[
            pltpu.VMEM((total, width), low),
            pltpu.VMEM((total, width), low),
            pltpu.VMEM((total, width), low),
            pltpu.VMEM((total, 128), jnp.int32),
            pltpu.VMEM((total + RIM, wide), full),
            pltpu.VMEM((total, wide), full),
            pltpu.VMEM((total, wide), full),
            pltpu.VMEM((total, wide), full),
            pltpu.VMEM((total, 128), full),
            pltpu.VMEM((total, wide), low),
            pltpu.VMEM((total, narrow), low),
            pltpu.VMEM((tokens, width), full),
            pltpu.VMEM((seq_count, half, second_count * step), low),
            pltpu.VMEM((second_count, seq_count, half, step), low),
            pltpu.VMEM((second_count, seq_count - 1, half, step), low),
            dma((count, slots)),
            dma((count, slots)),
            dma((first_count,)),
            dma(()),
        ],
        compiler_params=pltpu.CompilerParams(
            collective_id=1, has_side_effects=True, vmem_limit_bytes=HOST_VMEM
        ),
        cost_estimate=pl.CostEstimate(
            flops=tokens * width * wide * 40, bytes_accessed=tokens * width * 40, transcendentals=tokens * wide
        ),
        name="conv_bwd",
    )(
        g2, brim, c_l, rims[:, :width], c_r, rims[:, width:], c_m, a2, h1, left,
        taps_l, taps_r, taps_m, mid_gain, gain, proj_left, proj_right, proj_mid,
        mine, second.reshape(seq_count, 2, half, second.shape[1]),
    )


MIDDLE_VMEM = 60 * 2**20
DOT_ROWS = 256


def load_weight(copies, sems, target_ref, own_ref, pieces, each, offset, place, near, core):
    width, size = own_ref.shape
    half, quarter = width // 2, width // 4
    count = len(pieces) // each + 1
    columns = slice(offset, offset + size)
    parts = [(own_ref, place * width, width)]
    for d in range(1, count):
        source = lax.rem(place + d, count) * width
        same, *more = pieces[each * (d - 1) : each * d]
        if each == 2:
            parts.append((same.at[:, columns], source + core * half, half))
            parts.append((more[0].at[:, columns], source + (1 - core) * half, half))
            continue
        close, across = more
        parts.append((same.at[:, columns], source + (2 * near + core) * quarter, quarter))
        parts.append((close.at[:, columns], source + (2 - 2 * near + core) * quarter, quarter))
        parts.append((across.at[:quarter, columns], source + (2 * near + 1 - core) * quarter, quarter))
        parts.append((across.at[quarter:, columns], source + (3 - 2 * near - core) * quarter, quarter))
    for source_ref, start, rows in parts:
        copy = pltpu.make_async_copy(
            source_ref, target_ref.at[pl.ds(pl.multiple_of(start, quarter), rows), :], sems.at[len(copies)]
        )
        copy.start()
        copies.append(copy)
    return offset + size


def wait_for(copies):
    for copy in copies:
        copy.wait()


def norm_into(target_ref, source_ref, gain_vec):
    def body(rows):
        normed, _ = rows_normed(source_ref[rows, :])
        target_ref[rows, :] = (normed * gain_vec).astype(jnp.bfloat16)

    loop_rows(source_ref.shape[0], 64, body)


def norm_back_into(target_ref, base_ref, source_ref, gain_vec, upstream_ref):
    def body(k, held):
        rows = pl.ds(pl.multiple_of(k * 64, 64), 64)
        normed, inverse = rows_normed(source_ref[rows, :])
        upstream = upstream_ref[rows, :]
        target_ref[rows, :] = base_ref[rows, :].astype(jnp.float32) + rows_norm_back(
            normed, inverse, gain_vec, upstream
        )
        return held + folded(upstream * normed)

    held = jnp.zeros((8, source_ref.shape[1]), jnp.float32)
    return jnp.sum(lax.fori_loop(0, source_ref.shape[0] // 64, body, held), axis=0, keepdims=True)


def chunks(extent):
    return row_tiles(extent, DOT_ROWS)


def project_into(target_ref, weight_ref, turned_ref, low, high):
    for start, stop in chunks(high - low):
        target_ref[start:stop, :] = tn_dot(weight_ref[:, low + start : low + stop], turned_ref[...]).astype(jnp.bfloat16)


def store_grad(target_ref, start, values):
    target_ref[:, start : start + values.shape[1]] = values.astype(jnp.bfloat16)


def middle_kernel(
    piece_count,
    h2_ref, a3_ref, crow_ref, mem_ref, gout_ref, gain_ref, qseg_ref, kseg_ref, mseg_ref, down_ref,
    qkv_own, out2_own, query_own, kv_own, out_own, up_own, *rest,
):
    pieces, rest = rest[:piece_count], rest[piece_count:]
    up_pieces, rest = rest[: piece_count // 3 * 2], rest[piece_count // 3 * 2 :]
    (
        result_ref, g2_ref, brim_ref, crim_ref, dw_ref, dgain_ref, dmem_ref, mine_ref,
        wqkv_ref, wout2_ref, wquery_ref, wkv_ref, wout_ref, wup_ref, sems,
        turned_ref, memt_ref, a4_ref, a4t_ref, qt_ref, pair_ref, attc_ref, totalc_ref,
        qdt_ref, paird_ref, attd_ref, totald_ref, h3_ref, h4_ref, act_ref, dup_ref, low_ref, gt_ref, dq_ref, dpair_ref, dpaird_ref,
        back_ref, kmark_ref, mmark_ref, sum_ref, peak_ref, score_ref,
        dkh_ref, dvh_ref, dkm_ref, dvm_ref, dqh_ref, qrow_ref, grow_ref, weight_ref, slope_ref,
        first_ref, core_ref, across_ref, send_sem, recv_sem,
        close_ref, piece_ref, g3_ref, a3in_ref, da3_ref, da3in_ref, rim_ref, rimin_ref, crimin_ref, swap_send, swap_recv,
    ) = rest
    tokens, width = h2_ref.shape
    share = ShareSum(
        send_sem, recv_sem, core=core_ref, across=across_ref, close=close_ref, piece=piece_ref, mine=mine_ref
    )
    place, near, core = share.place, share.near, share.core
    share.enter([share.mate, share.close] + share.peers[1:] + share.sides[1:])
    seq_count = piece_count // 3 + 1

    def swap(kind, away, source, target):
        return pltpu.make_async_remote_copy(
            src_ref=source,
            dst_ref=target,
            send_sem=swap_send.at[kind, away - 1],
            recv_sem=swap_recv.at[kind, away - 1],
            device_id=share.sides[away],
            device_id_type=pl.DeviceIdType.MESH,
        )

    def ahead_swap(away):
        return swap(0, away, a3_ref, a3in_ref.at[away - 1])

    def behind_swap(away):
        return swap(1, away, da3_ref.at[away - 1], da3in_ref.at[away - 1])

    def rim_swap():
        return swap(2, seq_count - 1, rim_ref, rimin_ref)

    def conv_swap():
        return swap(3, seq_count - 1, crow_ref, crimin_ref)

    for away in range(1, seq_count):
        pl.when(place + away < seq_count)(ahead_swap(away).start)
    pl.when(place > 0)(conv_swap().start)
    crim_ref[...] = jnp.zeros_like(crim_ref)
    high_width = wup_ref.shape[1]
    first, copies = [], []
    offset = load_weight(first, sems.at[0], wqkv_ref, qkv_own, pieces, 3, 0, place, near, core)
    for target, own in ((wout2_ref, out2_own), (wquery_ref, query_own), (wkv_ref, kv_own), (wout_ref, out_own)):
        offset = load_weight(copies, sems.at[1], target, own, pieces, 3, offset, place, near, core)
    load_weight(copies, sems.at[1], wup_ref, up_own, up_pieces, 2, 0, place, near, core)

    own = pl.ds(pl.multiple_of(place * tokens, 128), tokens)
    turned_ref[:, own] = a3_ref[...].T
    memt_ref[...] = mem_ref[...].T
    wait_for(first)
    project_into(qt_ref, wqkv_ref, turned_ref.at[:, own], 0, width)
    project_into(pair_ref.at[:, own], wqkv_ref, turned_ref.at[:, own], width, 3 * width)

    def fetch():
        for away in range(1, seq_count):
            start = lax.rem(place + seq_count - away, seq_count) * tokens
            there = pl.ds(pl.multiple_of(start, 128), tokens)

            @pl.when(place >= away)
            def _():
                ahead_swap(away).wait_recv()
                turned_ref[:, there] = a3in_ref[away - 1].T
                project_into(pair_ref.at[:, there], wqkv_ref, turned_ref.at[:, there], width, 3 * width)

            @pl.when(place < away)
            def _():
                turned_ref[:, there] = jnp.zeros((width, tokens), jnp.bfloat16)

    attend_core(
        H_CROSS, True, place, qt_ref, pair_ref, qseg_ref, kseg_ref, attc_ref, totalc_ref, kmark_ref, sum_ref, peak_ref, score_ref,
        fetch,
    )
    wait_for(copies)
    for low, high in chunks(tokens):
        h3_ref[low:high, :] = h2_ref[low:high, :] + tn_dot(attc_ref[:, low:high], wout2_ref[...])
    norm_into(a4_ref, h3_ref, gain_ref[1:2, :])
    a4t_ref[...] = a4_ref[...].T
    project_into(qdt_ref, wquery_ref, a4t_ref, 0, width)
    project_into(paird_ref, wkv_ref, memt_ref, 0, 2 * width)
    attend_core(
        H_CROSS, False, 0, qdt_ref, paird_ref, qseg_ref, mseg_ref, attd_ref, totald_ref, mmark_ref, sum_ref, peak_ref, score_ref
    )
    for low, high in chunks(tokens):
        h4_ref[low:high, :] = h3_ref[low:high, :] + tn_dot(attd_ref[:, low:high], wout_ref[...])
    norm_into(a4_ref, h4_ref, gain_ref[2:3, :])

    for left, right in row_tiles(high_width, 512):
        for low, high in chunks(tokens):
            pre = nn_dot(a4_ref[low:high, :], wup_ref[:, left:right])
            sigma = 1.0 / (1.0 + jnp.exp(-pre))
            act_ref[low:high, left:right] = (pre * sigma).astype(jnp.bfloat16)
            slope = nt_dot(gout_ref[low:high, :], down_ref[left:right, :])
            dup_ref[low:high, left:right] = (slope * (sigma * (1.0 + pre * (1.0 - sigma)))).astype(jnp.bfloat16)
    for low, high in chunks(tokens):
        result_ref[low:high, :] = (h4_ref[low:high, :] + nn_dot(act_ref[low:high, :], down_ref[...])).astype(jnp.bfloat16)
        back_ref[low:high, :] = nt_dot(dup_ref[low:high, :], wup_ref[...])
    _, _, half, first_total = first_ref.shape
    firsts = range(first_total // share.step)

    def store_first(start, values):
        size = values.shape[1]
        first_ref[:, :, :, start : start + size] = values.astype(jnp.bfloat16).reshape(seq_count, 2, half, size)

    for left, right in row_tiles(high_width, 512):
        store_first(left, tn_dot(a4_ref[...], dup_ref[:, left:right]))
        store_first(high_width + left, tn_dot(gout_ref[...], act_ref[:, left:right]))

    for chunk in firsts:
        share.core_copy(chunk, first_ref, chunk).start()
    at = 0
    dgain_ref[2:3, :] = norm_back_into(h4_ref, gout_ref, h4_ref, gain_ref[2:3, :], back_ref)
    low_ref[...] = h4_ref[...].astype(jnp.bfloat16)
    store_grad(dw_ref, at, nn_dot(attd_ref[...], low_ref[...]))
    gt_ref[...] = nt_dot(wout_ref[...], low_ref[...]).astype(jnp.bfloat16)
    attend_back_core(
        H_CROSS, False, 0, qdt_ref, paird_ref, gt_ref, attd_ref, totald_ref, qseg_ref, mseg_ref,
        dq_ref, dpaird_ref, mmark_ref, dkm_ref, dvm_ref, dqh_ref, qrow_ref, grow_ref, weight_ref, slope_ref,
    )
    store_grad(dw_ref, at + width, nt_dot(a4t_ref[...], dq_ref[...]))
    store_grad(dw_ref, at + 2 * width, nt_dot(memt_ref[...], dpaird_ref[...]))
    for chunk in firsts:
        share.core_copy(chunk, first_ref, chunk).wait_recv()
        share.run_side(chunk, first_ref[:, core, :, chunk * share.step : (chunk + 1) * share.step])
    dmem_ref[...] = nn_dot(wkv_ref[...], dpaird_ref[...]).astype(jnp.bfloat16)
    back_ref[...] = nn_dot(wquery_ref[...], dq_ref[...]).T
    dgain_ref[1:2, :] = norm_back_into(g3_ref, h4_ref, h3_ref, gain_ref[1:2, :], back_ref)
    low_ref[...] = g3_ref[...].astype(jnp.bfloat16)
    at = at + 4 * width
    store_grad(dw_ref, at + 3 * width, nn_dot(attc_ref[...], low_ref[...]))
    gt_ref[...] = nt_dot(wout2_ref[...], low_ref[...]).astype(jnp.bfloat16)
    attend_back_core(
        H_CROSS, True, place, qt_ref, pair_ref, gt_ref, attc_ref, totalc_ref, qseg_ref, kseg_ref,
        dq_ref, dpair_ref, kmark_ref, dkh_ref, dvh_ref, dqh_ref, qrow_ref, grow_ref, weight_ref, slope_ref,
    )
    store_grad(dw_ref, at, nt_dot(turned_ref[:, own], dq_ref[...]))
    for low, high in chunks(2 * width):
        store_grad(dw_ref, at + width + low, nt_dot(turned_ref[...], dpair_ref[low:high, :]))
    for chunk in firsts:
        share.run_near(chunk)
    for away in [*range(1, seq_count), 0]:
        start = lax.rem(place + away, seq_count) * tokens
        for low, high in row_tiles(tokens, DOT_ROWS):
            lanes = pl.ds(pl.multiple_of(start + low, 128), high - low)
            upstream = nn_dot(wqkv_ref[:, width:], dpair_ref[:, lanes])
            if away == 0:
                back_ref[low:high, :] = (upstream + nn_dot(wqkv_ref[:, :width], dq_ref[:, low:high])).T
            else:
                da3_ref[away - 1, low:high, :] = upstream.T.astype(jnp.bfloat16)
        if away:
            pl.when(place + away >= seq_count)(behind_swap(away).start)
    for chunk in firsts:
        share.run_peer(chunk)
    for away in range(1, seq_count):

        @pl.when(place < away)
        def _():
            behind_swap(away).wait_recv()
            back_ref[...] += da3in_ref[away - 1].astype(jnp.float32)

    dgain_ref[0:1, :] = norm_back_into(g2_ref, g3_ref, h2_ref, gain_ref[0:1, :], back_ref)
    rim_ref[...] = g2_ref[:RIM, :].astype(jnp.bfloat16)
    pl.when(place > 0)(rim_swap().start)
    brim_ref[...] = jnp.zeros_like(brim_ref)
    for chunk in firsts:
        share.peer_sum(chunk)

    @pl.when(place < seq_count - 1)
    def _():
        rim_swap().wait_recv()
        brim_ref[...] = rimin_ref[...]
        conv_swap().wait_recv()
        crim_ref[...] = crimin_ref[...]

    pl.when(place > 0)(rim_swap().wait_send)
    pl.when(place > 0)(conv_swap().wait_send)
    for away in range(1, seq_count):
        pl.when(place + away < seq_count)(ahead_swap(away).wait_send)
        pl.when(place + away >= seq_count)(behind_swap(away).wait_send)
    for chunk in firsts:
        share.core_copy(chunk, first_ref, chunk).wait_send()
        share.sent_sides(chunk)
        share.near_copy(chunk).wait_send()
        share.sent_peers(chunk)


def middle(h2, a3, conv_rows, mem_rows, grad_out, gains, own_seg, seg_row, mem_seg, down, owns, pieces, up_pieces):
    tokens, width = h2.shape
    keys, mems = seg_row.shape[0], mem_seg.shape[0]
    high_width = down.shape[0]
    seq_count = keys // tokens
    size = width // H_CROSS
    low, full = jnp.bfloat16, jnp.float32
    longest = max(tokens, mems)
    v = pltpu.VMEM
    in_hbm = pl.BlockSpec(memory_space=pl.ANY)
    half = width // (2 * seq_count)
    step = lax.axis_size("rows") // 2 * LANE_GROUP
    count = 2 * high_width // step
    far_count = lax.axis_size("rows") // 4
    slots = seq_count + far_count
    dma = pltpu.SemaphoreType.DMA
    return pl.pallas_call(
        functools.partial(middle_kernel, len(pieces)),
        out_shape=(
            jax.ShapeDtypeStruct((tokens, width), low),
            jax.ShapeDtypeStruct((tokens, width), full),
            jax.ShapeDtypeStruct((RIM, width), low),
            jax.ShapeDtypeStruct((RIM, 2 * width), low),
            jax.ShapeDtypeStruct((width, 8 * width), low),
            jax.ShapeDtypeStruct((3, width), full),
            jax.ShapeDtypeStruct((width, mems), low),
            jax.ShapeDtypeStruct((count, half, LANE_GROUP), low),
        ),
        in_specs=[IN_VMEM] * 10 + [in_hbm] * (6 + len(pieces) + len(up_pieces)),
        out_specs=(IN_VMEM,) * 8,
        scratch_shapes=[
            v((width, 3 * width), low),
            v((width, width), low),
            v((width, width), low),
            v((width, 2 * width), low),
            v((width, width), low),
            v((width, high_width), low),
            pltpu.SemaphoreType.DMA((2, 5 * (4 * seq_count - 3))),
            v((width, keys), low),
            v((width, mems), low),
            v((tokens, width), low),
            v((width, tokens), low),
            v((width, tokens), low),
            v((2 * width, keys), low),
            v((width, tokens), low),
            v((H_CROSS, 1, tokens), full),
            v((width, tokens), low),
            v((2 * width, mems), low),
            v((width, tokens), low),
            v((H_CROSS, 1, tokens), full),
            v((tokens, width), full),
            v((tokens, width), full),
            v((tokens, high_width), low),
            v((tokens, high_width), low),
            v((tokens, width), low),
            v((width, tokens), low),
            v((width, tokens), low),
            v((2 * width, keys), low),
            v((2 * width, mems), low),
            v((tokens, width), full),
            v((SEG_ROWS, keys), low),
            v((SEG_ROWS, mems), low),
            v((H_CROSS, size + SEG_ROWS, tokens), full),
            v((H_CROSS, 1, tokens), full),
            v((2, longest, TILE), full),
            v((BWD_HEADS, size, keys), full),
            v((BWD_HEADS, size, keys), full),
            v((BWD_HEADS, size, mems), full),
            v((BWD_HEADS, size, mems), full),
            v((BWD_HEADS, size, tokens), full),
            v((BWD_HEADS, size + SEG_ROWS, tokens), low),
            v((BWD_HEADS, size + SEG_ROWS, tokens), low),
            v((2, longest, TILE), low),
            v((2, longest, TILE), low),
            v((seq_count, 2, half, 2 * high_width), low),
            v((count, seq_count, half, step), low),
            v((count, seq_count - 1, half, step), low),
            dma((count, slots)),
            dma((count, slots)),
            v((count, half, step // 2), low),
            v((count, far_count - 1, half, LANE_GROUP), low),
            v((tokens, width), full),
            v((seq_count - 1, tokens, width), low),
            v((seq_count - 1, tokens, width), low),
            v((seq_count - 1, tokens, width), low),
            v((RIM, width), low),
            v((RIM, width), low),
            v((RIM, 2 * width), low),
            dma((4, seq_count - 1)),
            dma((4, seq_count - 1)),
        ],
        compiler_params=pltpu.CompilerParams(
            collective_id=0, has_side_effects=True, vmem_limit_bytes=HOST_VMEM
        ),
        cost_estimate=pl.CostEstimate(
            flops=tokens * width * width * 200, bytes_accessed=tokens * width * 40, transcendentals=tokens * width * 20
        ),
        name="middle",
    )(
        h2, a3, conv_rows, mem_rows, grad_out, gains, own_seg[None], seg_row[None], mem_seg[None], down,
        *owns, *pieces, *up_pieces,
    )


class ShareSum:
    def __init__(self, send_sem, recv_sem, core=None, across=None, close=None, piece=None, mine=None, out=None, local_sem=None):
        self.send_sem, self.recv_sem, self.local_sem = send_sem, recv_sem, local_sem
        self.core_ref, self.across_ref, self.close_ref = core, across, close
        self.piece_ref, self.mine_ref, self.out_ref = piece, mine, out
        self.seq_count = lax.axis_size("seq")
        self.far_count = lax.axis_size("rows") // 4
        row, place = lax.axis_index("rows"), lax.axis_index("seq")
        self.core, self.near, self.far, self.place = lax.rem(row, 2), lax.rem(row // 2, 2), row // 4, place
        self.mate = (row + 1 - 2 * self.core, place)
        self.close = (row + 2 - 4 * self.near, place)
        self.peers = [None] + [
            (lax.rem(self.far + d, self.far_count) * 4 + self.near * 2 + self.core, place)
            for d in range(1, self.far_count)
        ]
        self.sides = [None] + [(row, lax.rem(place + d, self.seq_count)) for d in range(1, self.seq_count)]
        self.step = 2 * self.far_count * LANE_GROUP
        self.wide = self.far_count * LANE_GROUP
        self.core_first = 0
        self.early_sums = {}

    def enter(self, friends):
        barrier = pltpu.get_barrier_semaphore()
        for friend in friends:
            pl.semaphore_signal(barrier, inc=1, device_id=friend, device_id_type=pl.DeviceIdType.MESH)
        pl.semaphore_wait(barrier, len(friends))

    def columns(self, chunk):
        return pl.ds(pl.multiple_of(chunk * self.step, LANE_GROUP), self.step)

    def copy(self, chunk, slot, source, target, device):
        return pltpu.make_async_remote_copy(
            src_ref=source,
            dst_ref=target,
            send_sem=self.send_sem.at[chunk, slot],
            recv_sem=self.recv_sem.at[chunk, slot],
            device_id=device,
            device_id_type=pl.DeviceIdType.MESH,
        )

    def core_copy(self, chunk, source_ref, at):
        return self.copy(chunk, 0, source_ref.at[:, 1 - self.core, :, self.columns(at)], self.core_ref.at[chunk - self.core_first], self.mate)

    def side_copy(self, chunk, d):
        away = lax.rem(self.place + d, self.seq_count)
        return self.copy(chunk, d, self.core_ref.at[chunk - self.core_first, away], self.across_ref.at[chunk - self.core_first, d - 1], self.sides[d])

    def sum_at(self, chunk):
        if chunk in self.early_sums:
            return self.early_sums[chunk]
        return self.across_ref.at[chunk - self.core_first, 0]

    def near_copy(self, chunk):
        lanes = pl.ds(pl.multiple_of((1 - self.near) * self.wide, LANE_GROUP), self.wide)
        return self.copy(
            chunk, self.seq_count, self.sum_at(chunk).at[:, lanes], self.close_ref.at[chunk], self.close
        )

    def peer_copy(self, chunk, d):
        away = lax.rem(self.far + d, self.far_count)
        lanes = pl.ds(pl.multiple_of(away * LANE_GROUP, LANE_GROUP), LANE_GROUP)
        return self.copy(
            chunk, self.seq_count + d, self.close_ref.at[chunk, :, lanes], self.piece_ref.at[chunk, d - 1], self.peers[d]
        )

    def own_lanes(self, chunk):
        start = chunk * self.step + self.near * self.wide + self.far * LANE_GROUP
        return pl.ds(pl.multiple_of(start, LANE_GROUP), LANE_GROUP)

    def keep_copy(self, chunk):
        return pltpu.make_async_copy(
            self.mine_ref.at[chunk], self.out_ref.at[self.core, :, self.own_lanes(chunk)], self.local_sem.at[chunk]
        )

    def back_copy(self, chunk, d):
        return self.copy(
            chunk,
            self.seq_count + self.far_count - 1 + d,
            self.mine_ref.at[chunk],
            self.out_ref.at[self.core, :, self.own_lanes(chunk)],
            self.peers[d],
        )

    def near_back(self, chunk):
        start = pl.multiple_of(chunk * self.step + self.near * self.wide, LANE_GROUP)
        block = self.out_ref.at[self.core, :, pl.ds(start, self.wide)]
        return self.copy(chunk, self.seq_count + 2 * self.far_count - 1, block, block, self.close)

    def last_copy(self, chunk):
        block = self.out_ref.at[self.core, :, self.columns(chunk)]
        return self.copy(chunk, self.seq_count + 2 * self.far_count, block, block, self.mate)

    def run_side(self, chunk, kept):
        at = chunk - self.core_first
        self.core_ref[at] = (kept.astype(jnp.float32) + self.core_ref[at].astype(jnp.float32)).astype(jnp.bfloat16)
        for d in range(1, self.seq_count):
            self.side_copy(chunk, d).start()

    def side_sum(self, chunk, first=0):
        for d in range(1, self.seq_count):
            self.side_copy(chunk, d).wait_recv()
        summed = self.core_ref[chunk - first, self.place].astype(jnp.float32)
        for d in range(1, self.seq_count):
            summed = summed + self.across_ref[chunk - first, d - 1].astype(jnp.float32)
        return summed.astype(jnp.bfloat16)

    def run_near(self, chunk):
        self.sum_at(chunk)[...] = self.side_sum(chunk, self.core_first)
        self.near_copy(chunk).start()

    def run_peer(self, chunk):
        self.near_copy(chunk).wait_recv()
        lanes = pl.ds(pl.multiple_of(self.near * self.wide, LANE_GROUP), self.wide)
        summed = self.sum_at(chunk)[:, lanes].astype(jnp.float32) + self.close_ref[chunk].astype(jnp.float32)
        self.close_ref[chunk] = summed.astype(jnp.bfloat16)
        for d in range(1, self.far_count):
            self.peer_copy(chunk, d).start()

    def peer_sum(self, chunk):
        for d in range(1, self.far_count):
            self.peer_copy(chunk, d).wait_recv()
        lanes = pl.ds(pl.multiple_of(self.far * LANE_GROUP, LANE_GROUP), LANE_GROUP)
        summed = self.close_ref[chunk, :, lanes].astype(jnp.float32)
        for d in range(1, self.far_count):
            summed = summed + self.piece_ref[chunk, d - 1].astype(jnp.float32)
        self.mine_ref[chunk] = summed.astype(jnp.bfloat16)

    def run_back(self, chunk):
        self.peer_sum(chunk)
        self.start_back(chunk)

    def start_back(self, chunk):
        self.keep_copy(chunk).start()
        for d in range(1, self.far_count):
            self.back_copy(chunk, d).start()

    def run_near_back(self, chunk):
        self.keep_copy(chunk).wait()
        for d in range(1, self.far_count):
            self.back_copy(chunk, d).wait_recv()
        self.near_back(chunk).start()

    def run_last(self, chunk):
        self.near_back(chunk).wait_recv()
        self.last_copy(chunk).start()

    def sent_sides(self, chunk):
        for d in range(1, self.seq_count):
            self.side_copy(chunk, d).wait_send()

    def sent_peers(self, chunk):
        for d in range(1, self.far_count):
            self.peer_copy(chunk, d).wait_send()

    def sent_backs(self, chunk):
        for d in range(1, self.far_count):
            self.back_copy(chunk, d).wait_send()
        self.near_back(chunk).wait_send()
        self.last_copy(chunk).wait_send()


def closing_kernel(
    g1_ref, rows_ref, memt_ref, gain_ref, atta_ref, totala_ref, qa_ref, paira_ref,
    attb_ref, totalb_ref, qb_ref, pairb_ref, dmem_ref, gtwo_ref, glate_ref, dtl_ref, dtr_ref, dmg_ref, dtm_ref, qseg_ref, kseg_ref, mseg_ref,
    wqkv_ref, wquery_ref, wkv_ref, wout_ref, across_in_ref, second_ref, conv_ref,
    grad_in_ref, grad_mem_ref, out_ref,
    turned_ref, branch_ref, gt_ref, dqa_ref, dqb_ref, dpaira_ref, dpairb_ref, kmark_ref, mmark_ref,
    dkh_ref, dvh_ref, dkm_ref, dvm_ref, dqh_ref, qrow_ref, grow_ref, weight_ref, slope_ref,
    late_ref, core_ref, across_ref, close_ref, piece_ref, mine_ref,
    send_sem, recv_sem, local_sem, conv_sem,
    da1_ref, da1_in_ref, upstream_ref, dmemory_ref, dmemory_in_ref, swap_send, swap_recv, small_ref,
):
    tokens, width = g1_ref.shape
    keys = rows_ref.shape[0]
    place = lax.axis_index("seq")
    seq_count, _, half, conv_size = conv_ref.shape
    share = ShareSum(
        send_sem, recv_sem, core=core_ref, across=across_ref, close=close_ref, piece=piece_ref, mine=mine_ref,
        out=out_ref, local_sem=local_sem,
    )
    step = share.step
    second_count = early_count = across_in_ref.shape[1] // step
    count = out_ref.shape[-1] // step
    extra = second_ref.shape[-1] - second_count * step
    conv_end = extra + conv_size
    middle_count = (conv_end + 5 * width + step - 1) // step
    last_count = count - early_count - middle_count
    share.core_first = early_count
    share.enter([share.mate, share.close] + share.peers[1:] + share.sides[1:])
    late_copies = (
        pltpu.make_async_copy(second_ref.at[:, :, :, second_count * step :], late_ref.at[:, :, :, :extra], conv_sem.at[0]),
        pltpu.make_async_copy(conv_ref, late_ref.at[:, :, :, extra:conv_end], conv_sem.at[1]),
    )
    for copy in late_copies:
        copy.start()
    seconds = range(early_count)
    middles = range(early_count, early_count + middle_count)
    lasts = range(early_count + middle_count, count)
    for chunk in seconds:
        at = chunk * step
        share.early_sums[chunk] = across_in_ref.at[:, at : at + step]
        share.near_copy(chunk).start()

    def store_late(start, values):
        size = values.shape[1]
        late_ref[:, :, :, start : start + size] = values.astype(jnp.bfloat16).reshape(seq_count, 2, half, size)

    def start_late(chunk):
        share.core_copy(chunk, late_ref, chunk - early_count).start()

    def side_late(chunk):
        at = (chunk - early_count) * step
        share.core_copy(chunk, late_ref, chunk - early_count).wait_recv()
        share.run_side(chunk, late_ref[:, share.core, :, at : at + step])

    done = {}

    def advance(chunk):
        stages = (share.run_near, share.run_peer, share.run_back, share.run_near_back, share.run_last)
        stages[done.setdefault(chunk, 1 if chunk in seconds else 0)](chunk)
        done[chunk] += 1

    def advance_all(*groups):
        for group in groups:
            for chunk in group:
                advance(chunk)

    own = pl.ds(pl.multiple_of(place * tokens, 128), tokens)
    ready = conv_end // step
    with_out = (conv_end + 2 * width) // step
    branch_ref[...] = g1_ref[...].astype(jnp.bfloat16).T
    for copy in late_copies:
        copy.wait()
    for chunk in middles[:ready]:
        start_late(chunk)
    store_late(conv_end, nt_dot(branch_ref[...], atta_ref[...]))
    store_late(conv_end + width, nt_dot(branch_ref[...], attb_ref[...]))
    for chunk in middles[ready:with_out]:
        start_late(chunk)
    for chunk in middles[:ready]:
        side_late(chunk)
    gt_ref[...] = nn_dot(wout_ref[width:, :], branch_ref[...]).astype(jnp.bfloat16)
    for low, high in row_tiles(keys, 128):
        normed, _ = rows_normed(rows_ref[low:high, :].astype(jnp.float32))
        turned_ref[:, low:high] = (normed * gain_ref[...]).astype(jnp.bfloat16).T
    for chunk in middles[ready:with_out]:
        side_late(chunk)
    advance_all(seconds[:1])
    attend_back_core(
        H_CROSS, False, 0, qb_ref, pairb_ref, gt_ref, attb_ref, totalb_ref, qseg_ref, mseg_ref,
        dqb_ref, dpairb_ref, mmark_ref, dkm_ref, dvm_ref, dqh_ref, qrow_ref, grow_ref, weight_ref, slope_ref,
    )
    advance_all(seconds[1:])
    at = conv_end + 2 * width
    store_late(at, nt_dot(memt_ref[...], dpairb_ref[...]))
    store_late(at + 2 * width, nt_dot(turned_ref[:, own], dqb_ref[...]))
    at = at + 3 * width
    after = middle_count * step
    if at < after:
        late_ref[:, :, :, at:after] = jnp.zeros((seq_count, 2, half, after - at), jnp.bfloat16)
    for chunk in middles[with_out:]:
        start_late(chunk)
    dmemory_ref[...] = (dmem_ref[...].astype(jnp.float32) + nn_dot(wkv_ref[...], dpairb_ref[...])).T.astype(jnp.bfloat16)
    gt_ref[...] = nn_dot(wout_ref[:width, :], branch_ref[...]).astype(jnp.bfloat16)

    def first_pump():
        advance_all(middles[:1], seconds[:1])

    def second_pump():
        for chunk in middles[with_out:]:
            side_late(chunk)
        advance_all(reversed(middles[:2]), seconds)

    def third_pump():
        advance_all(reversed(middles[:3]), seconds)

    def fourth_pump():
        advance_all(reversed(middles[:4]), seconds[1:])

    def pump(k):
        for at, action in enumerate((first_pump, second_pump, third_pump, fourth_pump)):
            pl.when(k == at)(action)

    attend_back_core(
        H_SELF, True, place, qa_ref, paira_ref, gt_ref, atta_ref, totala_ref, qseg_ref, kseg_ref,
        dqa_ref, dpaira_ref, kmark_ref, dkh_ref, dvh_ref, dqh_ref, qrow_ref, grow_ref, weight_ref, slope_ref, pump,
    )
    entered = [len(middles[:4])]
    flow = list(middles) + list(lasts)

    def tick():
        newest = flow[entered[0] : entered[0] + 1]
        older = [chunk for chunk in flow[: entered[0]] if done[chunk] < 5]
        advance_all(newest, reversed(older))
        entered[0] += 1

    store_late(after, nt_dot(turned_ref[:, own], dqa_ref[...]))
    for low, high in chunks(2 * width):
        store_late(after + width + low, nt_dot(turned_ref[...], dpaira_ref[low:high, :]))
    start_late(lasts[0])
    tick()
    side_late(lasts[0])
    gain_sum = jnp.zeros((8, width), jnp.float32)
    for away in [*range(1, seq_count), 0]:
        start = lax.rem(place + away, seq_count) * tokens
        if away == 0:
            tick()
        for low, high in row_tiles(tokens, 128):
            lanes = pl.ds(pl.multiple_of(start + low, 128), high - low)
            upstream = nn_dot(wqkv_ref[:, width:], dpaira_ref[:, lanes])
            if away == 0:
                upstream = upstream + nn_dot(wqkv_ref[:, :width], dqa_ref[:, low:high])
                upstream = upstream + nn_dot(wquery_ref[...], dqb_ref[:, low:high])
            upstream = upstream.T
            normed, _ = rows_normed(rows_ref[lanes, :].astype(jnp.float32))
            gain_sum = gain_sum + folded(upstream * normed)
            if away == 0:
                upstream_ref[low:high, :] = upstream
            else:
                da1_ref[away - 1, low:high, :] = upstream.astype(jnp.bfloat16)

    def swap(kind, away, source, target):
        return pltpu.make_async_remote_copy(
            src_ref=source,
            dst_ref=target,
            send_sem=swap_send.at[kind, away - 1],
            recv_sem=swap_recv.at[kind, away - 1],
            device_id=share.sides[away],
            device_id_type=pl.DeviceIdType.MESH,
        )

    mem_own = dmemory_in_ref.shape[1]

    def row_swap(away):
        return swap(0, away, da1_ref.at[away - 1], da1_in_ref.at[away - 1])

    def mem_swap(away):
        start = pl.multiple_of(lax.rem(place + away, seq_count) * mem_own, mem_own)
        return swap(1, away, dmemory_ref.at[pl.ds(start, mem_own), :], dmemory_in_ref.at[away - 1])

    def start_swaps():
        for away in range(1, seq_count):
            pl.when(place + away >= seq_count)(row_swap(away).start)
            mem_swap(away).start()

    def finish_swaps():
        for away in range(1, seq_count):

            @pl.when(place < away)
            def _():
                row_swap(away).wait_recv()
                upstream_ref[...] += da1_in_ref[away - 1].astype(jnp.float32)

        own_start = pl.multiple_of(place * tokens, 128)
        for low, high in row_tiles(tokens, 128):
            values = rows_ref[pl.ds(pl.multiple_of(own_start + low, 128), high - low), :].astype(jnp.float32)
            normed, inverse = rows_normed(values)
            grad_in_ref[low:high, :] = g1_ref[low:high, :] + rows_norm_back(
                normed, inverse, gain_ref[...], upstream_ref[low:high, :]
            )
        total = dmemory_ref[pl.ds(pl.multiple_of(place * mem_own, mem_own), mem_own), :].astype(jnp.float32)
        for away in range(1, seq_count):
            mem_swap(away).wait_recv()
            total = total + dmemory_in_ref[away - 1].astype(jnp.float32)
        grad_mem_ref[...] = total
        for away in range(1, seq_count):
            pl.when(place + away >= seq_count)(row_swap(away).wait_send)
            mem_swap(away).wait_send()

    small_ref[...] = jnp.zeros_like(small_ref)
    small_ref[0:1, :] = jnp.sum(gain_sum, axis=0, keepdims=True)
    part = width // seq_count
    at = 1
    for source_ref in (gtwo_ref, glate_ref, dtl_ref, dtr_ref, dmg_ref, dtm_ref):
        for row in range(source_ref.shape[0]):
            span = source_ref.shape[1] // seq_count
            for start in range(0, span, part):
                for side in range(seq_count):
                    small_ref[at : at + 1, side * part : (side + 1) * part] = source_ref[
                        row : row + 1, side * span + start : side * span + start + part
                    ]
                at = at + 1
    at = after + 3 * width
    store_late(at, small_ref[...].T)
    at = at + small_ref.shape[0]
    if at < late_ref.shape[-1]:
        late_ref[:, :, :, at:] = jnp.zeros((seq_count, 2, half, late_ref.shape[-1] - at), jnp.bfloat16)
    for chunk in lasts[1:]:
        start_late(chunk)
    for chunk in lasts[1:]:
        side_late(chunk)
    start_swaps()
    ticks = 0
    while any(done.get(chunk, 0) < 5 for chunk in flow):
        tick()
        ticks += 1
        if ticks == SWAP_TICK:
            finish_swaps()
    for chunk in range(count):
        share.last_copy(chunk).wait_recv()
        share.sent_backs(chunk)
    for chunk in range(count):
        share.near_copy(chunk).wait_send()
        share.sent_peers(chunk)
    for chunk in range(early_count, count):
        share.core_copy(chunk, late_ref, chunk - early_count).wait_send()
        share.sent_sides(chunk)


def closing(
    g1, row_inputs, mem_turned, gain, self_kept, cross_kept, d_mem, small_grads, own_seg, seg_row, mem_seg,
    qkv, query, pairs_weight, out, across, second, conv,
):
    tokens, width = g1.shape
    keys, mems = row_inputs.shape[0], mem_turned.shape[1]
    seq_count = keys // tokens
    half = width // (2 * seq_count)
    far_count = lax.axis_size("rows") // 4
    step = 2 * far_count * LANE_GROUP
    size = width // H_CROSS
    middle_total = second.shape[1] - across.shape[1] + conv.shape[1] + 5 * width
    middle_total = middle_total + -middle_total % step
    last_total = 3 * width + 128
    last_total = last_total + -last_total % step
    early_total = across.shape[1]
    late = middle_total + last_total
    count = (early_total + late) // step
    slots = 3 + (seq_count - 1) + 2 * far_count
    low, full = jnp.bfloat16, jnp.float32
    longest = max(tokens, mems)
    v = pltpu.VMEM
    in_hbm = pl.BlockSpec(memory_space=pl.ANY)
    dma = pltpu.SemaphoreType.DMA
    grad_in, grad_mem, share = pl.pallas_call(
        closing_kernel,
        out_shape=(
            jax.ShapeDtypeStruct((tokens, width), full),
            jax.ShapeDtypeStruct((mems // seq_count, width), full),
            jax.ShapeDtypeStruct((2, half, early_total + late), low),
        ),
        in_specs=[IN_VMEM] * 27 + [in_hbm] * 2,
        out_specs=(IN_VMEM, IN_VMEM, in_hbm),
        scratch_shapes=[
            v((width, keys), low),
            v((width, tokens), low),
            v((width, tokens), low),
            v((width, tokens), low),
            v((width, tokens), low),
            v((2 * width, keys), low),
            v((2 * width, mems), low),
            v((SEG_ROWS, keys), low),
            v((SEG_ROWS, mems), low),
            v((BWD_HEADS, width // H_SELF, keys), full),
            v((BWD_HEADS, width // H_SELF, keys), full),
            v((BWD_HEADS, size, mems), full),
            v((BWD_HEADS, size, mems), full),
            v((BWD_HEADS, size, tokens), full),
            v((BWD_HEADS, size + SEG_ROWS, tokens), low),
            v((BWD_HEADS, size + SEG_ROWS, tokens), low),
            v((2, longest, TILE), low),
            v((2, longest, TILE), low),
            v((seq_count, 2, half, late), low),
            v((late // step, seq_count, half, step), low),
            v((late // step, seq_count - 1, half, step), low),
            v((count, half, step // 2), low),
            v((count, far_count - 1, half, LANE_GROUP), low),
            v((count, half, LANE_GROUP), low),
            dma((count, slots)),
            dma((count, slots)),
            dma((count,)),
            dma((2,)),
            v((seq_count - 1, tokens, width), low),
            v((seq_count - 1, tokens, width), low),
            v((tokens, width), full),
            v((mems, width), low),
            v((seq_count - 1, mems // seq_count, width), low),
            dma((2, seq_count - 1)),
            dma((2, seq_count - 1)),
            v((128, width), full),
        ],
        compiler_params=pltpu.CompilerParams(
            collective_id=2, has_side_effects=True, vmem_limit_bytes=HOST_VMEM
        ),
        cost_estimate=pl.CostEstimate(
            flops=tokens * width * width * 200, bytes_accessed=tokens * width * 40, transcendentals=tokens * width * 20
        ),
        name="closing",
    )(
        g1, row_inputs, mem_turned, gain, *self_kept, *cross_kept, d_mem, *small_grads,
        own_seg[None], seg_row[None], mem_seg[None], qkv, query, pairs_weight, out,
        across, second.reshape(seq_count, 2, half, second.shape[1]), conv.reshape(seq_count, 2, half, conv.shape[1]),
    )
    return grad_in, grad_mem, share.reshape(2 * half, early_total + late), early_total + middle_total


def finishing_kernel(plan, small_at, first_ref, share_ref, *outs):
    first_total = first_ref.shape[1]
    for (offset, size, dim), out_ref in zip(plan, outs):
        source_ref, offset = (first_ref, offset) if offset < first_total else (share_ref, offset - first_total)
        if dim == 0:
            out_ref[...] = source_ref[:, offset : offset + size].astype(jnp.float32)
        else:
            for low, high in row_tiles(size, 256):
                out_ref[low:high, :] = source_ref[:, offset + low : offset + high].astype(jnp.float32).T
    small_at = small_at - first_total
    rows = share_ref[:, small_at : small_at + 128].astype(jnp.float32).T
    width = rows.shape[1]
    at = 0
    for out_ref in outs[len(plan) :]:
        for row in range(out_ref.shape[0]):
            for low in range(0, out_ref.shape[1], width):
                out_ref[row : row + 1, low : low + width] = rows[at : at + 1, :]
                at = at + 1


def finishing(first, share, plan, small_at, small_shapes):
    width = share.shape[0]
    shapes = [(width, size) if dim == 0 else (size, width) for _, size, dim in plan] + small_shapes
    return pl.pallas_call(
        functools.partial(finishing_kernel, plan, small_at),
        out_shape=tuple(jax.ShapeDtypeStruct(shape, jnp.float32) for shape in shapes),
        in_specs=[IN_VMEM] * 2,
        out_specs=(IN_VMEM,) * len(shapes),
        compiler_params=pltpu.CompilerParams(vmem_limit_bytes=KERNEL_VMEM),
        name="finishing",
    )(first, share)


def segment_reach(seg_row):
    length = seg_row.shape[0]
    first = jnp.sum(seg_row == 0)
    second = first + jnp.sum(seg_row == 1)
    spots = jnp.arange(length, dtype=jnp.int32)
    start = jnp.where(seg_row == 0, 0, jnp.where(seg_row == 1, first, second))
    stop = jnp.where(seg_row == 0, first, jnp.where(seg_row == 1, second, length))
    return spots - start, stop - 1 - spots


def turned_dot(weight, values):
    return jnp.einsum("kn,tk->nt", weight, values, preferred_element_type=jnp.float32)


def out_dot(turned, weight):
    return jnp.einsum("nt,nk->tk", turned, weight, preferred_element_type=jnp.float32)


def weight_dot(values, turned):
    return jnp.einsum("tk,nt->kn", values, turned, preferred_element_type=jnp.float32)


def out_weight_dot(turned, grads_in):
    return jnp.einsum("nt,tk->kn", turned, grads_in, preferred_element_type=jnp.float32)


def turned_back(grads_in, weight):
    return jnp.einsum("tk,nk->nt", grads_in, weight, preferred_element_type=jnp.float32)


def input_back(turned, weight):
    return jnp.einsum("nt,kn->tk", turned, weight, preferred_element_type=jnp.float32)


def local(
    hidden_in,
    memory,
    grad_out,
    seg_ids,
    mem_seg_ids,
    gains,
    qkv_first,
    query_cross,
    kv_cross,
    out_first,
    taps_left,
    proj_left,
    taps_right,
    proj_right,
    mid_gain,
    taps_mid,
    proj_mid,
    qkv_second,
    out_second,
    query_last,
    kv_last,
    out_last,
    ffn_up,
    ffn_down,
):
    shards = (
        gains,
        qkv_first,
        query_cross,
        kv_cross,
        out_first,
        taps_left,
        proj_left,
        taps_right,
        proj_right,
        mid_gain,
        taps_mid,
        proj_mid,
        qkv_second,
        out_second,
        query_last,
        kv_last,
        out_last,
        ffn_up,
        ffn_down,
    )
    shard_dims = (1, 0, 0, 0, 1, 1, 0, 1, 0, 0, 1, 1, 0, 0, 0, 0, 0, 0, 1)
    small = (0, 5, 7, 9, 10)
    seq_count = lax.axis_size("seq")

    def select(group):
        return [shards[k] for k in group], [shard_dims[k] for k in group]

    first_group, second_group, conv_group, middle_group = (1,), (2, 3, 4), (6, 8, 11), (12, 13, 14, 15, 16)
    up_group = (17, 18)
    hidden_more = seq_rotated(hidden_in[0])
    first_same = seq_rotated(packed_half(*select(first_group)))
    gains, taps_left, taps_right, mid_gain, taps_mid = small_gather(*select(small))
    first_other = [core_swapped(piece) for piece in first_same]
    (qkv_first,) = joined_group(*select(first_group), interleaved(first_same, first_other), 2)
    packed, _ = after((packed_half(*select(second_group)), memory[0], packed_quarter(*select(conv_group))), first_same)
    second_same, mem_more, conv_same = [seq_rotated(block) for block in packed]
    row_inputs = in_place_order([hidden_in[0]] + hidden_more, 0)
    mem_rows = in_place_order([memory[0]] + mem_more, 0)
    inputs = hidden_in[0].astype(jnp.float32)
    seg_row = seg_ids[0]
    mem_seg = mem_seg_ids[0]
    tok_count, model_width = inputs.shape
    row_start = lax.axis_index("seq") * tok_count
    own_seg = lax.dynamic_slice_in_dim(seg_row, row_start, tok_count)
    since, left = segment_reach(seg_row)
    since = lax.dynamic_slice_in_dim(jnp.pad(since, (RIM, 0)), row_start, tok_count + RIM)[:, None]
    left = lax.dynamic_slice_in_dim(jnp.pad(left, (0, RIM)), row_start, tok_count + RIM)[:, None]
    gain_rows = gains.astype(jnp.float32)
    mid_gain_f = mid_gain.astype(jnp.float32)
    left_taps = taps_left.astype(jnp.float32)
    right_taps = taps_right.astype(jnp.float32)
    mid_taps = taps_mid.astype(jnp.float32)
    normed_a = layer_norm(inputs, gain_rows[0]).astype(jnp.bfloat16)
    normed_row = layer_norm(row_inputs.astype(jnp.float32), gain_rows[0]).astype(jnp.bfloat16)
    queries = turned_dot(qkv_first[:, :model_width], normed_a).astype(jnp.bfloat16)
    packed, _ = after(packed_quarter(*select(middle_group)), queries)
    middle_same = seq_rotated(packed)
    pairs_a = turned_dot(qkv_first[:, model_width:], normed_row).astype(jnp.bfloat16)
    kept_a = attend_forward(queries, pairs_a, H_SELF, True, own_seg, seg_row) + (queries, pairs_a)
    att_a, (second_same, conv_same) = after(kept_a[0], (second_same, conv_same))
    second_other = [core_swapped(piece) for piece in second_same]
    kept_a = (att_a,) + kept_a[1:]
    conv_near = [near_swapped(piece) for piece in conv_same]
    query_cross, kv_cross, out_first = joined_group(*select(second_group), interleaved(second_same, second_other), 2)
    pairs_b = turned_dot(kv_cross, mem_rows).astype(jnp.bfloat16)
    query_b = turned_dot(query_cross, normed_a).astype(jnp.bfloat16)
    out_b, total_b = attend_forward(query_b, pairs_b, H_CROSS, False, own_seg, mem_seg)
    out_b, conv_near = after(out_b, conv_near)
    conv_across = [core_swapped(jnp.concatenate(pair, 0)) for pair in zip(conv_same, conv_near)]
    hidden_b = (
        inputs
        + out_dot(kept_a[0], out_first[:model_width])
        + out_dot(out_b, out_first[model_width:])
    )
    hidden_b, middle_same = after(hidden_b, middle_same)
    middle_near = [near_swapped(piece) for piece in middle_same]
    proj_left, proj_right, proj_mid = joined_group(
        *select(conv_group), interleaved(conv_same, conv_near, conv_across), 4
    )
    normed_c = layer_norm(hidden_b, gain_rows[1]).astype(jnp.bfloat16)
    rim = passed_along(normed_c[tok_count - RIM :], "seq", 1)
    packed, _ = after(packed_half(*select(up_group)), rim)
    up_same = seq_rotated(packed)
    conv_l, conv_r, conv_m, hidden_c, normed_d = conv_forward(
        hidden_b,
        normed_c,
        rim,
        since,
        left_taps,
        right_taps,
        mid_taps,
        mid_gain_f[None],
        gain_rows[2:3],
        proj_left,
        proj_right,
        proj_mid,
    )
    normed_d, middle_near = after(normed_d, middle_near)
    middle_across = [core_swapped(jnp.concatenate(pair, 0)) for pair in zip(middle_same, middle_near)]
    middle_pieces = interleaved(middle_same, middle_near, middle_across)
    normed_d, up_same = after(normed_d, up_same)
    up_other = [core_swapped(piece) for piece in up_same]
    up_pieces = interleaved(up_same, up_other)
    down, _ = joined_weight(shards[18], 1, up_pieces, shards[17].shape[1], 2)
    result, grad_now, brim, conv_rims, d_middle, d_gains_late, d_mem, mine = middle(
        hidden_c,
        normed_d,
        jnp.concatenate([conv_l[:RIM], conv_r[:RIM]], 1),
        mem_rows,
        grad_out[0],
        gain_rows[2:5],
        own_seg,
        seg_row,
        mem_seg,
        down,
        shards[12:18],
        middle_pieces,
        up_pieces,
    )
    grad_now, d_projections, d_taps_left, d_taps_right, d_taps_mid, d_mid_gain, g_two, first_share, across = conv_back(
        grad_now,
        brim,
        conv_l,
        conv_r,
        conv_rims,
        conv_m,
        normed_c,
        hidden_b,
        left,
        left_taps,
        right_taps,
        mid_taps,
        mid_gain_f[None],
        gain_rows[1:2],
        proj_left,
        proj_right,
        proj_mid,
        mine,
        d_middle,
    )
    wide, narrow = proj_left.shape[1], proj_right.shape[1]
    first_share = first_share.reshape(-1, first_share.shape[2])
    small_grads = (g_two, d_gains_late, d_taps_left, d_taps_right, d_mid_gain, d_taps_mid)
    grad_in, grad_mem, share, last_at = closing(
        grad_now,
        row_inputs,
        mem_rows.T,
        gain_rows[:1],
        kept_a[:4],
        (out_b, total_b, query_b, pairs_b),
        d_mem,
        small_grads,
        own_seg,
        seg_row,
        mem_seg,
        qkv_first,
        query_cross,
        kv_cross,
        out_first,
        across,
        d_middle,
        d_projections,
    )
    shares = [None] * len(shards)
    up = down.shape[0]
    plan, order, offset = [], (17, 18, 16, 14, 15, 12, 13, 11, 6, 8, 4, 3, 2, 1), 0
    for k, size in zip(
        order,
        (up, up, model_width, model_width, 2 * model_width, 3 * model_width, model_width)
        + (wide, wide, narrow, 2 * model_width, 2 * model_width, model_width, 3 * model_width),
    ):
        offset = last_at + first_share.shape[1] if k == 1 else offset
        plan.append((offset, size, shard_dims[k]))
        offset = offset + size
    small_shapes = [shards[k].shape if k != 9 else (1, shards[k].shape[0]) for k in small]
    found = finishing(first_share, share, plan, offset, small_shapes)
    for k, piece in zip(order + small, found):
        shares[k] = piece.reshape(shards[k].shape)
    return (
        result[None],
        grad_in[None],
        grad_mem[None],
        shares[0],
        shares[1],
        shares[2],
        shares[3],
        shares[4],
        shares[5],
        shares[6],
        shares[7],
        shares[8],
        shares[9],
        shares[10],
        shares[11],
        shares[12],
        shares[13],
        shares[14],
        shares[15],
        shares[16],
        shares[17],
        shares[18],
    )


def solution(mesh):
    placed = (
        P("rows", "seq", None),
        P("rows", "seq", None),
        P("rows", "seq", None),
        P("rows", None),
        P("rows", None),
        P(None, "seq"),
        P("seq", None),
        P("seq", None),
        P("seq", None),
        P(None, "seq"),
        P(None, "seq"),
        P("seq", None),
        P(None, "seq"),
        P("seq", None),
        P("seq"),
        P(None, "seq"),
        P(None, "seq"),
        P("seq", None),
        P("seq", None),
        P("seq", None),
        P("seq", None),
        P("seq", None),
        P("seq", None),
        P(None, "seq"),
    )
    return jax.shard_map(
        local,
        mesh=mesh,
        in_specs=placed,
        out_specs=(
            P("rows", "seq", None),
            P("rows", "seq", None),
            P("rows", "seq", None),
            P(None, "seq"),
            P("seq", None),
            P("seq", None),
            P("seq", None),
            P(None, "seq"),
            P(None, "seq"),
            P("seq", None),
            P(None, "seq"),
            P("seq", None),
            P("seq"),
            P(None, "seq"),
            P(None, "seq"),
            P("seq", None),
            P("seq", None),
            P("seq", None),
            P("seq", None),
            P("seq", None),
            P("seq", None),
            P(None, "seq"),
        ),
        check_vma=False,
    )
```

```python
import functools

import jax
import jax.numpy as jnp
from jax import lax
from jax.experimental import pallas as pl
from jax.experimental.pallas import tpu as pltpu
from jax.sharding import PartitionSpec as P

H_SELF = 16
H_CROSS = 8
WIDE = 1024
NARROW = 256
LEFT_TAPS = 11
RIGHT_TAPS = 7


NEG_BIG = -1e30
EPSILON = 1e-06


def rotated(block, axis, distance):
    size = lax.axis_size(axis)
    return lax.ppermute(block, axis, [((i + distance) % size, i) for i in range(size)])


def core_swapped(block):
    return lax.ppermute(block, "rows", [(i, i ^ 1) for i in range(lax.axis_size("rows"))])


def in_place_order(relative, dim):
    count = len(relative)
    place = lax.axis_index("seq")
    orders = [
        jnp.concatenate([relative[(p - me) % count] for p in range(count)], dim)
        for me in range(count)
    ]
    result = orders[0]
    for me in range(1, count):
        result = jnp.where(place == me, orders[me], result)
    return result


def gathered(block, dim=0):
    count = lax.axis_size("seq")
    return in_place_order([block] + [rotated(block, "seq", d) for d in range(1, count)], dim)


def near_swapped(block):
    return lax.ppermute(block, "rows", [(i, i ^ 2) for i in range(lax.axis_size("rows"))])


def flat_share(shard, dim, index, count):
    size = shard.shape[0] // count
    part = lax.dynamic_slice_in_dim(shard, index * size, size)
    if dim == 0:
        return part
    width = shard.shape[1]
    blocks = part.reshape(-1, width // count, width)
    return jnp.swapaxes(blocks, 0, 1).reshape(width // count, -1)


def unflat_share(part, shape, dim, count):
    if dim == 0:
        return part
    width = shape[1]
    blocks = part.reshape(width // count, -1, width)
    return jnp.swapaxes(blocks, 0, 1).reshape(shape[0] // count, width)


def seq_rotated(packed):
    return [rotated(packed, "seq", d) for d in range(1, lax.axis_size("seq"))]


def packed_half(shards, dims):
    core = lax.axis_index("rows") & 1
    return jnp.concatenate([flat_share(shard, dim, core, 2) for shard, dim in zip(shards, dims)], 1)


def packed_quarter(shards, dims):
    index = lax.axis_index("rows") & 3
    return jnp.concatenate([flat_share(shard, dim, index, 4) for shard, dim in zip(shards, dims)], 1)


def ordered(bit, first, second):
    return jnp.where(bit == 0, jnp.concatenate([first, second], 0), jnp.concatenate([second, first], 0))


def joined_weight(shard, dim, pieces, offset, count):
    row = lax.axis_index("rows")
    size = shard.size // count // pieces[0].shape[0]

    def part(piece):
        return unflat_share(piece[:, offset : offset + size], shard.shape, dim, count)

    relative = [shard]
    if count == 2:
        for k in range(0, len(pieces), 2):
            relative.append(ordered(row & 1, part(pieces[k]), part(pieces[k + 1])))
    else:
        for k in range(0, len(pieces), 3):
            same, near, across = pieces[k : k + 3]
            rows = same.shape[0]
            own_pair = ordered(row & 1, part(same), part(across[:rows]))
            near_pair = ordered(row & 1, part(near), part(across[rows:]))
            relative.append(ordered(row & 2, own_pair, near_pair))
    return in_place_order(relative, dim), offset + size


def joined_group(shards, dims, pieces, count):
    results = []
    offset = 0
    for shard, dim in zip(shards, dims):
        full, offset = joined_weight(shard, dim, pieces, offset, count)
        results.append(full)
    return results


def interleaved(*lists):
    return [item for items in zip(*lists) for item in items]


def small_gather(shards, dims):
    sizes = [shard.size for shard in shards]
    flat = jnp.concatenate([shard.reshape(-1) for shard in shards])
    flat = padded_rows(flat, 2048, 0).reshape(-1, 128)
    parts = [flat] + [rotated(flat, "seq", d) for d in range(1, lax.axis_size("seq"))]
    parts = [part.reshape(-1) for part in parts]
    results = []
    offset = 0
    for shard, dim, size in zip(shards, dims, sizes):
        relative = [part[offset : offset + size].reshape(shard.shape) for part in parts]
        results.append(in_place_order(relative, dim))
        offset = offset + size
    return results


def padded_rows(block, multiple, dim):
    extra = -block.shape[dim] % multiple
    if not extra:
        return block
    widths = [(0, 0)] * block.ndim
    widths[dim] = (0, extra)
    return jnp.pad(block, widths)


def halved_sum(block, axis, bit, dim):
    half = block.shape[dim] // 2
    upper = ((lax.axis_index(axis) & bit) != 0).astype(jnp.int32)
    kept = lax.dynamic_slice_in_dim(block, upper * half, half, dim)
    sent = lax.dynamic_slice_in_dim(block, (1 - upper) * half, half, dim)
    got = lax.ppermute(sent, axis, [(i, i ^ bit) for i in range(lax.axis_size(axis))])
    return (kept.astype(jnp.float32) + got.astype(jnp.float32)).astype(jnp.bfloat16)


def row_sum_owned(partial):
    bit = lax.axis_size("seq") // 2
    while bit:
        partial = halved_sum(partial, "seq", bit, 0)
        bit = bit // 2
    return partial.astype(jnp.float32)


def after(values, others):
    return lax.optimization_barrier((values, others))


def passed_along(block, axis, distance):
    devices = range(lax.axis_size(axis))
    route = [(i - distance, i) for i in devices if i - distance in devices]
    return lax.ppermute(block, axis, route)


def layer_norm(values, gain_vec):
    centre = values - jnp.mean(values, axis=-1, keepdims=True)
    inverse = lax.rsqrt(jnp.mean(centre * centre, axis=-1, keepdims=True) + EPSILON)
    return centre * inverse * gain_vec


def norm_back(values, gain_vec, upstream):
    centre = values - jnp.mean(values, axis=-1, keepdims=True)
    inverse = lax.rsqrt(jnp.mean(centre * centre, axis=-1, keepdims=True) + EPSILON)
    normed = centre * inverse
    scaled = upstream * gain_vec
    d_values = inverse * (
        scaled
        - jnp.mean(scaled, axis=-1, keepdims=True)
        - normed * jnp.mean(scaled * normed, axis=-1, keepdims=True)
    )
    return (d_values, jnp.sum(upstream * normed, axis=0))


def swish_slope(pre_act):
    sigma = jax.nn.sigmoid(pre_act)
    return sigma * (1.0 + pre_act * (1.0 - sigma))


def plain_dot(first, second):
    return jnp.dot(first, second, preferred_element_type=jnp.float32)


def left_dot(first, second):
    return jnp.einsum("nk,nm->km", first, second, preferred_element_type=jnp.float32)


def right_dot(grads_in, weight):
    return jnp.einsum("nm,km->nk", grads_in, weight, preferred_element_type=jnp.float32)


TILE = 256
SEG_ROWS = 16
LOG2E = 1.4426950408889634


def tiles_of(extent):
    return [(low, min(low + TILE, extent)) for low in range(0, extent, TILE)]


def tn_dot(first, second):
    return lax.dot_general(first, second, (((0,), (0,)), ((), ())), preferred_element_type=jnp.float32)


def nn_dot(first, second):
    return lax.dot_general(first, second, (((1,), (0,)), ((), ())), preferred_element_type=jnp.float32)


def nt_dot(first, second):
    return lax.dot_general(first, second, (((1,), (1,)), ((), ())), preferred_element_type=jnp.float32)


def row_numbers(width):
    return lax.broadcasted_iota(jnp.int32, (SEG_ROWS, width), 0)


def split_low(values, count):
    pieces = []
    for _ in range(count):
        piece = values.astype(jnp.bfloat16).astype(jnp.float32)
        pieces.append(piece)
        values = values - piece
    return pieces


def key_marks(key_seg, ones):
    rows = row_numbers(key_seg.shape[1])
    marked = jnp.logical_or(rows == key_seg, jnp.logical_and(rows >= 3, rows < 3 + ones))
    return jnp.where(marked, 1.0, 0.0).astype(jnp.bfloat16)


def query_marks(query_seg):
    rows = row_numbers(query_seg.shape[1])
    other = jnp.logical_and(rows < 3, rows != query_seg)
    return jnp.where(other, NEG_BIG, 0.0)


def with_rows(marks, first, pieces):
    rows = row_numbers(marks.shape[1])
    for k, piece in enumerate(pieces):
        marks = jnp.where(rows == first + k, piece, marks)
    return marks.astype(jnp.bfloat16)


def triangle(scores, low):
    key_at = lax.broadcasted_iota(jnp.int32, scores.shape, 0)
    query_at = lax.broadcasted_iota(jnp.int32, scores.shape, 1) + low
    return jnp.where(key_at <= query_at, scores, NEG_BIG)


FWD_HEADS = 4
BWD_HEADS = 4


def attend_kernel(heads, causal, place_ref, *refs):
    attend_core(heads, causal, place_ref[0], *refs)


def attend_core(
    heads, causal, place, qt_ref, pair_ref, qseg_ref, kseg_ref, ot_ref, total_ref, kmark_ref, sum_ref, peak_ref, score_ref,
    between=None,
):
    width, tokens = qt_ref.shape
    size = width // heads
    factor = size ** (-0.5) * LOG2E
    block = tokens if causal else pair_ref.shape[1]
    place = place if causal else 0
    kmark_ref[...] = key_marks(kseg_ref[...], 0)
    value_marks = jnp.where(row_numbers(TILE) == 0, 1.0, 0.0).astype(jnp.bfloat16)
    qmarks = query_marks(qseg_ref[...]).astype(jnp.bfloat16)
    tiles = tiles_of(tokens)

    def head_rows(head, base=0):
        return pl.ds(pl.multiple_of(base + head * size, size), size)

    def on_units(several, start, first):
        units = [
            (k if between is None else head, head, low, high)
            for k, head in enumerate(several)
            for low, high in tiles
        ]

        def key_parts(unit):
            _, _, _, high = unit
            return tiles_of(high if first and causal else block)

        def lanes_of(part):
            return pl.ds(pl.multiple_of(start + part[0], 128), part[1] - part[0])

        def score_part(unit, slot, part):
            k, head, low, high = unit
            query_rows = jnp.concatenate([qt_ref[head_rows(head), low:high], qmarks[:, low:high]], 0)
            lanes = lanes_of(part)
            scores = tn_dot(jnp.concatenate([pair_ref[head_rows(head), lanes], kmark_ref[:, lanes]], 0), query_rows)
            if first and causal and part[0] >= low:
                scores = triangle(scores, low - part[0])
            score_ref[slot, part[0] : part[1], : high - low] = scores
            return jnp.max(scores, axis=0, keepdims=True)

        def value_part(unit, slot, part, peak):
            k, head, low, high = unit
            scores = score_ref[slot, part[0] : part[1], : high - low]
            weights = jnp.exp2((scores - peak) * factor).astype(jnp.bfloat16)
            value_rows = jnp.concatenate(
                [pair_ref[head_rows(head, width), lanes_of(part)], value_marks[:, : part[1] - part[0]]], 0
            )
            return nn_dot(value_rows, weights)

        held = None
        for at in range(len(units) + 1):
            unit = units[at] if at < len(units) else None
            parts = key_parts(unit) if unit else []
            old_parts = key_parts(held[0]) if held else []
            peak = None
            if unit and not first:
                peak = peak_ref[unit[0], :, unit[2] : unit[3]]
            before = peak
            summed = None
            for step in range(max(len(parts), len(old_parts))):
                if step < len(parts):
                    found = score_part(unit, at % 2, parts[step])
                    peak = found if peak is None else jnp.maximum(peak, found)
                if step < len(old_parts):
                    term = value_part(held[0], (at - 1) % 2, old_parts[step], held[1])
                    summed = term if summed is None else summed + term
            if held:
                k, _, low, high = held[0]
                if not first:
                    summed = summed + sum_ref[k, :, low:high] * jnp.exp2((held[2] - held[1]) * factor)
                sum_ref[k, :, low:high] = summed
                peak_ref[k, :, low:high] = held[1]
            held = (unit, peak, before)

    def group_of(step):
        return [step * FWD_HEADS + k for k in range(FWD_HEADS)]

    def start_heads(step, carry):
        on_units(group_of(step), place * block, True)
        return carry

    def finish_heads(step, carry):
        several = group_of(step)
        if causal:

            def earlier(back, held):
                on_units(several, back * block, False)
                return held

            lax.fori_loop(0, place, earlier, 0)
        for k, head in enumerate(several):
            slot = k if between is None else head
            total = sum_ref[slot, size : size + 1, :]
            ot_ref[head_rows(head), :] = (sum_ref[slot, :size, :] / total).astype(jnp.bfloat16)
            total_ref[head] = peak_ref[slot] + jnp.log2(total) / factor
        return carry

    if between is None:
        lax.fori_loop(0, heads // FWD_HEADS, lambda k, held: finish_heads(k, start_heads(k, held)), 0)
    else:
        lax.fori_loop(0, heads // FWD_HEADS, start_heads, 0)
        between()
        lax.fori_loop(0, heads // FWD_HEADS, finish_heads, 0)


def attend_back_kernel(heads, causal, place_ref, *refs):
    attend_back_core(heads, causal, place_ref[0], *refs)


def attend_back_core(
    heads, causal, place, qt_ref, pair_ref, gt_ref, ot_ref, total_ref, qseg_ref, kseg_ref,
    dq_ref, dpair_ref, kmark_ref, dkh_ref, dvh_ref, dqh_ref, qrow_ref, grow_ref, weight_ref, slope_ref,
    pump=None,
):
    width, tokens = qt_ref.shape
    size = width // heads
    scale = size ** (-0.5)
    factor = scale * LOG2E
    block = tokens if causal else pair_ref.shape[1]
    place = place if causal else 0
    kmark_ref[...] = key_marks(kseg_ref[...], 3)
    value_marks = jnp.where(row_numbers(TILE) < 2, 1.0, 0.0).astype(jnp.bfloat16)
    qmarks = query_marks(qseg_ref[...])
    tiles = tiles_of(tokens)

    def head_rows(head, base=0):
        return pl.ds(pl.multiple_of(base + head * size, size), size)

    def prepare(k, head):
        own = head_rows(head)
        grads = gt_ref[own, :]
        delta = jnp.sum(grads.astype(jnp.float32) * ot_ref[own, :].astype(jnp.float32), axis=0, keepdims=True)
        qrow_ref[k, :size, :] = qt_ref[own, :]
        qrow_ref[k, size : size + SEG_ROWS, :] = with_rows(qmarks, 3, split_low(-total_ref[head], 3))
        grow_ref[k, :size, :] = grads
        grow_ref[k, size : size + SEG_ROWS, :] = with_rows(jnp.zeros_like(qmarks), 0, split_low(-delta, 2))

    def on_units(several, start, first):
        units = [(k, head, low, high) for k, head in enumerate(several) for low, high in tiles]

        def key_parts(unit):
            _, _, _, high = unit
            return tiles_of(high if first and causal else block)

        def lanes_of(part):
            return pl.ds(pl.multiple_of(start + part[0], 128), part[1] - part[0])

        def score_part(unit, slot, part):
            k, head, low, high = unit
            lanes = lanes_of(part)
            key_rows = jnp.concatenate([pair_ref[head_rows(head), lanes], kmark_ref[:, lanes]], 0)
            value_rows = jnp.concatenate(
                [pair_ref[head_rows(head, width), lanes], value_marks[:, : part[1] - part[0]]], 0
            )
            scores = tn_dot(key_rows, qrow_ref[k, : size + SEG_ROWS, low:high])
            if first and causal and part[0] >= low:
                scores = triangle(scores, low - part[0])
            weights = jnp.exp2(scores * factor)
            slopes = tn_dot(value_rows, grow_ref[k, : size + SEG_ROWS, low:high])
            weight_ref[slot, part[0] : part[1], : high - low] = weights.astype(jnp.bfloat16)
            slope_ref[slot, part[0] : part[1], : high - low] = (weights * slopes).astype(jnp.bfloat16)

        def grad_part(unit, slot, part):
            k, head, low, high = unit
            lanes = lanes_of(part)
            weights = weight_ref[slot, part[0] : part[1], : high - low]
            slopes = slope_ref[slot, part[0] : part[1], : high - low]
            dvh_ref[k, :, lanes] += nt_dot(grow_ref[k, :size, low:high], weights)
            dkh_ref[k, :, lanes] += nt_dot(qrow_ref[k, :size, low:high], slopes)
            return nn_dot(pair_ref[head_rows(head), lanes], slopes)

        held = None
        for at in range(len(units) + 1):
            unit = units[at] if at < len(units) else None
            parts = key_parts(unit) if unit else []
            old_parts = key_parts(held) if held else []
            summed = None
            for step in range(max(len(parts), len(old_parts))):
                if step < len(parts):
                    score_part(unit, at % 2, parts[step])
                if step < len(old_parts):
                    term = grad_part(held, (at - 1) % 2, old_parts[step])
                    summed = term if summed is None else summed + term
            if held:
                k, _, low, high = held
                if first:
                    dqh_ref[k, :size, low:high] = summed
                else:
                    dqh_ref[k, :size, low:high] += summed
            held = unit

    def some_heads(step, carry):
        several = [step * BWD_HEADS + k for k in range(BWD_HEADS)]
        if pump is not None:
            pump(step)
        dkh_ref[...] = jnp.zeros_like(dkh_ref)
        dvh_ref[...] = jnp.zeros_like(dvh_ref)
        for k, head in enumerate(several):
            prepare(k, head)
        on_units(several, place * block, True)
        if causal:

            def earlier(back, held):
                on_units(several, back * block, False)
                return held

            lax.fori_loop(0, place, earlier, 0)
        for k, head in enumerate(several):
            dq_ref[head_rows(head), :] = (dqh_ref[k, :size, :] * scale).astype(jnp.bfloat16)
            dpair_ref[head_rows(head), :] = (dkh_ref[k] * scale).astype(jnp.bfloat16)
            dpair_ref[head_rows(head, width), :] = dvh_ref[k].astype(jnp.bfloat16)
        return carry

    lax.fori_loop(0, heads // BWD_HEADS, some_heads, 0)


IN_SMEM = pl.BlockSpec(memory_space=pltpu.SMEM)
IN_VMEM = pl.BlockSpec(memory_space=pltpu.VMEM)
KERNEL_VMEM = 48 * 2**20
HOST_VMEM = 63 * 2**20 + 2**19


LANE_GROUP = 128
SWAP_TICK = 4


def attend_forward(queries, pairs_t, heads, causal, query_seg, key_seg):
    width, tokens = queries.shape
    total_keys = pairs_t.shape[1]
    pairs = heads * tokens * total_keys
    return pl.pallas_call(
        functools.partial(attend_kernel, heads, causal),
        out_shape=(
            jax.ShapeDtypeStruct((width, tokens), jnp.bfloat16),
            jax.ShapeDtypeStruct((heads, 1, tokens), jnp.float32),
        ),
        in_specs=[IN_SMEM] + [IN_VMEM] * 4,
        out_specs=(IN_VMEM, IN_VMEM),
        scratch_shapes=[
            pltpu.VMEM((SEG_ROWS, total_keys), jnp.bfloat16),
            pltpu.VMEM((FWD_HEADS, width // heads + SEG_ROWS, tokens), jnp.float32),
            pltpu.VMEM((FWD_HEADS, 1, tokens), jnp.float32),
            pltpu.VMEM((2, tokens if causal else total_keys, TILE), jnp.float32),
        ],
        compiler_params=pltpu.CompilerParams(vmem_limit_bytes=KERNEL_VMEM),
        cost_estimate=pl.CostEstimate(
            flops=pairs * 600, bytes_accessed=4 * width * total_keys, transcendentals=pairs
        ),
        name="attend_fwd",
    )(lax.axis_index("seq").reshape(1), queries, pairs_t, query_seg[None], key_seg[None])


def attend_back(queries, pairs_t, grads, outs, totals, heads, causal, query_seg, key_seg):
    width, tokens = queries.shape
    total_keys = pairs_t.shape[1]
    pairs = heads * tokens * total_keys
    size = width // heads
    return pl.pallas_call(
        functools.partial(attend_back_kernel, heads, causal),
        out_shape=(
            jax.ShapeDtypeStruct((width, tokens), jnp.bfloat16),
            jax.ShapeDtypeStruct((2 * width, total_keys), jnp.bfloat16),
        ),
        in_specs=[IN_SMEM] + [IN_VMEM] * 7,
        out_specs=(IN_VMEM, IN_VMEM),
        scratch_shapes=[
            pltpu.VMEM((SEG_ROWS, total_keys), jnp.bfloat16),
            pltpu.VMEM((BWD_HEADS, size, total_keys), jnp.float32),
            pltpu.VMEM((BWD_HEADS, size, total_keys), jnp.float32),
            pltpu.VMEM((BWD_HEADS, size, tokens), jnp.float32),
            pltpu.VMEM((BWD_HEADS, size + SEG_ROWS, tokens), jnp.bfloat16),
            pltpu.VMEM((BWD_HEADS, size + SEG_ROWS, tokens), jnp.bfloat16),
            pltpu.VMEM((2, tokens if causal else total_keys, TILE), jnp.bfloat16),
            pltpu.VMEM((2, tokens if causal else total_keys, TILE), jnp.bfloat16),
        ],
        compiler_params=pltpu.CompilerParams(vmem_limit_bytes=KERNEL_VMEM),
        cost_estimate=pl.CostEstimate(
            flops=pairs * 1500, bytes_accessed=8 * width * total_keys, transcendentals=pairs
        ),
        name="attend_bwd",
    )(
        lax.axis_index("seq").reshape(1), queries, pairs_t, grads, outs, totals,
        query_seg[None], key_seg[None],
    )


RIM = 16
ROW_TILE = 64
MERGE_ROWS = 128


def row_tiles(extent, tile):
    return [(low, min(low + tile, extent)) for low in range(0, extent, tile)]


def halves_of(extent):
    middle = -(-extent // 32) * 16
    return [(0, middle), (middle, extent)]


def group_lanes(group):
    return pl.ds(pl.multiple_of(group * 128, 128), 128)


def wide_rows(column, width=128):
    return jnp.broadcast_to(column, (column.shape[0], width))


def loop_rows(extent, tile, body):
    def step(k, carry):
        body(pl.ds(pl.multiple_of(k * tile, tile), tile))
        return carry

    whole = extent // tile
    lax.fori_loop(0, whole, step, 0)
    if whole * tile < extent:
        body(pl.ds(whole * tile, extent - whole * tile))


def rows_normed(values):
    centre = values - jnp.mean(values, axis=-1, keepdims=True)
    inverse = lax.rsqrt(jnp.mean(centre * centre, axis=-1, keepdims=True) + EPSILON)
    return centre * inverse, inverse


def rows_norm_back(normed, inverse, gain_vec, upstream):
    scaled = upstream * gain_vec
    return inverse * (
        scaled
        - jnp.mean(scaled, axis=-1, keepdims=True)
        - normed * jnp.mean(scaled * normed, axis=-1, keepdims=True)
    )


def taps_forward(source_ref, first_row, since, lanes, low, high, weights):
    result = None
    for offset, weight in enumerate(weights):
        start = first_row + low - offset
        window = source_ref[start : start + high - low, lanes]
        if offset:
            window = jnp.where(since >= offset, window, 0.0)
        term = window * weight
        result = term if result is None else result + term
    return result


def conv_fwd_kernel(
    h1_ref, a2_ref, rim_ref, since_ref, tl_ref, tr_ref, tm_ref, mgain_ref, gain_ref, pl_ref, pr_ref, pm_ref,
    cl_ref, cr_ref, cm_ref, h2_ref, a3_ref,
    ext_ref, wide_ref, cle_ref, cre_ref, up_ref, mixed_ref,
):
    tokens, width = h1_ref.shape
    total = tokens + RIM
    narrow = pr_ref.shape[1]
    ext_ref[0:RIM, :] = jnp.zeros((RIM, width), jnp.float32)
    ext_ref[RIM : 2 * RIM, :] = rim_ref[...].astype(jnp.float32)
    ext_ref[2 * RIM :, :] = a2_ref[...].astype(jnp.float32)
    wide_ref[...] = wide_rows(since_ref[...])

    def first_convs(group, carry):
        lanes = group_lanes(group)
        left = [tl_ref[j : j + 1, lanes] for j in range(tl_ref.shape[0])]
        right = [tr_ref[j : j + 1, lanes] for j in range(tr_ref.shape[0])]
        for low, high in row_tiles(total, ROW_TILE):
            since = wide_ref[low:high, :]
            cle_ref[low:high, lanes] = taps_forward(ext_ref, RIM, since, lanes, low, high, left).astype(jnp.bfloat16)
            cre_ref[low:high, lanes] = taps_forward(ext_ref, RIM, since, lanes, low, high, right).astype(jnp.bfloat16)
        return carry

    lax.fori_loop(0, width // 128, first_convs, 0)
    cl_ref[...] = cle_ref[RIM:, :]
    cr_ref[...] = cre_ref[RIM:, :]
    for low, high in halves_of(total):
        up_ref[low:high, :] = nn_dot(cle_ref[low:high, :], pl_ref[...])
        mixed_ref[low:high, :narrow] = nn_dot(cre_ref[low:high, :], pr_ref[...])

    def merge_rows(rows):
        pre = up_ref[rows, :]
        merged = pre / (1.0 + jnp.exp(-pre))
        merged = jnp.concatenate([merged[:, :narrow] + mixed_ref[rows, :narrow], merged[:, narrow:]], 1)
        normed, _ = rows_normed(merged)
        mixed_ref[rows, :] = (normed * mgain_ref[...]).astype(jnp.bfloat16).astype(jnp.float32)

    loop_rows(total, MERGE_ROWS, merge_rows)

    def mid_conv(group, carry):
        lanes = group_lanes(group)
        weights = [tm_ref[j : j + 1, lanes] for j in range(tm_ref.shape[0])]
        for low, high in row_tiles(tokens, ROW_TILE):
            since = wide_ref[RIM + low : RIM + high, :]
            cm_ref[low:high, lanes] = taps_forward(mixed_ref, RIM, since, lanes, low, high, weights).astype(jnp.bfloat16)
        return carry

    lax.fori_loop(0, mixed_ref.shape[1] // 128, mid_conv, 0)
    for low, high in halves_of(tokens):
        h2_ref[low:high, :] = h1_ref[low:high, :] + nn_dot(cm_ref[low:high, :], pm_ref[...])

    def norm_rows(rows):
        normed, _ = rows_normed(h2_ref[rows, :])
        a3_ref[rows, :] = (normed * gain_ref[...]).astype(jnp.bfloat16)

    loop_rows(tokens, 64, norm_rows)


def conv_forward(h1, a2, rim, since, taps_l, taps_r, taps_m, mid_gain, gain, proj_left, proj_right, proj_mid):
    tokens, width = h1.shape
    wide = proj_left.shape[1]
    total = tokens + RIM
    low, full = jnp.bfloat16, jnp.float32
    return pl.pallas_call(
        conv_fwd_kernel,
        out_shape=(
            jax.ShapeDtypeStruct((tokens, width), low),
            jax.ShapeDtypeStruct((tokens, width), low),
            jax.ShapeDtypeStruct((tokens, wide), low),
            jax.ShapeDtypeStruct((tokens, width), full),
            jax.ShapeDtypeStruct((tokens, width), low),
        ),
        in_specs=[IN_VMEM] * 12,
        out_specs=(IN_VMEM,) * 5,
        scratch_shapes=[
            pltpu.VMEM((total + RIM, width), full),
            pltpu.VMEM((total, 128), jnp.int32),
            pltpu.VMEM((total, width), low),
            pltpu.VMEM((total, width), low),
            pltpu.VMEM((total, wide), full),
            pltpu.VMEM((total, wide), full),
        ],
        compiler_params=pltpu.CompilerParams(vmem_limit_bytes=KERNEL_VMEM),
        cost_estimate=pl.CostEstimate(
            flops=tokens * width * wide * 20, bytes_accessed=tokens * width * 16, transcendentals=tokens * wide
        ),
        name="conv_fwd",
    )(h1, a2, rim, since, taps_l, taps_r, taps_m, mid_gain, gain, proj_left, proj_right, proj_mid)


def folded(values):
    return jnp.sum(values.reshape(-1, 8, values.shape[-1]), axis=0)


def taps_back(grad_ref, value, left, lanes, low, high, weights, result, sums):
    for offset, weight in enumerate(weights):
        window = grad_ref[low + offset : high + offset, lanes]
        if offset:
            window = jnp.where(left >= offset, window, 0.0)
        term = window * weight
        result = term if result is None else result + term
        if value is not None:
            product = folded(window * value)
            sums[offset] = product if sums[offset] is None else sums[offset] + product
    return result


def conv_bwd_kernel(
    g2_ref, brim_ref, cl_ref, clrim_ref, cr_ref, crrim_ref, cm_ref, a2_ref, h1_ref, left_ref,
    tl_ref, tr_ref, tm_ref, mgain_ref, gain_ref, pl_ref, pr_ref, pm_ref, mine_ref, second_ref,
    g1_ref, dw_ref, dtl_ref, dtr_ref, dtm_ref, dmgain_ref, dgain_ref, out_ref, across_out_ref,
    bext_ref, cle_ref, cre_ref, wide_ref, grad_ref, up_ref, back_ref, normed_ref, inv_ref, dpl_ref, dpr_ref, a2f_ref,
    kept_ref, core_ref, across_ref, send_sem, recv_sem, local_sem, kept_sem,
):
    tokens, width = g2_ref.shape
    total = tokens + RIM
    wide, narrow = pl_ref.shape[1], pr_ref.shape[1]
    share = ShareSum(
        send_sem, recv_sem, core=core_ref, across=across_ref, mine=mine_ref, out=out_ref, local_sem=local_sem
    )
    first_count = mine_ref.shape[0]
    step = share.step
    firsts, seconds = range(first_count), range(first_count, first_count + core_ref.shape[0])
    share.core_first = first_count
    share.enter([share.mate, share.close] + share.peers[1:] + share.sides[1:])
    kept_copy = pltpu.make_async_copy(
        second_ref.at[:, share.core, :, : kept_ref.shape[-1]], kept_ref, kept_sem
    )
    kept_copy.start()
    for chunk in seconds:
        share.core_copy(chunk, second_ref, chunk - first_count).start()
    for chunk in firsts:
        share.start_back(chunk)
    bext_ref[:tokens, :] = g2_ref[...].astype(jnp.bfloat16)
    bext_ref[tokens:, :] = brim_ref[...]
    cle_ref[:tokens, :] = cl_ref[...]
    cle_ref[tokens:, :] = clrim_ref[...]
    cre_ref[:tokens, :] = cr_ref[...]
    cre_ref[tokens:, :] = crrim_ref[...]
    a2f_ref[...] = a2_ref[...].astype(jnp.float32)
    wide_ref[...] = wide_rows(left_ref[...])
    grad_ref[total:, :] = jnp.zeros((RIM, wide), jnp.float32)
    dw_ref[:, :wide] = tn_dot(bext_ref[:tokens, :], cm_ref[...]).astype(jnp.bfloat16)
    for low, high in halves_of(total):
        grad_ref[low:high, :] = nt_dot(bext_ref[low:high, :], pm_ref[...])
        up_ref[low:high, :] = nn_dot(cle_ref[low:high, :], pl_ref[...])
        back_ref[low:high, :narrow] = nn_dot(cre_ref[low:high, :], pr_ref[...])

    kept_copy.wait()
    for chunk in seconds:
        at = (chunk - first_count) * step
        share.core_copy(chunk, second_ref, chunk - first_count).wait_recv()
        share.run_side(chunk, kept_ref[:, :, at : at + step])

    def merge_rows(rows):
        pre = up_ref[rows, :]
        merged = pre / (1.0 + jnp.exp(-pre))
        merged = jnp.concatenate([merged[:, :narrow] + back_ref[rows, :narrow], merged[:, narrow:]], 1)
        normed, inverse = rows_normed(merged)
        normed_ref[rows, :] = normed
        inv_ref[rows, :] = wide_rows(inverse)

    loop_rows(total, MERGE_ROWS, merge_rows)

    def mid_back(group, carry):
        lanes = group_lanes(group)
        weights = [tm_ref[j : j + 1, lanes] for j in range(tm_ref.shape[0])]
        sums = [None] * len(weights)
        gain_vec = mgain_ref[:, lanes]
        for low, high in row_tiles(total, ROW_TILE):
            value = None
            if high <= tokens:
                value = (normed_ref[low:high, lanes] * gain_vec).astype(jnp.bfloat16).astype(jnp.float32)
            back_ref[low:high, lanes] = taps_back(
                grad_ref, value, wide_ref[low:high, :], lanes, low, high, weights, None, sums
            )
        for j, piece in enumerate(sums):
            dtm_ref[j : j + 1, lanes] = jnp.sum(piece, axis=0, keepdims=True)
        return carry

    lax.fori_loop(0, wide // 128, mid_back, 0)

    def merge_back(rows):
        pre = up_ref[rows, :]
        normed = normed_ref[rows, :]
        d_merged = rows_norm_back(normed, inv_ref[rows, :][:, :1], mgain_ref[...], back_ref[rows, :])
        sigma = 1.0 / (1.0 + jnp.exp(-pre))
        dpl_ref[rows, :] = (d_merged * (sigma * (1.0 + pre * (1.0 - sigma)))).astype(jnp.bfloat16)
        dpr_ref[rows, :] = d_merged[:, :narrow].astype(jnp.bfloat16)

    loop_rows(total, MERGE_ROWS, merge_back)
    for chunk in firsts:
        share.run_near_back(chunk)
    gain_sum = jnp.zeros((8, wide), jnp.float32)

    def gain_rows(k, held):
        rows = pl.ds(pl.multiple_of(k * 16, 16), 16)
        return held + folded(back_ref[rows, :] * normed_ref[rows, :])

    gain_sum = lax.fori_loop(0, tokens // 16, gain_rows, gain_sum)
    dmgain_ref[...] = jnp.sum(gain_sum, axis=0, keepdims=True)
    dw_ref[:, wide : 2 * wide] = tn_dot(cle_ref[:tokens, :], dpl_ref[:tokens, :]).astype(jnp.bfloat16)
    dw_ref[:, 2 * wide :] = tn_dot(cre_ref[:tokens, :], dpr_ref[:tokens, :]).astype(jnp.bfloat16)
    for low, high in halves_of(total):
        grad_ref[low:high, :width] = nt_dot(dpl_ref[low:high, :], pl_ref[...])
        grad_ref[low:high, width : 2 * width] = nt_dot(dpr_ref[low:high, :], pr_ref[...])

    def first_back(group, carry):
        lanes = group_lanes(group)
        other = group_lanes(group + width // 128)
        weights_l = [tl_ref[j : j + 1, lanes] for j in range(tl_ref.shape[0])]
        weights_r = [tr_ref[j : j + 1, lanes] for j in range(tr_ref.shape[0])]
        sums_l = [None] * len(weights_l)
        sums_r = [None] * len(weights_r)
        for low, high in row_tiles(tokens, ROW_TILE):
            left = wide_ref[low:high, :]
            value = a2f_ref[low:high, lanes]
            held = taps_back(grad_ref, value, left, lanes, low, high, weights_l, None, sums_l)
            held = taps_back(grad_ref, value, left, other, low, high, weights_r, held, sums_r)
            back_ref[low:high, lanes] = held
        for j, piece in enumerate(sums_l):
            dtl_ref[j : j + 1, lanes] = jnp.sum(piece, axis=0, keepdims=True)
        for j, piece in enumerate(sums_r):
            dtr_ref[j : j + 1, lanes] = jnp.sum(piece, axis=0, keepdims=True)
        return carry

    lax.fori_loop(0, width // 128, first_back, 0)

    def finish(k, held):
        rows = pl.ds(pl.multiple_of(k * 64, 64), 64)
        normed, inverse = rows_normed(h1_ref[rows, :])
        upstream = back_ref[rows, :width]
        g1_ref[rows, :] = g2_ref[rows, :] + rows_norm_back(normed, inverse, gain_ref[...], upstream)
        return held + folded(upstream * normed)

    gain_sum = lax.fori_loop(0, tokens // 64, finish, jnp.zeros((8, width), jnp.float32))
    dgain_ref[...] = jnp.sum(gain_sum, axis=0, keepdims=True)
    for chunk in firsts:
        share.run_last(chunk)
    for chunk in seconds:
        at = (chunk - first_count) * step
        across_out_ref[:, at : at + step] = share.side_sum(chunk, first_count)
        share.core_copy(chunk, second_ref, chunk - first_count).wait_send()
        share.sent_sides(chunk)
    for chunk in firsts:
        share.last_copy(chunk).wait_recv()
        share.sent_backs(chunk)


def conv_back(
    g2, brim, c_l, c_r, rims, c_m, a2, h1, left, taps_l, taps_r, taps_m, mid_gain, gain, proj_left, proj_right, proj_mid,
    mine, second,
):
    tokens, width = g2.shape
    wide, narrow = proj_left.shape[1], proj_right.shape[1]
    total = tokens + RIM
    low, full = jnp.bfloat16, jnp.float32
    seq_count, far_count = lax.axis_size("seq"), lax.axis_size("rows") // 4
    half = width // (2 * seq_count)
    step = 2 * far_count * LANE_GROUP
    first_count, second_count = mine.shape[0], second.shape[1] // step - 1
    count = first_count + second_count
    slots = seq_count + 1 + 2 * far_count
    in_hbm = pl.BlockSpec(memory_space=pl.ANY)
    dma = pltpu.SemaphoreType.DMA
    return pl.pallas_call(
        conv_bwd_kernel,
        out_shape=(
            jax.ShapeDtypeStruct((tokens, width), full),
            jax.ShapeDtypeStruct((width, 2 * wide + narrow), low),
            jax.ShapeDtypeStruct(taps_l.shape, full),
            jax.ShapeDtypeStruct(taps_r.shape, full),
            jax.ShapeDtypeStruct(taps_m.shape, full),
            jax.ShapeDtypeStruct((1, wide), full),
            jax.ShapeDtypeStruct((1, width), full),
            jax.ShapeDtypeStruct((2, half, first_count * step), low),
            jax.ShapeDtypeStruct((half, second_count * step), low),
        ),
        in_specs=[IN_VMEM] * 19 + [in_hbm],
        out_specs=(IN_VMEM,) * 7 + (in_hbm, IN_VMEM),
        scratch_shapes=[
            pltpu.VMEM((total, width), low),
            pltpu.VMEM((total, width), low),
            pltpu.VMEM((total, width), low),
            pltpu.VMEM((total, 128), jnp.int32),
            pltpu.VMEM((total + RIM, wide), full),
            pltpu.VMEM((total, wide), full),
            pltpu.VMEM((total, wide), full),
            pltpu.VMEM((total, wide), full),
            pltpu.VMEM((total, 128), full),
            pltpu.VMEM((total, wide), low),
            pltpu.VMEM((total, narrow), low),
            pltpu.VMEM((tokens, width), full),
            pltpu.VMEM((seq_count, half, second_count * step), low),
            pltpu.VMEM((second_count, seq_count, half, step), low),
            pltpu.VMEM((second_count, seq_count - 1, half, step), low),
            dma((count, slots)),
            dma((count, slots)),
            dma((first_count,)),
            dma(()),
        ],
        compiler_params=pltpu.CompilerParams(
            collective_id=1, has_side_effects=True, vmem_limit_bytes=HOST_VMEM
        ),
        cost_estimate=pl.CostEstimate(
            flops=tokens * width * wide * 40, bytes_accessed=tokens * width * 40, transcendentals=tokens * wide
        ),
        name="conv_bwd",
    )(
        g2, brim, c_l, rims[:, :width], c_r, rims[:, width:], c_m, a2, h1, left,
        taps_l, taps_r, taps_m, mid_gain, gain, proj_left, proj_right, proj_mid,
        mine, second.reshape(seq_count, 2, half, second.shape[1]),
    )


MIDDLE_VMEM = 60 * 2**20
DOT_ROWS = 256


def load_weight(copies, sems, target_ref, own_ref, pieces, each, offset, place, near, core):
    width, size = own_ref.shape
    half, quarter = width // 2, width // 4
    count = len(pieces) // each + 1
    columns = slice(offset, offset + size)
    parts = [(own_ref, place * width, width)]
    for d in range(1, count):
        source = lax.rem(place + d, count) * width
        same, *more = pieces[each * (d - 1) : each * d]
        if each == 2:
            parts.append((same.at[:, columns], source + core * half, half))
            parts.append((more[0].at[:, columns], source + (1 - core) * half, half))
            continue
        close, across = more
        parts.append((same.at[:, columns], source + (2 * near + core) * quarter, quarter))
        parts.append((close.at[:, columns], source + (2 - 2 * near + core) * quarter, quarter))
        parts.append((across.at[:quarter, columns], source + (2 * near + 1 - core) * quarter, quarter))
        parts.append((across.at[quarter:, columns], source + (3 - 2 * near - core) * quarter, quarter))
    for source_ref, start, rows in parts:
        copy = pltpu.make_async_copy(
            source_ref, target_ref.at[pl.ds(pl.multiple_of(start, quarter), rows), :], sems.at[len(copies)]
        )
        copy.start()
        copies.append(copy)
    return offset + size


def wait_for(copies):
    for copy in copies:
        copy.wait()


def norm_into(target_ref, source_ref, gain_vec):
    def body(rows):
        normed, _ = rows_normed(source_ref[rows, :])
        target_ref[rows, :] = (normed * gain_vec).astype(jnp.bfloat16)

    loop_rows(source_ref.shape[0], 128, body)


def norm_back_into(target_ref, base_ref, source_ref, gain_vec, upstream_ref):
    def body(k, held):
        rows = pl.ds(pl.multiple_of(k * 128, 128), 128)
        normed, inverse = rows_normed(source_ref[rows, :])
        upstream = upstream_ref[rows, :]
        target_ref[rows, :] = base_ref[rows, :].astype(jnp.float32) + rows_norm_back(
            normed, inverse, gain_vec, upstream
        )
        return held + folded(upstream * normed)

    held = jnp.zeros((8, source_ref.shape[1]), jnp.float32)
    return jnp.sum(lax.fori_loop(0, source_ref.shape[0] // 128, body, held), axis=0, keepdims=True)


def chunks(extent):
    return row_tiles(extent, DOT_ROWS)


def project_into(target_ref, weight_ref, turned_ref, low, high):
    for start, stop in chunks(high - low):
        target_ref[start:stop, :] = tn_dot(weight_ref[:, low + start : low + stop], turned_ref[...]).astype(jnp.bfloat16)


def store_grad(target_ref, start, values):
    target_ref[:, start : start + values.shape[1]] = values.astype(jnp.bfloat16)


def middle_kernel(
    piece_count,
    h2_ref, a3_ref, crow_ref, mem_ref, gout_ref, gain_ref, qseg_ref, kseg_ref, mseg_ref, down_ref,
    qkv_own, out2_own, query_own, kv_own, out_own, up_own, *rest,
):
    pieces, rest = rest[:piece_count], rest[piece_count:]
    up_pieces, rest = rest[: piece_count // 3 * 2], rest[piece_count // 3 * 2 :]
    (
        result_ref, g2_ref, brim_ref, crim_ref, dw_ref, dgain_ref, dmem_ref, mine_ref,
        wqkv_ref, wout2_ref, wquery_ref, wkv_ref, wout_ref, wup_ref, sems,
        turned_ref, memt_ref, a4_ref, a4t_ref, qt_ref, pair_ref, attc_ref, totalc_ref,
        qdt_ref, paird_ref, attd_ref, totald_ref, h3_ref, h4_ref, act_ref, dup_ref, low_ref, gt_ref, dq_ref, dpair_ref, dpaird_ref,
        back_ref, kmark_ref, mmark_ref, sum_ref, peak_ref, score_ref,
        dkh_ref, dvh_ref, dkm_ref, dvm_ref, dqh_ref, qrow_ref, grow_ref, weight_ref, slope_ref,
        first_ref, core_ref, across_ref, send_sem, recv_sem,
        close_ref, piece_ref, g3_ref, a3in_ref, da3_ref, da3in_ref, rim_ref, rimin_ref, crimin_ref, swap_send, swap_recv,
    ) = rest
    tokens, width = h2_ref.shape
    share = ShareSum(
        send_sem, recv_sem, core=core_ref, across=across_ref, close=close_ref, piece=piece_ref, mine=mine_ref
    )
    place, near, core = share.place, share.near, share.core
    share.enter([share.mate, share.close] + share.peers[1:] + share.sides[1:])
    seq_count = piece_count // 3 + 1

    def swap(kind, away, source, target):
        return pltpu.make_async_remote_copy(
            src_ref=source,
            dst_ref=target,
            send_sem=swap_send.at[kind, away - 1],
            recv_sem=swap_recv.at[kind, away - 1],
            device_id=share.sides[away],
            device_id_type=pl.DeviceIdType.MESH,
        )

    def ahead_swap(away):
        return swap(0, away, a3_ref, a3in_ref.at[away - 1])

    def behind_swap(away):
        return swap(1, away, da3_ref.at[away - 1], da3in_ref.at[away - 1])

    def rim_swap():
        return swap(2, seq_count - 1, rim_ref, rimin_ref)

    def conv_swap():
        return swap(3, seq_count - 1, crow_ref, crimin_ref)

    for away in range(1, seq_count):
        pl.when(place + away < seq_count)(ahead_swap(away).start)
    pl.when(place > 0)(conv_swap().start)
    crim_ref[...] = jnp.zeros_like(crim_ref)
    high_width = wup_ref.shape[1]
    first, copies = [], []
    offset = load_weight(first, sems.at[0], wqkv_ref, qkv_own, pieces, 3, 0, place, near, core)
    for target, own in ((wout2_ref, out2_own), (wquery_ref, query_own), (wkv_ref, kv_own), (wout_ref, out_own)):
        offset = load_weight(copies, sems.at[1], target, own, pieces, 3, offset, place, near, core)
    load_weight(copies, sems.at[1], wup_ref, up_own, up_pieces, 2, 0, place, near, core)

    own = pl.ds(pl.multiple_of(place * tokens, 128), tokens)
    turned_ref[:, own] = a3_ref[...].T
    memt_ref[...] = mem_ref[...].T
    wait_for(first)
    project_into(qt_ref, wqkv_ref, turned_ref.at[:, own], 0, width)
    project_into(pair_ref.at[:, own], wqkv_ref, turned_ref.at[:, own], width, 3 * width)

    def fetch():
        for away in range(1, seq_count):
            start = lax.rem(place + seq_count - away, seq_count) * tokens
            there = pl.ds(pl.multiple_of(start, 128), tokens)

            @pl.when(place >= away)
            def _():
                ahead_swap(away).wait_recv()
                turned_ref[:, there] = a3in_ref[away - 1].T
                project_into(pair_ref.at[:, there], wqkv_ref, turned_ref.at[:, there], width, 3 * width)

            @pl.when(place < away)
            def _():
                turned_ref[:, there] = jnp.zeros((width, tokens), jnp.bfloat16)

    attend_core(
        H_CROSS, True, place, qt_ref, pair_ref, qseg_ref, kseg_ref, attc_ref, totalc_ref, kmark_ref, sum_ref, peak_ref, score_ref,
        fetch,
    )
    wait_for(copies)
    for low, high in chunks(tokens):
        h3_ref[low:high, :] = h2_ref[low:high, :] + tn_dot(attc_ref[:, low:high], wout2_ref[...])
    norm_into(a4_ref, h3_ref, gain_ref[1:2, :])
    a4t_ref[...] = a4_ref[...].T
    project_into(qdt_ref, wquery_ref, a4t_ref, 0, width)
    project_into(paird_ref, wkv_ref, memt_ref, 0, 2 * width)
    attend_core(
        H_CROSS, False, 0, qdt_ref, paird_ref, qseg_ref, mseg_ref, attd_ref, totald_ref, mmark_ref, sum_ref, peak_ref, score_ref
    )
    for low, high in chunks(tokens):
        h4_ref[low:high, :] = h3_ref[low:high, :] + tn_dot(attd_ref[:, low:high], wout_ref[...])
    norm_into(a4_ref, h4_ref, gain_ref[2:3, :])

    for left, right in row_tiles(high_width, 512):
        for low, high in chunks(tokens):
            pre = nn_dot(a4_ref[low:high, :], wup_ref[:, left:right])
            sigma = 1.0 / (1.0 + jnp.exp(-pre))
            act_ref[low:high, left:right] = (pre * sigma).astype(jnp.bfloat16)
            slope = nt_dot(gout_ref[low:high, :], down_ref[left:right, :])
            dup_ref[low:high, left:right] = (slope * (sigma * (1.0 + pre * (1.0 - sigma)))).astype(jnp.bfloat16)
    for low, high in chunks(tokens):
        result_ref[low:high, :] = (h4_ref[low:high, :] + nn_dot(act_ref[low:high, :], down_ref[...])).astype(jnp.bfloat16)
        back_ref[low:high, :] = nt_dot(dup_ref[low:high, :], wup_ref[...])
    _, _, half, first_total = first_ref.shape
    firsts = range(first_total // share.step)

    def store_first(start, values):
        size = values.shape[1]
        first_ref[:, :, :, start : start + size] = values.astype(jnp.bfloat16).reshape(seq_count, 2, half, size)

    for left, right in row_tiles(high_width, 512):
        store_first(left, tn_dot(a4_ref[...], dup_ref[:, left:right]))
        store_first(high_width + left, tn_dot(gout_ref[...], act_ref[:, left:right]))

    for chunk in firsts:
        share.core_copy(chunk, first_ref, chunk).start()
    at = 0
    dgain_ref[2:3, :] = norm_back_into(h4_ref, gout_ref, h4_ref, gain_ref[2:3, :], back_ref)
    low_ref[...] = h4_ref[...].astype(jnp.bfloat16)
    store_grad(dw_ref, at, nn_dot(attd_ref[...], low_ref[...]))
    gt_ref[...] = nt_dot(wout_ref[...], low_ref[...]).astype(jnp.bfloat16)
    attend_back_core(
        H_CROSS, False, 0, qdt_ref, paird_ref, gt_ref, attd_ref, totald_ref, qseg_ref, mseg_ref,
        dq_ref, dpaird_ref, mmark_ref, dkm_ref, dvm_ref, dqh_ref, qrow_ref, grow_ref, weight_ref, slope_ref,
    )
    store_grad(dw_ref, at + width, nt_dot(a4t_ref[...], dq_ref[...]))
    store_grad(dw_ref, at + 2 * width, nt_dot(memt_ref[...], dpaird_ref[...]))
    for chunk in firsts:
        share.core_copy(chunk, first_ref, chunk).wait_recv()
        share.run_side(chunk, first_ref[:, core, :, chunk * share.step : (chunk + 1) * share.step])
    dmem_ref[...] = nn_dot(wkv_ref[...], dpaird_ref[...]).astype(jnp.bfloat16)
    back_ref[...] = nn_dot(wquery_ref[...], dq_ref[...]).T
    dgain_ref[1:2, :] = norm_back_into(g3_ref, h4_ref, h3_ref, gain_ref[1:2, :], back_ref)
    low_ref[...] = g3_ref[...].astype(jnp.bfloat16)
    at = at + 4 * width
    store_grad(dw_ref, at + 3 * width, nn_dot(attc_ref[...], low_ref[...]))
    gt_ref[...] = nt_dot(wout2_ref[...], low_ref[...]).astype(jnp.bfloat16)
    attend_back_core(
        H_CROSS, True, place, qt_ref, pair_ref, gt_ref, attc_ref, totalc_ref, qseg_ref, kseg_ref,
        dq_ref, dpair_ref, kmark_ref, dkh_ref, dvh_ref, dqh_ref, qrow_ref, grow_ref, weight_ref, slope_ref,
    )
    store_grad(dw_ref, at, nt_dot(turned_ref[:, own], dq_ref[...]))
    for low, high in chunks(2 * width):
        store_grad(dw_ref, at + width + low, nt_dot(turned_ref[...], dpair_ref[low:high, :]))
    for chunk in firsts:
        share.run_near(chunk)
    for away in [*range(1, seq_count), 0]:
        start = lax.rem(place + away, seq_count) * tokens
        for low, high in row_tiles(tokens, DOT_ROWS):
            lanes = pl.ds(pl.multiple_of(start + low, 128), high - low)
            upstream = nn_dot(wqkv_ref[:, width:], dpair_ref[:, lanes])
            if away == 0:
                back_ref[low:high, :] = (upstream + nn_dot(wqkv_ref[:, :width], dq_ref[:, low:high])).T
            else:
                da3_ref[away - 1, low:high, :] = upstream.T.astype(jnp.bfloat16)
        if away:
            pl.when(place + away >= seq_count)(behind_swap(away).start)
    for chunk in firsts:
        share.run_peer(chunk)
    for away in range(1, seq_count):

        @pl.when(place < away)
        def _():
            behind_swap(away).wait_recv()
            back_ref[...] += da3in_ref[away - 1].astype(jnp.float32)

    dgain_ref[0:1, :] = norm_back_into(g2_ref, g3_ref, h2_ref, gain_ref[0:1, :], back_ref)
    rim_ref[...] = g2_ref[:RIM, :].astype(jnp.bfloat16)
    pl.when(place > 0)(rim_swap().start)
    brim_ref[...] = jnp.zeros_like(brim_ref)
    for chunk in firsts:
        share.peer_sum(chunk)

    @pl.when(place < seq_count - 1)
    def _():
        rim_swap().wait_recv()
        brim_ref[...] = rimin_ref[...]
        conv_swap().wait_recv()
        crim_ref[...] = crimin_ref[...]

    pl.when(place > 0)(rim_swap().wait_send)
    pl.when(place > 0)(conv_swap().wait_send)
    for away in range(1, seq_count):
        pl.when(place + away < seq_count)(ahead_swap(away).wait_send)
        pl.when(place + away >= seq_count)(behind_swap(away).wait_send)
    for chunk in firsts:
        share.core_copy(chunk, first_ref, chunk).wait_send()
        share.sent_sides(chunk)
        share.near_copy(chunk).wait_send()
        share.sent_peers(chunk)


def middle(h2, a3, conv_rows, mem_rows, grad_out, gains, own_seg, seg_row, mem_seg, down, owns, pieces, up_pieces):
    tokens, width = h2.shape
    keys, mems = seg_row.shape[0], mem_seg.shape[0]
    high_width = down.shape[0]
    seq_count = keys // tokens
    size = width // H_CROSS
    low, full = jnp.bfloat16, jnp.float32
    longest = max(tokens, mems)
    v = pltpu.VMEM
    in_hbm = pl.BlockSpec(memory_space=pl.ANY)
    half = width // (2 * seq_count)
    step = lax.axis_size("rows") // 2 * LANE_GROUP
    count = 2 * high_width // step
    far_count = lax.axis_size("rows") // 4
    slots = seq_count + far_count
    dma = pltpu.SemaphoreType.DMA
    return pl.pallas_call(
        functools.partial(middle_kernel, len(pieces)),
        out_shape=(
            jax.ShapeDtypeStruct((tokens, width), low),
            jax.ShapeDtypeStruct((tokens, width), full),
            jax.ShapeDtypeStruct((RIM, width), low),
            jax.ShapeDtypeStruct((RIM, 2 * width), low),
            jax.ShapeDtypeStruct((width, 8 * width), low),
            jax.ShapeDtypeStruct((3, width), full),
            jax.ShapeDtypeStruct((width, mems), low),
            jax.ShapeDtypeStruct((count, half, LANE_GROUP), low),
        ),
        in_specs=[IN_VMEM] * 10 + [in_hbm] * (6 + len(pieces) + len(up_pieces)),
        out_specs=(IN_VMEM,) * 8,
        scratch_shapes=[
            v((width, 3 * width), low),
            v((width, width), low),
            v((width, width), low),
            v((width, 2 * width), low),
            v((width, width), low),
            v((width, high_width), low),
            pltpu.SemaphoreType.DMA((2, 5 * (4 * seq_count - 3))),
            v((width, keys), low),
            v((width, mems), low),
            v((tokens, width), low),
            v((width, tokens), low),
            v((width, tokens), low),
            v((2 * width, keys), low),
            v((width, tokens), low),
            v((H_CROSS, 1, tokens), full),
            v((width, tokens), low),
            v((2 * width, mems), low),
            v((width, tokens), low),
            v((H_CROSS, 1, tokens), full),
            v((tokens, width), full),
            v((tokens, width), full),
            v((tokens, high_width), low),
            v((tokens, high_width), low),
            v((tokens, width), low),
            v((width, tokens), low),
            v((width, tokens), low),
            v((2 * width, keys), low),
            v((2 * width, mems), low),
            v((tokens, width), full),
            v((SEG_ROWS, keys), low),
            v((SEG_ROWS, mems), low),
            v((H_CROSS, size + SEG_ROWS, tokens), full),
            v((H_CROSS, 1, tokens), full),
            v((2, longest, TILE), full),
            v((BWD_HEADS, size, keys), full),
            v((BWD_HEADS, size, keys), full),
            v((BWD_HEADS, size, mems), full),
            v((BWD_HEADS, size, mems), full),
            v((BWD_HEADS, size, tokens), full),
            v((BWD_HEADS, size + SEG_ROWS, tokens), low),
            v((BWD_HEADS, size + SEG_ROWS, tokens), low),
            v((2, longest, TILE), low),
            v((2, longest, TILE), low),
            v((seq_count, 2, half, 2 * high_width), low),
            v((count, seq_count, half, step), low),
            v((count, seq_count - 1, half, step), low),
            dma((count, slots)),
            dma((count, slots)),
            v((count, half, step // 2), low),
            v((count, far_count - 1, half, LANE_GROUP), low),
            v((tokens, width), full),
            v((seq_count - 1, tokens, width), low),
            v((seq_count - 1, tokens, width), low),
            v((seq_count - 1, tokens, width), low),
            v((RIM, width), low),
            v((RIM, width), low),
            v((RIM, 2 * width), low),
            dma((4, seq_count - 1)),
            dma((4, seq_count - 1)),
        ],
        compiler_params=pltpu.CompilerParams(
            collective_id=0, has_side_effects=True, vmem_limit_bytes=HOST_VMEM
        ),
        cost_estimate=pl.CostEstimate(
            flops=tokens * width * width * 200, bytes_accessed=tokens * width * 40, transcendentals=tokens * width * 20
        ),
        name="middle",
    )(
        h2, a3, conv_rows, mem_rows, grad_out, gains, own_seg[None], seg_row[None], mem_seg[None], down,
        *owns, *pieces, *up_pieces,
    )


class ShareSum:
    def __init__(self, send_sem, recv_sem, core=None, across=None, close=None, piece=None, mine=None, out=None, local_sem=None):
        self.send_sem, self.recv_sem, self.local_sem = send_sem, recv_sem, local_sem
        self.core_ref, self.across_ref, self.close_ref = core, across, close
        self.piece_ref, self.mine_ref, self.out_ref = piece, mine, out
        self.seq_count = lax.axis_size("seq")
        self.far_count = lax.axis_size("rows") // 4
        row, place = lax.axis_index("rows"), lax.axis_index("seq")
        self.core, self.near, self.far, self.place = lax.rem(row, 2), lax.rem(row // 2, 2), row // 4, place
        self.mate = (row + 1 - 2 * self.core, place)
        self.close = (row + 2 - 4 * self.near, place)
        self.peers = [None] + [
            (lax.rem(self.far + d, self.far_count) * 4 + self.near * 2 + self.core, place)
            for d in range(1, self.far_count)
        ]
        self.sides = [None] + [(row, lax.rem(place + d, self.seq_count)) for d in range(1, self.seq_count)]
        self.step = 2 * self.far_count * LANE_GROUP
        self.wide = self.far_count * LANE_GROUP
        self.core_first = 0
        self.early_sums = {}

    def enter(self, friends):
        barrier = pltpu.get_barrier_semaphore()
        for friend in friends:
            pl.semaphore_signal(barrier, inc=1, device_id=friend, device_id_type=pl.DeviceIdType.MESH)
        pl.semaphore_wait(barrier, len(friends))

    def columns(self, chunk):
        return pl.ds(pl.multiple_of(chunk * self.step, LANE_GROUP), self.step)

    def copy(self, chunk, slot, source, target, device):
        return pltpu.make_async_remote_copy(
            src_ref=source,
            dst_ref=target,
            send_sem=self.send_sem.at[chunk, slot],
            recv_sem=self.recv_sem.at[chunk, slot],
            device_id=device,
            device_id_type=pl.DeviceIdType.MESH,
        )

    def core_copy(self, chunk, source_ref, at):
        return self.copy(chunk, 0, source_ref.at[:, 1 - self.core, :, self.columns(at)], self.core_ref.at[chunk - self.core_first], self.mate)

    def side_copy(self, chunk, d):
        away = lax.rem(self.place + d, self.seq_count)
        return self.copy(chunk, d, self.core_ref.at[chunk - self.core_first, away], self.across_ref.at[chunk - self.core_first, d - 1], self.sides[d])

    def sum_at(self, chunk):
        if chunk in self.early_sums:
            return self.early_sums[chunk]
        return self.across_ref.at[chunk - self.core_first, 0]

    def near_copy(self, chunk):
        lanes = pl.ds(pl.multiple_of((1 - self.near) * self.wide, LANE_GROUP), self.wide)
        return self.copy(
            chunk, self.seq_count, self.sum_at(chunk).at[:, lanes], self.close_ref.at[chunk], self.close
        )

    def peer_copy(self, chunk, d):
        away = lax.rem(self.far + d, self.far_count)
        lanes = pl.ds(pl.multiple_of(away * LANE_GROUP, LANE_GROUP), LANE_GROUP)
        return self.copy(
            chunk, self.seq_count + d, self.close_ref.at[chunk, :, lanes], self.piece_ref.at[chunk, d - 1], self.peers[d]
        )

    def own_lanes(self, chunk):
        start = chunk * self.step + self.near * self.wide + self.far * LANE_GROUP
        return pl.ds(pl.multiple_of(start, LANE_GROUP), LANE_GROUP)

    def keep_copy(self, chunk):
        return pltpu.make_async_copy(
            self.mine_ref.at[chunk], self.out_ref.at[self.core, :, self.own_lanes(chunk)], self.local_sem.at[chunk]
        )

    def back_copy(self, chunk, d):
        return self.copy(
            chunk,
            self.seq_count + self.far_count - 1 + d,
            self.mine_ref.at[chunk],
            self.out_ref.at[self.core, :, self.own_lanes(chunk)],
            self.peers[d],
        )

    def near_back(self, chunk):
        start = pl.multiple_of(chunk * self.step + self.near * self.wide, LANE_GROUP)
        block = self.out_ref.at[self.core, :, pl.ds(start, self.wide)]
        return self.copy(chunk, self.seq_count + 2 * self.far_count - 1, block, block, self.close)

    def last_copy(self, chunk):
        block = self.out_ref.at[self.core, :, self.columns(chunk)]
        return self.copy(chunk, self.seq_count + 2 * self.far_count, block, block, self.mate)

    def run_side(self, chunk, kept):
        at = chunk - self.core_first
        self.core_ref[at] = (kept.astype(jnp.float32) + self.core_ref[at].astype(jnp.float32)).astype(jnp.bfloat16)
        for d in range(1, self.seq_count):
            self.side_copy(chunk, d).start()

    def side_sum(self, chunk, first=0):
        for d in range(1, self.seq_count):
            self.side_copy(chunk, d).wait_recv()
        summed = self.core_ref[chunk - first, self.place].astype(jnp.float32)
        for d in range(1, self.seq_count):
            summed = summed + self.across_ref[chunk - first, d - 1].astype(jnp.float32)
        return summed.astype(jnp.bfloat16)

    def run_near(self, chunk):
        self.sum_at(chunk)[...] = self.side_sum(chunk, self.core_first)
        self.near_copy(chunk).start()

    def run_peer(self, chunk):
        self.near_copy(chunk).wait_recv()
        lanes = pl.ds(pl.multiple_of(self.near * self.wide, LANE_GROUP), self.wide)
        summed = self.sum_at(chunk)[:, lanes].astype(jnp.float32) + self.close_ref[chunk].astype(jnp.float32)
        self.close_ref[chunk] = summed.astype(jnp.bfloat16)
        for d in range(1, self.far_count):
            self.peer_copy(chunk, d).start()

    def peer_sum(self, chunk):
        for d in range(1, self.far_count):
            self.peer_copy(chunk, d).wait_recv()
        lanes = pl.ds(pl.multiple_of(self.far * LANE_GROUP, LANE_GROUP), LANE_GROUP)
        summed = self.close_ref[chunk, :, lanes].astype(jnp.float32)
        for d in range(1, self.far_count):
            summed = summed + self.piece_ref[chunk, d - 1].astype(jnp.float32)
        self.mine_ref[chunk] = summed.astype(jnp.bfloat16)

    def run_back(self, chunk):
        self.peer_sum(chunk)
        self.start_back(chunk)

    def start_back(self, chunk):
        self.keep_copy(chunk).start()
        for d in range(1, self.far_count):
            self.back_copy(chunk, d).start()

    def run_near_back(self, chunk):
        self.keep_copy(chunk).wait()
        for d in range(1, self.far_count):
            self.back_copy(chunk, d).wait_recv()
        self.near_back(chunk).start()

    def run_last(self, chunk):
        self.near_back(chunk).wait_recv()
        self.last_copy(chunk).start()

    def sent_sides(self, chunk):
        for d in range(1, self.seq_count):
            self.side_copy(chunk, d).wait_send()

    def sent_peers(self, chunk):
        for d in range(1, self.far_count):
            self.peer_copy(chunk, d).wait_send()

    def sent_backs(self, chunk):
        for d in range(1, self.far_count):
            self.back_copy(chunk, d).wait_send()
        self.near_back(chunk).wait_send()
        self.last_copy(chunk).wait_send()


def closing_kernel(
    g1_ref, rows_ref, memt_ref, gain_ref, atta_ref, totala_ref, qa_ref, paira_far,
    attb_ref, totalb_ref, qb_ref, pairb_ref, dmem_ref, gtwo_ref, glate_ref, dtl_ref, dtr_ref, dmg_ref, dtm_ref, qseg_ref, kseg_ref, mseg_ref,
    wqkv_far, wquery_ref, wkv_ref, wout_ref, across_in_ref, second_ref, conv_ref,
    grad_in_ref, grad_mem_ref, out_ref,
    turned_ref, branch_ref, gt_ref, dqa_ref, dqb_ref, dpaira_ref, dpairb_ref, kmark_ref, mmark_ref,
    dkh_ref, dvh_ref, dkm_ref, dvm_ref, dqh_ref, qrow_ref, grow_ref, weight_ref, slope_ref,
    late_ref, core_ref, across_ref, close_ref, piece_ref, mine_ref,
    send_sem, recv_sem, local_sem, conv_sem,
    da1_ref, da1_in_ref, upstream_ref, dmemory_ref, dmemory_in_ref, swap_send, swap_recv, small_ref,
    paira_ref, wqkv_ref, far_sem,
):
    tokens, width = g1_ref.shape
    keys = rows_ref.shape[0]
    place = lax.axis_index("seq")
    seq_count, _, half, conv_size = conv_ref.shape
    share = ShareSum(
        send_sem, recv_sem, core=core_ref, across=across_ref, close=close_ref, piece=piece_ref, mine=mine_ref,
        out=out_ref, local_sem=local_sem,
    )
    step = share.step
    second_count = early_count = across_in_ref.shape[1] // step
    count = out_ref.shape[-1] // step
    extra = second_ref.shape[-1] - second_count * step
    conv_end = extra + conv_size
    middle_count = (conv_end + 5 * width + step - 1) // step
    last_count = count - early_count - middle_count
    share.core_first = early_count
    share.enter([share.mate, share.close] + share.peers[1:] + share.sides[1:])
    late_copies = (
        pltpu.make_async_copy(second_ref.at[:, :, :, second_count * step :], late_ref.at[:, :, :, :extra], conv_sem.at[0]),
        pltpu.make_async_copy(conv_ref, late_ref.at[:, :, :, extra:conv_end], conv_sem.at[1]),
    )
    for copy in late_copies:
        copy.start()
    far_copies = (
        pltpu.make_async_copy(paira_far, paira_ref, far_sem.at[0]),
        pltpu.make_async_copy(wqkv_far, wqkv_ref, far_sem.at[1]),
    )
    for copy in far_copies:
        copy.start()
    seconds = range(early_count)
    middles = range(early_count, early_count + middle_count)
    lasts = range(early_count + middle_count, count)
    for chunk in seconds:
        at = chunk * step
        share.early_sums[chunk] = across_in_ref.at[:, at : at + step]
        share.near_copy(chunk).start()

    def store_late(start, values):
        size = values.shape[1]
        late_ref[:, :, :, start : start + size] = values.astype(jnp.bfloat16).reshape(seq_count, 2, half, size)

    def start_late(chunk):
        share.core_copy(chunk, late_ref, chunk - early_count).start()

    def side_late(chunk):
        at = (chunk - early_count) * step
        share.core_copy(chunk, late_ref, chunk - early_count).wait_recv()
        share.run_side(chunk, late_ref[:, share.core, :, at : at + step])

    done = {}

    def advance(chunk):
        stages = (share.run_near, share.run_peer, share.run_back, share.run_near_back, share.run_last)
        stages[done.setdefault(chunk, 1 if chunk in seconds else 0)](chunk)
        done[chunk] += 1

    def advance_all(*groups):
        for group in groups:
            for chunk in group:
                advance(chunk)

    own = pl.ds(pl.multiple_of(place * tokens, 128), tokens)
    ready = conv_end // step
    with_out = (conv_end + 2 * width) // step
    branch_ref[...] = g1_ref[...].astype(jnp.bfloat16).T
    for copy in late_copies:
        copy.wait()
    for chunk in middles[:ready]:
        start_late(chunk)
    store_late(conv_end, nt_dot(branch_ref[...], atta_ref[...]))
    store_late(conv_end + width, nt_dot(branch_ref[...], attb_ref[...]))
    for chunk in middles[ready:with_out]:
        start_late(chunk)
    for chunk in middles[:ready]:
        side_late(chunk)
    gt_ref[...] = nn_dot(wout_ref[width:, :], branch_ref[...]).astype(jnp.bfloat16)
    for low, high in row_tiles(keys, 128):
        normed, _ = rows_normed(rows_ref[low:high, :].astype(jnp.float32))
        turned_ref[:, low:high] = (normed * gain_ref[...]).astype(jnp.bfloat16).T
    for chunk in middles[ready:with_out]:
        side_late(chunk)
    advance_all(seconds[:1])
    attend_back_core(
        H_CROSS, False, 0, qb_ref, pairb_ref, gt_ref, attb_ref, totalb_ref, qseg_ref, mseg_ref,
        dqb_ref, dpairb_ref, mmark_ref, dkm_ref, dvm_ref, dqh_ref, qrow_ref, grow_ref, weight_ref, slope_ref,
    )
    advance_all(seconds[1:])
    at = conv_end + 2 * width
    store_late(at, nt_dot(memt_ref[...], dpairb_ref[...]))
    store_late(at + 2 * width, nt_dot(turned_ref[:, own], dqb_ref[...]))
    at = at + 3 * width
    after = middle_count * step
    if at < after:
        late_ref[:, :, :, at:after] = jnp.zeros((seq_count, 2, half, after - at), jnp.bfloat16)
    for chunk in middles[with_out:]:
        start_late(chunk)
    dmemory_ref[...] = (dmem_ref[...].astype(jnp.float32) + nn_dot(wkv_ref[...], dpairb_ref[...])).T.astype(jnp.bfloat16)
    gt_ref[...] = nn_dot(wout_ref[:width, :], branch_ref[...]).astype(jnp.bfloat16)

    def first_pump():
        advance_all(middles[:1], seconds[:1])
        for chunk in middles[with_out:]:
            side_late(chunk)

    def second_pump():
        advance_all(seconds, reversed(middles[:2]))

    def third_pump():
        advance_all(seconds, reversed(middles[:3]))

    def fourth_pump():
        advance_all(seconds[1:], reversed(middles[:4]))

    def pump(k):
        for at, action in enumerate((first_pump, second_pump, third_pump, fourth_pump)):
            pl.when(k == at)(action)

    for copy in far_copies:
        copy.wait()
    attend_back_core(
        H_SELF, True, place, qa_ref, paira_ref, gt_ref, atta_ref, totala_ref, qseg_ref, kseg_ref,
        dqa_ref, dpaira_ref, kmark_ref, dkh_ref, dvh_ref, dqh_ref, qrow_ref, grow_ref, weight_ref, slope_ref, pump,
    )
    entered = [len(middles[:4])]
    flow = list(middles) + list(lasts)

    def tick():
        newest = flow[entered[0] : entered[0] + 1]
        older = [chunk for chunk in flow[: entered[0]] if done[chunk] < 5]
        advance_all(newest, reversed(older))
        entered[0] += 1

    store_late(after, nt_dot(turned_ref[:, own], dqa_ref[...]))
    for low, high in chunks(2 * width):
        store_late(after + width + low, nt_dot(turned_ref[...], dpaira_ref[low:high, :]))
    start_late(lasts[0])
    tick()
    side_late(lasts[0])
    gain_sum = jnp.zeros((8, width), jnp.float32)
    for away in [*range(1, seq_count), 0]:
        start = lax.rem(place + away, seq_count) * tokens
        if away == 0:
            tick()
        for low, high in row_tiles(tokens, 128):
            lanes = pl.ds(pl.multiple_of(start + low, 128), high - low)
            upstream = nn_dot(wqkv_ref[:, width:], dpaira_ref[:, lanes])
            if away == 0:
                upstream = upstream + nn_dot(wqkv_ref[:, :width], dqa_ref[:, low:high])
                upstream = upstream + nn_dot(wquery_ref[...], dqb_ref[:, low:high])
            upstream = upstream.T
            normed, _ = rows_normed(rows_ref[lanes, :].astype(jnp.float32))
            gain_sum = gain_sum + folded(upstream * normed)
            if away == 0:
                upstream_ref[low:high, :] = upstream
            else:
                da1_ref[away - 1, low:high, :] = upstream.astype(jnp.bfloat16)

    def swap(kind, away, source, target):
        return pltpu.make_async_remote_copy(
            src_ref=source,
            dst_ref=target,
            send_sem=swap_send.at[kind, away - 1],
            recv_sem=swap_recv.at[kind, away - 1],
            device_id=share.sides[away],
            device_id_type=pl.DeviceIdType.MESH,
        )

    mem_own = dmemory_in_ref.shape[1]

    def row_swap(away):
        return swap(0, away, da1_ref.at[away - 1], da1_in_ref.at[away - 1])

    def mem_swap(away):
        start = pl.multiple_of(lax.rem(place + away, seq_count) * mem_own, mem_own)
        return swap(1, away, dmemory_ref.at[pl.ds(start, mem_own), :], dmemory_in_ref.at[away - 1])

    def start_swaps():
        for away in range(1, seq_count):
            pl.when(place + away >= seq_count)(row_swap(away).start)
            mem_swap(away).start()

    def finish_swaps():
        for away in range(1, seq_count):

            @pl.when(place < away)
            def _():
                row_swap(away).wait_recv()
                upstream_ref[...] += da1_in_ref[away - 1].astype(jnp.float32)

        own_start = pl.multiple_of(place * tokens, 128)
        for low, high in row_tiles(tokens, 128):
            values = rows_ref[pl.ds(pl.multiple_of(own_start + low, 128), high - low), :].astype(jnp.float32)
            normed, inverse = rows_normed(values)
            grad_in_ref[low:high, :] = g1_ref[low:high, :] + rows_norm_back(
                normed, inverse, gain_ref[...], upstream_ref[low:high, :]
            )
        total = dmemory_ref[pl.ds(pl.multiple_of(place * mem_own, mem_own), mem_own), :].astype(jnp.float32)
        for away in range(1, seq_count):
            mem_swap(away).wait_recv()
            total = total + dmemory_in_ref[away - 1].astype(jnp.float32)
        grad_mem_ref[...] = total
        for away in range(1, seq_count):
            pl.when(place + away >= seq_count)(row_swap(away).wait_send)
            mem_swap(away).wait_send()

    small_ref[...] = jnp.zeros_like(small_ref)
    small_ref[0:1, :] = jnp.sum(gain_sum, axis=0, keepdims=True)
    part = width // seq_count
    at = 1
    for source_ref in (gtwo_ref, glate_ref, dtl_ref, dtr_ref, dmg_ref, dtm_ref):
        for row in range(source_ref.shape[0]):
            span = source_ref.shape[1] // seq_count
            for start in range(0, span, part):
                for side in range(seq_count):
                    small_ref[at : at + 1, side * part : (side + 1) * part] = source_ref[
                        row : row + 1, side * span + start : side * span + start + part
                    ]
                at = at + 1
    at = after + 3 * width
    store_late(at, small_ref[...].T)
    at = at + small_ref.shape[0]
    if at < late_ref.shape[-1]:
        late_ref[:, :, :, at:] = jnp.zeros((seq_count, 2, half, late_ref.shape[-1] - at), jnp.bfloat16)
    for chunk in lasts[1:]:
        start_late(chunk)
    for chunk in lasts[1:]:
        side_late(chunk)
    start_swaps()
    ticks = 0
    while any(done.get(chunk, 0) < 5 for chunk in flow):
        tick()
        ticks += 1
        if ticks == SWAP_TICK:
            finish_swaps()
    for chunk in range(count):
        share.last_copy(chunk).wait_recv()
        share.sent_backs(chunk)
    for chunk in range(count):
        share.near_copy(chunk).wait_send()
        share.sent_peers(chunk)
    for chunk in range(early_count, count):
        share.core_copy(chunk, late_ref, chunk - early_count).wait_send()
        share.sent_sides(chunk)


def closing(
    g1, row_inputs, mem_turned, gain, self_kept, cross_kept, d_mem, small_grads, own_seg, seg_row, mem_seg,
    qkv, query, pairs_weight, out, across, second, conv,
):
    tokens, width = g1.shape
    keys, mems = row_inputs.shape[0], mem_turned.shape[1]
    seq_count = keys // tokens
    half = width // (2 * seq_count)
    far_count = lax.axis_size("rows") // 4
    step = 2 * far_count * LANE_GROUP
    size = width // H_CROSS
    middle_total = second.shape[1] - across.shape[1] + conv.shape[1] + 5 * width
    middle_total = middle_total + -middle_total % step
    last_total = 3 * width + 128
    last_total = last_total + -last_total % step
    early_total = across.shape[1]
    late = middle_total + last_total
    count = (early_total + late) // step
    slots = 3 + (seq_count - 1) + 2 * far_count
    low, full = jnp.bfloat16, jnp.float32
    longest = max(tokens, mems)
    v = pltpu.VMEM
    in_hbm = pl.BlockSpec(memory_space=pl.ANY)
    dma = pltpu.SemaphoreType.DMA
    grad_in, grad_mem, share = pl.pallas_call(
        closing_kernel,
        out_shape=(
            jax.ShapeDtypeStruct((tokens, width), full),
            jax.ShapeDtypeStruct((mems // seq_count, width), full),
            jax.ShapeDtypeStruct((2, half, early_total + late), low),
        ),
        in_specs=[IN_VMEM] * 7 + [in_hbm] + [IN_VMEM] * 14 + [in_hbm] + [IN_VMEM] * 4 + [in_hbm] * 2,
        out_specs=(IN_VMEM, IN_VMEM, in_hbm),
        scratch_shapes=[
            v((width, keys), low),
            v((width, tokens), low),
            v((width, tokens), low),
            v((width, tokens), low),
            v((width, tokens), low),
            v((2 * width, keys), low),
            v((2 * width, mems), low),
            v((SEG_ROWS, keys), low),
            v((SEG_ROWS, mems), low),
            v((BWD_HEADS, width // H_SELF, keys), full),
            v((BWD_HEADS, width // H_SELF, keys), full),
            v((BWD_HEADS, size, mems), full),
            v((BWD_HEADS, size, mems), full),
            v((BWD_HEADS, size, tokens), full),
            v((BWD_HEADS, size + SEG_ROWS, tokens), low),
            v((BWD_HEADS, size + SEG_ROWS, tokens), low),
            v((2, longest, TILE), low),
            v((2, longest, TILE), low),
            v((seq_count, 2, half, late), low),
            v((late // step, seq_count, half, step), low),
            v((late // step, seq_count - 1, half, step), low),
            v((count, half, step // 2), low),
            v((count, far_count - 1, half, LANE_GROUP), low),
            v((count, half, LANE_GROUP), low),
            dma((count, slots)),
            dma((count, slots)),
            dma((count,)),
            dma((2,)),
            v((seq_count - 1, tokens, width), low),
            v((seq_count - 1, tokens, width), low),
            v((tokens, width), full),
            v((mems, width), low),
            v((seq_count - 1, mems // seq_count, width), low),
            dma((2, seq_count - 1)),
            dma((2, seq_count - 1)),
            v((128, width), full),
            v((2 * width, keys), low),
            v((width, 3 * width), low),
            dma((2,)),
        ],
        compiler_params=pltpu.CompilerParams(
            collective_id=2, has_side_effects=True, vmem_limit_bytes=HOST_VMEM
        ),
        cost_estimate=pl.CostEstimate(
            flops=tokens * width * width * 200, bytes_accessed=tokens * width * 40, transcendentals=tokens * width * 20
        ),
        name="closing",
    )(
        g1, row_inputs, mem_turned, gain, *self_kept, *cross_kept, d_mem, *small_grads,
        own_seg[None], seg_row[None], mem_seg[None], qkv, query, pairs_weight, out,
        across, second.reshape(seq_count, 2, half, second.shape[1]), conv.reshape(seq_count, 2, half, conv.shape[1]),
    )
    return grad_in, grad_mem, share.reshape(2 * half, early_total + late), early_total + middle_total


def finishing_kernel(plan, small_at, first_ref, share_ref, *outs):
    first_total = first_ref.shape[1]
    for (offset, size, dim), out_ref in zip(plan, outs):
        source_ref, offset = (first_ref, offset) if offset < first_total else (share_ref, offset - first_total)
        if dim == 0:
            out_ref[...] = source_ref[:, offset : offset + size].astype(jnp.float32)
        else:
            for low, high in row_tiles(size, 256):
                out_ref[low:high, :] = source_ref[:, offset + low : offset + high].astype(jnp.float32).T
    small_at = small_at - first_total
    rows = share_ref[:, small_at : small_at + 128].astype(jnp.float32).T
    width = rows.shape[1]
    at = 0
    for out_ref in outs[len(plan) :]:
        for row in range(out_ref.shape[0]):
            for low in range(0, out_ref.shape[1], width):
                out_ref[row : row + 1, low : low + width] = rows[at : at + 1, :]
                at = at + 1


def finishing(first, share, plan, small_at, small_shapes):
    width = share.shape[0]
    shapes = [(width, size) if dim == 0 else (size, width) for _, size, dim in plan] + small_shapes
    return pl.pallas_call(
        functools.partial(finishing_kernel, plan, small_at),
        out_shape=tuple(jax.ShapeDtypeStruct(shape, jnp.float32) for shape in shapes),
        in_specs=[IN_VMEM] * 2,
        out_specs=(IN_VMEM,) * len(shapes),
        compiler_params=pltpu.CompilerParams(vmem_limit_bytes=KERNEL_VMEM),
        name="finishing",
    )(first, share)


def segment_reach(seg_row):
    length = seg_row.shape[0]
    first = jnp.sum(seg_row == 0)
    second = first + jnp.sum(seg_row == 1)
    spots = jnp.arange(length, dtype=jnp.int32)
    start = jnp.where(seg_row == 0, 0, jnp.where(seg_row == 1, first, second))
    stop = jnp.where(seg_row == 0, first, jnp.where(seg_row == 1, second, length))
    return spots - start, stop - 1 - spots


def turned_dot(weight, values):
    return jnp.einsum("kn,tk->nt", weight, values, preferred_element_type=jnp.float32)


def out_dot(turned, weight):
    return jnp.einsum("nt,nk->tk", turned, weight, preferred_element_type=jnp.float32)


def weight_dot(values, turned):
    return jnp.einsum("tk,nt->kn", values, turned, preferred_element_type=jnp.float32)


def out_weight_dot(turned, grads_in):
    return jnp.einsum("nt,tk->kn", turned, grads_in, preferred_element_type=jnp.float32)


def turned_back(grads_in, weight):
    return jnp.einsum("tk,nk->nt", grads_in, weight, preferred_element_type=jnp.float32)


def input_back(turned, weight):
    return jnp.einsum("nt,kn->tk", turned, weight, preferred_element_type=jnp.float32)


def local(
    hidden_in,
    memory,
    grad_out,
    seg_ids,
    mem_seg_ids,
    gains,
    qkv_first,
    query_cross,
    kv_cross,
    out_first,
    taps_left,
    proj_left,
    taps_right,
    proj_right,
    mid_gain,
    taps_mid,
    proj_mid,
    qkv_second,
    out_second,
    query_last,
    kv_last,
    out_last,
    ffn_up,
    ffn_down,
):
    shards = (
        gains,
        qkv_first,
        query_cross,
        kv_cross,
        out_first,
        taps_left,
        proj_left,
        taps_right,
        proj_right,
        mid_gain,
        taps_mid,
        proj_mid,
        qkv_second,
        out_second,
        query_last,
        kv_last,
        out_last,
        ffn_up,
        ffn_down,
    )
    shard_dims = (1, 0, 0, 0, 1, 1, 0, 1, 0, 0, 1, 1, 0, 0, 0, 0, 0, 0, 1)
    small = (0, 5, 7, 9, 10)
    seq_count = lax.axis_size("seq")

    def select(group):
        return [shards[k] for k in group], [shard_dims[k] for k in group]

    first_group, second_group, conv_group, middle_group = (1,), (2, 3, 4), (6, 8, 11), (12, 13, 14, 15, 16)
    up_group = (17, 18)
    hidden_more = seq_rotated(hidden_in[0])
    first_same = seq_rotated(packed_half(*select(first_group)))
    gains, taps_left, taps_right, mid_gain, taps_mid = small_gather(*select(small))
    first_other = [core_swapped(piece) for piece in first_same]
    (qkv_first,) = joined_group(*select(first_group), interleaved(first_same, first_other), 2)
    packed, _ = after((packed_half(*select(second_group)), memory[0], packed_quarter(*select(conv_group))), first_same)
    second_same, mem_more, conv_same = [seq_rotated(block) for block in packed]
    row_inputs = in_place_order([hidden_in[0]] + hidden_more, 0)
    mem_rows = in_place_order([memory[0]] + mem_more, 0)
    inputs = hidden_in[0].astype(jnp.float32)
    seg_row = seg_ids[0]
    mem_seg = mem_seg_ids[0]
    tok_count, model_width = inputs.shape
    row_start = lax.axis_index("seq") * tok_count
    own_seg = lax.dynamic_slice_in_dim(seg_row, row_start, tok_count)
    since, left = segment_reach(seg_row)
    since = lax.dynamic_slice_in_dim(jnp.pad(since, (RIM, 0)), row_start, tok_count + RIM)[:, None]
    left = lax.dynamic_slice_in_dim(jnp.pad(left, (0, RIM)), row_start, tok_count + RIM)[:, None]
    gain_rows = gains.astype(jnp.float32)
    mid_gain_f = mid_gain.astype(jnp.float32)
    left_taps = taps_left.astype(jnp.float32)
    right_taps = taps_right.astype(jnp.float32)
    mid_taps = taps_mid.astype(jnp.float32)
    normed_a = layer_norm(inputs, gain_rows[0]).astype(jnp.bfloat16)
    normed_row = layer_norm(row_inputs.astype(jnp.float32), gain_rows[0]).astype(jnp.bfloat16)
    queries = turned_dot(qkv_first[:, :model_width], normed_a).astype(jnp.bfloat16)
    packed, _ = after(packed_quarter(*select(middle_group)), queries)
    middle_same = seq_rotated(packed)
    pairs_a = turned_dot(qkv_first[:, model_width:], normed_row).astype(jnp.bfloat16)
    kept_a = attend_forward(queries, pairs_a, H_SELF, True, own_seg, seg_row) + (queries, pairs_a)
    att_a, (second_same, conv_same) = after(kept_a[0], (second_same, conv_same))
    second_other = [core_swapped(piece) for piece in second_same]
    kept_a = (att_a,) + kept_a[1:]
    conv_near = [near_swapped(piece) for piece in conv_same]
    query_cross, kv_cross, out_first = joined_group(*select(second_group), interleaved(second_same, second_other), 2)
    pairs_b = turned_dot(kv_cross, mem_rows).astype(jnp.bfloat16)
    query_b = turned_dot(query_cross, normed_a).astype(jnp.bfloat16)
    out_b, total_b = attend_forward(query_b, pairs_b, H_CROSS, False, own_seg, mem_seg)
    out_b, conv_near = after(out_b, conv_near)
    conv_across = [core_swapped(jnp.concatenate(pair, 0)) for pair in zip(conv_same, conv_near)]
    hidden_b = (
        inputs
        + out_dot(kept_a[0], out_first[:model_width])
        + out_dot(out_b, out_first[model_width:])
    )
    hidden_b, middle_same = after(hidden_b, middle_same)
    middle_near = [near_swapped(piece) for piece in middle_same]
    proj_left, proj_right, proj_mid = joined_group(
        *select(conv_group), interleaved(conv_same, conv_near, conv_across), 4
    )
    normed_c = layer_norm(hidden_b, gain_rows[1]).astype(jnp.bfloat16)
    rim = passed_along(normed_c[tok_count - RIM :], "seq", 1)
    packed, _ = after(packed_half(*select(up_group)), rim)
    up_same = seq_rotated(packed)
    conv_l, conv_r, conv_m, hidden_c, normed_d = conv_forward(
        hidden_b,
        normed_c,
        rim,
        since,
        left_taps,
        right_taps,
        mid_taps,
        mid_gain_f[None],
        gain_rows[2:3],
        proj_left,
        proj_right,
        proj_mid,
    )
    normed_d, middle_near = after(normed_d, middle_near)
    middle_across = [core_swapped(jnp.concatenate(pair, 0)) for pair in zip(middle_same, middle_near)]
    middle_pieces = interleaved(middle_same, middle_near, middle_across)
    normed_d, up_same = after(normed_d, up_same)
    up_other = [core_swapped(piece) for piece in up_same]
    up_pieces = interleaved(up_same, up_other)
    down, _ = joined_weight(shards[18], 1, up_pieces, shards[17].shape[1], 2)
    result, grad_now, brim, conv_rims, d_middle, d_gains_late, d_mem, mine = middle(
        hidden_c,
        normed_d,
        jnp.concatenate([conv_l[:RIM], conv_r[:RIM]], 1),
        mem_rows,
        grad_out[0],
        gain_rows[2:5],
        own_seg,
        seg_row,
        mem_seg,
        down,
        shards[12:18],
        middle_pieces,
        up_pieces,
    )
    grad_now, d_projections, d_taps_left, d_taps_right, d_taps_mid, d_mid_gain, g_two, first_share, across = conv_back(
        grad_now,
        brim,
        conv_l,
        conv_r,
        conv_rims,
        conv_m,
        normed_c,
        hidden_b,
        left,
        left_taps,
        right_taps,
        mid_taps,
        mid_gain_f[None],
        gain_rows[1:2],
        proj_left,
        proj_right,
        proj_mid,
        mine,
        d_middle,
    )
    wide, narrow = proj_left.shape[1], proj_right.shape[1]
    first_share = first_share.reshape(-1, first_share.shape[2])
    small_grads = (g_two, d_gains_late, d_taps_left, d_taps_right, d_mid_gain, d_taps_mid)
    grad_in, grad_mem, share, last_at = closing(
        grad_now,
        row_inputs,
        mem_rows.T,
        gain_rows[:1],
        kept_a[:4],
        (out_b, total_b, query_b, pairs_b),
        d_mem,
        small_grads,
        own_seg,
        seg_row,
        mem_seg,
        qkv_first,
        query_cross,
        kv_cross,
        out_first,
        across,
        d_middle,
        d_projections,
    )
    shares = [None] * len(shards)
    up = down.shape[0]
    plan, order, offset = [], (17, 18, 16, 14, 15, 12, 13, 11, 6, 8, 4, 3, 2, 1), 0
    for k, size in zip(
        order,
        (up, up, model_width, model_width, 2 * model_width, 3 * model_width, model_width)
        + (wide, wide, narrow, 2 * model_width, 2 * model_width, model_width, 3 * model_width),
    ):
        offset = last_at + first_share.shape[1] if k == 1 else offset
        plan.append((offset, size, shard_dims[k]))
        offset = offset + size
    small_shapes = [shards[k].shape if k != 9 else (1, shards[k].shape[0]) for k in small]
    found = finishing(first_share, share, plan, offset, small_shapes)
    for k, piece in zip(order + small, found):
        shares[k] = piece.reshape(shards[k].shape)
    return (
        result[None],
        grad_in[None],
        grad_mem[None],
        shares[0],
        shares[1],
        shares[2],
        shares[3],
        shares[4],
        shares[5],
        shares[6],
        shares[7],
        shares[8],
        shares[9],
        shares[10],
        shares[11],
        shares[12],
        shares[13],
        shares[14],
        shares[15],
        shares[16],
        shares[17],
        shares[18],
    )


def solution(mesh):
    placed = (
        P("rows", "seq", None),
        P("rows", "seq", None),
        P("rows", "seq", None),
        P("rows", None),
        P("rows", None),
        P(None, "seq"),
        P("seq", None),
        P("seq", None),
        P("seq", None),
        P(None, "seq"),
        P(None, "seq"),
        P("seq", None),
        P(None, "seq"),
        P("seq", None),
        P("seq"),
        P(None, "seq"),
        P(None, "seq"),
        P("seq", None),
        P("seq", None),
        P("seq", None),
        P("seq", None),
        P("seq", None),
        P("seq", None),
        P(None, "seq"),
    )
    return jax.shard_map(
        local,
        mesh=mesh,
        in_specs=placed,
        out_specs=(
            P("rows", "seq", None),
            P("rows", "seq", None),
            P("rows", "seq", None),
            P(None, "seq"),
            P("seq", None),
            P("seq", None),
            P("seq", None),
            P(None, "seq"),
            P(None, "seq"),
            P("seq", None),
            P(None, "seq"),
            P("seq", None),
            P("seq"),
            P(None, "seq"),
            P(None, "seq"),
            P("seq", None),
            P("seq", None),
            P("seq", None),
            P("seq", None),
            P("seq", None),
            P("seq", None),
            P(None, "seq"),
        ),
        check_vma=False,
    )
```
